32 devices in a mesh: rows: 8 (over y, x, core), batch: 4 (over z).
Axes of the slice: x: 2, y: 2, z: 4, core: 2. Of those that a mesh axis runs over, the one named last changes fastest.
Arguments:
- layer_input: bfloat16 [8, 128, 128, 256], P('batch', 'rows'), may hold values from -6 to 6
- hidden_state: bfloat16 [8, 128, 128, 256], P('batch', 'rows'), may hold values from -6 to 6
- crop_rows: int32 [8], P('batch'), may hold values from 113 to 128, as said below
- crop_cols: int32 [8], P('batch'), may hold values from 64 to 128, as said below
- first_gain: float32 [256], replicated, may hold values from 0.1 to 1.9
- first_shift: float32 [256], replicated, may hold values from -3 to 3
- qkv_weight: float32 [256, 768], P(('rows', 'batch')), may hold values from -0.375 to 0.375
- bias_table: float32 [225, 8], replicated, may hold values from -4 to 4
- output_weight: float32 [256, 256], P(('rows', 'batch')), may hold values from -1 to 1
- output_bias: float32 [256], replicated, may hold values from -3 to 3
- second_gain: float32 [256], replicated, may hold values from 0.1 to 1.9
- second_shift: float32 [256], replicated, may hold values from -3 to 3
- up_weight: float32 [256, 1024], P(('rows', 'batch')), may hold values from -0.375 to 0.375
- up_bias: float32 [1024], replicated, may hold values from -3 to 3
- down_weight: float32 [1024, 256], P(('rows', 'batch')), may hold values from -0.1875 to 0.1875
- down_bias: float32 [256], replicated, may hold values from -3 to 3
- conv_weight: float32 [4608, 256], P(('rows', 'batch')), may hold values from -0.09375 to 0.09375
- conv_bias: float32 [256], replicated, may hold values from -3 to 3
- cotangent: bfloat16 [8, 128, 128, 256], P('batch', 'rows'), may hold values from -6 to 6
Outputs:
- layer_output: bfloat16 [8, 128, 128, 256], P('batch', 'rows')
- input_grad: float32 [8, 128, 128, 256], P('batch', 'rows')
- hidden_grad: float32 [8, 128, 128, 256], P('batch', 'rows')
- first_gain_grad: float32 [256], replicated
- first_shift_grad: float32 [256], replicated
- qkv_weight_grad: float32 [256, 768], P(('rows', 'batch'))
- bias_table_grad: float32 [225, 8], replicated
- output_weight_grad: float32 [256, 256], P(('rows', 'batch'))
- output_bias_grad: float32 [256], replicated
- second_gain_grad: float32 [256], replicated
- second_shift_grad: float32 [256], replicated
- up_weight_grad: float32 [256, 1024], P(('rows', 'batch'))
- up_bias_grad: float32 [1024], replicated
- down_weight_grad: float32 [1024, 256], P(('rows', 'batch'))
- down_bias_grad: float32 [256], replicated
- conv_weight_grad: float32 [4608, 256], P(('rows', 'batch'))
- conv_bias_grad: float32 [256], replicated
The draws below stay inside these ranges and needn't reach their ends.
Inputs may be any that keep to these rules, and one draw needn't show every extreme that they name: `crop_rows`: every crop reaches into the last 16 rows of the grid; one crop of the batch has all 128 rows. `crop_cols`: some crop has all 128 columns.
All inputs are finite; a program needn't handle non-finite values.
Results may differ from the reference program's by a relative error of at most 0.012.
The reference program's roundings to bfloat16 on the way count: a program that leaves them out, or rounds other values in their place, can miss the bound.
Values may be sent and summed in bfloat16 or wider, within the bound.
No kernel may reach another device: no remote copies, remote signals or barrier semaphores. Data moves between devices by JAX's collectives and lax.ppermute only.
A program may use at most 320 MiB of HBM per device.

```python
import jax
import jax.numpy as jnp
from jax import lax

D = 256
FF = 1024
HEADS = 8
HEAD_DIM = 32
WIN = 8
RH = 16
W = 128
BATCH = 8
HEIGHT = 128
REL = 225


def draw_crop_rows(key, part):
    key = jax.random.fold_in(key, 11)
    first_key, second_key = jax.random.split(key)
    heights = jax.random.randint(first_key, (BATCH,), HEIGHT - RH + 1, HEIGHT + 1)
    chosen = jax.random.randint(second_key, (), 0, BATCH)
    heights = jnp.where(jnp.arange(BATCH) == chosen, HEIGHT, heights)
    return heights.astype(jnp.int32)


def draw_crop_cols(key, part):
    key = jax.random.fold_in(key, 23)
    first_key, second_key = jax.random.split(key)
    widths = jax.random.randint(first_key, (BATCH,), W // 2, W + 1)
    chosen = jax.random.randint(second_key, (), 0, BATCH)
    widths = jnp.where(jnp.arange(BATCH) == chosen, W, widths)
    return widths.astype(jnp.int32)


def shard_levels(key, shape, cuts, least, largest):
    loudness = 1.0
    for position, shards_of in cuts:
        steps = jax.random.uniform(jax.random.fold_in(jax.random.fold_in(key, 6), position), (shards_of,), jnp.float32, least / len(cuts), largest / len(cuts))
        loudness = loudness * jnp.repeat(jnp.exp(steps), shape[position] // shards_of).reshape((-1,) + (1,) * (len(shape) - 1 - position))
    return loudness


def normal_values(rng, extent, scale, bound, pieces=(), held_as=jnp.bfloat16):
    values = jax.random.normal(rng, extent, jnp.float32) * scale
    if len(pieces) > 0:
        values = shard_levels(rng, extent, pieces, -0.22, 0.18) * values
    return jnp.clip(values, min=-bound, max=bound).astype(held_as)


def setup_inputs(seed: int = 0) -> dict:
    splits = jax.random.split(jax.random.key(seed), 20)
    return {
        "layer_input": normal_values(splits[0], (BATCH, HEIGHT, W, D), 1.0, 6.0, ((0, 4), (1, 8))),
        "hidden_state": normal_values(splits[1], (BATCH, HEIGHT, W, D), 1.0, 6.0, ((0, 4), (1, 8))),
        "crop_rows": draw_crop_rows(jax.random.fold_in(splits[19], 71), 0),
        "crop_cols": draw_crop_cols(jax.random.fold_in(splits[19], 71), 0),
        "first_gain": jnp.clip(1.0 + 0.18 * jax.random.normal(splits[4], (D,), jnp.float32), 0.1, 1.9),
        "first_shift": normal_values(splits[5], (D,), 0.3, 3.0, (), jnp.float32),
        "qkv_weight": normal_values(splits[6], (D, 3 * D), D ** -0.5, 0.375, ((0, 32),), jnp.float32),
        "bias_table": normal_values(splits[7], (REL, HEADS), 1.0, 4.0, (), jnp.float32),
        "output_weight": normal_values(splits[8], (D, D), (D // 8) ** -0.5, 1.0, ((0, 32),), jnp.float32),
        "output_bias": normal_values(splits[9], (D,), 0.3, 3.0, (), jnp.float32),
        "second_gain": jnp.clip(1.0 + 0.18 * jax.random.normal(splits[10], (D,), jnp.float32), 0.1, 1.9),
        "second_shift": normal_values(splits[11], (D,), 0.3, 3.0, (), jnp.float32),
        "up_weight": normal_values(splits[12], (D, FF), D ** -0.5, 0.375, ((0, 32),), jnp.float32),
        "up_bias": normal_values(splits[13], (FF,), 0.5, 3.0, (), jnp.float32),
        "down_weight": normal_values(splits[14], (FF, D), FF ** -0.5, 0.1875, ((0, 32),), jnp.float32),
        "down_bias": normal_values(splits[15], (D,), 0.3, 3.0, (), jnp.float32),
        "conv_weight": normal_values(splits[16], (18 * D, D), (18 * D) ** -0.5, 0.09375, ((0, 32),), jnp.float32),
        "conv_bias": normal_values(splits[17], (D,), 0.5, 3.0, (), jnp.float32),
        "cotangent": normal_values(splits[18], (BATCH, HEIGHT, W, D), 1.0, 6.0, ((0, 4), (1, 8))),
    }


HIGHEST = lax.Precision.HIGHEST
EPSILON = 1e-05
MASKED = -100.0

@jax.custom_vjp
def low(v):
    return lax.optimization_barrier(v.astype(jnp.bfloat16)).astype(jnp.float32)

@jax.custom_vjp
def low_back(v):
    return v

def low_keep(v):
    return (low(v), None)

def low_pass(kept, grad):
    return (grad,)

def back_keep(v):
    return (v, None)

def back_low(kept, grad):
    return (low(grad),)
low.defvjp(low_keep, low_pass)
low_back.defvjp(back_keep, back_low)

def layer_norm(features, gain_vec, offset_vec):
    centred = features - lax.optimization_barrier(jnp.mean(features, -1, keepdims=True))
    spread = lax.optimization_barrier(jnp.mean(centred * centred, -1, keepdims=True))
    return centred * lax.rsqrt(spread + EPSILON) * gain_vec + offset_vec

def high_matmul(left, right):
    return jnp.matmul(left, right, precision=HIGHEST)

def windows_of(field):
    half_win = WIN // 2
    rolled = jnp.roll(field, (half_win, half_win), (1, 2))
    channels = field.shape[-1]
    blocks = rolled.reshape(BATCH, HEIGHT // WIN, WIN, W // WIN, WIN, channels)
    return blocks.transpose(0, 1, 3, 2, 4, 5).reshape(-1, WIN * WIN, channels)

def field_of(windowed):
    half_win = WIN // 2
    channels = windowed.shape[-1]
    blocks = windowed.reshape(BATCH, HEIGHT // WIN, W // WIN, WIN, WIN, channels)
    field = blocks.transpose(0, 1, 3, 2, 4, 5).reshape(BATCH, HEIGHT, W, channels)
    return jnp.roll(field, (-half_win, -half_win), (1, 2))

def reference(layer_input, hidden_state, crop_rows, crop_cols, first_gain, first_shift, qkv_weight, bias_table, output_weight, output_bias, second_gain, second_shift, up_weight, up_bias, down_weight, down_bias, conv_weight, conv_bias, cotangent):
    half_win = WIN // 2
    row_ids = jnp.arange(HEIGHT)
    col_ids = jnp.arange(W)
    validity = ((row_ids[None, :, None] < crop_rows[:, None, None]) & (col_ids[None, None, :] < crop_cols[:, None, None])).astype(jnp.float32)
    region = 2 * (row_ids[:, None] >= HEIGHT - half_win).astype(jnp.int32) + (col_ids[None, :] >= W - half_win).astype(jnp.int32)
    region = jnp.broadcast_to(region[None, :, :, None], (BATCH, HEIGHT, W, 1))
    region_win = windows_of(region)[..., 0]
    valid_win = windows_of(validity[..., None])[..., 0]
    score_mask = MASKED * (region_win[:, :, None] != region_win[:, None, :]).astype(jnp.float32) + MASKED * (1.0 - valid_win[:, None, :])
    places = jnp.arange(WIN * WIN)
    place_row = places // WIN
    place_col = places % WIN
    offsets = (place_row[:, None] - place_row[None, :] + WIN - 1) * (2 * WIN - 1) + (place_col[:, None] - place_col[None, :] + WIN - 1)
    score_scale = HEAD_DIM ** (-0.5)

    def forward(inputs, hidden, first_gain, first_shift, qkv_weight, bias_table, output_weight, output_bias, second_gain, second_shift, up_weight, up_bias, down_weight, down_bias, conv_weight, conv_bias):
        normed = low(layer_norm(inputs, first_gain, first_shift))
        windowed = windows_of(normed)
        window_count = windowed.shape[0]
        projected = low(low_back(high_matmul(windowed, low(qkv_weight))))
        queries = projected[..., :D].reshape(window_count, WIN * WIN, HEADS, HEAD_DIM)
        key_part = projected[..., D:2 * D].reshape(window_count, WIN * WIN, HEADS, HEAD_DIM)
        value_part = projected[..., 2 * D:].reshape(window_count, WIN * WIN, HEADS, HEAD_DIM)
        pos_bias = bias_table[offsets].transpose(2, 0, 1)
        scores = jnp.einsum('wqhe,wkhe->whqk', queries, key_part, precision=HIGHEST) * score_scale
        scores = low_back(scores + pos_bias[None] + score_mask[:, None])
        probs = low(jax.nn.softmax(scores, -1))
        combined = jnp.einsum('whqk,wkhe->wqhe', probs, value_part, precision=HIGHEST)
        combined = low(low_back(combined)).reshape(window_count, WIN * WIN, D)
        combined = field_of(combined)
        first_sum = inputs + low_back(high_matmul(combined, low(output_weight)) + output_bias)
        second_norm = low(layer_norm(first_sum, second_gain, second_shift))
        raised = low_back(high_matmul(second_norm, low(up_weight)) + up_bias)
        activated = low(jax.nn.gelu(raised, approximate=False))
        second_sum = first_sum + low_back(high_matmul(activated, low(down_weight)) + down_bias)
        joined = low(jnp.concatenate([second_sum, hidden], -1) * validity[..., None])
        padded = jnp.pad(joined, ((0, 0), (1, 1), (1, 1), (0, 0)))
        conv_low = low(conv_weight)
        summed = conv_bias
        for tap_row in range(3):
            for tap_col in range(3):
                first_row = (tap_row * 3 + tap_col) * 2 * D
                summed = summed + high_matmul(padded[:, tap_row:tap_row + HEIGHT, tap_col:tap_col + W], conv_low[first_row:first_row + 2 * D])
        return summed * validity[..., None]
    primal = (layer_input.astype(jnp.float32), hidden_state.astype(jnp.float32), first_gain, first_shift, qkv_weight, bias_table, output_weight, output_bias, second_gain, second_shift, up_weight, up_bias, down_weight, down_bias, conv_weight, conv_bias)
    result, backward = jax.vjp(forward, *primal)
    grads = backward(cotangent.astype(jnp.float32))
    return (result.astype(jnp.bfloat16), grads[0], grads[1], grads[2], grads[3], grads[4], grads[5], grads[6], grads[7], grads[8], grads[9], grads[10], grads[11], grads[12], grads[13], grads[14], grads[15])
```

```python
import functools

import jax
import jax.numpy as jnp
import numpy as np
from jax import lax
from jax.experimental import pallas as pl
from jax.experimental.pallas import tpu as pltpu
from jax.sharding import PartitionSpec as P

WIN = 8
EPSILON = 1e-05
MASKED = -100.0
HIGHEST = lax.Precision.HIGHEST
AXES = ("rows", "batch")
BF = jnp.bfloat16
F32 = jnp.float32
VMEM_LIMIT = 56 * 1024 * 1024
LOG2E = 1.4426950408889634


def dot(left, right):
    return jnp.dot(left, right, preferred_element_type=F32)


def dot_nt(left, right):
    return lax.dot_general(left, right, (((1,), (1,)), ((), ())), preferred_element_type=F32)


def dot_tn(left, right):
    return lax.dot_general(left, right, (((0,), (0,)), ((), ())), preferred_element_type=F32)


def iota(shape, dim):
    return lax.broadcasted_iota(jnp.int32, shape, dim)


def device_index():
    return lax.axis_index("rows") * lax.axis_size("batch") + lax.axis_index("batch")


def device_count():
    return lax.axis_size("rows") * lax.axis_size("batch")


def stages():
    batch = lax.axis_size("batch")
    rows = lax.axis_size("rows")
    row_bits = [batch << k for k in range(rows.bit_length() - 1)]
    batch_bits = [1 << k for k in range(batch.bit_length() - 1)]
    groups = [row_bits[:1]]
    rest = row_bits[1:]
    groups += [rest[k : k + 2] for k in range(0, len(rest), 2)]
    groups += [batch_bits[k : k + 2] for k in range(0, len(batch_bits), 2)]
    return [g for g in groups if g]


def flips(group):
    masks = [0]
    for bit in group:
        masks = masks + [m | bit for m in masks]
    return masks


def swap(x, mask):
    devices = device_count()
    return lax.ppermute(x, AXES, [(i, i ^ mask) for i in range(devices)])


def gather_parts(x):
    held = x[None]
    places = [0]
    for group in stages()[::-1]:
        masks = flips(group)
        held = jnp.concatenate([held] + [swap(held, m) for m in masks[1:]], 0)
        places = [p ^ m for m in masks for p in places]
    order = np.zeros(len(places), np.int32)
    for place, mask in enumerate(places):
        order[mask] = place
    wanted = jnp.asarray(order)[jnp.arange(len(places)) ^ device_index()]
    return jnp.take(held, wanted, axis=0)


def scatter_sums(x):
    devices = device_count()
    me = device_index()
    bits = devices.bit_length() - 1
    held = x.reshape((2,) * bits + x.shape[1:])
    left = [1 << k for k in range(bits)][::-1]
    for group in stages():
        for bit in group:
            k = left.index(bit)
            left.pop(k)
            held = jnp.moveaxis(held, k, 0) if k else held
            held = held.reshape(held.shape)
            left.insert(0, bit)
        lead = left[: len(group)]
        left = left[len(group) :]
        count = 1 << len(group)
        flat = held.reshape((count,) + held.shape[len(group) :])
        mine = 0
        for k, bit in enumerate(lead):
            mine = mine + ((me // bit) % 2) * (1 << (len(lead) - 1 - k))
        total = lax.dynamic_index_in_dim(flat, mine, 0, False).astype(F32)
        for mask in flips(group)[1:]:
            local = sum((1 << (len(lead) - 1 - k)) for k, bit in enumerate(lead) if mask & bit)
            piece = lax.dynamic_index_in_dim(flat, mine ^ local, 0, False).astype(BF)
            total = total + swap(piece, mask).astype(F32)
        held = total
    return held


def sum_all(x):
    for group in stages():
        total = x
        for mask in flips(group)[1:]:
            total = total + swap(x, mask)
        x = total
    return x


def ring(x, by):
    devices = lax.axis_size("rows")
    return lax.ppermute(x, "rows", [(i, (i + by) % devices) for i in range(devices)])


def norm_parts(x):
    centred = x - jnp.mean(x, -1, keepdims=True)
    rstd = lax.rsqrt(jnp.mean(centred * centred, -1, keepdims=True) + EPSILON)
    return centred * rstd, rstd


def norm_back(dy, xhat, rstd, gain):
    scaled = dy * gain
    first = jnp.mean(scaled, -1, keepdims=True)
    second = jnp.mean(scaled * xhat, -1, keepdims=True)
    return (scaled - first - xhat * second) * rstd


def head_mask():
    rows, lanes = np.arange(256)[:, None], np.arange(256)[None, :]
    return (rows // 64 == (lanes % 128) // 32).astype(np.float32)


def pair_of(ref, pair, column):
    first = ref[pl.ds(pair * 128, 64), column : column + 128]
    second = ref[pl.ds(pair * 128 + 64, 64), column : column + 128]
    return jnp.concatenate([first, second], 1)


def blocks_of(ref, pair, column):
    first = ref[pl.ds(pair * 128, 64), column : column + 128]
    second = ref[pl.ds(pair * 128 + 64, 64), column : column + 128]
    nothing = jnp.zeros_like(first)
    return jnp.concatenate(
        [jnp.concatenate([first, nothing], 1), jnp.concatenate([nothing, second], 1)], 0
    )


def spread_heads(pair, mask):
    return jnp.concatenate([pair] * 4, 0) * mask


def attn_forward_body(
    height, scale, step_of, place, x_ref, gain, shift, weight, bias, mask,
    x_out, norm_out, xhat_out, rstd_out, qkv_out, prob_out, mix_out, xs,
):
    sample, band = step_of(pl.program_id(0))
    columns = x_ref.shape[2]

    def rows_in(r, _):
        x = pltpu.roll(x_ref[0, r].astype(F32), WIN // 2, 0)
        xs[:, r] = x.reshape(columns // WIN, WIN, 256)
        return 0

    lax.fori_loop(0, WIN, rows_in, 0)

    def norm_in(k, _):
        tokens = pl.ds(k * 128, 128)
        x = xs[pl.ds(k * 2, 2)].reshape(128, 256)
        xhat, rstd = norm_parts(x)
        x_out[tokens] = x.astype(BF)
        xhat_out[tokens] = xhat
        rstd_out[tokens] = jnp.broadcast_to(rstd, (128, 128))
        norm_out[tokens] = (xhat * gain[...] + shift[...]).astype(BF)
        return 0

    lax.fori_loop(0, columns // 16, norm_in, 0)
    for k in range(0, columns * WIN, 256):
        qkv_out[k : k + 256] = dot(norm_out[k : k + 256], weight[...]).astype(BF)

    key_at, query_at = iota((64, 128), 0), iota((64, 128), 1)
    window_at = query_at // 64
    query_at = query_at % 64
    row_base = place[0] + band * WIN
    key_row, query_row = key_at // WIN + row_base, query_at // WIN + row_base
    key_row = jnp.where(key_row < 0, key_row + height, key_row)
    query_row = jnp.where(query_row < 0, query_row + height, query_row)
    rows_differ = (key_row >= height - WIN // 2) != (query_row >= height - WIN // 2)
    row_bad = key_row >= place[1 + sample]

    def attend(pair, _):
        key_col = (pair * 2 + window_at) * WIN + key_at % WIN - WIN // 2
        query_col = (pair * 2 + window_at) * WIN + query_at % WIN - WIN // 2
        key_col = jnp.where(key_col < 0, key_col + columns, key_col)
        query_col = jnp.where(query_col < 0, query_col + columns, query_col)
        cols_differ = (key_col >= columns - WIN // 2) != (query_col >= columns - WIN // 2)
        bad = row_bad | (key_col >= place[3 + sample])
        minus = jnp.where(rows_differ | cols_differ, MASKED / scale, 0.0) + jnp.where(
            bad, MASKED / scale, 0.0
        )
        for half in range(2):
            keys = spread_heads(pair_of(qkv_out, pair, 256 + 128 * half), mask[...])
            queries = blocks_of(qkv_out, pair, 128 * half)
            scores = dot_nt(keys, queries).reshape(4, 64, 128)
            scores = scores + (bias[256 * half : 256 * half + 256].reshape(4, 64, 128) + minus[None])
            top = jnp.max(scores, 1, keepdims=True)
            raised = jnp.exp2((scores - top) * (scale * LOG2E))
            probs = raised * (1.0 / jnp.sum(raised, 1, keepdims=True))
            probs = probs.reshape(256, 128).astype(BF)
            prob_out[pair, 256 * half : 256 * half + 256] = probs
            values = spread_heads(pair_of(qkv_out, pair, 512 + 128 * half), mask[...])
            mixed = dot_tn(probs, values).astype(BF)
            mix_out[pl.ds(pair * 128, 64), 128 * half : 128 * half + 128] = mixed[:64, :128]
            mix_out[pl.ds(pair * 128 + 64, 64), 128 * half : 128 * half + 128] = mixed[64:, 128:]
        return 0

    lax.fori_loop(0, columns // 16, attend, 0, unroll=2)


def const_spec(shape):
    return pl.BlockSpec(shape, lambda *_: (0,) * len(shape))


def params():
    return pltpu.CompilerParams(vmem_limit_bytes=VMEM_LIMIT)


SMEM_SPEC = pl.BlockSpec(memory_space=pltpu.SMEM)


def band_steps(samples, bands):
    def step_of(step):
        return step % samples, bands[0] + step // samples

    return step_of, samples * len(bands)


def attn_forward(place, framed, gain, shift, weight, bias, mask, height, scale):
    samples, grid_rows, columns, width = framed.shape
    bands = grid_rows // WIN
    tokens = WIN * columns
    steps = samples * bands

    def step_of(step):
        return step // bands, step % bands

    def row_block(step):
        return (step, 0)

    total = steps * tokens
    cost = pl.CostEstimate(flops=9 * 10**9, bytes_accessed=30 * 10**6, transcendentals=2 * 10**6)
    return pl.pallas_call(
        functools.partial(attn_forward_body, height, scale, step_of),
        grid=(steps,),
        in_specs=[
            SMEM_SPEC,
            pl.BlockSpec((1, WIN, columns, width), lambda s: (*step_of(s), 0, 0)),
            const_spec((1, width)),
            const_spec((1, width)),
            const_spec(weight.shape),
            const_spec(bias.shape),
            const_spec(mask.shape),
        ],
        out_specs=[
            pl.BlockSpec((tokens, width), row_block),
            pl.BlockSpec((tokens, width), row_block),
            pl.BlockSpec((tokens, width), row_block),
            pl.BlockSpec((tokens, 128), row_block),
            pl.BlockSpec((tokens, 3 * width), row_block),
            pl.BlockSpec((columns // 16, 512, 128), lambda s: (s, 0, 0)),
            pl.BlockSpec((tokens, width), row_block),
        ],
        out_shape=[
            jax.ShapeDtypeStruct((total, width), BF),
            jax.ShapeDtypeStruct((total, width), BF),
            jax.ShapeDtypeStruct((total, width), F32),
            jax.ShapeDtypeStruct((total, 128), F32),
            jax.ShapeDtypeStruct((total, 3 * width), BF),
            jax.ShapeDtypeStruct((total // 128, 512, 128), BF),
            jax.ShapeDtypeStruct((total, width), BF),
        ],
        scratch_shapes=[pltpu.VMEM((columns // WIN, WIN, WIN, width), F32)],
        compiler_params=params(),
        cost_estimate=cost,
        name="attn_forward",
    )(place, framed, gain, shift, weight, bias, mask)


def gelu_parts(x):
    size = jnp.abs(x)
    near = 1.0 / (1.0 + (0.3275911 * 0.7071067811865476) * size)
    bell = jnp.exp2(x * x * (-0.5 * LOG2E))
    tail = (
        (
            (((0.5 * 1.061405429 * near - 0.5 * 1.453152027) * near + 0.5 * 1.421413741) * near)
            - 0.5 * 0.284496736
        )
        * near
        + 0.5 * 0.254829592
    ) * (near * bell)
    share = jnp.where(x > 0, 1.0 - tail, tail)
    return x * share, share + x * (bell * 0.3989422804014327)


def ffn_forward_body(
    height, step_of, place, x_ref, mix, out_w, out_b, gain, shift, up_w, up_b, down_w, down_b,
    norm_out, xhat_out, rstd_out, act_out, slope_out, sum_out, sums,
):
    sample, band = step_of(pl.program_id(0))
    columns = sum_out.shape[2]
    chunk = 256

    def part(k, _):
        tokens = pl.ds(k * chunk, chunk)
        first = x_ref[tokens].astype(F32) + dot(mix[tokens], out_w[...]) + out_b[...]
        xhat, rstd = norm_parts(first)
        normed = (xhat * gain[...] + shift[...]).astype(BF)
        norm_out[tokens] = normed
        xhat_out[tokens] = xhat
        rstd_out[tokens] = jnp.broadcast_to(rstd, (chunk, 128))
        for f in range(0, 1024, 256):
            raised = dot(normed, up_w[:, f : f + 256]) + up_b[:, f : f + 256]
            act, slope = gelu_parts(raised)
            act_out[tokens, f : f + 256] = act.astype(BF)
            slope_out[tokens, f : f + 256] = slope.astype(BF)
        second = first + dot(act_out[tokens], down_w[...]) + down_b[...]
        sums[pl.ds(k * (chunk // 64), chunk // 64)] = second.reshape(chunk // 64, WIN, WIN, 256)
        return 0

    lax.fori_loop(0, columns * WIN // chunk, part, 0)
    column = iota((columns, 1), 0)

    def rows_out(r, _):
        row = place[0] + band * WIN + r
        row = jnp.where(row < 0, row + height, row)
        limit = jnp.where(row < place[1 + sample], place[3 + sample], 0)
        back = pltpu.roll(sums[:, r].reshape(columns, 256), columns - WIN // 2, 0)
        sum_out[0, r] = jnp.where(column < limit, back, 0.0).astype(BF)
        return 0

    lax.fori_loop(0, WIN, rows_out, 0)


def ffn_forward(place, x, mix, out_w, out_b, gain, shift, up_w, up_b, down_w, down_b, height, shape):
    samples, grid_rows, columns, width = shape
    bands = grid_rows // WIN
    tokens = WIN * columns
    steps = samples * bands
    hidden = up_w.shape[1]
    total = steps * tokens

    def step_of(step):
        return step // bands, step % bands

    def row_block(step):
        return (step, 0)

    rows = [width, width, 128, hidden, hidden]
    types = [BF, F32, F32, BF, BF]
    cost = pl.CostEstimate(flops=15 * 10**9, bytes_accessed=32 * 10**6, transcendentals=8 * 10**6)
    return pl.pallas_call(
        functools.partial(ffn_forward_body, height, step_of),
        grid=(steps,),
        in_specs=[SMEM_SPEC]
        + [pl.BlockSpec((tokens, width), row_block)] * 2
        + [const_spec(a.shape) for a in (out_w, out_b, gain, shift, up_w, up_b, down_w, down_b)],
        out_specs=[pl.BlockSpec((tokens, n), row_block) for n in rows]
        + [pl.BlockSpec((1, WIN, columns, width), lambda s: (*step_of(s), 0, 0))],
        out_shape=[jax.ShapeDtypeStruct((total, n), t) for n, t in zip(rows, types)]
        + [jax.ShapeDtypeStruct(shape, BF)],
        scratch_shapes=[pltpu.VMEM((columns // WIN, WIN, WIN, width), F32)],
        compiler_params=params(),
        cost_estimate=cost,
        name="ffn_forward",
    )(place, x, mix, out_w, out_b, gain, shift, up_w, up_b, down_w, down_b)


def column_sum(x):
    return jnp.sum(x, 0, keepdims=True)


def ffn_backward_body(
    branch, act, slope, normed, xhat_ref, rstd_ref, mix, out_w, gain, up_w, down_w,
    first_out, mixed_out, down_acc, up_acc, out_acc, vec_acc, up_vec, raised_s,
):
    @pl.when(pl.program_id(0) == 0)
    def _():
        for ref in (down_acc, up_acc, out_acc, vec_acc, up_vec):
            ref[...] = jnp.zeros_like(ref)

    chunk = branch.shape[0]
    upper = branch[...]
    low = upper.astype(BF)
    for f in range(0, 1024, 256):
        raised = (dot_nt(low, down_w[f : f + 256]) * slope[:, f : f + 256].astype(F32)).astype(BF)
        raised_s[:, f : f + 256] = raised
        up_vec[0:1, f : f + 256] += column_sum(raised.astype(F32))
    low_t = low.T
    normed_t = normed[...].T
    for f in range(0, 1024, 256):
        down_acc[:, f : f + 256] += dot(low_t, act[:, f : f + 256])
        up_acc[:, f : f + 256] += dot(normed_t, raised_s[:, f : f + 256])
    dy = dot_nt(raised_s[...], up_w[...])
    xhat = xhat_ref[...]
    rstd = rstd_ref[...]
    rstd = jnp.concatenate([rstd, rstd], 1)
    first = upper + norm_back(dy, xhat, rstd, gain[...])
    first_out[...] = first
    attn = first.astype(BF)
    out_acc[...] += dot(mix[...].T, attn)
    mixed_out[...] = dot_nt(attn, out_w[...]).astype(BF)
    vec_acc[0:1] += column_sum(low.astype(F32))
    vec_acc[1:2] += column_sum(dy * xhat)
    vec_acc[2:3] += column_sum(dy)
    vec_acc[3:4] += column_sum(attn.astype(F32))


def ffn_backward(branch, act, slope, normed, xhat, rstd, mix, out_w, gain, up_w, down_w):
    total, width = branch.shape
    hidden = up_w.shape[1]
    chunk = 512
    steps = total // chunk

    def row_block(step):
        return (step, 0)

    cost = pl.CostEstimate(flops=19 * 10**9, bytes_accessed=40 * 10**6, transcendentals=0)
    return pl.pallas_call(
        ffn_backward_body,
        grid=(steps,),
        in_specs=[
            pl.BlockSpec((chunk, a.shape[1]), row_block)
            for a in (branch, act, slope, normed, xhat, rstd, mix)
        ]
        + [const_spec(a.shape) for a in (out_w, gain, up_w, down_w)],
        out_specs=[
            pl.BlockSpec((chunk, width), row_block),
            pl.BlockSpec((chunk, width), row_block),
            const_spec((width, hidden)),
            const_spec((width, hidden)),
            const_spec((width, width)),
            const_spec((8, width)),
            const_spec((8, hidden)),
        ],
        out_shape=[
            jax.ShapeDtypeStruct((total, width), F32),
            jax.ShapeDtypeStruct((total, width), BF),
            jax.ShapeDtypeStruct((width, hidden), F32),
            jax.ShapeDtypeStruct((width, hidden), F32),
            jax.ShapeDtypeStruct((width, width), F32),
            jax.ShapeDtypeStruct((8, width), F32),
            jax.ShapeDtypeStruct((8, hidden), F32),
        ],
        scratch_shapes=[pltpu.VMEM((chunk, hidden), BF)],
        compiler_params=params(),
        cost_estimate=cost,
        name="ffn_backward",
    )(branch, act, slope, normed, xhat, rstd, mix, out_w, gain, up_w, down_w)


def attn_backward_body(
    scale, mixed, qkv, prob, normed, xhat_ref, rstd_ref, first, weight, gain, mask,
    input_out, qkv_acc, table_acc, vec_acc, grads, sums,
):
    @pl.when(pl.program_id(0) == 0)
    def _():
        for ref in (qkv_acc, table_acc, vec_acc):
            ref[...] = jnp.zeros_like(ref)

    columns = input_out.shape[2]
    tokens = columns * WIN

    def attend(pair, _):
        head_at = mask[...]
        for half in range(2):
            lanes = slice(256 * half, 256 * half + 256)
            low = prob[pair, lanes]
            mixed_blocks = blocks_of(mixed, pair, 128 * half)
            values = spread_heads(pair_of(qkv, pair, 512 + 128 * half), head_at)
            prob_grad = dot_nt(values, mixed_blocks).reshape(4, 64, 128)
            probs = low.astype(F32).reshape(4, 64, 128)
            shared = jnp.sum(prob_grad * probs, 1, keepdims=True)
            score_grad = (probs * (prob_grad - shared)).astype(BF).reshape(256, 128)
            table_acc[lanes] += score_grad.astype(F32)
            keys = spread_heads(pair_of(qkv, pair, 256 + 128 * half), head_at)
            queries = blocks_of(qkv, pair, 128 * half)
            query_grad = (dot_tn(score_grad, keys) * scale).astype(BF)
            out = slice(128 * half, 128 * half + 128)
            grads[pl.ds(pair * 128, 64), out] = query_grad[:64, :128]
            grads[pl.ds(pair * 128 + 64, 64), out] = query_grad[64:, 128:]
            wide = head_at.astype(F32)
            key_grad = (dot(score_grad, queries) * wide).reshape(4, 64, 256)
            key_grad = (jnp.sum(key_grad, 0) * scale).astype(BF)
            out = slice(256 + 128 * half, 256 + 128 * half + 128)
            grads[pl.ds(pair * 128, 64), out] = key_grad[:, :128]
            grads[pl.ds(pair * 128 + 64, 64), out] = key_grad[:, 128:]
            value_grad = (dot(low, mixed_blocks) * wide).reshape(4, 64, 256)
            value_grad = jnp.sum(value_grad, 0).astype(BF)
            out = slice(512 + 128 * half, 512 + 128 * half + 128)
            grads[pl.ds(pair * 128, 64), out] = value_grad[:, :128]
            grads[pl.ds(pair * 128 + 64, 64), out] = value_grad[:, 128:]
        return 0

    lax.fori_loop(0, columns // 16, attend, 0)
    for f in range(0, 768, 256):
        qkv_acc[:, f : f + 256] += dot_tn(normed[...], grads[:, f : f + 256])

    def part(k, _):
        at = pl.ds(k * 256, 256)
        dy = dot_nt(grads[at], weight[...])
        xhat = xhat_ref[at]
        rstd = rstd_ref[at]
        rstd = jnp.concatenate([rstd, rstd], 1)
        total = first[at] + norm_back(dy, xhat, rstd, gain[...])
        sums[pl.ds(k * 4, 4)] = total.reshape(4, WIN, WIN, 256)
        vec_acc[0:1] += column_sum(dy * xhat)
        vec_acc[1:2] += column_sum(dy)
        return 0

    lax.fori_loop(0, tokens // 256, part, 0)

    def rows_out(r, _):
        input_out[0, r] = pltpu.roll(sums[:, r].reshape(columns, 256), columns - WIN // 2, 0)
        return 0

    lax.fori_loop(0, WIN, rows_out, 0)


def attn_backward(mixed, qkv, prob, normed, xhat, rstd, first, weight, gain, mask, scale, shape, band):
    samples, grid_rows, columns, width = shape
    bands = grid_rows // WIN
    tokens = WIN * columns

    def row_block(step):
        return (step * bands + band, 0)

    cost = pl.CostEstimate(flops=8 * 10**9, bytes_accessed=16 * 10**6, transcendentals=0)
    return pl.pallas_call(
        functools.partial(attn_backward_body, scale),
        grid=(samples,),
        in_specs=[
            pl.BlockSpec((tokens, width), row_block),
            pl.BlockSpec((tokens, 3 * width), row_block),
            pl.BlockSpec((columns // 16, 512, 128), lambda s: (s * bands + band, 0, 0)),
            pl.BlockSpec((tokens, width), row_block),
            pl.BlockSpec((tokens, width), row_block),
            pl.BlockSpec((tokens, 128), row_block),
            pl.BlockSpec((tokens, width), row_block),
            const_spec(weight.shape),
            const_spec(gain.shape),
            const_spec(mask.shape),
        ],
        out_specs=[
            pl.BlockSpec((1, WIN, columns, width), lambda s: (s, 0, 0, 0)),
            const_spec((width, 3 * width)),
            const_spec((512, 128)),
            const_spec((8, width)),
        ],
        out_shape=[
            jax.ShapeDtypeStruct((samples, WIN, columns, width), F32),
            jax.ShapeDtypeStruct((width, 3 * width), F32),
            jax.ShapeDtypeStruct((512, 128), F32),
            jax.ShapeDtypeStruct((8, width), F32),
        ],
        scratch_shapes=[
            pltpu.VMEM((tokens, 3 * width), BF),
            pltpu.VMEM((columns // WIN, WIN, WIN, width), F32),
        ],
        compiler_params=params(),
        cost_estimate=cost,
        name="attn_backward",
    )(mixed, qkv, prob, normed, xhat, rstd, first, weight, gain, mask)


def shifted(row, column, by):
    columns = row.shape[0]
    moved = pltpu.roll(row, by % columns, 0)
    edge = 0 if by == 1 else columns - 1
    return jnp.where(column == edge, 0.0, moved)


def taps_in(source, target, rows, lanes):
    columns = source.shape[-2]
    column = iota((columns, 1), 0)

    def one(r, _):
        row = source[0, r]
        wide = row.astype(F32)
        target[r, :, lanes[0] : lanes[0] + 256] = shifted(wide, column, -1).astype(BF)
        target[r, :, lanes[1] : lanes[1] + 256] = row
        target[r, :, lanes[2] : lanes[2] + 256] = shifted(wide, column, 1).astype(BF)
        return 0

    lax.fori_loop(0, rows, one, 0)


def conv_weight_body(groups, joined, grad, acc, taps):
    @pl.when(pl.program_id(0) == 0)
    def _():
        acc[...] = jnp.zeros_like(acc)

    columns = joined.shape[2]
    taps_in(grad, taps, grad.shape[1], (0, 256, 512))
    for start, target, rows in groups:
        turned = joined[0, target : target + rows].reshape(rows * columns, 256).T
        for a in range(3):
            piece = taps[start + 2 - a : start + 2 - a + rows].reshape(rows * columns, 768)
            acc[a] += dot(turned, piece)


def conv_weight(groups, joined, grad):
    samples, rows, columns, width = joined.shape
    cost = pl.CostEstimate(flops=48 * 10**8, bytes_accessed=8 * 10**6, transcendentals=0)
    return pl.pallas_call(
        functools.partial(conv_weight_body, groups),
        grid=(samples,),
        in_specs=[
            pl.BlockSpec((1, rows, columns, width), lambda s: (s, 0, 0, 0)),
            pl.BlockSpec((1,) + grad.shape[1:], lambda s: (s, 0, 0, 0)),
        ],
        out_specs=const_spec((3, width, 3 * width)),
        out_shape=jax.ShapeDtypeStruct((3, width, 3 * width), F32),
        scratch_shapes=[pltpu.VMEM((grad.shape[1], columns, 3 * width), BF)],
        compiler_params=params(),
        cost_estimate=cost,
        name="conv_weight",
    )(joined, grad)


def conv_data_body(groups, height, framed, place, grad, weight, out, taps):
    sample = pl.program_id(0)
    columns = grad.shape[2]
    column = iota((columns, 1), 0)
    taps_in(grad, taps, grad.shape[1], (0, 256, 512))
    for start, target, rows in groups:
        for r in range(0, rows, 4):
            total = 0.0
            for a in range(3):
                first = start + r + 2 - a
                piece = taps[first : first + 4].reshape(4 * columns, 768)
                total = total + dot_nt(piece, weight[a])
            for k in range(4):
                at = target + r + k
                row = place[0] + at
                if framed:
                    row = jnp.where(row < 0, row + height, row)
                else:
                    row = row + WIN // 2
                limit = jnp.where(row < place[1 + sample], place[3 + sample], 0)
                part = jnp.where(column < limit, total[k * columns : (k + 1) * columns], 0.0)
                if framed:
                    part = pltpu.roll(part, WIN // 2, 0)
                    out[at // WIN, :, at % WIN] = part.reshape(columns // WIN, WIN, 256)
                else:
                    out[0, at] = part


def conv_data(groups, place, grad, weight, rows, height, framed):
    samples, _, columns, width = grad.shape
    if framed:
        shape = (samples * rows // WIN, columns // WIN, WIN, WIN, width)
        spec = pl.BlockSpec((rows // WIN,) + shape[1:], lambda s: (s, 0, 0, 0, 0))
    else:
        shape = (samples, rows, columns, width)
        spec = pl.BlockSpec((1,) + shape[1:], lambda s: (s, 0, 0, 0))
    cost = pl.CostEstimate(flops=48 * 10**8, bytes_accessed=8 * 10**6, transcendentals=0)
    return pl.pallas_call(
        functools.partial(conv_data_body, groups, height, framed),
        grid=(samples,),
        in_specs=[
            SMEM_SPEC,
            pl.BlockSpec((1,) + grad.shape[1:], lambda s: (s, 0, 0, 0)),
            const_spec(weight.shape),
        ],
        out_specs=spec,
        out_shape=jax.ShapeDtypeStruct(shape, F32),
        scratch_shapes=[pltpu.VMEM((grad.shape[1], columns, 3 * width), BF)],
        compiler_params=params(),
        cost_estimate=cost,
        name="conv_data",
    )(place, grad, weight)


def conv_forward_body(place, sums, hidden, weight, bias, out, taps):
    sample = pl.program_id(0)
    columns = sums.shape[2]
    rows = out.shape[1]
    column = iota((columns, 1), 0)
    taps_in(sums, taps, rows + 2, (1024, 512, 0))
    taps_in(hidden, taps, rows + 2, (1280, 768, 256))
    for r in range(0, rows, 4):
        total = bias[...]
        for a in range(3):
            piece = taps[r + a : r + a + 4].reshape(4 * columns, 1536)
            total = total + dot(piece, weight[a * 1536 : (a + 1) * 1536])
        for k in range(4):
            row = place[0] + WIN // 2 + r + k
            limit = jnp.where(row < place[1 + sample], place[3 + sample], 0)
            part = total[k * columns : (k + 1) * columns]
            out[0, r + k] = jnp.where(column < limit, part, 0.0).astype(BF)


def conv_forward(place, sums, hidden, weight, bias):
    samples, padded, columns, width = sums.shape
    rows = padded - 2
    cost = pl.CostEstimate(flops=96 * 10**8, bytes_accessed=10 * 10**6, transcendentals=0)
    return pl.pallas_call(
        conv_forward_body,
        grid=(samples,),
        in_specs=[
            SMEM_SPEC,
            pl.BlockSpec((1, padded, columns, width), lambda s: (s, 0, 0, 0)),
            pl.BlockSpec((1, padded, columns, width), lambda s: (s, 0, 0, 0)),
            const_spec(weight.shape),
            const_spec(bias.shape),
        ],
        out_specs=pl.BlockSpec((1, rows, columns, width), lambda s: (s, 0, 0, 0)),
        out_shape=jax.ShapeDtypeStruct((samples, rows, columns, width), BF),
        scratch_shapes=[pltpu.VMEM((padded, columns, 6 * width), BF)],
        compiler_params=params(),
        cost_estimate=cost,
        name="conv_forward",
    )(place, sums, hidden, weight, bias)


def offset_onehot():
    places = jnp.arange(WIN * WIN)
    row, col = places // WIN, places % WIN
    offsets = (row[None, :] - row[:, None] + WIN - 1) * (2 * WIN - 1) + (
        col[None, :] - col[:, None] + WIN - 1
    )
    return (offsets.reshape(-1)[:, None] == jnp.arange((2 * WIN - 1) ** 2)[None, :]).astype(F32)


def shards(
    layer_input,
    hidden_state,
    crop_rows,
    crop_cols,
    first_gain,
    first_shift,
    qkv_weight,
    bias_table,
    output_weight,
    output_bias,
    second_gain,
    second_shift,
    up_weight,
    up_bias,
    down_weight,
    down_bias,
    conv_weight_in,
    conv_bias,
    cotangent,
):
    samples, grid_rows, columns, width = layer_input.shape
    shape = layer_input.shape
    heads = bias_table.shape[1]
    scale = float((width // heads) ** (-0.5))
    half = WIN // 2
    devices = device_count()
    row_devices = lax.axis_size("rows")
    height = grid_rows * row_devices
    row_place = lax.axis_index("rows")
    row_start = row_place * grid_rows
    place = jnp.concatenate(
        [(row_start - half)[None].astype(jnp.int32), crop_rows, crop_cols]
    ).astype(jnp.int32)

    input_above = ring(layer_input[:, grid_rows - half :], 1)
    qkv_full = gather_parts(qkv_weight.astype(BF)).reshape(width, -1)
    grad_above = ring(cotangent[:, grid_rows - half - 1 :], 1)
    grad_below = ring(cotangent[:, :1], -1)
    hidden_above = ring(hidden_state[:, grid_rows - 1 :], 1)
    hidden_below = ring(hidden_state[:, :1], -1)
    mid = jnp.concatenate([output_weight, up_weight], 1).astype(BF)
    mid_full = gather_parts(mid).reshape(width, -1)
    output_full, up_full = mid_full[:, :width], mid_full[:, width:]
    tall = jnp.concatenate([down_weight, conv_weight_in], 0).astype(BF)
    down_rows = down_weight.shape[0]
    tall_full = gather_parts(tall)
    down_full = tall_full[:, :down_rows].reshape(-1, width)
    conv_full = tall_full[:, down_rows:].reshape(-1, width)
    conv_turned = (
        conv_full.reshape(3, 3, 2, width, width).transpose(2, 0, 3, 1, 4).reshape(2, 3, width, 3 * width)
    )

    first_device = row_place == 0
    last_device = row_place == row_devices - 1
    framed = jnp.concatenate([input_above, layer_input[:, : grid_rows - half]], 1)
    row_ids = jnp.concatenate(
        [jnp.arange(-half - 1, grid_rows + 1)]
    ) + row_start
    row_ids = row_ids % height
    valid = (row_ids[None, :, None] < crop_rows[:, None, None]) & (
        jnp.arange(columns)[None, None, :] < crop_cols[:, None, None]
    )
    zero = jnp.zeros((), BF)
    grad_all = jnp.concatenate([grad_above, cotangent, grad_below], 1)
    grad_all = jnp.where(valid[..., None], grad_all, zero)
    grad_first = jnp.where(first_device, zero, grad_all[:, half : half + 1])
    grad_zero = jnp.where(first_device, zero, grad_all[:, half + 1 : half + 2])
    grad_last = jnp.where(last_device, zero, grad_all[:, -1:])
    grad_frame = jnp.concatenate(
        [grad_all[:, : half + 1], grad_zero, grad_first, grad_all[:, half + 1 : grid_rows + 2]], 1
    )
    grad_own = jnp.concatenate([grad_first, grad_all[:, half + 1 : -1], grad_last], 1)
    hidden_all = jnp.concatenate([hidden_above, hidden_state, hidden_below], 1)
    own_valid = valid[:, half:]
    edge = jnp.arange(grid_rows + 2)
    inside = ~((edge == 0) & first_device) & ~((edge == grid_rows + 1) & last_device)
    own_valid = own_valid & inside[None, :, None]
    hidden_all = jnp.where(own_valid[..., None], hidden_all, zero)
    frame_groups = ((0, 0, half), (half + 2, half, grid_rows - half))
    own_groups = ((0, 0, grid_rows),)

    onehot = offset_onehot()
    pos_bias = jnp.dot(onehot, bias_table, precision=HIGHEST).reshape(WIN * WIN, WIN * WIN, heads)
    pos_bias = pos_bias.transpose(2, 0, 1).reshape(heads * WIN * WIN, WIN * WIN) * (1.0 / scale)
    pos_bias = jnp.concatenate([pos_bias, pos_bias], 1)
    mask = jnp.asarray(head_mask(), BF)

    def vec(v):
        return v.reshape(1, -1)

    conv_hidden = conv_weight(own_groups, hidden_all[:, 1:-1], grad_own)
    x, normed, xhat, rstd, qkv, prob, mix = attn_forward(
        place, framed, vec(first_gain), vec(first_shift), qkv_full, pos_bias, mask, height, scale
    )
    normed_2, xhat_2, rstd_2, act, slope, sums = ffn_forward(
        place, x, mix, output_full, vec(output_bias), vec(second_gain), vec(second_shift),
        up_full, vec(up_bias), down_full, vec(down_bias), height, shape,
    )
    sums_below = ring(sums[:, : half + 1], -1)
    branch = conv_data(frame_groups, place, grad_frame, conv_turned[0], grid_rows, height, True)
    branch = branch.reshape(-1, width)
    conv_sums = conv_weight(frame_groups, sums, grad_frame)
    first_grad, mixed, down_acc, up_acc, out_acc, vec_ffn, vec_up = ffn_backward(
        branch, act, slope, normed_2, xhat_2, rstd_2, mix, output_full, vec(second_gain),
        up_full, down_full,
    )
    conv_local = jnp.stack([conv_sums, conv_hidden], 0).astype(BF)
    conv_local = conv_local.reshape(2, 3, width, 3, width).transpose(1, 3, 0, 2, 4)
    conv_weight_grad = scatter_sums(conv_local.reshape(devices, -1, width))
    up_weight_grad = scatter_sums(up_acc.reshape(devices, -1, up_acc.shape[1]))
    down_weight_grad = scatter_sums(down_acc.T.reshape(devices, -1, width))
    output_weight_grad = scatter_sums(out_acc.reshape(devices, -1, width))

    back = functools.partial(
        attn_backward, mixed, qkv, prob, normed, xhat, rstd, first_grad, qkv_full,
        vec(first_gain), mask, scale, shape,
    )
    input_top, qkv_top, table_top, vec_top = back(0)
    input_from_below = ring(input_top[:, :half].astype(BF), -1).astype(F32)
    input_low, qkv_low, table_low, vec_low = back(1)
    qkv_acc = qkv_top + qkv_low
    table_acc = table_top + table_low
    vec_attn = vec_top + vec_low
    input_grad = jnp.concatenate([input_top[:, half:], input_low, input_from_below], 1)
    qkv_weight_grad = scatter_sums(qkv_acc.reshape(devices, -1, qkv_acc.shape[1]))
    pair_grad = (table_acc[:, :64] + table_acc[:, 64:]).reshape(heads, -1)
    table_local = jnp.dot(pair_grad, onehot, precision=HIGHEST).T
    conv_bias_local = jnp.sum(grad_own[:, 1:-1].astype(F32), (0, 1, 2))
    small = [
        vec_attn[0], vec_attn[1], table_local, vec_ffn[3], vec_ffn[1], vec_ffn[2], vec_up[0],
        vec_ffn[0], conv_bias_local,
    ]
    flat = jnp.concatenate([v.reshape(-1) for v in small])
    count = flat.shape[0]
    flat = jnp.pad(flat, (0, -count % 1024)).reshape(-1, 128)
    flat = sum_all(flat).reshape(-1)[:count]
    summed = []
    for v in small:
        summed.append(flat[: v.size].reshape(v.shape))
        flat = flat[v.size :]
    (
        first_gain_grad, first_shift_grad, bias_table_grad, output_bias_grad, second_gain_grad,
        second_shift_grad, up_bias_grad, down_bias_grad, conv_bias_grad,
    ) = summed

    hidden_grad = conv_data(own_groups, place, grad_own, conv_turned[1], grid_rows, height, False)
    sums_own = jnp.concatenate([sums[:, half - 1 :], sums_below], 1)
    sums_own = jnp.where(inside[None, :, None, None], sums_own, zero)
    layer_output = conv_forward(place, sums_own, hidden_all, conv_full, vec(conv_bias))
    return (
        layer_output,
        input_grad,
        hidden_grad,
        first_gain_grad,
        first_shift_grad,
        qkv_weight_grad,
        bias_table_grad,
        output_weight_grad,
        output_bias_grad,
        second_gain_grad,
        second_shift_grad,
        up_weight_grad,
        up_bias_grad,
        down_weight_grad,
        down_bias_grad,
        conv_weight_grad,
        conv_bias_grad,
    )


def solution(mesh):
    field = P("batch", "rows", None, None)
    weight = P(AXES, None)
    in_specs = (
        field, field, P("batch"), P("batch"), P(), P(), weight, P(), weight, P(), P(), P(),
        weight, P(), weight, P(), weight, P(), field,
    )
    out_specs = (
        field, field, field, P(), P(), weight, P(), weight, P(), P(), P(), weight, P(), weight,
        P(), weight, P(),
    )
    return jax.shard_map(shards, mesh=mesh, in_specs=in_specs, out_specs=out_specs, check_vma=False)
```

```python
import functools

import jax
import jax.numpy as jnp
import numpy as np
from jax import lax
from jax.experimental import pallas as pl
from jax.experimental.pallas import tpu as pltpu
from jax.sharding import PartitionSpec as P

WIN = 8
EPSILON = 1e-05
MASKED = -100.0
HIGHEST = lax.Precision.HIGHEST
AXES = ("rows", "batch")
BF = jnp.bfloat16
F32 = jnp.float32
VMEM_LIMIT = 56 * 1024 * 1024
LOG2E = 1.4426950408889634


def dot(left, right):
    return jnp.dot(left, right, preferred_element_type=F32)


def dot_nt(left, right):
    return lax.dot_general(left, right, (((1,), (1,)), ((), ())), preferred_element_type=F32)


def dot_tn(left, right):
    return lax.dot_general(left, right, (((0,), (0,)), ((), ())), preferred_element_type=F32)


def iota(shape, dim):
    return lax.broadcasted_iota(jnp.int32, shape, dim)


def device_index():
    return lax.axis_index("rows") * lax.axis_size("batch") + lax.axis_index("batch")


def device_count():
    return lax.axis_size("rows") * lax.axis_size("batch")


def gather_copies(x):
    copies = jnp.broadcast_to(x[None], (device_count(),) + x.shape)
    return lax.all_to_all(copies, AXES, 0, 0, tiled=True)


def gather_behind(x):
    return lax.all_gather(x, AXES, axis=0, tiled=False)


def split_sums(v):
    high = v.astype(BF)
    low = (v - high.astype(F32)).astype(BF)
    return high, low


def pack_vectors(parts, width):
    flat = jnp.concatenate([v.reshape(-1) for v in parts])
    flat = jnp.pad(flat, (0, -flat.shape[0] % (8 * width))).reshape(-1, width)
    return jnp.concatenate(split_sums(flat), 0)


def unpack_vectors(rows, parts):
    total = jnp.sum(rows.astype(F32), 0)
    half = total.shape[0] // 2
    flat = (total[:half] + total[half:]).reshape(-1)
    out = []
    for v in parts:
        out.append(flat[: v.size].reshape(v.shape))
        flat = flat[v.size :]
    return out


def ring(x, by):
    devices = lax.axis_size("rows")
    return lax.ppermute(x, "rows", [(i, (i + by) % devices) for i in range(devices)])


def norm_parts(x):
    centred = x - jnp.mean(x, -1, keepdims=True)
    rstd = lax.rsqrt(jnp.mean(centred * centred, -1, keepdims=True) + EPSILON)
    return centred * rstd, rstd


def norm_back(dy, xhat, rstd, gain):
    scaled = dy * gain
    first = jnp.mean(scaled, -1, keepdims=True)
    second = jnp.mean(scaled * xhat, -1, keepdims=True)
    return (scaled - first - xhat * second) * rstd


def head_mask():
    rows, lanes = np.arange(256)[:, None], np.arange(256)[None, :]
    return (rows // 64 == (lanes % 128) // 32).astype(np.float32)


def pair_of(ref, pair, column):
    first = ref[pl.ds(pair * 128, 64), column : column + 128]
    second = ref[pl.ds(pair * 128 + 64, 64), column : column + 128]
    return jnp.concatenate([first, second], 1)


def blocks_of(ref, pair, column):
    first = ref[pl.ds(pair * 128, 64), column : column + 128]
    second = ref[pl.ds(pair * 128 + 64, 64), column : column + 128]
    nothing = jnp.zeros_like(first)
    return jnp.concatenate(
        [jnp.concatenate([first, nothing], 1), jnp.concatenate([nothing, second], 1)], 0
    )


def spread_heads(pair, mask):
    return jnp.concatenate([pair] * 4, 0) * mask


def attn_forward_body(
    height, scale, step_of, place, above, upper, lower, gain, shift, weight, bias, mask,
    x_out, norm_out, xhat_out, rstd_out, qkv_out, prob_out, mix_out, xs,
):
    sample, band = step_of(pl.program_id(0))
    columns = lower.shape[2]

    def rows_from(ref, first):
        def rows_in(r, _):
            x = pltpu.roll(ref[0, r].astype(F32), WIN // 2, 0)
            xs[:, first + r] = x.reshape(columns // WIN, WIN, 256)
            return 0

        lax.fori_loop(0, WIN // 2, rows_in, 0, unroll=True)

    @pl.when(band == 0)
    def _():
        rows_from(above, 0)

    @pl.when(band > 0)
    def _():
        rows_from(upper, 0)

    rows_from(lower, WIN // 2)

    def norm_in(k, _):
        tokens = pl.ds(k * 128, 128)
        x = xs[pl.ds(k * 2, 2)].reshape(128, 256)
        xhat, rstd = norm_parts(x)
        x_out[tokens] = x.astype(BF)
        xhat_out[tokens] = xhat
        rstd_out[tokens] = jnp.broadcast_to(rstd, (128, 128))
        norm_out[tokens] = (xhat * gain[...] + shift[...]).astype(BF)
        return 0

    lax.fori_loop(0, columns // 16, norm_in, 0, unroll=8)
    for k in range(0, columns * WIN, 256):
        qkv_out[k : k + 256] = dot(norm_out[k : k + 256], weight[...]).astype(BF)

    key_at, query_at = iota((64, 128), 0), iota((64, 128), 1)
    window_at = query_at // 64
    query_at = query_at % 64
    row_base = place[0] + band * WIN
    key_row, query_row = key_at // WIN + row_base, query_at // WIN + row_base
    key_row = jnp.where(key_row < 0, key_row + height, key_row)
    query_row = jnp.where(query_row < 0, query_row + height, query_row)
    rows_differ = (key_row >= height - WIN // 2) != (query_row >= height - WIN // 2)
    row_bad = key_row >= place[1 + sample]

    def attend(pair, _):
        key_col = (pair * 2 + window_at) * WIN + key_at % WIN - WIN // 2
        query_col = (pair * 2 + window_at) * WIN + query_at % WIN - WIN // 2
        key_col = jnp.where(key_col < 0, key_col + columns, key_col)
        query_col = jnp.where(query_col < 0, query_col + columns, query_col)
        cols_differ = (key_col >= columns - WIN // 2) != (query_col >= columns - WIN // 2)
        bad = row_bad | (key_col >= place[3 + sample])
        minus = jnp.where(rows_differ | cols_differ, MASKED / scale, 0.0) + jnp.where(
            bad, MASKED / scale, 0.0
        )
        for half in range(2):
            keys = spread_heads(pair_of(qkv_out, pair, 256 + 128 * half), mask[...])
            queries = blocks_of(qkv_out, pair, 128 * half)
            scores = dot_nt(keys, queries).reshape(4, 64, 128)
            scores = scores + (bias[256 * half : 256 * half + 256].reshape(4, 64, 128) + minus[None])
            top = jnp.max(scores, 1, keepdims=True)
            raised = jnp.exp2((scores - top) * (scale * LOG2E))
            probs = raised * (1.0 / jnp.sum(raised, 1, keepdims=True))
            probs = probs.reshape(256, 128).astype(BF)
            prob_out[pair, 256 * half : 256 * half + 256] = probs
        return 0

    def mix(pair, _):
        for half in range(2):
            probs = prob_out[pair, 256 * half : 256 * half + 256]
            values = spread_heads(pair_of(qkv_out, pair, 512 + 128 * half), mask[...])
            mixed = dot_tn(probs, values).astype(BF)
            mix_out[pl.ds(pair * 128, 64), 128 * half : 128 * half + 128] = mixed[:64, :128]
            mix_out[pl.ds(pair * 128 + 64, 64), 128 * half : 128 * half + 128] = mixed[64:, 128:]
        return 0

    lax.fori_loop(0, columns // 16, attend, 0, unroll=8)
    lax.fori_loop(0, columns // 16, mix, 0, unroll=8)


def const_spec(shape):
    return pl.BlockSpec(shape, lambda *_: (0,) * len(shape))


def params():
    return pltpu.CompilerParams(vmem_limit_bytes=VMEM_LIMIT)


SMEM_SPEC = pl.BlockSpec(memory_space=pltpu.SMEM)


def band_steps(samples, bands):
    def step_of(step):
        return step % samples, bands[0] + step // samples

    return step_of, samples * len(bands)


def attn_forward(place, above, own, gain, shift, weight, bias, mask, height, scale):
    samples, grid_rows, columns, width = own.shape
    half = WIN // 2
    bands = grid_rows // WIN
    tokens = WIN * columns
    steps = samples * bands

    def step_of(step):
        return step // bands, step % bands

    def row_block(step):
        return (step, 0)

    total = steps * tokens
    cost = pl.CostEstimate(flops=9 * 10**9, bytes_accessed=30 * 10**6, transcendentals=2 * 10**6)
    return pl.pallas_call(
        functools.partial(attn_forward_body, height, scale, step_of),
        grid=(steps,),
        in_specs=[
            SMEM_SPEC,
            pl.BlockSpec((1, half, columns, width), lambda s: (step_of(s)[0], 0, 0, 0)),
            pl.BlockSpec(
                (1, half, columns, width),
                lambda s: (step_of(s)[0], jnp.maximum(2 * step_of(s)[1] - 1, 0), 0, 0),
            ),
            pl.BlockSpec(
                (1, half, columns, width), lambda s: (step_of(s)[0], 2 * step_of(s)[1], 0, 0)
            ),
            const_spec((1, width)),
            const_spec((1, width)),
            const_spec(weight.shape),
            const_spec(bias.shape),
            const_spec(mask.shape),
        ],
        out_specs=[
            pl.BlockSpec((tokens, width), row_block),
            pl.BlockSpec((tokens, width), row_block),
            pl.BlockSpec((tokens, width), row_block),
            pl.BlockSpec((tokens, 128), row_block),
            pl.BlockSpec((tokens, 3 * width), row_block),
            pl.BlockSpec((columns // 16, 512, 128), lambda s: (s, 0, 0)),
            pl.BlockSpec((tokens, width), row_block),
        ],
        out_shape=[
            jax.ShapeDtypeStruct((total, width), BF),
            jax.ShapeDtypeStruct((total, width), BF),
            jax.ShapeDtypeStruct((total, width), F32),
            jax.ShapeDtypeStruct((total, 128), F32),
            jax.ShapeDtypeStruct((total, 3 * width), BF),
            jax.ShapeDtypeStruct((total // 128, 512, 128), BF),
            jax.ShapeDtypeStruct((total, width), BF),
        ],
        scratch_shapes=[pltpu.VMEM((columns // WIN, WIN, WIN, width), F32)],
        compiler_params=params(),
        cost_estimate=cost,
        name="attn_forward",
    )(place, above, own, own, gain, shift, weight, bias, mask)


def gelu_parts(x):
    share = 0.5 + 0.5 * lax.erf(x * 0.7071067811865476)
    bell = jnp.exp2(x * x * (-0.5 * LOG2E))
    return x * share, share + x * (bell * 0.3989422804014327)


def ffn_forward_body(
    height, step_of, place, x_ref, mix, out_w, out_b, gain, shift, up_w, up_b, down_w, down_b,
    norm_out, xhat_out, rstd_out, act_out, slope_out, sum_out, sums,
):
    sample, band = step_of(pl.program_id(0))
    columns = sum_out.shape[2]
    chunk = 256
    chunks = columns * WIN // chunk

    def attend_sum(k, _):
        tokens = pl.ds(k * chunk, chunk)
        first = x_ref[tokens].astype(F32) + dot(mix[tokens], out_w[...]) + out_b[...]
        sums[pl.ds(k * (chunk // 64), chunk // 64)] = first.reshape(chunk // 64, WIN, WIN, 256)
        xhat, rstd = norm_parts(first)
        norm_out[tokens] = (xhat * gain[...] + shift[...]).astype(BF)
        xhat_out[tokens] = xhat
        rstd_out[tokens] = jnp.broadcast_to(rstd, (chunk, 128))
        return 0

    def raise_up(k, _):
        tokens = pl.ds(k * chunk, chunk)
        for f in range(0, 1024, 256):
            raised = dot(norm_out[tokens], up_w[:, f : f + 256]) + up_b[:, f : f + 256]
            act, slope = gelu_parts(raised)
            act_out[tokens, f : f + 256] = act.astype(BF)
            slope_out[tokens, f : f + 256] = slope.astype(BF)
        return 0

    def put_down(k, _):
        tokens = pl.ds(k * chunk, chunk)
        windows = pl.ds(k * (chunk // 64), chunk // 64)
        second = dot(act_out[tokens], down_w[...]) + down_b[...]
        sums[windows] += second.reshape(chunk // 64, WIN, WIN, 256)
        return 0

    lax.fori_loop(0, chunks, attend_sum, 0, unroll=True)
    lax.fori_loop(0, chunks, raise_up, 0, unroll=True)
    lax.fori_loop(0, chunks, put_down, 0, unroll=True)
    column = iota((columns, 1), 0)

    def rows_out(r, _):
        row = place[0] + band * WIN + r
        row = jnp.where(row < 0, row + height, row)
        limit = jnp.where(row < place[1 + sample], place[3 + sample], 0)
        back = pltpu.roll(sums[:, r].reshape(columns, 256), columns - WIN // 2, 0)
        sum_out[0, r] = jnp.where(column < limit, back, 0.0).astype(BF)
        return 0

    lax.fori_loop(0, WIN, rows_out, 0, unroll=True)


def ffn_forward(place, x, mix, out_w, out_b, gain, shift, up_w, up_b, down_w, down_b, height, shape):
    samples, grid_rows, columns, width = shape
    bands = grid_rows // WIN
    tokens = WIN * columns
    steps = samples * bands
    hidden = up_w.shape[1]
    total = steps * tokens

    def step_of(step):
        return step // bands, step % bands

    def row_block(step):
        return (step, 0)

    rows = [width, width, 128, hidden, hidden]
    types = [BF, F32, F32, BF, BF]
    cost = pl.CostEstimate(flops=15 * 10**9, bytes_accessed=32 * 10**6, transcendentals=8 * 10**6)
    return pl.pallas_call(
        functools.partial(ffn_forward_body, height, step_of),
        grid=(steps,),
        in_specs=[SMEM_SPEC]
        + [pl.BlockSpec((tokens, width), row_block)] * 2
        + [const_spec(a.shape) for a in (out_w, out_b, gain, shift, up_w, up_b, down_w, down_b)],
        out_specs=[pl.BlockSpec((tokens, n), row_block) for n in rows]
        + [pl.BlockSpec((1, WIN, columns, width), lambda s: (*step_of(s), 0, 0))],
        out_shape=[jax.ShapeDtypeStruct((total, n), t) for n, t in zip(rows, types)]
        + [jax.ShapeDtypeStruct(shape, BF)],
        scratch_shapes=[pltpu.VMEM((columns // WIN, WIN, WIN, width), F32)],
        compiler_params=params(),
        cost_estimate=cost,
        name="ffn_forward",
    )(place, x, mix, out_w, out_b, gain, shift, up_w, up_b, down_w, down_b)


def column_sum(x):
    return jnp.sum(x, 0, keepdims=True)


def ffn_backward_body(
    branch, act, slope, normed, xhat_ref, rstd_ref, mix, out_w, gain, up_w, down_w,
    first_out, mixed_out, down_acc, up_acc, out_acc, vec_acc, up_vec, raised_s,
):
    @pl.when(pl.program_id(0) == 0)
    def _():
        for ref in (down_acc, up_acc, out_acc, vec_acc, up_vec):
            ref[...] = jnp.zeros_like(ref)

    chunk = branch.shape[0]
    upper = branch[...]
    low = upper.astype(BF)
    for f in range(0, 1024, 256):
        raised = (dot_nt(low, down_w[f : f + 256]) * slope[:, f : f + 256].astype(F32)).astype(BF)
        raised_s[:, f : f + 256] = raised
        up_vec[0:1, f : f + 256] += column_sum(raised.astype(F32))
    low_t = low.T
    normed_t = normed[...].T
    for f in range(0, 1024, 256):
        down_acc[:, f : f + 256] += dot(low_t, act[:, f : f + 256])
        up_acc[:, f : f + 256] += dot(normed_t, raised_s[:, f : f + 256])
    dy = dot_nt(raised_s[...], up_w[...])
    xhat = xhat_ref[...]
    rstd = rstd_ref[...]
    rstd = jnp.concatenate([rstd, rstd], 1)
    first = upper + norm_back(dy, xhat, rstd, gain[...])
    first_out[...] = first
    attn = first.astype(BF)
    out_acc[...] += dot(mix[...].T, attn)
    mixed_out[...] = dot_nt(attn, out_w[...]).astype(BF)
    vec_acc[0:1] += column_sum(low.astype(F32))
    vec_acc[1:2] += column_sum(dy * xhat)
    vec_acc[2:3] += column_sum(dy)
    vec_acc[3:4] += column_sum(attn.astype(F32))


def ffn_backward(branch, act, slope, normed, xhat, rstd, mix, out_w, gain, up_w, down_w):
    total, width = branch.shape
    hidden = up_w.shape[1]
    chunk = 512
    steps = total // chunk

    def row_block(step):
        return (step, 0)

    cost = pl.CostEstimate(flops=19 * 10**9, bytes_accessed=40 * 10**6, transcendentals=0)
    return pl.pallas_call(
        ffn_backward_body,
        grid=(steps,),
        in_specs=[
            pl.BlockSpec((chunk, a.shape[1]), row_block)
            for a in (branch, act, slope, normed, xhat, rstd, mix)
        ]
        + [const_spec(a.shape) for a in (out_w, gain, up_w, down_w)],
        out_specs=[
            pl.BlockSpec((chunk, width), row_block),
            pl.BlockSpec((chunk, width), row_block),
            const_spec((width, hidden)),
            const_spec((width, hidden)),
            const_spec((width, width)),
            const_spec((8, width)),
            const_spec((8, hidden)),
        ],
        out_shape=[
            jax.ShapeDtypeStruct((total, width), F32),
            jax.ShapeDtypeStruct((total, width), BF),
            jax.ShapeDtypeStruct((width, hidden), F32),
            jax.ShapeDtypeStruct((width, hidden), F32),
            jax.ShapeDtypeStruct((width, width), F32),
            jax.ShapeDtypeStruct((8, width), F32),
            jax.ShapeDtypeStruct((8, hidden), F32),
        ],
        scratch_shapes=[pltpu.VMEM((chunk, hidden), BF)],
        compiler_params=params(),
        cost_estimate=cost,
        name="ffn_backward",
    )(branch, act, slope, normed, xhat, rstd, mix, out_w, gain, up_w, down_w)


def attn_backward_body(
    scale, mixed, qkv, prob, normed, xhat_ref, rstd_ref, first, weight, gain, mask,
    qkv_before, table_before, vec_before, input_out, qkv_acc, table_acc, vec_acc, grads, score_grads, sums,
):
    @pl.when(pl.program_id(0) == 0)
    def _():
        qkv_acc[...] = qkv_before[...]
        table_acc[...] = table_before[...]
        vec_acc[...] = vec_before[...]

    columns = input_out.shape[2]
    tokens = columns * WIN

    def attend(pair, _):
        head_at = mask[...]
        for half in range(2):
            lanes = slice(256 * half, 256 * half + 256)
            low = prob[pair, lanes]
            mixed_blocks = blocks_of(mixed, pair, 128 * half)
            values = spread_heads(pair_of(qkv, pair, 512 + 128 * half), head_at)
            prob_grad = dot_nt(values, mixed_blocks).reshape(4, 64, 128)
            probs = low.astype(F32).reshape(4, 64, 128)
            shared = jnp.sum(prob_grad * probs, 1, keepdims=True)
            score_grad = (probs * (prob_grad - shared)).astype(BF).reshape(256, 128)
            table_acc[lanes] += score_grad.astype(F32)
            score_grads[pair, lanes] = score_grad
        return 0

    def project(pair, _):
        head_at = mask[...]
        for half in range(2):
            lanes = slice(256 * half, 256 * half + 256)
            low = prob[pair, lanes]
            mixed_blocks = blocks_of(mixed, pair, 128 * half)
            score_grad = score_grads[pair, lanes]
            keys = spread_heads(pair_of(qkv, pair, 256 + 128 * half), head_at)
            queries = blocks_of(qkv, pair, 128 * half)
            query_grad = (dot_tn(score_grad, keys) * scale).astype(BF)
            out = slice(128 * half, 128 * half + 128)
            grads[pl.ds(pair * 128, 64), out] = query_grad[:64, :128]
            grads[pl.ds(pair * 128 + 64, 64), out] = query_grad[64:, 128:]
            wide = head_at.astype(F32)
            key_grad = (dot(score_grad, queries) * wide).reshape(4, 64, 256)
            key_grad = (jnp.sum(key_grad, 0) * scale).astype(BF)
            out = slice(256 + 128 * half, 256 + 128 * half + 128)
            grads[pl.ds(pair * 128, 64), out] = key_grad[:, :128]
            grads[pl.ds(pair * 128 + 64, 64), out] = key_grad[:, 128:]
            value_grad = (dot(low, mixed_blocks) * wide).reshape(4, 64, 256)
            value_grad = jnp.sum(value_grad, 0).astype(BF)
            out = slice(512 + 128 * half, 512 + 128 * half + 128)
            grads[pl.ds(pair * 128, 64), out] = value_grad[:, :128]
            grads[pl.ds(pair * 128 + 64, 64), out] = value_grad[:, 128:]
        return 0

    lax.fori_loop(0, columns // 16, attend, 0, unroll=8)
    lax.fori_loop(0, columns // 16, project, 0, unroll=8)
    for f in range(0, 768, 256):
        qkv_acc[:, f : f + 256] += dot_tn(normed[...], grads[:, f : f + 256])

    def part(k, _):
        at = pl.ds(k * 256, 256)
        dy = dot_nt(grads[at], weight[...])
        xhat = xhat_ref[at]
        rstd = rstd_ref[at]
        rstd = jnp.concatenate([rstd, rstd], 1)
        total = first[at] + norm_back(dy, xhat, rstd, gain[...])
        sums[pl.ds(k * 4, 4)] = total.reshape(4, WIN, WIN, 256)
        vec_acc[0:1] += column_sum(dy * xhat)
        vec_acc[1:2] += column_sum(dy)
        return 0

    lax.fori_loop(0, tokens // 256, part, 0, unroll=True)

    def rows_out(r, _):
        input_out[0, r] = pltpu.roll(sums[:, r].reshape(columns, 256), columns - WIN // 2, 0)
        return 0

    lax.fori_loop(0, WIN, rows_out, 0, unroll=True)


def attn_backward(
    mixed, qkv, prob, normed, xhat, rstd, first, weight, gain, mask, scale, shape, band, before
):
    samples, grid_rows, columns, width = shape
    bands = grid_rows // WIN
    tokens = WIN * columns

    def row_block(step):
        return (step * bands + band, 0)

    cost = pl.CostEstimate(flops=8 * 10**9, bytes_accessed=16 * 10**6, transcendentals=0)
    return pl.pallas_call(
        functools.partial(attn_backward_body, scale),
        grid=(samples,),
        in_specs=[
            pl.BlockSpec((tokens, width), row_block),
            pl.BlockSpec((tokens, 3 * width), row_block),
            pl.BlockSpec((columns // 16, 512, 128), lambda s: (s * bands + band, 0, 0)),
            pl.BlockSpec((tokens, width), row_block),
            pl.BlockSpec((tokens, width), row_block),
            pl.BlockSpec((tokens, 128), row_block),
            pl.BlockSpec((tokens, width), row_block),
            const_spec(weight.shape),
            const_spec(gain.shape),
            const_spec(mask.shape),
        ]
        + [const_spec(a.shape) for a in before],
        out_specs=[
            pl.BlockSpec((1, WIN, columns, width), lambda s: (s, 0, 0, 0)),
            const_spec((width, 3 * width)),
            const_spec((512, 128)),
            const_spec((8, width)),
        ],
        out_shape=[
            jax.ShapeDtypeStruct((samples, WIN, columns, width), F32),
            jax.ShapeDtypeStruct((width, 3 * width), F32),
            jax.ShapeDtypeStruct((512, 128), F32),
            jax.ShapeDtypeStruct((8, width), F32),
        ],
        scratch_shapes=[
            pltpu.VMEM((tokens, 3 * width), BF),
            pltpu.VMEM((columns // 16, 512, 128), BF),
            pltpu.VMEM((columns // WIN, WIN, WIN, width), F32),
        ],
        compiler_params=params(),
        cost_estimate=cost,
        name="attn_backward",
    )(mixed, qkv, prob, normed, xhat, rstd, first, weight, gain, mask, *before)


def shifted(row, column, by):
    columns = row.shape[0]
    moved = pltpu.roll(row, by % columns, 0)
    edge = 0 if by == 1 else columns - 1
    return jnp.where(column == edge, 0.0, moved)


def row_limit(place, sample, row, allowed=True):
    return jnp.where((row < place[1 + sample]) & allowed, place[3 + sample], 0)


def put_taps(row, limit, target, at, lanes):
    column = iota((row.shape[0], 1), 0)
    wide = jnp.where(column < limit, row.astype(F32), 0.0)
    target[at, :, lanes[0] : lanes[0] + 256] = shifted(wide, column, -1).astype(BF)
    target[at, :, lanes[1] : lanes[1] + 256] = wide.astype(BF)
    target[at, :, lanes[2] : lanes[2] + 256] = shifted(wide, column, 1).astype(BF)


def put_rows(source, count, first, sample, place, row, target, at, lanes):
    def one(r, _):
        put_taps(source[0, first + r], row_limit(place, sample, row + r), target, at + r, lanes)
        return 0

    lax.fori_loop(0, count, one, 0, unroll=True)


def grad_taps(framed, height, place, above, own, below, taps):
    sample = pl.program_id(0)
    half = WIN // 2
    rows = own.shape[1]
    start = place[0] + half
    lanes = (0, 256, 512)
    is_first, is_last = start == 0, start + rows == height
    before = jnp.where(is_first, height, start) - half - 1
    if framed:
        put_rows(above, half + 1, 0, sample, place, before, taps, 0, lanes)
        put_taps(own[0, 0], row_limit(place, sample, start, ~is_first), taps, half + 1, lanes)
        limit = row_limit(place, sample, start - 1, ~is_first)
        put_taps(above[0, half], limit, taps, half + 2, lanes)
        put_rows(own, rows - half + 1, 0, sample, place, start, taps, half + 3, lanes)
        return ((0, 0, half), (half + 2, half, rows - half))
    limit = row_limit(place, sample, start - 1, ~is_first)
    put_taps(above[0, half], limit, taps, 0, lanes)
    put_rows(own, rows, 0, sample, place, start, taps, 1, lanes)
    limit = row_limit(place, sample, start + rows, ~is_last)
    put_taps(below[0, 0], limit, taps, rows + 1, lanes)
    return ((0, 0, rows),)


def tap_rows(rows, framed):
    return rows + 4 if framed else rows + 2


def weight_sums(groups, source, taps, acc):
    columns = taps.shape[1]
    for start, target, rows in groups:
        turned = source(target, rows).T
        for a in range(3):
            piece = taps[start + 2 - a : start + 2 - a + rows].reshape(rows * columns, 768)
            acc[a] += dot(turned, piece)


def conv_hidden_body(height, place, above, own, below, hidden, out, vec, taps, held, acc):
    sample = pl.program_id(0)

    @pl.when(sample == 0)
    def _():
        acc[...] = jnp.zeros_like(acc)
        vec[...] = jnp.zeros_like(vec)

    columns = hidden.shape[2]
    rows = hidden.shape[1]
    column = iota((columns, 1), 0)
    groups = grad_taps(False, height, place, above, own, below, taps)

    def one(r, _):
        limit = row_limit(place, sample, place[0] + WIN // 2 + r)
        held[r] = jnp.where(column < limit, hidden[0, r].astype(F32), 0.0).astype(BF)
        vec[0:1] += jnp.sum(taps[r + 1, :, 256:512].astype(F32), 0, keepdims=True)
        return 0

    lax.fori_loop(0, rows, one, 0, unroll=4)
    weight_sums(groups, lambda t, n: held[t : t + n].reshape(n * columns, 256), taps, acc)

    @pl.when(sample == pl.num_programs(0) - 1)
    def _():
        for k in range(9):
            at = 256 * (k % 3)
            out[k] = acc[k // 3, :, at : at + 256].astype(BF)


def conv_sums_body(height, place, above, own, below, sums, hidden_part, out, taps, acc):
    sample = pl.program_id(0)

    @pl.when(sample == 0)
    def _():
        acc[...] = jnp.zeros_like(acc)

    columns = sums.shape[2]
    groups = grad_taps(True, height, place, above, own, below, taps)
    weight_sums(groups, lambda t, n: sums[0, t : t + n].reshape(n * columns, 256), taps, acc)

    @pl.when(sample == pl.num_programs(0) - 1)
    def _():
        for k in range(9):
            at = 256 * (k % 3)
            out[k, 0] = acc[k // 3, :, at : at + 256].astype(BF)
            out[k, 1] = hidden_part[k]


def field_spec(a):
    return pl.BlockSpec((1,) + a.shape[1:], lambda s: (s, 0, 0, 0))


def conv_call(body, name, place, fields, consts, framed, height, out_specs, out_shape, scratch):
    samples, rows, columns, width = fields[1].shape
    cost = pl.CostEstimate(flops=48 * 10**8, bytes_accessed=8 * 10**6, transcendentals=0)
    taps = pltpu.VMEM((tap_rows(rows, framed), columns, 3 * width), BF)
    return pl.pallas_call(
        functools.partial(body, height),
        grid=(samples,),
        in_specs=[SMEM_SPEC] + [field_spec(a) for a in fields] + [s for s, _ in consts],
        out_specs=out_specs,
        out_shape=out_shape,
        scratch_shapes=[taps] + scratch,
        compiler_params=params(),
        cost_estimate=cost,
        name=name,
    )(place, *fields, *[a for _, a in consts])


def conv_hidden(place, grads, hidden, height):
    _, rows, columns, width = hidden.shape
    return conv_call(
        conv_hidden_body, "conv_hidden", place, (*grads, hidden), (), False, height,
        [const_spec((9, width, width)), const_spec((8, width))],
        [jax.ShapeDtypeStruct((9, width, width), BF), jax.ShapeDtypeStruct((8, width), F32)],
        [pltpu.VMEM((rows, columns, width), BF), pltpu.VMEM((3, width, 3 * width), F32)],
    )


def conv_sums(place, grads, sums, hidden_part, height):
    width = sums.shape[-1]
    shape = (9, 2, width, width)
    return conv_call(
        conv_sums_body, "conv_sums", place, (*grads, sums),
        ((const_spec(hidden_part.shape), hidden_part),), True, height,
        const_spec(shape), jax.ShapeDtypeStruct(shape, BF),
        [pltpu.VMEM((3, width, 3 * width), F32)],
    )


def conv_data_body(framed, height, place, above, own, below, weight, out, taps, turned):
    sample = pl.program_id(0)
    columns = own.shape[2]
    column = iota((columns, 1), 0)

    @pl.when(sample == 0)
    def _():
        for k in range(9):
            at = 256 * (k % 3)
            turned[k // 3, :, at : at + 256] = weight[k, 0]

    groups = grad_taps(framed, height, place, above, own, below, taps)
    for start, target, rows in groups:
        for r in range(0, rows, 4):
            total = 0.0
            for a in range(3):
                first = start + r + 2 - a
                piece = taps[first : first + 4].reshape(4 * columns, 768)
                total = total + dot_nt(piece, turned[a])
            for k in range(4):
                at = target + r + k
                row = place[0] + at
                if framed:
                    row = jnp.where(row < 0, row + height, row)
                else:
                    row = row + WIN // 2
                limit = row_limit(place, sample, row)
                part = jnp.where(column < limit, total[k * columns : (k + 1) * columns], 0.0)
                if framed:
                    part = pltpu.roll(part, WIN // 2, 0)
                    out[at // WIN, :, at % WIN] = part.reshape(columns // WIN, WIN, 256)
                else:
                    out[0, at] = part


def conv_data(place, grads, weight, part, height):
    samples, rows, columns, width = grads[1].shape
    framed = part == 0
    if framed:
        shape = (samples * rows // WIN, columns // WIN, WIN, WIN, width)
        spec = pl.BlockSpec((rows // WIN,) + shape[1:], lambda s: (s, 0, 0, 0, 0))
    else:
        shape = (samples, rows, columns, width)
        spec = pl.BlockSpec((1,) + shape[1:], lambda s: (s, 0, 0, 0))
    weight_spec = pl.BlockSpec((9, 1, width, width), lambda s: (0, part, 0, 0))
    return conv_call(
        functools.partial(conv_data_body, framed), "conv_data", place, grads,
        ((weight_spec, weight),), framed, height, spec, jax.ShapeDtypeStruct(shape, F32),
        [pltpu.VMEM((3, width, 3 * width), BF)],
    )


def conv_forward_body(
    height, place, sums, sums_below, hidden_above, hidden, hidden_below, weight, bias, out, taps
):
    sample = pl.program_id(0)
    rows, columns = out.shape[1:3]
    column = iota((columns, 1), 0)
    half = WIN // 2
    start = place[0] + half
    not_first, not_last = start != 0, start + rows != height
    lanes = (1024, 512, 0)
    limit = row_limit(place, sample, start - 1, not_first)
    put_taps(sums[0, half - 1], limit, taps, 0, lanes)
    put_rows(sums, rows - half, half, sample, place, start, taps, 1, lanes)
    put_rows(sums_below, half, 0, sample, place, start + rows - half, taps, rows - half + 1, lanes)
    after = row_limit(place, sample, start + rows, not_last)
    put_taps(sums_below[0, half], after, taps, rows + 1, lanes)
    lanes = (1280, 768, 256)
    put_taps(hidden_above[0, 0], limit, taps, 0, lanes)
    put_rows(hidden, rows, 0, sample, place, start, taps, 1, lanes)
    put_taps(hidden_below[0, 0], after, taps, rows + 1, lanes)
    for r in range(0, rows, 4):
        total = bias[...]
        for a in range(3):
            piece = taps[r + a : r + a + 4].reshape(4 * columns, 1536)
            total = total + dot(piece, weight[a * 1536 : (a + 1) * 1536])
        for k in range(4):
            limit = row_limit(place, sample, start + r + k)
            part = total[k * columns : (k + 1) * columns]
            out[0, r + k] = jnp.where(column < limit, part, 0.0).astype(BF)


def conv_forward(place, sums, sums_below, hidden, weight, bias, height):
    samples, rows, columns, width = sums.shape
    fields = (sums, sums_below, *hidden)
    cost = pl.CostEstimate(flops=96 * 10**8, bytes_accessed=10 * 10**6, transcendentals=0)
    return pl.pallas_call(
        functools.partial(conv_forward_body, height),
        grid=(samples,),
        in_specs=[SMEM_SPEC]
        + [field_spec(a) for a in fields]
        + [const_spec(weight.shape), const_spec(bias.shape)],
        out_specs=field_spec(sums),
        out_shape=jax.ShapeDtypeStruct(sums.shape, BF),
        scratch_shapes=[pltpu.VMEM((rows + 2, columns, 6 * width), BF)],
        compiler_params=params(),
        cost_estimate=cost,
        name="conv_forward",
    )(place, *fields, weight, bias)


def offset_onehot():
    places = jnp.arange(WIN * WIN)
    row, col = places // WIN, places % WIN
    offsets = (row[None, :] - row[:, None] + WIN - 1) * (2 * WIN - 1) + (
        col[None, :] - col[:, None] + WIN - 1
    )
    return (offsets.reshape(-1)[:, None] == jnp.arange((2 * WIN - 1) ** 2)[None, :]).astype(F32)


def shards(
    layer_input,
    hidden_state,
    crop_rows,
    crop_cols,
    first_gain,
    first_shift,
    qkv_weight,
    bias_table,
    output_weight,
    output_bias,
    second_gain,
    second_shift,
    up_weight,
    up_bias,
    down_weight,
    down_bias,
    conv_weight_in,
    conv_bias,
    cotangent,
):
    samples, grid_rows, columns, width = layer_input.shape
    shape = layer_input.shape
    heads = bias_table.shape[1]
    scale = float((width // heads) ** (-0.5))
    half = WIN // 2
    devices = device_count()
    row_devices = lax.axis_size("rows")
    height = grid_rows * row_devices
    row_place = lax.axis_index("rows")
    row_start = row_place * grid_rows
    place = jnp.concatenate(
        [(row_start - half)[None].astype(jnp.int32), crop_rows, crop_cols]
    ).astype(jnp.int32)

    hidden_width = up_weight.shape[1]
    blocks = hidden_width // width

    def vec(v):
        return v.reshape(1, -1)

    def after(x, *others):
        return lax.optimization_barrier((x, *others))[0]

    conv_full = gather_behind(conv_weight_in.astype(BF)).reshape(-1, width)
    input_above = ring(layer_input[:, grid_rows - half :], 1)
    qkv_full = gather_copies(qkv_weight.astype(BF)).reshape(width, -1)
    grad_above = ring(cotangent[:, grid_rows - half - 1 :], 1)
    grad_below = ring(cotangent[:, :1], -1)
    hidden_above = ring(after(hidden_state[:, grid_rows - 1 :], qkv_full), 1)
    hidden_below = ring(after(hidden_state[:, :1], qkv_full), -1)
    grads = (grad_above, cotangent, grad_below)

    def in_blocks(w):
        return w.reshape(-1, blocks, width).transpose(1, 0, 2)

    rows_out, rows_up, rows_down = (
        output_weight.shape[0], up_weight.shape[0], down_weight.shape[0],
    )
    mid = jnp.concatenate(
        [output_weight, in_blocks(up_weight).reshape(-1, width), down_weight], 0
    ).astype(BF)
    mid_full = gather_copies(after(mid, qkv_full))
    output_full = mid_full[:, :rows_out].reshape(width, width)
    up_full = mid_full[:, rows_out : rows_out + blocks * rows_up]
    up_full = up_full.reshape(devices, blocks, rows_up, width).transpose(0, 2, 1, 3)
    up_full = up_full.reshape(width, hidden_width)
    down_full = mid_full[:, rows_out + blocks * rows_up :].reshape(hidden_width, width)

    onehot = offset_onehot()
    pos_bias = jnp.dot(onehot, bias_table, precision=HIGHEST).reshape(WIN * WIN, WIN * WIN, heads)
    pos_bias = pos_bias.transpose(2, 0, 1).reshape(heads * WIN * WIN, WIN * WIN) * (1.0 / scale)
    pos_bias = jnp.concatenate([pos_bias, pos_bias], 1)
    mask = jnp.asarray(head_mask(), BF)

    conv_part, conv_bias_part = conv_hidden(place, grads, hidden_state, height)
    x, normed, xhat, rstd, qkv, prob, mix = attn_forward(
        place, input_above, layer_input, vec(first_gain), vec(first_shift),
        after(qkv_full, conv_bias_part), pos_bias, mask, height, scale,
    )
    normed_2, xhat_2, rstd_2, act, slope, sums = ffn_forward(
        place, x, mix, output_full, vec(output_bias), vec(second_gain), vec(second_shift),
        up_full, vec(up_bias), down_full, vec(down_bias), height, shape,
    )
    sums_below = ring(sums[:, : half + 1], -1)
    conv_local = conv_sums(place, grads, sums, conv_part, height)
    conv_all = lax.all_to_all(conv_local.reshape(devices, -1, width), AXES, 0, 0, tiled=True)
    conv_blocks = conv_full.reshape(9, 2, width, width)
    branch = conv_data(place, grads, after(conv_blocks, conv_local), 0, height)
    branch = branch.reshape(-1, width)
    first_grad, mixed, down_acc, up_acc, out_acc, vec_ffn, vec_up = ffn_backward(
        branch, act, slope, normed_2, xhat_2, rstd_2, mix, output_full, vec(second_gain),
        up_full, down_full,
    )
    small_ffn = [vec_ffn[3], vec_ffn[1], vec_ffn[2], vec_up[0], vec_ffn[0], conv_bias_part[0]]
    packed = pack_vectors(small_ffn, width)
    up_local = up_acc.astype(BF).reshape(devices, rows_up, blocks, width).transpose(0, 2, 1, 3)
    ffn_local = jnp.concatenate(
        [
            out_acc.astype(BF).reshape(devices, rows_out, width),
            up_local.reshape(devices, blocks * rows_up, width),
            down_acc.astype(BF).T.reshape(devices, rows_down, width),
            jnp.broadcast_to(packed[None], (devices,) + packed.shape),
        ],
        1,
    )
    ffn_all = lax.all_to_all(ffn_local, AXES, 0, 0, tiled=True)

    back = functools.partial(
        attn_backward, after(mixed, ffn_local), qkv, prob, normed, xhat, rstd, first_grad, qkv_full,
        vec(first_gain), mask, scale, shape,
    )
    none = (
        jnp.zeros((width, 3 * width), F32), jnp.zeros((512, 128), F32), jnp.zeros((8, width), F32),
    )
    input_top, *partial = back(0, none)
    input_from_below = ring(input_top[:, :half].astype(BF), -1).astype(F32)
    partial = after(tuple(partial), conv_all)
    input_low, qkv_acc, table_acc, vec_attn = back(1, partial)
    input_grad = jnp.concatenate([input_top[:, half:], input_low, input_from_below], 1)
    pair_grad = (table_acc[:, :64] + table_acc[:, 64:]).reshape(heads, -1)
    table_local = jnp.dot(pair_grad, onehot, precision=HIGHEST).T
    small_attn = [vec_attn[0], vec_attn[1], table_local]
    packed = pack_vectors(small_attn, width)
    qkv_rows = qkv_weight.shape[0]
    qkv_local = qkv_acc.astype(BF).reshape(devices, qkv_rows, 3, width).transpose(0, 2, 1, 3)
    qkv_local = jnp.concatenate(
        [
            qkv_local.reshape(devices, 3 * qkv_rows, width),
            jnp.broadcast_to(packed[None], (devices,) + packed.shape),
        ],
        1,
    )
    qkv_all = lax.all_to_all(qkv_local, AXES, 0, 0, tiled=True)

    hidden_grad = conv_data(after(place, qkv_acc), grads, conv_blocks, 1, height)
    layer_output = conv_forward(
        after(place, qkv_local, ffn_all, hidden_grad), sums, sums_below, (hidden_above, hidden_state, hidden_below), conv_full,
        vec(conv_bias), height,
    )

    def total(parts):
        return jnp.sum(parts.astype(F32), 0)

    conv_weight_grad = total(conv_all)
    output_weight_grad = total(ffn_all[:, :rows_out])
    up_rows = slice(rows_out, rows_out + blocks * rows_up)
    up_weight_grad = total(ffn_all[:, up_rows]).reshape(blocks, rows_up, width)
    up_weight_grad = up_weight_grad.transpose(1, 0, 2).reshape(rows_up, hidden_width)
    down_rows = slice(up_rows.stop, up_rows.stop + rows_down)
    down_weight_grad = total(ffn_all[:, down_rows])
    (
        output_bias_grad, second_gain_grad, second_shift_grad, up_bias_grad, down_bias_grad,
        conv_bias_grad,
    ) = unpack_vectors(ffn_all[:, down_rows.stop :], small_ffn)
    qkv_weight_grad = total(qkv_all[:, : 3 * qkv_rows]).reshape(3, qkv_rows, width)
    qkv_weight_grad = qkv_weight_grad.transpose(1, 0, 2).reshape(qkv_rows, 3 * width)
    first_gain_grad, first_shift_grad, bias_table_grad = unpack_vectors(
        qkv_all[:, 3 * qkv_rows :], small_attn
    )
    return (
        layer_output,
        input_grad,
        hidden_grad,
        first_gain_grad,
        first_shift_grad,
        qkv_weight_grad,
        bias_table_grad,
        output_weight_grad,
        output_bias_grad,
        second_gain_grad,
        second_shift_grad,
        up_weight_grad,
        up_bias_grad,
        down_weight_grad,
        down_bias_grad,
        conv_weight_grad,
        conv_bias_grad,
    )


def solution(mesh):
    field = P("batch", "rows", None, None)
    weight = P(AXES, None)
    in_specs = (
        field, field, P("batch"), P("batch"), P(), P(), weight, P(), weight, P(), P(), P(),
        weight, P(), weight, P(), weight, P(), field,
    )
    out_specs = (
        field, field, field, P(), P(), weight, P(), weight, P(), P(), P(), weight, P(), weight,
        P(), weight, P(),
    )
    return jax.shard_map(shards, mesh=mesh, in_specs=in_specs, out_specs=out_specs, check_vma=False)
```

```python
import functools

import jax
import jax.numpy as jnp
import numpy as np
from jax import lax
from jax.experimental import pallas as pl
from jax.experimental.pallas import tpu as pltpu
from jax.sharding import PartitionSpec as P

WIN = 8
EPSILON = 1e-05
MASKED = -100.0
HIGHEST = lax.Precision.HIGHEST
AXES = ("rows", "batch")
BF = jnp.bfloat16
F32 = jnp.float32
VMEM_LIMIT = 56 * 1024 * 1024
LOG2E = 1.4426950408889634


def dot(left, right):
    return jnp.dot(left, right, preferred_element_type=F32)


def dot_nt(left, right):
    return lax.dot_general(left, right, (((1,), (1,)), ((), ())), preferred_element_type=F32)


def dot_tn(left, right):
    return lax.dot_general(left, right, (((0,), (0,)), ((), ())), preferred_element_type=F32)


def iota(shape, dim):
    return lax.broadcasted_iota(jnp.int32, shape, dim)


def device_index():
    return lax.axis_index("rows") * lax.axis_size("batch") + lax.axis_index("batch")


def device_count():
    return lax.axis_size("rows") * lax.axis_size("batch")


def bit_groups():
    batch, rows = lax.axis_size("batch"), lax.axis_size("rows")
    batch_bits = [1 << k for k in range(batch.bit_length() - 1)]
    row_bits = [batch << k for k in range(rows.bit_length() - 1)]
    chips = row_bits[1:]
    groups = [batch_bits[k : k + 2] for k in range(0, len(batch_bits), 2)]
    groups += [chips[k : k + 2] for k in range(0, len(chips), 2)]
    return groups + [row_bits[:1]]


def gather_steps(x):
    devices = device_count()
    held = x[None]
    places = [0]
    for group in bit_groups():
        masks = [0]
        for bit in group:
            masks = masks + [m | bit for m in masks]
        pieces = [held]
        for mask in masks[1:]:
            pieces.append(lax.ppermute(held, AXES, [(i, i ^ mask) for i in range(devices)]))
        held = jnp.concatenate(pieces, 0)
        places = [p ^ m for m in masks for p in places]
    order = np.zeros(devices, np.int32)
    for place, mask in enumerate(places):
        order[mask] = place
    return held, jnp.asarray(order)[jnp.arange(devices) ^ device_index()]


def scatter_pairs(x):
    rows, batch = lax.axis_size("rows"), lax.axis_size("batch")
    core = lax.axis_index("rows") % 2
    by_core = x.reshape((rows // 2, 2, batch) + x.shape[1:])
    mine = lax.dynamic_index_in_dim(by_core, core, 1, False)
    other = lax.dynamic_index_in_dim(by_core, 1 - core, 1, False)
    other = lax.ppermute(other, "rows", [(i, i ^ 1) for i in range(rows)])
    pairs = (mine.astype(F32) + other.astype(F32)).astype(BF)
    pairs = pairs.reshape((rows // 2 * batch,) + x.shape[1:])
    groups = [
        [(2 * chip + k) * batch + b for chip in range(rows // 2) for b in range(batch)]
        for k in range(2)
    ]
    return pairs, lambda a: lax.all_to_all(a, AXES, 0, 0, axis_index_groups=groups, tiled=True)


def gather_behind(x):
    return lax.all_gather(x, AXES, axis=0, tiled=False)


def with_vectors(parts, vectors):
    rows = parts[0].shape[1]
    flat = vectors.reshape(1, rows, -1)
    flat = jnp.broadcast_to(flat, (parts[0].shape[0],) + flat.shape[1:])
    return jnp.concatenate(list(parts) + [flat], 2)


def vector_sums(rows, width):
    total = jnp.sum(rows.astype(F32), 0).reshape(8, -1, width)
    return [total[:, k] for k in range(total.shape[1])]


def ring(x, by):
    devices = lax.axis_size("rows")
    return lax.ppermute(x, "rows", [(i, (i + by) % devices) for i in range(devices)])


def norm_parts(x):
    centred = x - jnp.mean(x, -1, keepdims=True)
    rstd = lax.rsqrt(jnp.mean(centred * centred, -1, keepdims=True) + EPSILON)
    return centred * rstd, rstd


def norm_back(dy, xhat, rstd, gain):
    scaled = dy * gain
    first = jnp.mean(scaled, -1, keepdims=True)
    second = jnp.mean(scaled * xhat, -1, keepdims=True)
    return (scaled - first - xhat * second) * rstd


def head_mask():
    rows, lanes = np.arange(256)[:, None], np.arange(256)[None, :]
    return (rows // 64 == (lanes % 128) // 32).astype(np.float32)


def pair_of(ref, pair, column):
    first = ref[pl.ds(pair * 128, 64), column : column + 128]
    second = ref[pl.ds(pair * 128 + 64, 64), column : column + 128]
    return jnp.concatenate([first, second], 1)


def blocks_of(ref, pair, column):
    first = ref[pl.ds(pair * 128, 64), column : column + 128]
    second = ref[pl.ds(pair * 128 + 64, 64), column : column + 128]
    nothing = jnp.zeros_like(first)
    return jnp.concatenate(
        [jnp.concatenate([first, nothing], 1), jnp.concatenate([nothing, second], 1)], 0
    )


def spread_heads(pair, mask):
    return jnp.concatenate([pair] * 4, 0) * mask


def offset_places(turned):
    rows, lanes = np.arange(256)[:, None], np.arange(128)[None, :] % 64
    row, col = lanes // WIN, lanes % WIN
    if turned:
        row, col = WIN - 1 - row, WIN - 1 - col
    return (rows == row * (2 * WIN - 1) + col).astype(np.float32)


def three_parts(x):
    high = x.astype(BF)
    rest = x - high.astype(F32)
    middle = rest.astype(BF)
    return high, middle, (rest - middle.astype(F32)).astype(BF)


def spread_bias(table, places, bias, factor):
    line = 2 * WIN - 1
    for head in range(8):
        row = jnp.broadcast_to(table[head : head + 1], (WIN, 256))
        turns = []
        for r in range(WIN):
            by = 256 - (WIN - 1 - r) * line - (WIN - 1)
            turns.append(pltpu.roll(row, by, 1, stride=1, stride_axis=0))
        wide = jnp.concatenate(turns, 0)
        total = 0.0
        for part in three_parts(wide):
            total = total + dot(part, places[...])
        bias[head * 64 : head * 64 + 64] = total * factor


def collect_bias(grad, places):
    line = 2 * WIN - 1
    wide = 0.0
    for part in three_parts(grad):
        wide = wide + dot(part, places)
    out = []
    for head in range(8):
        total = jnp.zeros((WIN, 256), F32)
        for r in range(WIN):
            at = head * 64 + r * WIN
            total = total + pltpu.roll(wide[at : at + WIN], r * line, 1, stride=1, stride_axis=0)
        out.append(jnp.sum(total, 0, keepdims=True))
    return jnp.concatenate(out, 0)


def attn_forward_body(
    height, scale, step_of, place, above, upper, lower, gain, shift, weight, table, places, mask,
    x_out, norm_out, xhat_out, rstd_out, qkv_out, prob_out, mix_out, xs, bias,
):
    sample, band = step_of(pl.program_id(0))
    columns = lower.shape[2]

    @pl.when(pl.program_id(0) == 0)
    def _():
        spread_bias(table, places, bias, 1.0 / scale)

    def rows_from(ref, first):
        def rows_in(r, _):
            x = pltpu.roll(ref[0, r].astype(F32), WIN // 2, 0)
            xs[:, first + r] = x.reshape(columns // WIN, WIN, 256)
            return 0

        lax.fori_loop(0, WIN // 2, rows_in, 0, unroll=True)

    @pl.when(band == 0)
    def _():
        rows_from(above, 0)

    @pl.when(band > 0)
    def _():
        rows_from(upper, 0)

    rows_from(lower, WIN // 2)

    def norm_in(k, _):
        tokens = pl.ds(k * 128, 128)
        x = xs[pl.ds(k * 2, 2)].reshape(128, 256)
        xhat, rstd = norm_parts(x)
        x_out[tokens] = x.astype(BF)
        xhat_out[tokens] = xhat.astype(BF)
        rstd_out[tokens] = jnp.broadcast_to(rstd, (128, 128))
        norm_out[tokens] = (xhat * gain[...] + shift[...]).astype(BF)
        return 0

    lax.fori_loop(0, columns // 16, norm_in, 0, unroll=8)
    for k in range(0, columns * WIN, 256):
        qkv_out[k : k + 256] = dot(norm_out[k : k + 256], weight[...]).astype(BF)

    key_at, query_at = iota((64, 128), 0), iota((64, 128), 1)
    window_at = query_at // 64
    query_at = query_at % 64
    row_base = place[0] + band * WIN
    key_row, query_row = key_at // WIN + row_base, query_at // WIN + row_base
    key_row = jnp.where(key_row < 0, key_row + height, key_row)
    query_row = jnp.where(query_row < 0, query_row + height, query_row)
    rows_differ = (key_row >= height - WIN // 2) != (query_row >= height - WIN // 2)
    row_bad = key_row >= place[1 + sample]

    def attend(pair, _):
        key_col = (pair * 2 + window_at) * WIN + key_at % WIN - WIN // 2
        query_col = (pair * 2 + window_at) * WIN + query_at % WIN - WIN // 2
        key_col = jnp.where(key_col < 0, key_col + columns, key_col)
        query_col = jnp.where(query_col < 0, query_col + columns, query_col)
        cols_differ = (key_col >= columns - WIN // 2) != (query_col >= columns - WIN // 2)
        bad = row_bad | (key_col >= place[3 + sample])
        minus = jnp.where(rows_differ | cols_differ, MASKED / scale, 0.0) + jnp.where(
            bad, MASKED / scale, 0.0
        )
        for half in range(2):
            keys = spread_heads(pair_of(qkv_out, pair, 256 + 128 * half), mask[...])
            queries = blocks_of(qkv_out, pair, 128 * half)
            scores = dot_nt(keys, queries).reshape(4, 64, 128)
            scores = scores + (bias[256 * half : 256 * half + 256].reshape(4, 64, 128) + minus[None])
            top = jnp.max(scores, 1, keepdims=True)
            raised = jnp.exp2((scores - top) * (scale * LOG2E))
            probs = raised * (1.0 / jnp.sum(raised, 1, keepdims=True))
            probs = probs.reshape(256, 128).astype(BF)
            prob_out[pair, 256 * half : 256 * half + 256] = probs
        return 0

    def mix(pair, _):
        for half in range(2):
            probs = prob_out[pair, 256 * half : 256 * half + 256]
            values = spread_heads(pair_of(qkv_out, pair, 512 + 128 * half), mask[...])
            mixed = dot_tn(probs, values).astype(BF)
            mix_out[pl.ds(pair * 128, 64), 128 * half : 128 * half + 128] = mixed[:64, :128]
            mix_out[pl.ds(pair * 128 + 64, 64), 128 * half : 128 * half + 128] = mixed[64:, 128:]
        return 0

    lax.fori_loop(0, columns // 16, attend, 0, unroll=8)
    lax.fori_loop(0, columns // 16, mix, 0, unroll=8)


def const_spec(shape):
    return pl.BlockSpec(shape, lambda *_: (0,) * len(shape))


SMALL_COST = pl.CostEstimate(flops=10**6, bytes_accessed=10**4, transcendentals=0)


def params():
    return pltpu.CompilerParams(vmem_limit_bytes=VMEM_LIMIT)


SMEM_SPEC = pl.BlockSpec(memory_space=pltpu.SMEM)


def band_steps(samples, bands):
    def step_of(step):
        return step % samples, bands[0] + step // samples

    return step_of, samples * len(bands)


def attn_forward(place, above, own, gain, shift, weight, table, places, mask, height, scale):
    samples, grid_rows, columns, width = own.shape
    half = WIN // 2
    bands = grid_rows // WIN
    tokens = WIN * columns
    steps = samples * bands

    def step_of(step):
        return step // bands, step % bands

    def row_block(step):
        return (step, 0)

    total = steps * tokens
    return pl.pallas_call(
        functools.partial(attn_forward_body, height, scale, step_of),
        grid=(steps,),
        in_specs=[
            SMEM_SPEC,
            pl.BlockSpec((1, half, columns, width), lambda s: (step_of(s)[0], 0, 0, 0)),
            pl.BlockSpec(
                (1, half, columns, width),
                lambda s: (step_of(s)[0], jnp.maximum(2 * step_of(s)[1] - 1, 0), 0, 0),
            ),
            pl.BlockSpec(
                (1, half, columns, width), lambda s: (step_of(s)[0], 2 * step_of(s)[1], 0, 0)
            ),
            const_spec((1, width)),
            const_spec((1, width)),
            const_spec(weight.shape),
            const_spec(table.shape),
            const_spec(places.shape),
            const_spec(mask.shape),
        ],
        out_specs=[
            pl.BlockSpec((tokens, width), row_block),
            pl.BlockSpec((tokens, width), row_block),
            pl.BlockSpec((tokens, width), row_block),
            pl.BlockSpec((tokens, 128), row_block),
            pl.BlockSpec((tokens, 3 * width), row_block),
            pl.BlockSpec((columns // 16, 512, 128), lambda s: (s, 0, 0)),
            pl.BlockSpec((tokens, width), row_block),
        ],
        out_shape=[
            jax.ShapeDtypeStruct((total, width), BF),
            jax.ShapeDtypeStruct((total, width), BF),
            jax.ShapeDtypeStruct((total, width), BF),
            jax.ShapeDtypeStruct((total, 128), F32),
            jax.ShapeDtypeStruct((total, 3 * width), BF),
            jax.ShapeDtypeStruct((total // 128, 512, 128), BF),
            jax.ShapeDtypeStruct((total, width), BF),
        ],
        scratch_shapes=[
            pltpu.VMEM((columns // WIN, WIN, WIN, width), F32),
            pltpu.VMEM((512, 128), F32),
        ],
        compiler_params=params(),
        cost_estimate=SMALL_COST,
        name="attn_forward",
    )(place, above, own, own, gain, shift, weight, table, places, mask)


def gelu_parts(x):
    share = 0.5 + 0.5 * lax.erf(x * 0.7071067811865476)
    bell = jnp.exp2(x * x * (-0.5 * LOG2E))
    return x * share, share + x * (bell * 0.3989422804014327)


def ffn_forward_body(
    height, step_of, place, x_ref, mix, out_w, out_b, gain, shift, up_w, up_b, down_w, down_b,
    norm_out, xhat_out, rstd_out, act_out, slope_out, sum_out, sums,
):
    sample, band = step_of(pl.program_id(0))
    columns = sum_out.shape[2]
    chunk = 256
    chunks = columns * WIN // chunk

    def attend_sum(k, _):
        tokens = pl.ds(k * chunk, chunk)
        first = x_ref[tokens].astype(F32) + dot(mix[tokens], out_w[...]) + out_b[...]
        sums[pl.ds(k * (chunk // 64), chunk // 64)] = first.reshape(chunk // 64, WIN, WIN, 256)
        xhat, rstd = norm_parts(first)
        norm_out[tokens] = (xhat * gain[...] + shift[...]).astype(BF)
        xhat_out[tokens] = xhat.astype(BF)
        rstd_out[tokens] = jnp.broadcast_to(rstd, (chunk, 128))
        return 0

    def raise_up(k, _):
        tokens = pl.ds(k * chunk, chunk)
        for f in range(0, 1024, 256):
            raised = dot(norm_out[tokens], up_w[:, f : f + 256]) + up_b[:, f : f + 256]
            act, slope = gelu_parts(raised)
            act_out[tokens, f : f + 256] = act.astype(BF)
            slope_out[tokens, f : f + 256] = slope.astype(BF)
        return 0

    def put_down(k, _):
        tokens = pl.ds(k * chunk, chunk)
        windows = pl.ds(k * (chunk // 64), chunk // 64)
        second = dot(act_out[tokens], down_w[...]) + down_b[...]
        sums[windows] += second.reshape(chunk // 64, WIN, WIN, 256)
        return 0

    lax.fori_loop(0, chunks, attend_sum, 0, unroll=True)
    lax.fori_loop(0, chunks, raise_up, 0, unroll=True)
    lax.fori_loop(0, chunks, put_down, 0, unroll=True)
    column = iota((columns, 1), 0)

    def rows_out(r, _):
        row = place[0] + band * WIN + r
        row = jnp.where(row < 0, row + height, row)
        limit = jnp.where(row < place[1 + sample], place[3 + sample], 0)
        back = pltpu.roll(sums[:, r].reshape(columns, 256), columns - WIN // 2, 0)
        sum_out[0, r] = jnp.where(column < limit, back, 0.0).astype(BF)
        return 0

    lax.fori_loop(0, WIN, rows_out, 0, unroll=True)


def ffn_forward(place, x, mix, out_w, out_b, gain, shift, up_w, up_b, down_w, down_b, height, shape):
    samples, grid_rows, columns, width = shape
    bands = grid_rows // WIN
    tokens = WIN * columns
    steps = samples * bands
    hidden = up_w.shape[1]
    total = steps * tokens

    def step_of(step):
        return step // bands, step % bands

    def row_block(step):
        return (step, 0)

    rows = [width, width, 128, hidden, hidden]
    types = [BF, BF, F32, BF, BF]
    return pl.pallas_call(
        functools.partial(ffn_forward_body, height, step_of),
        grid=(steps,),
        in_specs=[SMEM_SPEC]
        + [pl.BlockSpec((tokens, width), row_block)] * 2
        + [const_spec(a.shape) for a in (out_w, out_b, gain, shift, up_w, up_b, down_w, down_b)],
        out_specs=[pl.BlockSpec((tokens, n), row_block) for n in rows]
        + [pl.BlockSpec((1, WIN, columns, width), lambda s: (*step_of(s), 0, 0))],
        out_shape=[jax.ShapeDtypeStruct((total, n), t) for n, t in zip(rows, types)]
        + [jax.ShapeDtypeStruct(shape, BF)],
        scratch_shapes=[pltpu.VMEM((columns // WIN, WIN, WIN, width), F32)],
        compiler_params=params(),
        cost_estimate=SMALL_COST,
        name="ffn_forward",
    )(place, x, mix, out_w, out_b, gain, shift, up_w, up_b, down_w, down_b)


def column_sum(x):
    return jnp.sum(x, 0, keepdims=True)


def ffn_backward_body(
    height, step_of, place, above, own, act, slope, normed, xhat_ref, rstd_ref, mix, conv_w,
    out_w, gain, up_w, down_w, first_out, mixed_out, down_out, up_out, out_out, vec_out,
    taps, turned, branch, low, raised_s, attn, down_acc, up_acc, out_acc, vec,
):
    step = pl.program_id(0)
    sample, band = step_of(step)
    columns = own.shape[2]
    tokens = columns * WIN
    half = WIN // 2
    column = iota((columns, 1), 0)

    @pl.when(step == 0)
    def _():
        for ref in (down_acc, up_acc, out_acc, vec):
            ref[...] = jnp.zeros_like(ref)
        for k in range(9):
            at = 256 * (k % 3)
            turned[k // 3, :, at : at + 256] = conv_w[k, 0]

    start = place[0] + half
    not_first = start != 0
    lanes = (0, 256, 512)

    @pl.when(band == 0)
    def _():
        before = jnp.where(not_first, start, height) - half - 1
        put_rows(above, half + 1, 0, sample, place, before, taps, 0, lanes)
        put_taps(own[0, 0], row_limit(place, sample, start, not_first), taps, half + 1, lanes)
        limit = row_limit(place, sample, start - 1, not_first)
        put_taps(above[0, half], limit, taps, half + 2, lanes)
        put_rows(own, half + 1, 0, sample, place, start, taps, half + 3, lanes)

    @pl.when(band > 0)
    def _():
        for group in range(2):
            first = band * WIN + (group - 1) * half - 1
            put_rows(own, half + 2, first, sample, place, start + first, taps, group * (half + 2), lanes)

    for group in range(2):
        total = 0.0
        for a in range(3):
            at = group * (half + 2) + 2 - a
            piece = taps[at : at + half].reshape(half * columns, 768)
            total = total + dot_nt(piece, turned[a])
        for k in range(half):
            row = place[0] + band * WIN + group * half + k
            row = jnp.where(row < 0, row + height, row)
            limit = row_limit(place, sample, row)
            part = jnp.where(column < limit, total[k * columns : (k + 1) * columns], 0.0)
            part = pltpu.roll(part, half, 0)
            branch[:, group * half + k] = part.reshape(columns // WIN, WIN, 256)

    chunk = 256
    windows = chunk // 64
    for k in range(tokens // chunk):
        at = slice(k * chunk, (k + 1) * chunk)
        upper = branch[k * windows : (k + 1) * windows].reshape(chunk, 256)
        low[at] = upper.astype(BF)
        vec[0:1] += column_sum(upper.astype(BF).astype(F32))
    for k in range(tokens // chunk):
        at = slice(k * chunk, (k + 1) * chunk)
        for f in range(0, 1024, 256):
            wide = slice(f, f + 256)
            raised = (dot_nt(low[at], down_w[wide]) * slope[at, wide].astype(F32)).astype(BF)
            raised_s[at, wide] = raised
            row = 4 + f // 256
            vec[row : row + 1] += column_sum(raised.astype(F32))
    for k in range(tokens // chunk):
        at = slice(k * chunk, (k + 1) * chunk)
        dy = dot_nt(raised_s[at], up_w[...])
        xhat = xhat_ref[at].astype(F32)
        rstd = rstd_ref[at]
        rstd = jnp.concatenate([rstd, rstd], 1)
        upper = branch[k * windows : (k + 1) * windows].reshape(chunk, 256)
        first = upper + norm_back(dy, xhat, rstd, gain[...])
        first_out[at] = first
        attn[at] = first.astype(BF)
        vec[1:2] += column_sum(dy * xhat)
        vec[2:3] += column_sum(dy)
        vec[3:4] += column_sum(first.astype(BF).astype(F32))
    for k in range(tokens // chunk):
        at = slice(k * chunk, (k + 1) * chunk)
        mixed_out[at] = dot_nt(attn[at], out_w[...]).astype(BF)
    low_t = low[...].T
    normed_t = normed[...].T
    for f in range(0, 1024, 256):
        wide = slice(f, f + 256)
        down_acc[:, wide] += dot(low_t, act[:, wide])
        up_acc[:, wide] += dot(normed_t, raised_s[:, wide])
    out_acc[...] += dot(mix[...].T, attn[...])

    @pl.when(step == pl.num_programs(0) - 1)
    def _():
        for f in range(0, 1024, 256):
            wide = slice(f, f + 256)
            down_out[wide] = down_acc[:, wide].T.astype(BF)
            up_out[:, wide] = up_acc[:, wide].astype(BF)
        out_out[...] = out_acc[...].astype(BF)
        vec_out[...] = vec[...].astype(BF)


def ffn_backward(
    place, above, own, act, slope, normed, xhat, rstd, mix, conv_w, out_w, gain, up_w, down_w, height
):
    samples, grid_rows, columns, width = own.shape
    bands = grid_rows // WIN
    tokens = WIN * columns
    steps = samples * bands
    total = steps * tokens
    hidden = up_w.shape[1]

    def step_of(step):
        return step // bands, step % bands

    def row_block(step):
        return (step, 0)

    def sample_block(step):
        return (step_of(step)[0], 0, 0, 0)

    rows = (act, slope, normed, xhat, rstd, mix)
    return pl.pallas_call(
        functools.partial(ffn_backward_body, height, step_of),
        grid=(steps,),
        in_specs=[
            SMEM_SPEC,
            pl.BlockSpec((1,) + above.shape[1:], sample_block),
            pl.BlockSpec((1,) + own.shape[1:], sample_block),
        ]
        + [pl.BlockSpec((tokens, a.shape[1]), row_block) for a in rows]
        + [pl.BlockSpec((9, 1, width, width), lambda s: (0, 0, 0, 0))]
        + [const_spec(a.shape) for a in (out_w, gain, up_w, down_w)],
        out_specs=[
            pl.BlockSpec((tokens, width), row_block),
            pl.BlockSpec((tokens, width), row_block),
            const_spec((hidden, width)),
            const_spec((width, hidden)),
            const_spec((width, width)),
            const_spec((8, width)),
        ],
        out_shape=[
            jax.ShapeDtypeStruct((total, width), F32),
            jax.ShapeDtypeStruct((total, width), BF),
            jax.ShapeDtypeStruct((hidden, width), BF),
            jax.ShapeDtypeStruct((width, hidden), BF),
            jax.ShapeDtypeStruct((width, width), BF),
            jax.ShapeDtypeStruct((8, width), BF),
        ],
        scratch_shapes=[
            pltpu.VMEM((WIN + 4, columns, 3 * width), BF),
            pltpu.VMEM((3, width, 3 * width), BF),
            pltpu.VMEM((columns // WIN, WIN, WIN, width), F32),
            pltpu.VMEM((tokens, width), BF),
            pltpu.VMEM((tokens, hidden), BF),
            pltpu.VMEM((tokens, width), BF),
            pltpu.VMEM((width, hidden), F32),
            pltpu.VMEM((width, hidden), F32),
            pltpu.VMEM((width, width), F32),
            pltpu.VMEM((8, width), F32),
        ],
        compiler_params=params(),
        cost_estimate=SMALL_COST,
        name="ffn_backward",
    )(place, above, own, *rows, conv_w, out_w, gain, up_w, down_w)


def attn_backward_body(
    scale, first_band, mixed, qkv, prob, normed, xhat_ref, rstd_ref, first, weight, gain, mask, *rest
):
    if first_band:
        input_out, up_out, qkv_acc, table_acc, vec_acc, grads, score_grads, sums = rest
    else:
        (
            conv_vec, places, qkv_before, table_before, vec_before, _, input_out, qkv_out, vec_out,
            qkv_acc, table_acc, vec_acc, grads, score_grads, sums,
        ) = rest
    sample, part_of = pl.program_id(0), pl.program_id(1)
    columns = input_out.shape[2]
    tokens = columns * WIN
    half = WIN // 2

    def rows_out(target, before):
        for r in range(half):
            row = sums[:, before + r].reshape(columns, 256)
            target[0, r] = pltpu.roll(row, columns - half, 0).astype(target.dtype)

    @pl.when((sample == 0) & (part_of == 0))
    def _():
        if first_band:
            for ref in (qkv_acc, table_acc, vec_acc):
                ref[...] = jnp.zeros_like(ref)
        else:
            qkv_acc[...] = qkv_before[...]
            table_acc[...] = table_before[...]
            vec_acc[...] = vec_before[...]

    @pl.when(part_of == 0)
    def _():
        attn_backward_step(
            scale, mixed, qkv, prob, normed, xhat_ref, rstd_ref, first, weight, gain, mask,
            qkv_acc, table_acc, vec_acc, grads, score_grads, sums,
        )
        if first_band:
            rows_out(up_out, 0)
            rows_out(input_out, half)
        else:
            rows_out(input_out, 0)

    if not first_band:

        @pl.when(part_of == 1)
        def _():
            rows_out(input_out, half)

        @pl.when((part_of == 1) & (sample == pl.num_programs(0) - 1))
        def _():
            for f in range(0, 768, 256):
                qkv_out[:, f : f + 256] = qkv_acc[:, f : f + 256].astype(BF)
            table = collect_bias(table_acc[...], places[...])
            rest = jnp.concatenate([vec_acc[0:2], conv_vec[0:1], jnp.zeros((5, 256), F32)], 0)
            vec_out[...] = jnp.concatenate([table, rest], 1).astype(BF)


def attn_backward_step(
    scale, mixed, qkv, prob, normed, xhat_ref, rstd_ref, first, weight, gain, mask,
    qkv_acc, table_acc, vec_acc, grads, score_grads, sums,
):
    tokens = qkv.shape[0]
    columns = tokens // WIN

    def attend(pair, _):
        head_at = mask[...]
        for half in range(2):
            lanes = slice(256 * half, 256 * half + 256)
            low = prob[pair, lanes]
            mixed_blocks = blocks_of(mixed, pair, 128 * half)
            values = spread_heads(pair_of(qkv, pair, 512 + 128 * half), head_at)
            prob_grad = dot_nt(values, mixed_blocks).reshape(4, 64, 128)
            probs = low.astype(F32).reshape(4, 64, 128)
            shared = jnp.sum(prob_grad * probs, 1, keepdims=True)
            score_grad = (probs * (prob_grad - shared)).astype(BF).reshape(256, 128)
            table_acc[lanes] += score_grad.astype(F32)
            score_grads[pair, lanes] = score_grad
        return 0

    def project(pair, _):
        head_at = mask[...]
        for half in range(2):
            lanes = slice(256 * half, 256 * half + 256)
            low = prob[pair, lanes]
            mixed_blocks = blocks_of(mixed, pair, 128 * half)
            score_grad = score_grads[pair, lanes]
            keys = spread_heads(pair_of(qkv, pair, 256 + 128 * half), head_at)
            queries = blocks_of(qkv, pair, 128 * half)
            query_grad = (dot_tn(score_grad, keys) * scale).astype(BF)
            out = slice(128 * half, 128 * half + 128)
            grads[pl.ds(pair * 128, 64), out] = query_grad[:64, :128]
            grads[pl.ds(pair * 128 + 64, 64), out] = query_grad[64:, 128:]
            wide = head_at.astype(F32)
            key_grad = (dot(score_grad, queries) * wide).reshape(4, 64, 256)
            key_grad = (jnp.sum(key_grad, 0) * scale).astype(BF)
            out = slice(256 + 128 * half, 256 + 128 * half + 128)
            grads[pl.ds(pair * 128, 64), out] = key_grad[:, :128]
            grads[pl.ds(pair * 128 + 64, 64), out] = key_grad[:, 128:]
            value_grad = (dot(low, mixed_blocks) * wide).reshape(4, 64, 256)
            value_grad = jnp.sum(value_grad, 0).astype(BF)
            out = slice(512 + 128 * half, 512 + 128 * half + 128)
            grads[pl.ds(pair * 128, 64), out] = value_grad[:, :128]
            grads[pl.ds(pair * 128 + 64, 64), out] = value_grad[:, 128:]
        return 0

    lax.fori_loop(0, columns // 16, attend, 0, unroll=8)
    lax.fori_loop(0, columns // 16, project, 0, unroll=8)
    for f in range(0, 768, 256):
        qkv_acc[:, f : f + 256] += dot_tn(normed[...], grads[:, f : f + 256])

    def part(k, _):
        at = pl.ds(k * 256, 256)
        dy = dot_nt(grads[at], weight[...])
        xhat = xhat_ref[at].astype(F32)
        rstd = rstd_ref[at]
        rstd = jnp.concatenate([rstd, rstd], 1)
        total = first[at] + norm_back(dy, xhat, rstd, gain[...])
        sums[pl.ds(k * 4, 4)] = total.reshape(4, WIN, WIN, 256)
        vec_acc[0:1] += column_sum(dy * xhat)
        vec_acc[1:2] += column_sum(dy)
        return 0

    lax.fori_loop(0, tokens // 256, part, 0, unroll=True)


def attn_backward(
    mixed, qkv, prob, normed, xhat, rstd, first, weight, gain, mask, scale, shape, band, before
):
    samples, grid_rows, columns, width = shape
    bands = grid_rows // WIN
    tokens = WIN * columns
    half = WIN // 2

    def row_block(s, _):
        return (s * bands + band, 0)

    rows = (mixed, qkv, prob, normed, xhat, rstd, first)
    consts = (weight, gain, mask)
    in_specs = [pl.BlockSpec((tokens, a.shape[1]), row_block) for a in rows]
    in_specs[2] = pl.BlockSpec((columns // 16, 512, 128), lambda s, _: (s * bands + band, 0, 0))
    in_specs += [const_spec(a.shape) for a in consts]
    sums = [(width, 3 * width), (512, 128), (8, width)]
    field = jax.ShapeDtypeStruct(shape, F32)
    scratch = [
        pltpu.VMEM((tokens, 3 * width), BF),
        pltpu.VMEM((columns // 16, 512, 128), BF),
        pltpu.VMEM((columns // WIN, WIN, WIN, width), F32),
    ]
    if band == 0:
        out_specs = [
            pl.BlockSpec((1, half, columns, width), lambda s, _: (s, 0, 0, 0)),
            pl.BlockSpec((1, half, columns, width), lambda s, _: (s, 0, 0, 0)),
        ] + [const_spec(a) for a in sums]
        out_shape = [field, jax.ShapeDtypeStruct((samples, half, columns, width), BF)]
        out_shape += [jax.ShapeDtypeStruct(a, F32) for a in sums]
        aliases = {}
    else:
        in_specs += [const_spec(a.shape) for a in before[:-1]]
        in_specs += [pl.BlockSpec(memory_space=pl.ANY)]
        out_specs = [
            pl.BlockSpec((1, half, columns, width), lambda s, j: (s, 2 * band - 1 + j, 0, 0)),
            const_spec((width, 3 * width)),
            const_spec((8, 2 * width)),
        ]
        out_shape = [
            field,
            jax.ShapeDtypeStruct((width, 3 * width), BF),
            jax.ShapeDtypeStruct((8, 2 * width), BF),
        ]
        scratch = [pltpu.VMEM(a, F32) for a in sums] + scratch
        aliases = {len(in_specs) - 1: 0}
    return pl.pallas_call(
        functools.partial(attn_backward_body, scale, band == 0),
        grid=(samples, 1 if band == 0 else 2),
        in_specs=in_specs,
        out_specs=out_specs,
        out_shape=out_shape,
        scratch_shapes=scratch,
        input_output_aliases=aliases,
        compiler_params=params(),
        cost_estimate=SMALL_COST,
        name="attn_backward",
    )(*rows, *consts, *before)


def shifted(row, column, by):
    columns = row.shape[0]
    moved = pltpu.roll(row, by % columns, 0)
    edge = 0 if by == 1 else columns - 1
    return jnp.where(column == edge, 0.0, moved)


def row_limit(place, sample, row, allowed=True):
    return jnp.where((row < place[1 + sample]) & allowed, place[3 + sample], 0)


def put_taps(row, limit, target, at, lanes):
    column = iota((row.shape[0], 1), 0)
    wide = jnp.where(column < limit, row.astype(F32), 0.0)
    target[at, :, lanes[0] : lanes[0] + 256] = shifted(wide, column, -1).astype(BF)
    target[at, :, lanes[1] : lanes[1] + 256] = wide.astype(BF)
    target[at, :, lanes[2] : lanes[2] + 256] = shifted(wide, column, 1).astype(BF)


def put_rows(source, count, first, sample, place, row, target, at, lanes):
    def one(r, _):
        put_taps(source[0, first + r], row_limit(place, sample, row + r), target, at + r, lanes)
        return 0

    lax.fori_loop(0, count, one, 0, unroll=True)


def grad_taps(framed, height, place, above, own, below, taps):
    sample = pl.program_id(0)
    half = WIN // 2
    rows = own.shape[1]
    start = place[0] + half
    lanes = (0, 256, 512)
    is_first, is_last = start == 0, start + rows == height
    before = jnp.where(is_first, height, start) - half - 1
    if framed:
        put_rows(above, half + 1, 0, sample, place, before, taps, 0, lanes)
        put_taps(own[0, 0], row_limit(place, sample, start, ~is_first), taps, half + 1, lanes)
        limit = row_limit(place, sample, start - 1, ~is_first)
        put_taps(above[0, half], limit, taps, half + 2, lanes)
        put_rows(own, rows - half + 1, 0, sample, place, start, taps, half + 3, lanes)
        return ((0, 0, half), (half + 2, half, rows - half))
    limit = row_limit(place, sample, start - 1, ~is_first)
    put_taps(above[0, above.shape[1] - 1], limit, taps, 0, lanes)
    put_rows(own, rows, 0, sample, place, start, taps, 1, lanes)
    limit = row_limit(place, sample, start + rows, ~is_last)
    put_taps(below[0, 0], limit, taps, rows + 1, lanes)
    return ((0, 0, rows),)


def tap_rows(rows, framed):
    return rows + 5 if framed else rows + 2


def weight_sums(groups, source, taps, acc):
    columns = taps.shape[1]
    for start, target, rows in groups:
        turned = source(target, rows).T
        for a in range(3):
            piece = taps[start + 2 - a : start + 2 - a + rows].reshape(rows * columns, 768)
            acc[a] += dot(turned, piece)


def conv_hidden_body(height, place, own, hidden, acc, vec, taps, held):
    sample = pl.program_id(0)

    @pl.when(sample == 0)
    def _():
        acc[...] = jnp.zeros_like(acc)
        vec[...] = jnp.zeros_like(vec)

    columns = hidden.shape[2]
    rows = hidden.shape[1]
    column = iota((columns, 1), 0)
    start = place[0] + WIN // 2
    put_rows(own, rows, 0, sample, place, start, taps, 1, (0, 256, 512))
    for r in (0, rows + 1):
        taps[r] = jnp.zeros(taps.shape[1:], BF)

    def one(r, _):
        limit = row_limit(place, sample, start + r)
        held[r] = jnp.where(column < limit, hidden[0, r].astype(F32), 0.0).astype(BF)
        vec[0:1] += jnp.sum(taps[r + 1, :, 256:512].astype(F32), 0, keepdims=True)
        return 0

    lax.fori_loop(0, rows, one, 0, unroll=4)
    groups = ((0, 0, rows),)
    weight_sums(groups, lambda t, n: held[t : t + n].reshape(n * columns, 256), taps, acc)


def conv_sums_body(
    height, place, above, own, below, sums, first_row, last_row, hidden_part, out, taps, acc, acc_h
):
    sample = pl.program_id(0)

    @pl.when(sample == 0)
    def _():
        acc[...] = jnp.zeros_like(acc)
        acc_h[...] = hidden_part[...]

    columns = sums.shape[2]
    rows = own.shape[1]
    half = WIN // 2
    groups = grad_taps(True, height, place, above, own, below, taps)
    weight_sums(groups, lambda t, n: sums[0, t : t + n].reshape(n * columns, 256), taps, acc)

    start = place[0] + half
    column = iota((columns, 1), 0)
    after_last = rows + half
    limit = row_limit(place, sample, start + rows, start + rows != height)
    put_taps(below[0, 0], limit, taps, after_last, (0, 256, 512))
    for a, row, at, tap in ((2, first_row, start, half + 2), (0, last_row, start + rows - 1, after_last)):
        held = jnp.where(column < row_limit(place, sample, at), row[0, 0].astype(F32), 0.0)
        acc_h[a] += dot(held.astype(BF).T, taps[tap])

    @pl.when(sample == pl.num_programs(0) - 1)
    def _():
        for k in range(9):
            at = 256 * (k % 3)
            out[k, 0] = acc[k // 3, :, at : at + 256].astype(BF)
            out[k, 1] = acc_h[k // 3, :, at : at + 256].astype(BF)


def field_spec(a):
    return pl.BlockSpec((1,) + a.shape[1:], lambda s: (s, 0, 0, 0))


def conv_call(
    body, name, place, fields, consts, height, out_specs, out_shape, scratch, cost=None
):
    return pl.pallas_call(
        functools.partial(body, height),
        grid=(fields[0][1].shape[0],),
        in_specs=[SMEM_SPEC] + [s for s, _ in fields] + [s for s, _ in consts],
        out_specs=out_specs,
        out_shape=out_shape,
        scratch_shapes=scratch,
        compiler_params=params(),
        cost_estimate=cost or SMALL_COST,
        name=name,
    )(place, *[a for _, a in fields], *[a for _, a in consts])


def whole(a):
    return field_spec(a), a


def conv_hidden(place, own, hidden, height):
    _, rows, columns, width = hidden.shape
    sums = (3, width, 3 * width)
    return conv_call(
        conv_hidden_body, "conv_hidden", place, (whole(own), whole(hidden)), (), height,
        [const_spec(sums), const_spec((8, width))],
        [jax.ShapeDtypeStruct(sums, F32), jax.ShapeDtypeStruct((8, width), F32)],
        [
            pltpu.VMEM((tap_rows(rows, False), columns, 3 * width), BF),
            pltpu.VMEM((rows, columns, width), BF),
        ],
        pl.CostEstimate(flops=10**10, bytes_accessed=8 * 10**6, transcendentals=0),
    )


def conv_sums(place, grads, sums, hidden, hidden_part, height):
    _, rows, columns, width = sums.shape
    shape = (9, 2, width, width)
    first_row = pl.BlockSpec((1, 1, columns, width), lambda s: (s, 0, 0, 0))
    last_row = pl.BlockSpec((1, 1, columns, width), lambda s: (s, rows - 1, 0, 0))
    fields = [whole(a) for a in (*grads, sums)] + [(first_row, hidden), (last_row, hidden)]
    return conv_call(
        conv_sums_body, "conv_sums", place, fields,
        ((const_spec(hidden_part.shape), hidden_part),), height,
        const_spec(shape), jax.ShapeDtypeStruct(shape, BF),
        [
            pltpu.VMEM((tap_rows(rows, True), columns, 3 * width), BF),
            pltpu.VMEM((3, width, 3 * width), F32),
            pltpu.VMEM((3, width, 3 * width), F32),
        ],
    )


def conv_data_body(height, place, above, own, below, weight, out, taps, turned):
    sample = pl.program_id(0)
    columns = own.shape[2]
    column = iota((columns, 1), 0)

    @pl.when(sample == 0)
    def _():
        for k in range(9):
            at = 256 * (k % 3)
            turned[k // 3, :, at : at + 256] = weight[k, 0]

    grad_taps(False, height, place, above, own, below, taps)
    for r in range(0, own.shape[1], 4):
        total = 0.0
        for a in range(3):
            piece = taps[r + 2 - a : r + 6 - a].reshape(4 * columns, 768)
            total = total + dot_nt(piece, turned[a])
        for k in range(4):
            limit = row_limit(place, sample, place[0] + WIN // 2 + r + k)
            part = total[k * columns : (k + 1) * columns]
            out[0, r + k] = jnp.where(column < limit, part, 0.0)


def conv_data(place, grads, weight, height):
    own = grads[1]
    width = own.shape[-1]
    weight_spec = pl.BlockSpec((9, 1, width, width), lambda s: (0, 1, 0, 0))
    return conv_call(
        conv_data_body, "conv_data", place, [whole(a) for a in grads], ((weight_spec, weight),),
        height, field_spec(own), jax.ShapeDtypeStruct(own.shape, F32),
        [
            pltpu.VMEM((tap_rows(own.shape[1], False), own.shape[2], 3 * width), BF),
            pltpu.VMEM((3, width, 3 * width), BF),
        ],
    )


def conv_forward_body(
    height, place, sums, sums_below, hidden_above, hidden, hidden_below, weight, bias, out, taps
):
    sample = pl.program_id(0)
    rows, columns = out.shape[1:3]
    column = iota((columns, 1), 0)
    half = WIN // 2
    start = place[0] + half
    not_first, not_last = start != 0, start + rows != height
    lanes = (1024, 512, 0)
    limit = row_limit(place, sample, start - 1, not_first)
    put_taps(sums[0, half - 1], limit, taps, 0, lanes)
    put_rows(sums, rows - half, half, sample, place, start, taps, 1, lanes)
    put_rows(sums_below, half, 0, sample, place, start + rows - half, taps, rows - half + 1, lanes)
    after = row_limit(place, sample, start + rows, not_last)
    put_taps(sums_below[0, half], after, taps, rows + 1, lanes)
    lanes = (1280, 768, 256)
    put_taps(hidden_above[0, 0], limit, taps, 0, lanes)
    put_rows(hidden, rows, 0, sample, place, start, taps, 1, lanes)
    put_taps(hidden_below[0, 0], after, taps, rows + 1, lanes)
    for r in range(0, rows, 4):
        total = bias[...]
        for a in range(3):
            piece = taps[r + a : r + a + 4].reshape(4 * columns, 1536)
            total = total + dot(piece, weight[a * 1536 : (a + 1) * 1536])
        for k in range(4):
            limit = row_limit(place, sample, start + r + k)
            part = total[k * columns : (k + 1) * columns]
            out[0, r + k] = jnp.where(column < limit, part, 0.0).astype(BF)


def conv_forward(place, sums, sums_below, hidden, weight, bias, height):
    samples, rows, columns, width = sums.shape
    fields = (sums, sums_below, *hidden)
    return pl.pallas_call(
        functools.partial(conv_forward_body, height),
        grid=(samples,),
        in_specs=[SMEM_SPEC]
        + [field_spec(a) for a in fields]
        + [const_spec(weight.shape), const_spec(bias.shape)],
        out_specs=field_spec(sums),
        out_shape=jax.ShapeDtypeStruct(sums.shape, BF),
        scratch_shapes=[pltpu.VMEM((rows + 2, columns, 6 * width), BF)],
        compiler_params=params(),
        cost_estimate=SMALL_COST,
        name="conv_forward",
    )(place, *fields, weight, bias)


def shards(
    layer_input,
    hidden_state,
    crop_rows,
    crop_cols,
    first_gain,
    first_shift,
    qkv_weight,
    bias_table,
    output_weight,
    output_bias,
    second_gain,
    second_shift,
    up_weight,
    up_bias,
    down_weight,
    down_bias,
    conv_weight_in,
    conv_bias,
    cotangent,
):
    samples, grid_rows, columns, width = layer_input.shape
    shape = layer_input.shape
    heads = bias_table.shape[1]
    scale = float((width // heads) ** (-0.5))
    half = WIN // 2
    devices = device_count()
    row_devices = lax.axis_size("rows")
    height = grid_rows * row_devices
    row_place = lax.axis_index("rows")
    row_start = row_place * grid_rows
    place = jnp.concatenate(
        [(row_start - half)[None].astype(jnp.int32), crop_rows, crop_cols]
    ).astype(jnp.int32)

    hidden_width = up_weight.shape[1]

    def vec(v):
        return v.reshape(1, -1)

    def after(x, *others):
        return lax.optimization_barrier((x, *others))[0]

    conv_low = conv_weight_in.astype(BF)
    conv_full = gather_behind(conv_low).reshape(-1, width)
    input_above = ring(layer_input[:, grid_rows - half :], 1)
    conv_part, conv_bias_part = conv_hidden(place, cotangent, hidden_state, height)

    rows_out, rows_down = output_weight.shape[0], down_weight.shape[0]
    down_lanes = down_weight.reshape(-1, rows_out, width).transpose(1, 0, 2).reshape(rows_out, -1)
    near = jnp.concatenate([qkv_weight, output_weight, up_weight, down_lanes], 1).astype(BF)
    held, order = gather_steps(after(near, conv_low))

    def rows_of(start, stop):
        return jnp.take(held[:, :, start:stop], order, axis=0)

    at = [3 * width, 4 * width, 4 * width + hidden_width, 4 * width + 2 * hidden_width]
    qkv_full = rows_of(0, at[0]).reshape(width, -1)
    output_full = rows_of(at[0], at[1]).reshape(width, width)
    up_full = rows_of(at[1], at[2]).reshape(width, hidden_width)
    down_full = rows_of(at[2], at[3]).reshape(devices, rows_out, -1, width).transpose(0, 2, 1, 3)
    down_full = down_full.reshape(hidden_width, width)

    offsets = bias_table.shape[0]
    table = jnp.pad(bias_table.T, ((0, 0), (0, 256 - offsets)))
    mask = jnp.asarray(head_mask(), BF)

    x, normed, xhat, rstd, qkv, prob, mix = attn_forward(
        place, input_above, layer_input, vec(first_gain), vec(first_shift),
        after(qkv_full, conv_bias_part), table, jnp.asarray(offset_places(False), BF), mask,
        height, scale,
    )
    late_cotangent, late_hidden = after((cotangent, hidden_state), mix)
    grad_above = ring(late_cotangent[:, grid_rows - half - 1 :], 1)
    grad_below = ring(late_cotangent[:, :1], -1)
    hidden_above = ring(late_hidden[:, grid_rows - 1 :], 1)
    hidden_below = ring(late_hidden[:, :1], -1)
    grads = (grad_above, cotangent, grad_below)
    normed_2, xhat_2, rstd_2, act, slope, sums = ffn_forward(
        place, x, mix, output_full, vec(output_bias), vec(second_gain), vec(second_shift),
        up_full, vec(up_bias), down_full, vec(down_bias), height, shape,
    )
    conv_local = conv_sums(place, grads, sums, hidden_state, conv_part, height)
    conv_local, exchange = scatter_pairs(conv_local.reshape(devices, -1, width))
    conv_all = exchange(conv_local)
    conv_blocks = after(conv_full.reshape(9, 2, width, width), conv_local)
    sums_below = ring(after(sums[:, : half + 1], conv_local), -1)
    first_grad, mixed, down_acc, up_acc, out_acc, vec_ffn = ffn_backward(
        place, grad_above, cotangent, act, slope, normed_2, xhat_2, rstd_2, mix, conv_blocks,
        output_full, vec(second_gain), up_full, down_full, height,
    )
    down_local = down_acc.reshape(devices, -1, rows_out, width).transpose(0, 2, 1, 3)
    down_local = down_local.reshape(devices, rows_out, -1)
    ffn_local = with_vectors(
        [
            out_acc.reshape(devices, rows_out, -1), up_acc.reshape(devices, rows_out, -1), down_local,
        ],
        vec_ffn,
    )
    ffn_local, exchange = scatter_pairs(ffn_local)

    back = functools.partial(
        attn_backward, mixed, qkv, prob, normed, xhat, rstd, first_grad, qkv_full,
        vec(first_gain), mask, scale, shape,
    )
    input_grad, input_up, *partial = back(0, ())
    input_from_below = ring(input_up, -1)
    ffn_all = exchange(after(ffn_local, partial[0]))
    partial = after(tuple(partial), conv_all)
    input_grad, qkv_acc, vec_attn = back(
        1, (conv_bias_part, jnp.asarray(offset_places(True), BF).T, *partial, input_grad)
    )
    input_grad = lax.dynamic_update_slice(
        input_grad, input_from_below.astype(F32), (0, grid_rows - half, 0, 0)
    )
    qkv_local = with_vectors([qkv_acc.reshape(devices, rows_out, -1)], vec_attn)
    layer_output = conv_forward(
        after(place, qkv_local), sums, sums_below, (hidden_above, hidden_state, hidden_below),
        conv_full, vec(conv_bias), height,
    )
    qkv_local = after(qkv_local, ffn_all, layer_output)
    qkv_all = lax.all_to_all(qkv_local, AXES, 0, 0, tiled=True)
    hidden_grad = conv_data(after(place, qkv_local), grads, conv_blocks, height)

    def total(parts):
        return jnp.sum(parts.astype(F32), 0)

    conv_weight_grad = total(conv_all)
    ends = [width, width + hidden_width, width + 2 * hidden_width]
    output_weight_grad = total(ffn_all[:, :, : ends[0]])
    up_weight_grad = total(ffn_all[:, :, ends[0] : ends[1]])
    down_weight_grad = total(ffn_all[:, :, ends[1] : ends[2]]).reshape(rows_out, -1, width)
    down_weight_grad = down_weight_grad.transpose(1, 0, 2).reshape(rows_down, width)
    (ffn_vec,) = vector_sums(ffn_all[:, :, ends[2] :], width)
    down_bias_grad, second_gain_grad, second_shift_grad, output_bias_grad = (
        ffn_vec[k] for k in range(4)
    )
    up_bias_grad = ffn_vec[4:].reshape(-1)
    qkv_weight_grad = total(qkv_all[:, :, : 3 * width])
    table_grad, attn_vec = vector_sums(qkv_all[:, :, 3 * width :], width)
    bias_table_grad = table_grad[:, :offsets][:, ::-1].T
    first_gain_grad, first_shift_grad, conv_bias_grad = (attn_vec[k] for k in range(3))
    return (
        layer_output,
        input_grad,
        hidden_grad,
        first_gain_grad,
        first_shift_grad,
        qkv_weight_grad,
        bias_table_grad,
        output_weight_grad,
        output_bias_grad,
        second_gain_grad,
        second_shift_grad,
        up_weight_grad,
        up_bias_grad,
        down_weight_grad,
        down_bias_grad,
        conv_weight_grad,
        conv_bias_grad,
    )


def solution(mesh):
    field = P("batch", "rows", None, None)
    weight = P(AXES, None)
    in_specs = (
        field, field, P("batch"), P("batch"), P(), P(), weight, P(), weight, P(), P(), P(),
        weight, P(), weight, P(), weight, P(), field,
    )
    out_specs = (
        field, field, field, P(), P(), weight, P(), weight, P(), P(), P(), weight, P(), weight,
        P(), weight, P(),
    )
    return jax.shard_map(shards, mesh=mesh, in_specs=in_specs, out_specs=out_specs, check_vma=False)
```

```python
import functools

import jax
import jax.numpy as jnp
import numpy as np
from jax import lax
from jax.experimental import pallas as pl
from jax.experimental.pallas import tpu as pltpu
from jax.sharding import PartitionSpec as P

WIN = 8
EPSILON = 1e-05
MASKED = -100.0
HIGHEST = lax.Precision.HIGHEST
AXES = ("rows", "batch")
BF = jnp.bfloat16
F32 = jnp.float32
VMEM_LIMIT = 56 * 1024 * 1024
LOG2E = 1.4426950408889634


def dot(left, right):
    return jnp.dot(left, right, preferred_element_type=F32)


def dot_nt(left, right):
    return lax.dot_general(left, right, (((1,), (1,)), ((), ())), preferred_element_type=F32)


def dot_tn(left, right):
    return lax.dot_general(left, right, (((0,), (0,)), ((), ())), preferred_element_type=F32)


def iota(shape, dim):
    return lax.broadcasted_iota(jnp.int32, shape, dim)


def device_index():
    return lax.axis_index("rows") * lax.axis_size("batch") + lax.axis_index("batch")


def device_count():
    return lax.axis_size("rows") * lax.axis_size("batch")


def after(x, *others):
    return lax.optimization_barrier((x, *others))[0]


def bit_groups():
    batch, rows = lax.axis_size("batch"), lax.axis_size("rows")
    batch_bits = [1 << k for k in range(batch.bit_length() - 1)]
    row_bits = [batch << k for k in range(rows.bit_length() - 1)]
    chips = row_bits[1:]
    groups = [batch_bits[k : k + 2] for k in range(0, len(batch_bits), 2)]
    groups += [chips[k : k + 2] for k in range(0, len(chips), 2)]
    return groups + [row_bits[:1]]


def gather_steps(x, other):
    devices = device_count()
    held = x[None]
    places = [0]
    for group in bit_groups():
        masks = [0]
        for bit in group:
            masks = masks + [m | bit for m in masks]
        if group == bit_groups()[-1]:
            held = after(held, other)
        pieces = [held]
        for mask in masks[1:]:
            pieces.append(lax.ppermute(held, AXES, [(i, i ^ mask) for i in range(devices)]))
        held = jnp.concatenate(pieces, 0)
        places = [p ^ m for m in masks for p in places]
    order = np.zeros(devices, np.int32)
    for place, mask in enumerate(places):
        order[mask] = place
    return held, jnp.asarray(order)[jnp.arange(devices) ^ device_index()]


def scatter_pairs(x):
    rows, batch = lax.axis_size("rows"), lax.axis_size("batch")
    core = lax.axis_index("rows") % 2
    by_core = x.reshape((rows // 2, 2, batch) + x.shape[1:])
    mine = lax.dynamic_index_in_dim(by_core, core, 1, False)
    other = lax.dynamic_index_in_dim(by_core, 1 - core, 1, False)
    other = lax.ppermute(other, "rows", [(i, i ^ 1) for i in range(rows)])
    pairs = (mine.astype(F32) + other.astype(F32)).astype(BF)
    pairs = pairs.reshape((rows // 2 * batch,) + x.shape[1:])
    groups = [
        [(2 * chip + k) * batch + b for chip in range(rows // 2) for b in range(batch)]
        for k in range(2)
    ]
    return pairs, lambda a: lax.all_to_all(a, AXES, 0, 0, axis_index_groups=groups, tiled=True)


def gather_copies(copies):
    return lax.all_to_all(copies, AXES, 0, 0, tiled=True)


def with_vectors(parts, vectors):
    rows = parts[0].shape[1]
    flat = vectors.reshape(1, rows, -1)
    flat = jnp.broadcast_to(flat, (parts[0].shape[0],) + flat.shape[1:])
    return jnp.concatenate(list(parts) + [flat], 2)


def ring(x, by):
    devices = lax.axis_size("rows")
    return lax.ppermute(x, "rows", [(i, (i + by) % devices) for i in range(devices)])


def norm_parts(x):
    centred = x - jnp.mean(x, -1, keepdims=True)
    rstd = lax.rsqrt(jnp.mean(centred * centred, -1, keepdims=True) + EPSILON)
    return centred * rstd, rstd


def norm_back(dy, xhat, rstd, gain):
    scaled = dy * gain
    first = jnp.mean(scaled, -1, keepdims=True)
    second = jnp.mean(scaled * xhat, -1, keepdims=True)
    return (scaled - first - xhat * second) * rstd


def head_mask():
    rows, lanes = np.arange(256)[:, None], np.arange(256)[None, :]
    return (rows // 64 == (lanes % 128) // 32).astype(np.float32)


def pair_of(ref, pair, column):
    first = ref[pl.ds(pair * 128, 64), column : column + 128]
    second = ref[pl.ds(pair * 128 + 64, 64), column : column + 128]
    return jnp.concatenate([first, second], 1)


def blocks_of(ref, pair, column):
    first = ref[pl.ds(pair * 128, 64), column : column + 128]
    second = ref[pl.ds(pair * 128 + 64, 64), column : column + 128]
    nothing = jnp.zeros_like(first)
    return jnp.concatenate(
        [jnp.concatenate([first, nothing], 1), jnp.concatenate([nothing, second], 1)], 0
    )


def spread_heads(pair, mask):
    return jnp.concatenate([pair] * 4, 0) * mask


def offset_places(turned):
    rows, lanes = np.arange(256)[:, None], np.arange(128)[None, :] % 64
    row, col = lanes // WIN, lanes % WIN
    if turned:
        row, col = WIN - 1 - row, WIN - 1 - col
    return (rows == row * (2 * WIN - 1) + col).astype(np.float32)


def three_parts(x):
    high = x.astype(BF)
    rest = x - high.astype(F32)
    middle = rest.astype(BF)
    return high, middle, (rest - middle.astype(F32)).astype(BF)


def spread_bias(table, places, bias, factor):
    line = 2 * WIN - 1
    for head in range(8):
        row = jnp.broadcast_to(table[head : head + 1], (WIN, 256))
        turns = []
        for r in range(WIN):
            by = 256 - (WIN - 1 - r) * line - (WIN - 1)
            turns.append(pltpu.roll(row, by, 1, stride=1, stride_axis=0))
        wide = jnp.concatenate(turns, 0)
        total = 0.0
        for part in three_parts(wide):
            total = total + dot(part, places[...])
        bias[head * 64 : head * 64 + 64] = total * factor


def collect_bias(grad, places):
    line = 2 * WIN - 1
    wide = 0.0
    for part in three_parts(grad):
        wide = wide + dot(part, places)
    out = []
    for head in range(8):
        total = jnp.zeros((WIN, 256), F32)
        for r in range(WIN):
            at = head * 64 + r * WIN
            total = total + pltpu.roll(wide[at : at + WIN], r * line, 1, stride=1, stride_axis=0)
        out.append(jnp.sum(total, 0, keepdims=True))
    return jnp.concatenate(out, 0)


def attn_forward_body(
    height, scale, step_of, place, above, upper, lower, gain, shift, weight, table, places, mask,
    x_out, norm_out, xhat_out, rstd_out, qkv_out, prob_out, mix_out, xs, bias,
):
    sample, band = step_of(pl.program_id(0))
    columns = lower.shape[2]

    @pl.when(pl.program_id(0) == 0)
    def _():
        spread_bias(table, places, bias, 1.0 / scale)

    def rows_from(ref, first):
        def rows_in(r, _):
            x = pltpu.roll(ref[0, r].astype(F32), WIN // 2, 0)
            xs[:, first + r] = x.reshape(columns // WIN, WIN, 256)
            return 0

        lax.fori_loop(0, WIN // 2, rows_in, 0, unroll=True)

    @pl.when(band == 0)
    def _():
        rows_from(above, 0)

    @pl.when(band > 0)
    def _():
        rows_from(upper, 0)

    rows_from(lower, WIN // 2)

    def norm_in(k, _):
        tokens = pl.ds(k * 128, 128)
        x = xs[pl.ds(k * 2, 2)].reshape(128, 256)
        xhat, rstd = norm_parts(x)
        x_out[tokens] = x.astype(BF)
        xhat_out[tokens] = xhat.astype(BF)
        rstd_out[tokens] = jnp.broadcast_to(rstd, (128, 128))
        norm_out[tokens] = (xhat * gain[...] + shift[...]).astype(BF)
        return 0

    lax.fori_loop(0, columns // 16, norm_in, 0, unroll=8)
    for k in range(0, columns * WIN, 256):
        qkv_out[k : k + 256] = dot(norm_out[k : k + 256], weight[...]).astype(BF)

    key_at, query_at = iota((64, 128), 0), iota((64, 128), 1)
    window_at = query_at // 64
    query_at = query_at % 64
    row_base = place[0] + band * WIN
    key_row, query_row = key_at // WIN + row_base, query_at // WIN + row_base
    key_row = jnp.where(key_row < 0, key_row + height, key_row)
    query_row = jnp.where(query_row < 0, query_row + height, query_row)
    rows_differ = (key_row >= height - WIN // 2) != (query_row >= height - WIN // 2)
    row_bad = key_row >= place[1 + sample]

    def attend(pair, _):
        key_col = (pair * 2 + window_at) * WIN + key_at % WIN - WIN // 2
        query_col = (pair * 2 + window_at) * WIN + query_at % WIN - WIN // 2
        key_col = jnp.where(key_col < 0, key_col + columns, key_col)
        query_col = jnp.where(query_col < 0, query_col + columns, query_col)
        cols_differ = (key_col >= columns - WIN // 2) != (query_col >= columns - WIN // 2)
        bad = row_bad | (key_col >= place[3 + sample])
        minus = jnp.where(rows_differ | cols_differ, MASKED / scale, 0.0) + jnp.where(
            bad, MASKED / scale, 0.0
        )
        for half in range(2):
            keys = spread_heads(pair_of(qkv_out, pair, 256 + 128 * half), mask[...])
            queries = blocks_of(qkv_out, pair, 128 * half)
            scores = dot_nt(keys, queries).reshape(4, 64, 128)
            scores = scores + (bias[256 * half : 256 * half + 256].reshape(4, 64, 128) + minus[None])
            top = jnp.max(scores, 1, keepdims=True)
            raised = jnp.exp2((scores - top) * (scale * LOG2E))
            probs = raised * (1.0 / jnp.sum(raised, 1, keepdims=True))
            probs = probs.reshape(256, 128).astype(BF)
            prob_out[pair, 256 * half : 256 * half + 256] = probs
        return 0

    def mix(pair, _):
        for half in range(2):
            probs = prob_out[pair, 256 * half : 256 * half + 256]
            values = spread_heads(pair_of(qkv_out, pair, 512 + 128 * half), mask[...])
            mixed = dot_tn(probs, values).astype(BF)
            mix_out[pl.ds(pair * 128, 64), 128 * half : 128 * half + 128] = mixed[:64, :128]
            mix_out[pl.ds(pair * 128 + 64, 64), 128 * half : 128 * half + 128] = mixed[64:, 128:]
        return 0

    lax.fori_loop(0, columns // 16, attend, 0, unroll=8)
    lax.fori_loop(0, columns // 16, mix, 0, unroll=8)


def const_spec(shape):
    return pl.BlockSpec(shape, lambda *_: (0,) * len(shape))


SMALL_COST = pl.CostEstimate(flops=10**6, bytes_accessed=10**4, transcendentals=0)


def params():
    return pltpu.CompilerParams(vmem_limit_bytes=VMEM_LIMIT)


SMEM_SPEC = pl.BlockSpec(memory_space=pltpu.SMEM)


def band_steps(samples, bands):
    def step_of(step):
        return step % samples, bands[0] + step // samples

    return step_of, samples * len(bands)


def attn_forward(place, above, own, gain, shift, weight, table, places, mask, height, scale):
    samples, grid_rows, columns, width = own.shape
    half = WIN // 2
    bands = grid_rows // WIN
    tokens = WIN * columns
    steps = samples * bands

    def step_of(step):
        return step // bands, step % bands

    def row_block(step):
        return (step, 0)

    total = steps * tokens
    return pl.pallas_call(
        functools.partial(attn_forward_body, height, scale, step_of),
        grid=(steps,),
        in_specs=[
            SMEM_SPEC,
            pl.BlockSpec((1, half, columns, width), lambda s: (step_of(s)[0], 0, 0, 0)),
            pl.BlockSpec(
                (1, half, columns, width),
                lambda s: (step_of(s)[0], jnp.maximum(2 * step_of(s)[1] - 1, 0), 0, 0),
            ),
            pl.BlockSpec(
                (1, half, columns, width), lambda s: (step_of(s)[0], 2 * step_of(s)[1], 0, 0)
            ),
            const_spec((1, width)),
            const_spec((1, width)),
            const_spec(weight.shape),
            const_spec(table.shape),
            const_spec(places.shape),
            const_spec(mask.shape),
        ],
        out_specs=[
            pl.BlockSpec((tokens, width), row_block),
            pl.BlockSpec((tokens, width), row_block),
            pl.BlockSpec((tokens, width), row_block),
            pl.BlockSpec((tokens, 128), row_block),
            pl.BlockSpec((tokens, 3 * width), row_block),
            pl.BlockSpec((columns // 16, 512, 128), lambda s: (s, 0, 0)),
            pl.BlockSpec((tokens, width), row_block),
        ],
        out_shape=[
            jax.ShapeDtypeStruct((total, width), BF),
            jax.ShapeDtypeStruct((total, width), BF),
            jax.ShapeDtypeStruct((total, width), BF),
            jax.ShapeDtypeStruct((total, 128), F32),
            jax.ShapeDtypeStruct((total, 3 * width), BF),
            jax.ShapeDtypeStruct((total // 128, 512, 128), BF),
            jax.ShapeDtypeStruct((total, width), BF),
        ],
        scratch_shapes=[
            pltpu.VMEM((columns // WIN, WIN, WIN, width), F32),
            pltpu.VMEM((512, 128), F32),
        ],
        compiler_params=params(),
        cost_estimate=SMALL_COST,
        name="attn_forward",
    )(place, above, own, own, gain, shift, weight, table, places, mask)


def gelu_parts(x):
    share = 0.5 + 0.5 * lax.erf(x * 0.7071067811865476)
    bell = jnp.exp2(x * x * (-0.5 * LOG2E))
    return x * share, share + x * (bell * 0.3989422804014327)


def ffn_forward_body(
    height, step_of, place, x_ref, mix, out_w, out_b, gain, shift, up_w, up_b, down_w, down_b,
    norm_out, xhat_out, rstd_out, act_out, slope_out, sum_out, first_rows, sums,
):
    sample, band = step_of(pl.program_id(0))
    columns = sum_out.shape[2]
    chunk = 256
    chunks = columns * WIN // chunk

    def attend_sum(k, _):
        tokens = pl.ds(k * chunk, chunk)
        first = x_ref[tokens].astype(F32) + dot(mix[tokens], out_w[...]) + out_b[...]
        sums[pl.ds(k * (chunk // 64), chunk // 64)] = first.reshape(chunk // 64, WIN, WIN, 256)
        xhat, rstd = norm_parts(first)
        norm_out[tokens] = (xhat * gain[...] + shift[...]).astype(BF)
        xhat_out[tokens] = xhat.astype(BF)
        rstd_out[tokens] = jnp.broadcast_to(rstd, (chunk, 128))
        return 0

    def raise_up(k, _):
        tokens = pl.ds(k * chunk, chunk)
        for f in range(0, 1024, 256):
            raised = dot(norm_out[tokens], up_w[:, f : f + 256]) + up_b[:, f : f + 256]
            act, slope = gelu_parts(raised)
            act_out[tokens, f : f + 256] = act.astype(BF)
            slope_out[tokens, f : f + 256] = slope.astype(BF)
        return 0

    def put_down(k, _):
        tokens = pl.ds(k * chunk, chunk)
        windows = pl.ds(k * (chunk // 64), chunk // 64)
        second = dot(act_out[tokens], down_w[...]) + down_b[...]
        sums[windows] += second.reshape(chunk // 64, WIN, WIN, 256)
        return 0

    lax.fori_loop(0, chunks, attend_sum, 0, unroll=True)
    lax.fori_loop(0, chunks, raise_up, 0, unroll=True)
    lax.fori_loop(0, chunks, put_down, 0, unroll=True)
    column = iota((columns, 1), 0)

    def rows_out(r, _):
        row = place[0] + band * WIN + r
        row = jnp.where(row < 0, row + height, row)
        limit = jnp.where(row < place[1 + sample], place[3 + sample], 0)
        back = pltpu.roll(sums[:, r].reshape(columns, 256), columns - WIN // 2, 0)
        sum_out[0, r] = jnp.where(column < limit, back, 0.0).astype(BF)
        return 0

    lax.fori_loop(0, WIN, rows_out, 0, unroll=True)

    @pl.when(band == 0)
    def _():
        first_rows[0] = sum_out[0, : WIN // 2 + 1]


def ffn_forward(place, x, mix, out_w, out_b, gain, shift, up_w, up_b, down_w, down_b, height, shape):
    samples, grid_rows, columns, width = shape
    bands = grid_rows // WIN
    tokens = WIN * columns
    steps = samples * bands
    hidden = up_w.shape[1]
    total = steps * tokens

    def step_of(step):
        return step // bands, step % bands

    def row_block(step):
        return (step, 0)

    rows = [width, width, 128, hidden, hidden]
    types = [BF, BF, F32, BF, BF]
    return pl.pallas_call(
        functools.partial(ffn_forward_body, height, step_of),
        grid=(steps,),
        in_specs=[SMEM_SPEC]
        + [pl.BlockSpec((tokens, width), row_block)] * 2
        + [const_spec(a.shape) for a in (out_w, out_b, gain, shift, up_w, up_b, down_w, down_b)],
        out_specs=[pl.BlockSpec((tokens, n), row_block) for n in rows]
        + [
            pl.BlockSpec((1, WIN, columns, width), lambda s: (*step_of(s), 0, 0)),
            pl.BlockSpec((1, WIN // 2 + 1, columns, width), lambda s: (step_of(s)[0], 0, 0, 0)),
        ],
        out_shape=[jax.ShapeDtypeStruct((total, n), t) for n, t in zip(rows, types)]
        + [
            jax.ShapeDtypeStruct(shape, BF),
            jax.ShapeDtypeStruct((samples, WIN // 2 + 1, columns, width), BF),
        ],
        scratch_shapes=[pltpu.VMEM((columns // WIN, WIN, WIN, width), F32)],
        compiler_params=params(),
        cost_estimate=SMALL_COST,
        name="ffn_forward",
    )(place, x, mix, out_w, out_b, gain, shift, up_w, up_b, down_w, down_b)


def column_sum(x):
    return jnp.sum(x, 0, keepdims=True)


def ffn_backward_body(
    height, step_of, place, above, own, act, slope, normed, xhat_ref, rstd_ref, mix, conv_w,
    out_w, gain, up_w, down_w, first_out, mixed_out, down_out, up_out, out_out, vec_out,
    taps, turned, branch, low, raised_s, attn, down_acc, up_acc, out_acc, vec,
):
    step = pl.program_id(0)
    sample, band = step_of(step)
    columns = own.shape[2]
    tokens = columns * WIN
    half = WIN // 2
    column = iota((columns, 1), 0)

    @pl.when(step == 0)
    def _():
        for ref in (down_acc, up_acc, out_acc, vec):
            ref[...] = jnp.zeros_like(ref)
        for k in range(9):
            at = 256 * (k % 3)
            turned[k // 3, :, at : at + 256] = conv_w[k, 0]

    start = place[0] + half
    not_first = start != 0
    lanes = (0, 256, 512)

    @pl.when(band == 0)
    def _():
        before = jnp.where(not_first, start, height) - half - 1
        put_rows(above, half + 1, 0, sample, place, before, taps, 0, lanes)
        put_taps(own[0, 0], row_limit(place, sample, start, not_first), taps, half + 1, lanes)
        limit = row_limit(place, sample, start - 1, not_first)
        put_taps(above[0, ABOVE_LAST], limit, taps, half + 2, lanes)
        put_rows(own, half + 1, 0, sample, place, start, taps, half + 3, lanes)

    @pl.when(band > 0)
    def _():
        for group in range(2):
            first = band * WIN + (group - 1) * half - 1
            put_rows(own, half + 2, first, sample, place, start + first, taps, group * (half + 2), lanes)

    for group in range(2):
        total = 0.0
        for a in range(3):
            at = group * (half + 2) + 2 - a
            piece = taps[at : at + half].reshape(half * columns, 768)
            total = total + dot_nt(piece, turned[a])
        for k in range(half):
            row = place[0] + band * WIN + group * half + k
            row = jnp.where(row < 0, row + height, row)
            limit = row_limit(place, sample, row)
            part = jnp.where(column < limit, total[k * columns : (k + 1) * columns], 0.0)
            part = pltpu.roll(part, half, 0)
            branch[:, group * half + k] = part.reshape(columns // WIN, WIN, 256)

    chunk = 256
    windows = chunk // 64
    for k in range(tokens // chunk):
        at = slice(k * chunk, (k + 1) * chunk)
        upper = branch[k * windows : (k + 1) * windows].reshape(chunk, 256)
        low[at] = upper.astype(BF)
        vec[0:1] += column_sum(upper.astype(BF).astype(F32))
    for k in range(tokens // chunk):
        at = slice(k * chunk, (k + 1) * chunk)
        for f in range(0, 1024, 256):
            wide = slice(f, f + 256)
            raised = (dot_nt(low[at], down_w[wide]) * slope[at, wide].astype(F32)).astype(BF)
            raised_s[at, wide] = raised
            row = 4 + f // 256
            vec[row : row + 1] += column_sum(raised.astype(F32))
    for k in range(tokens // chunk):
        at = slice(k * chunk, (k + 1) * chunk)
        dy = dot_nt(raised_s[at], up_w[...])
        xhat = xhat_ref[at].astype(F32)
        rstd = rstd_ref[at]
        rstd = jnp.concatenate([rstd, rstd], 1)
        upper = branch[k * windows : (k + 1) * windows].reshape(chunk, 256)
        first = upper + norm_back(dy, xhat, rstd, gain[...])
        first_out[at] = first
        attn[at] = first.astype(BF)
        vec[1:2] += column_sum(dy * xhat)
        vec[2:3] += column_sum(dy)
        vec[3:4] += column_sum(first.astype(BF).astype(F32))
    for k in range(tokens // chunk):
        at = slice(k * chunk, (k + 1) * chunk)
        mixed_out[at] = dot_nt(attn[at], out_w[...]).astype(BF)
    low_t = low[...].T
    normed_t = normed[...].T
    for f in range(0, 1024, 256):
        wide = slice(f, f + 256)
        down_acc[:, wide] += dot(low_t, act[:, wide])
        up_acc[:, wide] += dot(normed_t, raised_s[:, wide])
    out_acc[...] += dot(mix[...].T, attn[...])

    @pl.when(step == pl.num_programs(0) - 1)
    def _():
        for f in range(0, 1024, 256):
            wide = slice(f, f + 256)
            down_out[wide] = down_acc[:, wide].T.astype(BF)
            up_out[:, wide] = up_acc[:, wide].astype(BF)
        out_out[...] = out_acc[...].astype(BF)
        vec_out[...] = vec[...].astype(BF)


def ffn_backward(
    place, above, own, act, slope, normed, xhat, rstd, mix, conv_w, out_w, gain, up_w, down_w, height
):
    samples, grid_rows, columns, width = own.shape
    bands = grid_rows // WIN
    tokens = WIN * columns
    steps = samples * bands
    total = steps * tokens
    hidden = up_w.shape[1]

    def step_of(step):
        return step // bands, step % bands

    def row_block(step):
        return (step, 0)

    def sample_block(step):
        return (step_of(step)[0], 0, 0, 0)

    rows = (act, slope, normed, xhat, rstd, mix)
    return pl.pallas_call(
        functools.partial(ffn_backward_body, height, step_of),
        grid=(steps,),
        in_specs=[
            SMEM_SPEC,
            pl.BlockSpec((1,) + above.shape[1:], sample_block),
            pl.BlockSpec((1,) + own.shape[1:], sample_block),
        ]
        + [pl.BlockSpec((tokens, a.shape[1]), row_block) for a in rows]
        + [pl.BlockSpec((9, 1, width, width), lambda s: (0, 0, 0, 0))]
        + [const_spec(a.shape) for a in (out_w, gain, up_w, down_w)],
        out_specs=[
            pl.BlockSpec((tokens, width), row_block),
            pl.BlockSpec((tokens, width), row_block),
            const_spec((hidden, width)),
            const_spec((width, hidden)),
            const_spec((width, width)),
            const_spec((8, width)),
        ],
        out_shape=[
            jax.ShapeDtypeStruct((total, width), F32),
            jax.ShapeDtypeStruct((total, width), BF),
            jax.ShapeDtypeStruct((hidden, width), BF),
            jax.ShapeDtypeStruct((width, hidden), BF),
            jax.ShapeDtypeStruct((width, width), BF),
            jax.ShapeDtypeStruct((8, width), BF),
        ],
        scratch_shapes=[
            pltpu.VMEM((WIN + 4, columns, 3 * width), BF),
            pltpu.VMEM((3, width, 3 * width), BF),
            pltpu.VMEM((columns // WIN, WIN, WIN, width), F32),
            pltpu.VMEM((tokens, width), BF),
            pltpu.VMEM((tokens, hidden), BF),
            pltpu.VMEM((tokens, width), BF),
            pltpu.VMEM((width, hidden), F32),
            pltpu.VMEM((width, hidden), F32),
            pltpu.VMEM((width, width), F32),
            pltpu.VMEM((8, width), F32),
        ],
        compiler_params=params(),
        cost_estimate=pl.CostEstimate(
            flops=2 * 10**10, bytes_accessed=10**7, transcendentals=0
        ),
        name="ffn_backward",
    )(place, above, own, *rows, conv_w, out_w, gain, up_w, down_w)


def attn_backward_body(
    scale, step_of, mixed, qkv, prob, normed, xhat_ref, rstd_ref, first, weight, gain, mask, conv_vec,
    places, input_out, up_out, qkv_out, vec_out, qkv_acc, table_acc, vec_acc, grads, score_grads, sums,
):
    step = pl.program_id(0)
    _, band = step_of(step)
    columns = input_out.shape[2]
    half = WIN // 2

    @pl.when(step == 0)
    def _():
        for ref in (qkv_acc, table_acc, vec_acc):
            ref[...] = jnp.zeros_like(ref)

    attn_backward_step(
        scale, mixed, qkv, prob, normed, xhat_ref, rstd_ref, first, weight, gain, mask,
        qkv_acc, table_acc, vec_acc, grads, score_grads, sums,
    )

    def row_out(r):
        return pltpu.roll(sums[:, r].reshape(columns, 256), columns - half, 0)

    @pl.when(band == 0)
    def _():
        for r in range(half):
            up_out[0, r] = row_out(r).astype(BF)
            input_out[0, r] = row_out(half + r)

    @pl.when(band > 0)
    def _():
        for r in range(WIN):
            input_out[0, band * WIN - half + r] = row_out(r)

    @pl.when(step == pl.num_programs(0) - 1)
    def _():
        for f in range(0, 768, 256):
            qkv_out[:, f : f + 256] = qkv_acc[:, f : f + 256].astype(BF)
        table = collect_bias(table_acc[...], places[...])
        rest = jnp.concatenate([vec_acc[0:2], conv_vec[0:1], jnp.zeros((5, 256), F32)], 0)
        vec_out[...] = jnp.concatenate([table, rest], 1).astype(BF)


def attn_backward_step(
    scale, mixed, qkv, prob, normed, xhat_ref, rstd_ref, first, weight, gain, mask,
    qkv_acc, table_acc, vec_acc, grads, score_grads, sums,
):
    tokens = qkv.shape[0]
    columns = tokens // WIN

    def attend(pair, _):
        head_at = mask[...]
        for half in range(2):
            lanes = slice(256 * half, 256 * half + 256)
            low = prob[pair, lanes]
            mixed_blocks = blocks_of(mixed, pair, 128 * half)
            values = spread_heads(pair_of(qkv, pair, 512 + 128 * half), head_at)
            prob_grad = dot_nt(values, mixed_blocks).reshape(4, 64, 128)
            probs = low.astype(F32).reshape(4, 64, 128)
            shared = jnp.sum(prob_grad * probs, 1, keepdims=True)
            score_grad = (probs * (prob_grad - shared)).astype(BF).reshape(256, 128)
            table_acc[lanes] += score_grad.astype(F32)
            score_grads[pair, lanes] = score_grad
        return 0

    def project(pair, _):
        head_at = mask[...]
        for half in range(2):
            lanes = slice(256 * half, 256 * half + 256)
            low = prob[pair, lanes]
            mixed_blocks = blocks_of(mixed, pair, 128 * half)
            score_grad = score_grads[pair, lanes]
            keys = spread_heads(pair_of(qkv, pair, 256 + 128 * half), head_at)
            queries = blocks_of(qkv, pair, 128 * half)
            query_grad = (dot_tn(score_grad, keys) * scale).astype(BF)
            out = slice(128 * half, 128 * half + 128)
            grads[pl.ds(pair * 128, 64), out] = query_grad[:64, :128]
            grads[pl.ds(pair * 128 + 64, 64), out] = query_grad[64:, 128:]
            wide = head_at.astype(F32)
            key_grad = (dot(score_grad, queries) * wide).reshape(4, 64, 256)
            key_grad = (jnp.sum(key_grad, 0) * scale).astype(BF)
            out = slice(256 + 128 * half, 256 + 128 * half + 128)
            grads[pl.ds(pair * 128, 64), out] = key_grad[:, :128]
            grads[pl.ds(pair * 128 + 64, 64), out] = key_grad[:, 128:]
            value_grad = (dot(low, mixed_blocks) * wide).reshape(4, 64, 256)
            value_grad = jnp.sum(value_grad, 0).astype(BF)
            out = slice(512 + 128 * half, 512 + 128 * half + 128)
            grads[pl.ds(pair * 128, 64), out] = value_grad[:, :128]
            grads[pl.ds(pair * 128 + 64, 64), out] = value_grad[:, 128:]
        return 0

    lax.fori_loop(0, columns // 16, attend, 0, unroll=8)
    lax.fori_loop(0, columns // 16, project, 0, unroll=8)
    for f in range(0, 768, 256):
        qkv_acc[:, f : f + 256] += dot_tn(normed[...], grads[:, f : f + 256])

    def part(k, _):
        at = pl.ds(k * 256, 256)
        dy = dot_nt(grads[at], weight[...])
        xhat = xhat_ref[at].astype(F32)
        rstd = rstd_ref[at]
        rstd = jnp.concatenate([rstd, rstd], 1)
        total = first[at] + norm_back(dy, xhat, rstd, gain[...])
        sums[pl.ds(k * 4, 4)] = total.reshape(4, WIN, WIN, 256)
        vec_acc[0:1] += column_sum(dy * xhat)
        vec_acc[1:2] += column_sum(dy)
        return 0

    lax.fori_loop(0, tokens // 256, part, 0, unroll=True)


def attn_backward(
    mixed, qkv, prob, normed, xhat, rstd, first, weight, gain, mask, conv_vec, places, scale, shape
):
    samples, grid_rows, columns, width = shape
    bands = grid_rows // WIN
    tokens = WIN * columns
    half = WIN // 2

    def step_of(step):
        return step // bands, step % bands

    def row_block(step):
        return (step, 0)

    def sample_block(step):
        return (step_of(step)[0], 0, 0, 0)

    rows = (mixed, qkv, prob, normed, xhat, rstd, first)
    consts = (weight, gain, mask, conv_vec, places)
    in_specs = [pl.BlockSpec((tokens, a.shape[1]), row_block) for a in rows]
    in_specs[2] = pl.BlockSpec((columns // 16, 512, 128), lambda s: (s, 0, 0))
    in_specs += [const_spec(a.shape) for a in consts]
    return pl.pallas_call(
        functools.partial(attn_backward_body, scale, step_of),
        grid=(samples * bands,),
        in_specs=in_specs,
        out_specs=[
            pl.BlockSpec((1,) + shape[1:], sample_block),
            pl.BlockSpec((1, half, columns, width), sample_block),
            const_spec((width, 3 * width)),
            const_spec((8, 2 * width)),
        ],
        out_shape=[
            jax.ShapeDtypeStruct(shape, F32),
            jax.ShapeDtypeStruct((samples, half, columns, width), BF),
            jax.ShapeDtypeStruct((width, 3 * width), BF),
            jax.ShapeDtypeStruct((8, 2 * width), BF),
        ],
        scratch_shapes=[
            pltpu.VMEM((width, 3 * width), F32),
            pltpu.VMEM((512, 128), F32),
            pltpu.VMEM((8, width), F32),
            pltpu.VMEM((tokens, 3 * width), BF),
            pltpu.VMEM((columns // 16, 512, 128), BF),
            pltpu.VMEM((columns // WIN, WIN, WIN, width), F32),
        ],
        compiler_params=params(),
        cost_estimate=SMALL_COST,
        name="attn_backward",
    )(*rows, *consts)


def shifted(row, column, by):
    columns = row.shape[0]
    moved = pltpu.roll(row, by % columns, 0)
    edge = 0 if by == 1 else columns - 1
    return jnp.where(column == edge, 0.0, moved)


def pack_near_body(qkv, out_w, up, down, near):
    rows = qkv.shape[0]
    at = 0
    for ref in (qkv, out_w, up):
        near[:, at : at + ref.shape[1]] = ref[...].astype(BF)
        at += ref.shape[1]
    for k in range(down.shape[0] // rows):
        near[:, at : at + down.shape[1]] = down[k * rows : (k + 1) * rows].astype(BF)
        at += down.shape[1]


def pack_near(qkv, out_w, up, down):
    rows = qkv.shape[0]
    lanes = (qkv.size + out_w.size + up.size + down.size) // rows
    return pl.pallas_call(
        pack_near_body,
        out_shape=jax.ShapeDtypeStruct((rows, lanes), BF),
        compiler_params=params(),
        cost_estimate=SMALL_COST,
        name="pack_near",
    )(qkv, out_w, up, down)


def unpack_near_body(order, held, qkv, out_w, up, down):
    devices, rows, _ = held.shape
    count = max(16 // rows, 1)

    def some(k, _):
        pieces = [held[order[k * count + n]] for n in range(count)]
        at = 0
        place = pl.ds(pl.multiple_of(k * count * rows, count * rows), count * rows)
        for ref in (qkv, out_w, up):
            lanes = slice(at, at + ref.shape[1])
            ref[place] = jnp.concatenate([piece[:, lanes] for piece in pieces], 0)
            at = lanes.stop
        width = down.shape[1]
        parts = down.shape[0] // (devices * rows)
        tall = [
            piece[:, at + n * width : at + (n + 1) * width] for piece in pieces for n in range(parts)
        ]
        size = count * rows * parts
        down[pl.ds(pl.multiple_of(k * size, size), size)] = jnp.concatenate(tall, 0)
        return 0

    lax.fori_loop(0, devices // count, some, 0, unroll=4)


def unpack_near(order, held, weights):
    devices = held.shape[0]
    return pl.pallas_call(
        unpack_near_body,
        in_specs=[SMEM_SPEC, pl.BlockSpec(memory_space=pltpu.VMEM)],
        out_shape=[jax.ShapeDtypeStruct((devices * w.shape[0], w.shape[1]), BF) for w in weights],
        compiler_params=params(),
        cost_estimate=SMALL_COST,
        name="unpack_near",
    )(order, held)


def copies_body(x, out):
    low = x[...].astype(BF)
    for k in range(out.shape[0]):
        out[k] = low


def make_copies(x, count):
    return pl.pallas_call(
        copies_body,
        out_shape=jax.ShapeDtypeStruct((count,) + x.shape, BF),
        compiler_params=params(),
        cost_estimate=SMALL_COST,
        name="make_copies",
    )(x)


def row_limit(place, sample, row, allowed=True):
    return jnp.where((row < place[1 + sample]) & allowed, place[3 + sample], 0)


def put_taps(row, limit, target, at, lanes):
    column = iota((row.shape[0], 1), 0)
    wide = jnp.where(column < limit, row.astype(F32), 0.0)
    target[at, :, lanes[0] : lanes[0] + 256] = shifted(wide, column, -1).astype(BF)
    target[at, :, lanes[1] : lanes[1] + 256] = wide.astype(BF)
    target[at, :, lanes[2] : lanes[2] + 256] = shifted(wide, column, 1).astype(BF)


def put_rows(source, count, first, sample, place, row, target, at, lanes):
    def one(r, _):
        put_taps(source[0, first + r], row_limit(place, sample, row + r), target, at + r, lanes)
        return 0

    lax.fori_loop(0, count, one, 0, unroll=True)


ABOVE_LAST = WIN // 2
ABOVE_HIDDEN = WIN // 2 + 1


def own_taps(height, place, above, own, below, taps, at):
    sample = pl.program_id(0)
    rows = own.shape[1]
    start = place[0] + WIN // 2
    lanes = (0, 256, 512)
    limit = row_limit(place, sample, start - 1, start != 0)
    put_taps(above[0, ABOVE_LAST], limit, taps, at, lanes)
    put_rows(own, rows, 0, sample, place, start, taps, at + 1, lanes)
    limit = row_limit(place, sample, start + rows, start + rows != height)
    put_taps(below[0, 0], limit, taps, at + rows + 1, lanes)


def weight_sums(groups, source, taps, acc):
    columns = taps.shape[1]
    for start, target, rows in groups:
        turned = source(target, rows).T
        for a in range(3):
            piece = taps[start + 2 - a : start + 2 - a + rows].reshape(rows * columns, 768)
            acc[a] += dot(turned, piece)


def conv_weight_body(
    height, place, above, own, below, sums, hidden, out, vec, taps, held, acc, acc_hidden
):
    sample = pl.program_id(0)

    @pl.when(sample == 0)
    def _():
        for ref in (acc, acc_hidden, vec):
            ref[...] = jnp.zeros_like(ref)

    rows, columns = own.shape[1:3]
    half = WIN // 2
    column = iota((columns, 1), 0)
    start = place[0] + half
    not_first = start != 0

    before = jnp.where(not_first, start, height) - half - 1
    put_rows(above, half + 1, 0, sample, place, before, taps, 0, (0, 256, 512))
    limit = row_limit(place, sample, start, not_first)
    put_taps(own[0, 0], limit, taps, half + 1, (0, 256, 512))
    own_taps(height, place, above, own, below, taps, half + 2)

    def one(r, _):
        limit = row_limit(place, sample, start + r)
        held[r] = jnp.where(column < limit, hidden[0, r].astype(F32), 0.0).astype(BF)
        vec[0:1] += jnp.sum(taps[half + 3 + r, :, 256:512].astype(F32), 0, keepdims=True)
        return 0

    lax.fori_loop(0, rows, one, 0, unroll=4)
    groups = ((0, 0, half), (half + 2, half, rows - half))
    weight_sums(groups, lambda t, n: sums[0, t : t + n].reshape(n * columns, 256), taps, acc)
    groups = ((half + 2, 0, rows),)
    weight_sums(groups, lambda t, n: held[t : t + n].reshape(n * columns, 256), taps, acc_hidden)

    @pl.when(sample == pl.num_programs(0) - 1)
    def _():
        for k in range(9):
            at = 256 * (k % 3)
            out[k, 0] = acc[k // 3, :, at : at + 256].astype(BF)
            out[k, 1] = acc_hidden[k // 3, :, at : at + 256].astype(BF)


def field_spec(a):
    return pl.BlockSpec((1,) + a.shape[1:], lambda s: (s, 0, 0, 0))


def conv_call(
    body, name, place, fields, consts, height, out_specs, out_shape, scratch, cost=None
):
    return pl.pallas_call(
        functools.partial(body, height),
        grid=(fields[0][1].shape[0],),
        in_specs=[SMEM_SPEC] + [s for s, _ in fields] + [s for s, _ in consts],
        out_specs=out_specs,
        out_shape=out_shape,
        scratch_shapes=scratch,
        compiler_params=params(),
        cost_estimate=cost or SMALL_COST,
        name=name,
    )(place, *[a for _, a in fields], *[a for _, a in consts])


def whole(a):
    return field_spec(a), a


def conv_weight(place, grads, sums, hidden, height):
    _, rows, columns, width = sums.shape
    shape = (9, 2, width, width)
    acc = pltpu.VMEM((3, width, 3 * width), F32)
    return conv_call(
        conv_weight_body, "conv_weight", place, [whole(a) for a in (*grads, sums, hidden)], (),
        height, [const_spec(shape), const_spec((8, width))],
        [jax.ShapeDtypeStruct(shape, BF), jax.ShapeDtypeStruct((8, width), F32)],
        [
            pltpu.VMEM((rows + WIN, columns, 3 * width), BF),
            pltpu.VMEM((rows, columns, width), BF),
            acc,
            acc,
        ],
        pl.CostEstimate(flops=2 * 10**10, bytes_accessed=10**7, transcendentals=0),
    )


def conv_data_body(height, place, above, own, below, weight, out, taps, turned):
    sample = pl.program_id(0)
    columns = own.shape[2]
    column = iota((columns, 1), 0)

    @pl.when(sample == 0)
    def _():
        for k in range(9):
            at = 256 * (k % 3)
            turned[k // 3, :, at : at + 256] = weight[k, 0]

    own_taps(height, place, above, own, below, taps, 0)
    for r in range(0, own.shape[1], 4):
        total = 0.0
        for a in range(3):
            piece = taps[r + 2 - a : r + 6 - a].reshape(4 * columns, 768)
            total = total + dot_nt(piece, turned[a])
        for k in range(4):
            limit = row_limit(place, sample, place[0] + WIN // 2 + r + k)
            part = total[k * columns : (k + 1) * columns]
            out[0, r + k] = jnp.where(column < limit, part, 0.0)


def conv_data(place, grads, weight, height):
    own = grads[1]
    width = own.shape[-1]
    weight_spec = pl.BlockSpec((9, 1, width, width), lambda s: (0, 1, 0, 0))
    return conv_call(
        conv_data_body, "conv_data", place, [whole(a) for a in grads], ((weight_spec, weight),),
        height, field_spec(own), jax.ShapeDtypeStruct(own.shape, F32),
        [
            pltpu.VMEM((own.shape[1] + 2, own.shape[2], 3 * width), BF),
            pltpu.VMEM((3, width, 3 * width), BF),
        ],
        pl.CostEstimate(flops=10**10, bytes_accessed=10**7, transcendentals=0),
    )


def conv_forward_body(
    height, place, sums, sums_below, above, hidden, below, weight, bias, out, taps
):
    sample = pl.program_id(0)
    rows, columns = out.shape[1:3]
    column = iota((columns, 1), 0)
    half = WIN // 2
    start = place[0] + half
    not_first, not_last = start != 0, start + rows != height
    lanes = (1024, 512, 0)
    limit = row_limit(place, sample, start - 1, not_first)
    put_taps(sums[0, half - 1], limit, taps, 0, lanes)
    put_rows(sums, rows - half, half, sample, place, start, taps, 1, lanes)
    put_rows(sums_below, half, 0, sample, place, start + rows - half, taps, rows - half + 1, lanes)
    after = row_limit(place, sample, start + rows, not_last)
    put_taps(sums_below[0, half], after, taps, rows + 1, lanes)
    lanes = (1280, 768, 256)
    put_taps(above[0, ABOVE_HIDDEN], limit, taps, 0, lanes)
    put_rows(hidden, rows, 0, sample, place, start, taps, 1, lanes)
    put_taps(below[0, 1], after, taps, rows + 1, lanes)
    for r in range(0, rows, 4):
        total = bias[...]
        for a in range(3):
            piece = taps[r + a : r + a + 4].reshape(4 * columns, 1536)
            total = total + dot(piece, weight[a * 1536 : (a + 1) * 1536])
        for k in range(4):
            limit = row_limit(place, sample, start + r + k)
            part = total[k * columns : (k + 1) * columns]
            out[0, r + k] = jnp.where(column < limit, part, 0.0).astype(BF)


def conv_forward(place, sums, sums_below, hidden, weight, bias, height):
    samples, rows, columns, width = sums.shape
    fields = (sums, sums_below, *hidden)
    return pl.pallas_call(
        functools.partial(conv_forward_body, height),
        grid=(samples,),
        in_specs=[SMEM_SPEC]
        + [field_spec(a) for a in fields]
        + [const_spec(weight.shape), const_spec(bias.shape)],
        out_specs=field_spec(sums),
        out_shape=jax.ShapeDtypeStruct(sums.shape, BF),
        scratch_shapes=[pltpu.VMEM((rows + 2, columns, 6 * width), BF)],
        compiler_params=params(),
        cost_estimate=SMALL_COST,
        name="conv_forward",
    )(place, *fields, weight, bias)


def shards(
    layer_input,
    hidden_state,
    crop_rows,
    crop_cols,
    first_gain,
    first_shift,
    qkv_weight,
    bias_table,
    output_weight,
    output_bias,
    second_gain,
    second_shift,
    up_weight,
    up_bias,
    down_weight,
    down_bias,
    conv_weight_in,
    conv_bias,
    cotangent,
):
    samples, grid_rows, columns, width = layer_input.shape
    shape = layer_input.shape
    heads = bias_table.shape[1]
    scale = float((width // heads) ** (-0.5))
    half = WIN // 2
    devices = device_count()
    row_devices = lax.axis_size("rows")
    height = grid_rows * row_devices
    row_place = lax.axis_index("rows")
    row_start = row_place * grid_rows
    place = jnp.concatenate(
        [(row_start - half)[None].astype(jnp.int32), crop_rows, crop_cols]
    ).astype(jnp.int32)

    hidden_width = up_weight.shape[1]

    def vec(v):
        return v.reshape(1, -1)

    input_above = ring(layer_input[:, grid_rows - half :], 1)
    rows_out, rows_down = output_weight.shape[0], down_weight.shape[0]
    near = pack_near(qkv_weight, output_weight, up_weight, down_weight)
    held, order = gather_steps(near, input_above)
    late_cotangent, late_hidden = after((cotangent, hidden_state), held)
    halo_above = jnp.concatenate(
        [late_cotangent[:, grid_rows - half - 1 :], late_hidden[:, grid_rows - 1 :]], 1
    )
    halo_below = jnp.concatenate([late_cotangent[:, :1], late_hidden[:, :1]], 1)
    halo_above, halo_below = ring(halo_above, 1), ring(halo_below, -1)
    grads = (halo_above, cotangent, halo_below)
    conv_copies = after(make_copies(conv_weight_in, devices), held, input_above)
    conv_full = gather_copies(conv_copies).reshape(-1, width)

    qkv_full, output_full, up_full, down_full = unpack_near(
        order, held, (qkv_weight, output_weight, up_weight, down_weight)
    )
    offsets = bias_table.shape[0]
    table = jnp.pad(bias_table.T, ((0, 0), (0, 256 - offsets)))
    mask = jnp.asarray(head_mask(), BF)

    x, normed, xhat, rstd, qkv, prob, mix = attn_forward(
        place, input_above, layer_input, vec(first_gain), vec(first_shift), qkv_full, table,
        jnp.asarray(offset_places(False), BF), mask, height, scale,
    )
    normed_2, xhat_2, rstd_2, act, slope, sums, sums_first = ffn_forward(
        place, x, mix, output_full, vec(output_bias), vec(second_gain), vec(second_shift),
        up_full, vec(up_bias), down_full, vec(down_bias), height, shape,
    )
    conv_local, conv_bias_part = conv_weight(place, grads, sums, hidden_state, height)
    conv_local, exchange = scatter_pairs(conv_local.reshape(devices, -1, width))
    conv_all = exchange(conv_local)
    sums_below = ring(after(sums_first, conv_local), -1)
    conv_blocks = after(conv_full.reshape(9, 2, width, width), conv_local)
    first_grad, mixed, down_acc, up_acc, out_acc, vec_ffn = ffn_backward(
        place, halo_above, cotangent, act, slope, normed_2, xhat_2, rstd_2, mix, conv_blocks,
        output_full, vec(second_gain), up_full, down_full, height,
    )
    input_grad, input_up, qkv_acc, vec_attn = attn_backward(
        after(mixed, sums_below), qkv, prob, normed, xhat, rstd, first_grad, qkv_full,
        vec(first_gain), mask, conv_bias_part, jnp.asarray(offset_places(True), BF).T, scale, shape,
    )
    down_local = down_acc.reshape(devices, -1, rows_out, width).transpose(0, 2, 1, 3)
    parts = [
        down_local.reshape(devices, rows_out, -1),
        *(a.reshape(devices, rows_out, -1) for a in (out_acc, up_acc, qkv_acc)),
    ]
    last_local, exchange = scatter_pairs(
        with_vectors(parts, jnp.concatenate([vec_ffn, vec_attn], 1))
    )
    last_all = exchange(last_local)
    input_from_below = ring(after(input_up, last_local), -1)
    hidden_grad = conv_data(after(place, last_local), grads, conv_blocks, height)
    layer_output = conv_forward(
        after(place, hidden_grad), sums, sums_below, (halo_above, hidden_state, halo_below),
        conv_full, vec(conv_bias), height,
    )

    input_grad = lax.dynamic_update_slice(
        after(input_grad, layer_output), input_from_below.astype(F32), (0, grid_rows - half, 0, 0)
    )

    def total(parts):
        return jnp.sum(parts.astype(F32), 0)

    conv_weight_grad = total(conv_all)
    ends = np.cumsum([0, hidden_width, width, hidden_width, 3 * width])
    sums_all = total(last_all)
    parts = [sums_all[:, ends[k] : ends[k + 1]] for k in range(4)]
    down_weight_grad = parts[0].reshape(rows_out, -1, width).transpose(1, 0, 2)
    down_weight_grad = down_weight_grad.reshape(rows_down, width)
    output_weight_grad, up_weight_grad, qkv_weight_grad = parts[1:]
    vectors = sums_all[:, ends[4] :].reshape(8, 3, width)
    ffn_vec, table_grad, attn_vec = (vectors[:, k] for k in range(3))
    down_bias_grad, second_gain_grad, second_shift_grad, output_bias_grad = (
        ffn_vec[k] for k in range(4)
    )
    up_bias_grad = ffn_vec[4:].reshape(-1)
    bias_table_grad = table_grad[:, :offsets][:, ::-1].T
    first_gain_grad, first_shift_grad, conv_bias_grad = (attn_vec[k] for k in range(3))
    return (
        layer_output,
        input_grad,
        hidden_grad,
        first_gain_grad,
        first_shift_grad,
        qkv_weight_grad,
        bias_table_grad,
        output_weight_grad,
        output_bias_grad,
        second_gain_grad,
        second_shift_grad,
        up_weight_grad,
        up_bias_grad,
        down_weight_grad,
        down_bias_grad,
        conv_weight_grad,
        conv_bias_grad,
    )


def solution(mesh):
    field = P("batch", "rows", None, None)
    weight = P(AXES, None)
    in_specs = (
        field, field, P("batch"), P("batch"), P(), P(), weight, P(), weight, P(), P(), P(),
        weight, P(), weight, P(), weight, P(), field,
    )
    out_specs = (
        field, field, field, P(), P(), weight, P(), weight, P(), P(), P(), weight, P(), weight,
        P(), weight, P(),
    )
    return jax.shard_map(shards, mesh=mesh, in_specs=in_specs, out_specs=out_specs, check_vma=False)
```

```python
import functools

import jax
import jax.numpy as jnp
import numpy as np
from jax import lax
from jax.experimental import pallas as pl
from jax.experimental.pallas import tpu as pltpu
from jax.sharding import PartitionSpec as P

WIN = 8
EPSILON = 1e-05
MASKED = -100.0
HIGHEST = lax.Precision.HIGHEST
AXES = ("rows", "batch")
BF = jnp.bfloat16
F32 = jnp.float32
MIB = 1024 * 1024
LOG2E = 1.4426950408889634


def dot(left, right):
    return jnp.dot(left, right, preferred_element_type=F32)


def dot_nt(left, right):
    return lax.dot_general(left, right, (((1,), (1,)), ((), ())), preferred_element_type=F32)


def dot_tn(left, right):
    return lax.dot_general(left, right, (((0,), (0,)), ((), ())), preferred_element_type=F32)


def iota(shape, dim):
    return lax.broadcasted_iota(jnp.int32, shape, dim)


def device_index():
    return lax.axis_index("rows") * lax.axis_size("batch") + lax.axis_index("batch")


def device_count():
    return lax.axis_size("rows") * lax.axis_size("batch")


def after(x, *others):
    return lax.optimization_barrier((x, *others))[0]


def bit_groups():
    batch, rows = lax.axis_size("batch"), lax.axis_size("rows")
    batch_bits = [1 << k for k in range(batch.bit_length() - 1)]
    row_bits = [batch << k for k in range(rows.bit_length() - 1)]
    chips = row_bits[1:]
    groups = [batch_bits[k : k + 2] for k in range(0, len(batch_bits), 2)]
    groups += [chips[k : k + 2] for k in range(0, len(chips), 2)]
    return groups + [row_bits[:1]]


def gather_steps(x, beside):
    devices = device_count()
    held = x[None]
    places = [0]
    groups = bit_groups()
    for k, group in enumerate(groups):
        masks = [0]
        for bit in group:
            masks = masks + [m | bit for m in masks]
        if k == 1:
            other = beside(held)
        if k == len(groups) - 1:
            held = after(held, *other)
        pieces = [held]
        for mask in masks[1:]:
            pieces.append(lax.ppermute(held, AXES, [(i, i ^ mask) for i in range(devices)]))
        held = jnp.concatenate(pieces, 0)
        places = [p ^ m for m in masks for p in places]
    order = np.zeros(devices, np.int32)
    for place, mask in enumerate(places):
        order[mask] = place
    return held, jnp.asarray(order)[jnp.arange(devices) ^ device_index()], other


def scatter_pairs(x):
    rows, batch = lax.axis_size("rows"), lax.axis_size("batch")
    core = lax.axis_index("rows") % 2
    by_core = x.reshape((rows // 2, 2, batch) + x.shape[1:])
    mine = lax.dynamic_index_in_dim(by_core, core, 1, False)
    other = lax.dynamic_index_in_dim(by_core, 1 - core, 1, False)
    other = lax.ppermute(other, "rows", [(i, i ^ 1) for i in range(rows)])
    pairs = (mine.astype(F32) + other.astype(F32)).astype(BF)
    pairs = pairs.reshape((rows // 2 * batch,) + x.shape[1:])
    groups = [
        [(2 * chip + k) * batch + b for chip in range(rows // 2) for b in range(batch)]
        for k in range(2)
    ]
    return pairs, lambda a: lax.all_to_all(a, AXES, 0, 0, axis_index_groups=groups, tiled=True)


def gather_copies(copies):
    return lax.all_to_all(copies, AXES, 0, 0, tiled=True)


def with_vectors(parts, vectors):
    rows = parts[0].shape[1]
    flat = vectors.reshape(1, rows, -1)
    flat = jnp.broadcast_to(flat, (parts[0].shape[0],) + flat.shape[1:])
    return jnp.concatenate(list(parts) + [flat], 2)


def ring(x, by):
    devices = lax.axis_size("rows")
    return lax.ppermute(x, "rows", [(i, (i + by) % devices) for i in range(devices)])


def norm_parts(x):
    centred = x - jnp.mean(x, -1, keepdims=True)
    rstd = lax.rsqrt(jnp.mean(centred * centred, -1, keepdims=True) + EPSILON)
    return centred * rstd, rstd


def norm_back(dy, xhat, rstd, gain):
    scaled = dy * gain
    first = jnp.mean(scaled, -1, keepdims=True)
    second = jnp.mean(scaled * xhat, -1, keepdims=True)
    return (scaled - first - xhat * second) * rstd


def head_mask():
    rows, lanes = np.arange(256)[:, None], np.arange(256)[None, :]
    return (rows // 64 == (lanes % 128) // 32).astype(np.float32)


def pair_of(ref, pair, column):
    first = ref[pl.ds(pair * 128, 64), column : column + 128]
    second = ref[pl.ds(pair * 128 + 64, 64), column : column + 128]
    return jnp.concatenate([first, second], 1)


def blocks_of(ref, pair, column):
    first = ref[pl.ds(pair * 128, 64), column : column + 128]
    second = ref[pl.ds(pair * 128 + 64, 64), column : column + 128]
    nothing = jnp.zeros_like(first)
    return jnp.concatenate(
        [jnp.concatenate([first, nothing], 1), jnp.concatenate([nothing, second], 1)], 0
    )


def spread_heads(pair, mask):
    return jnp.concatenate([pair] * 4, 0) * mask


def offset_places(turned):
    rows, lanes = np.arange(256)[:, None], np.arange(128)[None, :] % 64
    row, col = lanes // WIN, lanes % WIN
    if turned:
        row, col = WIN - 1 - row, WIN - 1 - col
    return (rows == row * (2 * WIN - 1) + col).astype(np.float32)


def three_parts(x):
    high = x.astype(BF)
    rest = x - high.astype(F32)
    middle = rest.astype(BF)
    return high, middle, (rest - middle.astype(F32)).astype(BF)


def spread_bias(table, places, bias, factor):
    line = 2 * WIN - 1
    for head in range(8):
        row = jnp.broadcast_to(table[head : head + 1], (WIN, 256))
        turns = []
        for r in range(WIN):
            by = 256 - (WIN - 1 - r) * line - (WIN - 1)
            turns.append(pltpu.roll(row, by, 1, stride=1, stride_axis=0))
        wide = jnp.concatenate(turns, 0)
        total = 0.0
        for part in three_parts(wide):
            total = total + dot(part, places[...])
        bias[head * 64 : head * 64 + 64] = total * factor


def collect_bias(grad, places):
    line = 2 * WIN - 1
    wide = 0.0
    for part in three_parts(grad):
        wide = wide + dot(part, places)
    out = []
    for head in range(8):
        total = jnp.zeros((WIN, 256), F32)
        for r in range(WIN):
            at = head * 64 + r * WIN
            total = total + pltpu.roll(wide[at : at + WIN], r * line, 1, stride=1, stride_axis=0)
        out.append(jnp.sum(total, 0, keepdims=True))
    return jnp.concatenate(out, 0)


def attn_forward_body(
    height, scale, step_of, place, above, upper, lower, gain, shift, weight, table, places, mask,
    x_out, norm_out, xhat_out, rstd_out, qkv_out, prob_out, mix_out, xs, bias,
):
    sample, band = step_of(pl.program_id(0))
    columns = lower.shape[2]

    @pl.when(pl.program_id(0) == 0)
    def _():
        spread_bias(table, places, bias, 1.0 / scale)

    def rows_from(ref, first):
        def rows_in(r, _):
            x = pltpu.roll(ref[0, r].astype(F32), WIN // 2, 0)
            xs[:, first + r] = x.reshape(columns // WIN, WIN, 256)
            return 0

        lax.fori_loop(0, WIN // 2, rows_in, 0, unroll=True)

    @pl.when(band == 0)
    def _():
        rows_from(above, 0)

    @pl.when(band > 0)
    def _():
        rows_from(upper, 0)

    rows_from(lower, WIN // 2)

    def norm_in(k, _):
        tokens = pl.ds(k * 128, 128)
        x = xs[pl.ds(k * 2, 2)].reshape(128, 256)
        xhat, rstd = norm_parts(x)
        x_out[tokens] = x.astype(BF)
        xhat_out[tokens] = xhat.astype(BF)
        rstd_out[tokens] = jnp.broadcast_to(rstd, (128, 128))
        norm_out[tokens] = (xhat * gain[...] + shift[...]).astype(BF)
        return 0

    lax.fori_loop(0, columns // 16, norm_in, 0, unroll=8)
    for k in range(0, columns * WIN, 256):
        qkv_out[k : k + 256] = dot(norm_out[k : k + 256], weight[...]).astype(BF)

    key_at, query_at = iota((64, 128), 0), iota((64, 128), 1)
    window_at = query_at // 64
    query_at = query_at % 64
    row_base = place[0] + band * WIN
    key_row, query_row = key_at // WIN + row_base, query_at // WIN + row_base
    key_row = jnp.where(key_row < 0, key_row + height, key_row)
    query_row = jnp.where(query_row < 0, query_row + height, query_row)
    rows_differ = (key_row >= height - WIN // 2) != (query_row >= height - WIN // 2)
    row_bad = key_row >= place[1 + sample]

    def attend(pair, _):
        key_col = (pair * 2 + window_at) * WIN + key_at % WIN - WIN // 2
        query_col = (pair * 2 + window_at) * WIN + query_at % WIN - WIN // 2
        key_col = jnp.where(key_col < 0, key_col + columns, key_col)
        query_col = jnp.where(query_col < 0, query_col + columns, query_col)
        cols_differ = (key_col >= columns - WIN // 2) != (query_col >= columns - WIN // 2)
        bad = row_bad | (key_col >= place[3 + sample])
        minus = jnp.where(rows_differ | cols_differ, MASKED / scale, 0.0) + jnp.where(
            bad, MASKED / scale, 0.0
        )
        for half in range(2):
            keys = spread_heads(pair_of(qkv_out, pair, 256 + 128 * half), mask[...])
            queries = blocks_of(qkv_out, pair, 128 * half)
            scores = dot_nt(keys, queries).reshape(4, 64, 128)
            scores = scores + (bias[256 * half : 256 * half + 256].reshape(4, 64, 128) + minus[None])
            top = jnp.max(scores, 1, keepdims=True)
            raised = jnp.exp2((scores - top) * (scale * LOG2E))
            probs = raised * (1.0 / jnp.sum(raised, 1, keepdims=True))
            probs = probs.reshape(256, 128).astype(BF)
            prob_out[pair, 256 * half : 256 * half + 256] = probs
        return 0

    def mix(pair, _):
        for half in range(2):
            probs = prob_out[pair, 256 * half : 256 * half + 256]
            values = spread_heads(pair_of(qkv_out, pair, 512 + 128 * half), mask[...])
            mixed = dot_tn(probs, values).astype(BF)
            mix_out[pl.ds(pair * 128, 64), 128 * half : 128 * half + 128] = mixed[:64, :128]
            mix_out[pl.ds(pair * 128 + 64, 64), 128 * half : 128 * half + 128] = mixed[64:, 128:]
        return 0

    lax.fori_loop(0, columns // 16, attend, 0, unroll=8)
    lax.fori_loop(0, columns // 16, mix, 0, unroll=8)


def near(*arrays):
    return [pltpu.with_memory_space_constraint(a, pltpu.VMEM) for a in arrays]


def const_spec(shape):
    return pl.BlockSpec(shape, lambda *_: (0,) * len(shape))


SMALL_COST = pl.CostEstimate(flops=10**6, bytes_accessed=10**4, transcendentals=0)


def params(mib):
    return pltpu.CompilerParams(vmem_limit_bytes=mib * MIB)


def far(*arrays):
    return [pltpu.with_memory_space_constraint(a, pltpu.HBM) for a in arrays]


SMEM_SPEC = pl.BlockSpec(memory_space=pltpu.SMEM)


def band_steps(samples, bands):
    def step_of(step):
        return step % samples, bands[0] + step // samples

    return step_of, samples * len(bands)


def attn_forward(place, above, own, gain, shift, weight, table, places, mask, height, scale):
    samples, grid_rows, columns, width = own.shape
    half = WIN // 2
    bands = grid_rows // WIN
    tokens = WIN * columns
    steps = samples * bands

    def step_of(step):
        return step // bands, step % bands

    def row_block(step):
        return (step, 0)

    total = steps * tokens
    return pl.pallas_call(
        functools.partial(attn_forward_body, height, scale, step_of),
        grid=(steps,),
        in_specs=[
            SMEM_SPEC,
            pl.BlockSpec((1, half, columns, width), lambda s: (step_of(s)[0], 0, 0, 0)),
            pl.BlockSpec(
                (1, half, columns, width),
                lambda s: (step_of(s)[0], jnp.maximum(2 * step_of(s)[1] - 1, 0), 0, 0),
            ),
            pl.BlockSpec(
                (1, half, columns, width), lambda s: (step_of(s)[0], 2 * step_of(s)[1], 0, 0)
            ),
            const_spec((1, width)),
            const_spec((1, width)),
            const_spec(weight.shape),
            const_spec(table.shape),
            const_spec(places.shape),
            const_spec(mask.shape),
        ],
        out_specs=[
            pl.BlockSpec((tokens, width), row_block),
            pl.BlockSpec((tokens, width), row_block),
            pl.BlockSpec((tokens, width), row_block),
            pl.BlockSpec((tokens, 128), row_block),
            pl.BlockSpec((tokens, 3 * width), row_block),
            pl.BlockSpec((columns // 16, 512, 128), lambda s: (s, 0, 0)),
            pl.BlockSpec((tokens, width), row_block),
        ],
        out_shape=[
            pltpu.VMEM((total, width), BF),
            pltpu.HBM((total, width), BF),
            pltpu.HBM((total, width), BF),
            pltpu.HBM((total, 128), F32),
            pltpu.HBM((total, 3 * width), BF),
            pltpu.HBM((total // 128, 512, 128), BF),
            pltpu.VMEM((total, width), BF),
        ],
        scratch_shapes=[
            pltpu.VMEM((columns // WIN, WIN, WIN, width), F32),
            pltpu.VMEM((512, 128), F32),
        ],
        compiler_params=params(24),
        cost_estimate=SMALL_COST,
        name="attn_forward",
    )(place, *far(above, own, own, gain, shift), *near(weight), *far(table, places, mask))


def gelu_parts(x):
    share = 0.5 + 0.5 * lax.erf(x * 0.7071067811865476)
    bell = jnp.exp2(x * x * (-0.5 * LOG2E))
    return x * share, share + x * (bell * 0.3989422804014327)


def ffn_forward_body(
    height, step_of, place, x_ref, mix, out_w, out_b, gain, shift, up_w, up_b, down_w, down_b,
    norm_out, xhat_out, rstd_out, act_out, slope_out, sum_out, first_rows, sums,
):
    sample, band = step_of(pl.program_id(0))
    columns = sum_out.shape[2]
    chunk = 256
    chunks = columns * WIN // chunk

    def attend_sum(k, _):
        tokens = pl.ds(k * chunk, chunk)
        first = x_ref[tokens].astype(F32) + dot(mix[tokens], out_w[...]) + out_b[...]
        sums[pl.ds(k * (chunk // 64), chunk // 64)] = first.reshape(chunk // 64, WIN, WIN, 256)
        xhat, rstd = norm_parts(first)
        norm_out[tokens] = (xhat * gain[...] + shift[...]).astype(BF)
        xhat_out[tokens] = xhat.astype(BF)
        rstd_out[tokens] = jnp.broadcast_to(rstd, (chunk, 128))
        return 0

    def raise_up(k, _):
        tokens = pl.ds(k * chunk, chunk)
        for f in range(0, 1024, 256):
            raised = dot(norm_out[tokens], up_w[:, f : f + 256]) + up_b[:, f : f + 256]
            act, slope = gelu_parts(raised)
            act_out[tokens, f : f + 256] = act.astype(BF)
            slope_out[tokens, f : f + 256] = slope.astype(BF)
        return 0

    def put_down(k, _):
        tokens = pl.ds(k * chunk, chunk)
        windows = pl.ds(k * (chunk // 64), chunk // 64)
        second = dot(act_out[tokens], down_w[...]) + down_b[...]
        sums[windows] += second.reshape(chunk // 64, WIN, WIN, 256)
        return 0

    lax.fori_loop(0, chunks, attend_sum, 0, unroll=True)
    lax.fori_loop(0, chunks, raise_up, 0, unroll=True)
    lax.fori_loop(0, chunks, put_down, 0, unroll=True)
    column = iota((columns, 1), 0)

    def rows_out(r, _):
        row = place[0] + band * WIN + r
        row = jnp.where(row < 0, row + height, row)
        limit = jnp.where(row < place[1 + sample], place[3 + sample], 0)
        back = pltpu.roll(sums[:, r].reshape(columns, 256), columns - WIN // 2, 0)
        sum_out[0, r] = jnp.where(column < limit, back, 0.0).astype(BF)
        return 0

    lax.fori_loop(0, WIN, rows_out, 0, unroll=True)

    @pl.when(band == 0)
    def _():
        first_rows[0] = sum_out[0, : WIN // 2 + 1]


def ffn_forward(place, x, mix, out_w, out_b, gain, shift, up_w, up_b, down_w, down_b, height, shape):
    samples, grid_rows, columns, width = shape
    bands = grid_rows // WIN
    tokens = WIN * columns
    steps = samples * bands
    hidden = up_w.shape[1]
    total = steps * tokens

    def step_of(step):
        return step // bands, step % bands

    def row_block(step):
        return (step, 0)

    rows = [width, width, 128, hidden, hidden]
    types = [BF, BF, F32, BF, BF]
    return pl.pallas_call(
        functools.partial(ffn_forward_body, height, step_of),
        grid=(steps,),
        in_specs=[SMEM_SPEC]
        + [pl.BlockSpec((tokens, width), row_block)] * 2
        + [const_spec(a.shape) for a in (out_w, out_b, gain, shift, up_w, up_b, down_w, down_b)],
        out_specs=[pl.BlockSpec((tokens, n), row_block) for n in rows]
        + [
            pl.BlockSpec((1, WIN, columns, width), lambda s: (*step_of(s), 0, 0)),
            pl.BlockSpec((1, WIN // 2 + 1, columns, width), lambda s: (step_of(s)[0], 0, 0, 0)),
        ],
        out_shape=[pltpu.HBM((total, n), t) for n, t in zip(rows, types)]
        + [
            pltpu.VMEM(shape, BF),
            jax.ShapeDtypeStruct((samples, WIN // 2 + 1, columns, width), BF),
        ],
        scratch_shapes=[pltpu.VMEM((columns // WIN, WIN, WIN, width), F32)],
        compiler_params=params(32),
        cost_estimate=SMALL_COST,
        name="ffn_forward",
    )(
        place, *near(x, mix, out_w), *far(out_b, gain, shift), *near(up_w), *far(up_b), *near(down_w),
        *far(down_b),
    )


def column_sum(x):
    return jnp.sum(x, 0, keepdims=True)


def ffn_backward_body(
    height, step_of, place, above, own, act, slope, normed, xhat_ref, rstd_ref, mix, conv_w,
    out_w, gain, up_w, down_w, first_out, mixed_out, down_out, up_out, out_out, vec_out,
    taps, turned, branch, low, raised_s, attn, down_acc, up_acc, out_acc, vec,
):
    step = pl.program_id(0)
    sample, band = step_of(step)
    columns = own.shape[2]
    tokens = columns * WIN
    half = WIN // 2
    column = iota((columns, 1), 0)

    @pl.when(step == 0)
    def _():
        for ref in (down_acc, up_acc, out_acc, vec):
            ref[...] = jnp.zeros_like(ref)
        for k in range(9):
            at = 256 * (k % 3)
            turned[k // 3, :, at : at + 256] = conv_w[k, 0]

    start = place[0] + half
    not_first = start != 0
    lanes = (0, 256, 512)
    top = band == 0
    before = jnp.where(top, jnp.where(not_first, start, height), start + band * WIN) - half - 1

    def put_group(group):
        for k in range(half + 2):
            row = before + k if group == 0 else start + band * WIN + k - 1
            at = band * WIN + (group - 1) * half - 1 + k
            source = own[0, jnp.maximum(at, 0)]
            allowed = True
            if group == 0 and k <= half:
                source = jnp.where(top, above[0, k], source)
            elif group == 0:
                row = start + band * WIN
                allowed = ~top | not_first
            elif k == 0:
                source = jnp.where(top, above[0, ABOVE_LAST], source)
                allowed = ~top | not_first
            limit = row_limit(place, sample, row, allowed)
            put_taps(source, limit, taps, group * (half + 2) + k, lanes)

    put_group(0)
    for group in range(2):
        if group == 0:
            put_group(1)
        total = 0.0
        for a in range(3):
            at = group * (half + 2) + 2 - a
            piece = taps[at : at + half].reshape(half * columns, 768)
            total = total + dot_nt(piece, turned[a])
        for k in range(half):
            row = place[0] + band * WIN + group * half + k
            row = jnp.where(row < 0, row + height, row)
            limit = row_limit(place, sample, row)
            part = jnp.where(column < limit, total[k * columns : (k + 1) * columns], 0.0)
            part = pltpu.roll(part, half, 0)
            branch[:, group * half + k] = part.reshape(columns // WIN, WIN, 256)

    chunk = 256
    windows = chunk // 64
    for k in range(tokens // chunk):
        at = slice(k * chunk, (k + 1) * chunk)
        upper = branch[k * windows : (k + 1) * windows].reshape(chunk, 256)
        low[at] = upper.astype(BF)
        vec[0:1] += column_sum(upper.astype(BF).astype(F32))
    for k in range(tokens // chunk):
        at = slice(k * chunk, (k + 1) * chunk)
        for f in range(0, 1024, 256):
            wide = slice(f, f + 256)
            raised = (dot_nt(low[at], down_w[wide]) * slope[at, wide].astype(F32)).astype(BF)
            raised_s[at, wide] = raised
            row = 4 + f // 256
            vec[row : row + 1] += column_sum(raised.astype(F32))
    for k in range(tokens // chunk):
        at = slice(k * chunk, (k + 1) * chunk)
        dy = dot_nt(raised_s[at], up_w[...])
        xhat = xhat_ref[at].astype(F32)
        rstd = rstd_ref[at]
        rstd = jnp.concatenate([rstd, rstd], 1)
        upper = branch[k * windows : (k + 1) * windows].reshape(chunk, 256)
        first = upper + norm_back(dy, xhat, rstd, gain[...])
        first_out[at] = first
        attn[at] = first.astype(BF)
        vec[1:2] += column_sum(dy * xhat)
        vec[2:3] += column_sum(dy)
        vec[3:4] += column_sum(first.astype(BF).astype(F32))
    for k in range(tokens // chunk):
        at = slice(k * chunk, (k + 1) * chunk)
        mixed_out[at] = dot_nt(attn[at], out_w[...]).astype(BF)
    low_t = low[...].T
    normed_t = normed[...].T
    for f in range(0, 1024, 256):
        wide = slice(f, f + 256)
        down_acc[:, wide] += dot(low_t, act[:, wide])
        up_acc[:, wide] += dot(normed_t, raised_s[:, wide])
    out_acc[...] += dot(mix[...].T, attn[...])

    @pl.when(step == pl.num_programs(0) - 1)
    def _():
        for f in range(0, 1024, 256):
            wide = slice(f, f + 256)
            down_out[wide] = down_acc[:, wide].T.astype(BF)
            up_out[:, wide] = up_acc[:, wide].astype(BF)
        out_out[...] = out_acc[...].astype(BF)
        vec_out[...] = vec[...].astype(BF)


def ffn_backward(
    place, above, own, act, slope, normed, xhat, rstd, mix, conv_w, out_w, gain, up_w, down_w, height
):
    samples, grid_rows, columns, width = own.shape
    bands = grid_rows // WIN
    tokens = WIN * columns
    steps = samples * bands
    total = steps * tokens
    hidden = up_w.shape[1]

    def step_of(step):
        return step // bands, step % bands

    def row_block(step):
        return (step, 0)

    def sample_block(step):
        return (step_of(step)[0], 0, 0, 0)

    rows = (act, slope, normed, xhat, rstd, mix)
    return pl.pallas_call(
        functools.partial(ffn_backward_body, height, step_of),
        grid=(steps,),
        in_specs=[
            SMEM_SPEC,
            pl.BlockSpec((1,) + above.shape[1:], sample_block),
            pl.BlockSpec((1,) + own.shape[1:], sample_block),
        ]
        + [pl.BlockSpec((tokens, a.shape[1]), row_block) for a in rows]
        + [pl.BlockSpec((9, 1, width, width), lambda s: (0, 0, 0, 0))]
        + [const_spec(a.shape) for a in (out_w, gain, up_w, down_w)],
        out_specs=[
            pl.BlockSpec((tokens, width), row_block),
            pl.BlockSpec((tokens, width), row_block),
            const_spec((hidden, width)),
            const_spec((width, hidden)),
            const_spec((width, width)),
            const_spec((8, width)),
        ],
        out_shape=[
            pltpu.VMEM((total, width), F32),
            pltpu.VMEM((total, width), BF),
            pltpu.HBM((hidden, width), BF),
            pltpu.HBM((width, hidden), BF),
            pltpu.HBM((width, width), BF),
            jax.ShapeDtypeStruct((8, width), BF),
        ],
        scratch_shapes=[
            pltpu.VMEM((WIN + 4, columns, 3 * width), BF),
            pltpu.VMEM((3, width, 3 * width), BF),
            pltpu.VMEM((columns // WIN, WIN, WIN, width), F32),
            pltpu.VMEM((tokens, width), BF),
            pltpu.VMEM((tokens, hidden), BF),
            pltpu.VMEM((tokens, width), BF),
            pltpu.VMEM((width, hidden), F32),
            pltpu.VMEM((width, hidden), F32),
            pltpu.VMEM((width, width), F32),
            pltpu.VMEM((8, width), F32),
        ],
        compiler_params=params(44),
        cost_estimate=pl.CostEstimate(
            flops=2 * 10**10, bytes_accessed=10**7, transcendentals=0
        ),
        name="ffn_backward",
    )(
        place, *far(above, own, *rows[:5]), *near(mix), *far(conv_w), *near(out_w), *far(gain),
        *near(up_w, down_w),
    )


def attn_backward_body(
    scale, step_of, mixed, qkv, prob, normed, xhat_ref, rstd_ref, first, weight, gain, mask, conv_vec,
    places, input_out, up_out, qkv_out, vec_out, qkv_acc, table_acc, vec_acc, grads, score_grads, sums,
):
    step = pl.program_id(0)
    _, band = step_of(step)
    columns = input_out.shape[2]
    half = WIN // 2

    @pl.when(step == 0)
    def _():
        for ref in (qkv_acc, table_acc, vec_acc):
            ref[...] = jnp.zeros_like(ref)

    attn_backward_step(
        scale, mixed, qkv, prob, normed, xhat_ref, rstd_ref, first, weight, gain, mask,
        qkv_acc, table_acc, vec_acc, grads, score_grads, sums,
    )

    def row_out(r):
        return pltpu.roll(sums[:, r].reshape(columns, 256), columns - half, 0)

    @pl.when(band == 0)
    def _():
        for r in range(half):
            up_out[0, r] = row_out(r).astype(BF)
            input_out[0, r] = row_out(half + r)

    @pl.when(band > 0)
    def _():
        for r in range(WIN):
            input_out[0, band * WIN - half + r] = row_out(r)

    @pl.when(step == pl.num_programs(0) - 1)
    def _():
        for f in range(0, 768, 256):
            qkv_out[:, f : f + 256] = qkv_acc[:, f : f + 256].astype(BF)
        table = collect_bias(table_acc[...], places[...])
        rest = jnp.concatenate([vec_acc[0:2], conv_vec[0:1], jnp.zeros((5, 256), F32)], 0)
        vec_out[...] = jnp.concatenate([table, rest], 1).astype(BF)


def attn_backward_step(
    scale, mixed, qkv, prob, normed, xhat_ref, rstd_ref, first, weight, gain, mask,
    qkv_acc, table_acc, vec_acc, grads, score_grads, sums,
):
    tokens = qkv.shape[0]
    columns = tokens // WIN

    def attend(pair, _):
        head_at = mask[...]
        for half in range(2):
            lanes = slice(256 * half, 256 * half + 256)
            low = prob[pair, lanes]
            mixed_blocks = blocks_of(mixed, pair, 128 * half)
            values = spread_heads(pair_of(qkv, pair, 512 + 128 * half), head_at)
            prob_grad = dot_nt(values, mixed_blocks).reshape(4, 64, 128)
            probs = low.astype(F32).reshape(4, 64, 128)
            shared = jnp.sum(prob_grad * probs, 1, keepdims=True)
            score_grad = (probs * (prob_grad - shared)).astype(BF).reshape(256, 128)
            table_acc[lanes] += score_grad.astype(F32)
            score_grads[pair, lanes] = score_grad
        return 0

    def project(pair, _):
        head_at = mask[...]
        for half in range(2):
            lanes = slice(256 * half, 256 * half + 256)
            low = prob[pair, lanes]
            mixed_blocks = blocks_of(mixed, pair, 128 * half)
            score_grad = score_grads[pair, lanes]
            keys = spread_heads(pair_of(qkv, pair, 256 + 128 * half), head_at)
            queries = blocks_of(qkv, pair, 128 * half)
            query_grad = (dot_tn(score_grad, keys) * scale).astype(BF)
            out = slice(128 * half, 128 * half + 128)
            grads[pl.ds(pair * 128, 64), out] = query_grad[:64, :128]
            grads[pl.ds(pair * 128 + 64, 64), out] = query_grad[64:, 128:]
            wide = head_at.astype(F32)
            key_grad = (dot(score_grad, queries) * wide).reshape(4, 64, 256)
            key_grad = (jnp.sum(key_grad, 0) * scale).astype(BF)
            out = slice(256 + 128 * half, 256 + 128 * half + 128)
            grads[pl.ds(pair * 128, 64), out] = key_grad[:, :128]
            grads[pl.ds(pair * 128 + 64, 64), out] = key_grad[:, 128:]
            value_grad = (dot(low, mixed_blocks) * wide).reshape(4, 64, 256)
            value_grad = jnp.sum(value_grad, 0).astype(BF)
            out = slice(512 + 128 * half, 512 + 128 * half + 128)
            grads[pl.ds(pair * 128, 64), out] = value_grad[:, :128]
            grads[pl.ds(pair * 128 + 64, 64), out] = value_grad[:, 128:]
        return 0

    lax.fori_loop(0, columns // 16, attend, 0, unroll=8)
    lax.fori_loop(0, columns // 16, project, 0, unroll=8)
    for f in range(0, 768, 256):
        qkv_acc[:, f : f + 256] += dot_tn(normed[...], grads[:, f : f + 256])

    def part(k, _):
        at = pl.ds(k * 256, 256)
        dy = dot_nt(grads[at], weight[...])
        xhat = xhat_ref[at].astype(F32)
        rstd = rstd_ref[at]
        rstd = jnp.concatenate([rstd, rstd], 1)
        total = first[at] + norm_back(dy, xhat, rstd, gain[...])
        sums[pl.ds(k * 4, 4)] = total.reshape(4, WIN, WIN, 256)
        vec_acc[0:1] += column_sum(dy * xhat)
        vec_acc[1:2] += column_sum(dy)
        return 0

    lax.fori_loop(0, tokens // 256, part, 0, unroll=True)


def attn_backward(
    mixed, qkv, prob, normed, xhat, rstd, first, weight, gain, mask, conv_vec, places, scale, shape
):
    samples, grid_rows, columns, width = shape
    bands = grid_rows // WIN
    tokens = WIN * columns
    half = WIN // 2

    def step_of(step):
        return step // bands, step % bands

    def row_block(step):
        return (step, 0)

    def sample_block(step):
        return (step_of(step)[0], 0, 0, 0)

    rows = (mixed, qkv, prob, normed, xhat, rstd, first)
    consts = (weight, gain, mask, conv_vec, places)
    in_specs = [pl.BlockSpec((tokens, a.shape[1]), row_block) for a in rows]
    in_specs[2] = pl.BlockSpec((columns // 16, 512, 128), lambda s: (s, 0, 0))
    in_specs += [const_spec(a.shape) for a in consts]
    return pl.pallas_call(
        functools.partial(attn_backward_body, scale, step_of),
        grid=(samples * bands,),
        in_specs=in_specs,
        out_specs=[
            pl.BlockSpec((1,) + shape[1:], sample_block),
            pl.BlockSpec((1, half, columns, width), sample_block),
            const_spec((width, 3 * width)),
            const_spec((8, 2 * width)),
        ],
        out_shape=[
            jax.ShapeDtypeStruct(shape, F32),
            jax.ShapeDtypeStruct((samples, half, columns, width), BF),
            jax.ShapeDtypeStruct((width, 3 * width), BF),
            jax.ShapeDtypeStruct((8, 2 * width), BF),
        ],
        scratch_shapes=[
            pltpu.VMEM((width, 3 * width), F32),
            pltpu.VMEM((512, 128), F32),
            pltpu.VMEM((8, width), F32),
            pltpu.VMEM((tokens, 3 * width), BF),
            pltpu.VMEM((columns // 16, 512, 128), BF),
            pltpu.VMEM((columns // WIN, WIN, WIN, width), F32),
        ],
        compiler_params=params(32),
        cost_estimate=SMALL_COST,
        name="attn_backward",
    )(*near(mixed), *far(*rows[1:6]), *near(first, weight), *far(*consts[1:]))


def shifted(row, by):
    columns = row.shape[0]
    moved = pltpu.roll(row, by % columns, 0)
    place = iota((8, 1), 0)
    if by == 1:
        return jnp.concatenate([jnp.where(place == 0, 0.0, moved[:8]), moved[8:]], 0)
    return jnp.concatenate([moved[:-8], jnp.where(place == 7, 0.0, moved[-8:])], 0)


def pack_near_body(qkv, out_w, up, down, near):
    rows = qkv.shape[0]
    at = 0
    for ref in (qkv, out_w, up):
        near[:, at : at + ref.shape[1]] = ref[...].astype(BF)
        at += ref.shape[1]
    for k in range(down.shape[0] // rows):
        near[:, at : at + down.shape[1]] = down[k * rows : (k + 1) * rows].astype(BF)
        at += down.shape[1]


def pack_near(qkv, out_w, up, down):
    rows = qkv.shape[0]
    lanes = (qkv.size + out_w.size + up.size + down.size) // rows
    return pl.pallas_call(
        pack_near_body,
        out_shape=jax.ShapeDtypeStruct((rows, lanes), BF),
        compiler_params=params(16),
        cost_estimate=SMALL_COST,
        name="pack_near",
    )(*far(qkv, out_w, up, down))


def unpack_near_body(order, held, qkv, out_w, up, down):
    devices, rows, _ = held.shape
    count = max(16 // rows, 1)

    def some(k, _):
        pieces = [held[order[k * count + n]] for n in range(count)]
        at = 0
        place = pl.ds(pl.multiple_of(k * count * rows, count * rows), count * rows)
        for ref in (qkv, out_w, up):
            lanes = slice(at, at + ref.shape[1])
            ref[place] = jnp.concatenate([piece[:, lanes] for piece in pieces], 0)
            at = lanes.stop
        width = down.shape[1]
        parts = down.shape[0] // (devices * rows)
        tall = [
            piece[:, at + n * width : at + (n + 1) * width] for piece in pieces for n in range(parts)
        ]
        size = count * rows * parts
        down[pl.ds(pl.multiple_of(k * size, size), size)] = jnp.concatenate(tall, 0)
        return 0

    lax.fori_loop(0, devices // count, some, 0, unroll=4)


def unpack_near(order, held, weights):
    devices = held.shape[0]
    return pl.pallas_call(
        unpack_near_body,
        in_specs=[SMEM_SPEC, pl.BlockSpec(memory_space=pltpu.VMEM)],
        out_shape=[pltpu.VMEM((devices * w.shape[0], w.shape[1]), BF) for w in weights],
        compiler_params=params(24),
        cost_estimate=SMALL_COST,
        name="unpack_near",
    )(order, held)


def last_sums_body(parts, down, out_w, up, qkv, vec):
    count, rows, _ = parts.shape
    total = parts[0].astype(F32)
    for k in range(1, count):
        total = total + parts[k].astype(F32)
    width = down.shape[1]
    for k in range(down.shape[0] // rows):
        down[k * rows : (k + 1) * rows] = total[:, k * width : (k + 1) * width]
    at = down.size // rows
    for ref in (out_w, up, qkv, vec):
        ref[...] = total[:, at : at + ref.shape[1]]
        at += ref.shape[1]


def last_sums(parts, down, rest):
    shapes = (down, *rest)
    return pl.pallas_call(
        last_sums_body,
        out_shape=[jax.ShapeDtypeStruct(a, F32) for a in shapes],
        compiler_params=params(24),
        cost_estimate=SMALL_COST,
        name="last_sums",
    )(parts)


def copies_body(x, out):
    low = x[...].astype(BF)
    for k in range(out.shape[0]):
        out[k] = low


def make_copies(x, count):
    return pl.pallas_call(
        copies_body,
        out_shape=jax.ShapeDtypeStruct((count,) + x.shape, BF),
        compiler_params=params(16),
        cost_estimate=SMALL_COST,
        name="make_copies",
    )(*far(x))


def row_limit(place, sample, row, allowed=True):
    return jnp.where((row < place[1 + sample]) & allowed, place[3 + sample], 0)


def put_taps(row, limit, target, at, lanes):
    column = iota((row.shape[0], 1), 0)
    wide = jnp.where(column < limit, row.astype(F32), 0.0)
    target[at, :, lanes[0] : lanes[0] + 256] = shifted(wide, -1).astype(BF)
    target[at, :, lanes[1] : lanes[1] + 256] = wide.astype(BF)
    target[at, :, lanes[2] : lanes[2] + 256] = shifted(wide, 1).astype(BF)


ABOVE_LAST = WIN // 2
ABOVE_HIDDEN = WIN // 2 + 1


def own_taps(height, place, above, own, below, taps, at):
    sample = pl.program_id(0)
    rows = own.shape[1]
    start = place[0] + WIN // 2

    def put(r):
        allowed = True
        if r == 0:
            source, allowed = above[0, ABOVE_LAST], start != 0
        elif r <= rows:
            source = own[0, r - 1]
        else:
            source, allowed = below[0, 0], start + rows != height
        limit = row_limit(place, sample, start + r - 1, allowed)
        put_taps(source, limit, taps, at + r, (0, 256, 512))

    return put


def conv_weight_body(
    height, place, above, own, below, sums, hidden, out, vec, taps, held, acc, acc_hidden
):
    sample = pl.program_id(0)

    @pl.when(sample == 0)
    def _():
        for ref in (acc, acc_hidden, vec):
            ref[...] = jnp.zeros_like(ref)

    rows, columns = own.shape[1:3]
    half = WIN // 2
    column = iota((columns, 1), 0)
    start = place[0] + half
    not_first = start != 0

    before = jnp.where(not_first, start, height) - half - 1
    put = own_taps(height, place, above, own, below, taps, half + 2)
    for r in range(half + 1):
        limit = row_limit(place, sample, before + r)
        put_taps(above[0, r], limit, taps, r, (0, 256, 512))
    limit = row_limit(place, sample, start, not_first)
    put_taps(own[0, 0], limit, taps, half + 1, (0, 256, 512))

    def add(source, first, acc):
        count = source.shape[0]
        turned = source.reshape(count * columns, 256).T
        for a in range(3):
            piece = taps[first + 2 - a : first + 2 - a + count].reshape(count * columns, 768)
            acc[a] += dot(turned, piece)

    put(0)
    put(1)
    add(sums[0, :half], 0, acc)
    step = 8
    for r in range(0, rows, step):
        for k in range(r, r + step):
            put(k + 2)
            limit = row_limit(place, sample, start + k)
            held[k] = jnp.where(column < limit, hidden[0, k].astype(F32), 0.0).astype(BF)
            vec[0:1] += jnp.sum(taps[half + 3 + k, :, 256:512].astype(F32), 0, keepdims=True)
        add(held[r : r + step], half + 2 + r, acc_hidden)
        last = min(r + step, rows - half)
        add(sums[0, half + r : half + last], half + 2 + r, acc)

    @pl.when(sample == pl.num_programs(0) - 1)
    def _():
        for k in range(9):
            at = 256 * (k % 3)
            out[k, 0] = acc[k // 3, :, at : at + 256].astype(BF)
            out[k, 1] = acc_hidden[k // 3, :, at : at + 256].astype(BF)


def field_spec(a):
    return pl.BlockSpec((1,) + a.shape[1:], lambda s: (s, 0, 0, 0))


def conv_call(
    body, name, mib, place, fields, consts, height, out_specs, out_shape, scratch, cost=None
):
    return pl.pallas_call(
        functools.partial(body, height),
        grid=(fields[0][1].shape[0],),
        in_specs=[SMEM_SPEC] + [s for s, _ in fields] + [s for s, _ in consts],
        out_specs=out_specs,
        out_shape=out_shape,
        scratch_shapes=scratch,
        compiler_params=params(mib),
        cost_estimate=cost or SMALL_COST,
        name=name,
    )(place, *[a for _, a in fields], *far(*[a for _, a in consts]))


def whole(a):
    return field_spec(a), far(a)[0]


def conv_weight(place, grads, sums, hidden, height):
    _, rows, columns, width = sums.shape
    shape = (9, 2, width, width)
    acc = pltpu.VMEM((3, width, 3 * width), F32)
    return conv_call(
        conv_weight_body, "conv_weight", 34, place, [*map(whole, grads), (field_spec(sums), near(sums)[0]), whole(hidden)], (),
        height, [const_spec(shape), const_spec((8, width))],
        [jax.ShapeDtypeStruct(shape, BF), jax.ShapeDtypeStruct((8, width), F32)],
        [
            pltpu.VMEM((rows + WIN, columns, 3 * width), BF),
            pltpu.VMEM((rows, columns, width), BF),
            acc,
            acc,
        ],
        pl.CostEstimate(flops=2 * 10**10, bytes_accessed=10**7, transcendentals=0),
    )


def conv_data_body(height, place, above, own, below, weight, out, taps, turned):
    sample = pl.program_id(0)
    columns = own.shape[2]
    column = iota((columns, 1), 0)

    @pl.when(sample == 0)
    def _():
        for k in range(9):
            at = 256 * (k % 3)
            turned[k // 3, :, at : at + 256] = weight[k, 0]

    put = own_taps(height, place, above, own, below, taps, 0)
    for r in range(2):
        put(r)
    for r in range(0, own.shape[1], 4):
        for k in range(r + 2, r + 6):
            put(k)
        total = 0.0
        for a in range(3):
            piece = taps[r + 2 - a : r + 6 - a].reshape(4 * columns, 768)
            total = total + dot_nt(piece, turned[a])
        for k in range(4):
            limit = row_limit(place, sample, place[0] + WIN // 2 + r + k)
            part = total[k * columns : (k + 1) * columns]
            out[0, r + k] = jnp.where(column < limit, part, 0.0)


def conv_data(place, grads, weight, height):
    own = grads[1]
    width = own.shape[-1]
    weight_spec = pl.BlockSpec((9, 1, width, width), lambda s: (0, 1, 0, 0))
    return conv_call(
        conv_data_body, "conv_data", 28, place, [whole(a) for a in grads], ((weight_spec, weight),),
        height, field_spec(own), jax.ShapeDtypeStruct(own.shape, F32),
        [
            pltpu.VMEM((own.shape[1] + 2, own.shape[2], 3 * width), BF),
            pltpu.VMEM((3, width, 3 * width), BF),
        ],
        pl.CostEstimate(flops=10**10, bytes_accessed=10**7, transcendentals=0),
    )


def conv_forward_body(
    height, place, sums, sums_below, above, hidden, below, weight, bias, out, taps
):
    sample = pl.program_id(0)
    rows, columns = out.shape[1:3]
    column = iota((columns, 1), 0)
    half = WIN // 2
    start = place[0] + half
    not_first, not_last = start != 0, start + rows != height

    def put(r):
        allowed = True
        if r == 0:
            first, second, allowed = sums[0, half - 1], above[0, ABOVE_HIDDEN], not_first
        elif r <= rows:
            first, second = None, hidden[0, r - 1]
            if r <= rows - half:
                first = sums[0, half + r - 1]
            else:
                first = sums_below[0, r - 1 - rows + half]
        else:
            first, second, allowed = sums_below[0, half], below[0, 1], not_last
        limit = row_limit(place, sample, start + r - 1, allowed)
        put_taps(first, limit, taps, r, (1024, 512, 0))
        put_taps(second, limit, taps, r, (1280, 768, 256))

    for r in range(2):
        put(r)
    for r in range(0, rows, 4):
        for k in range(r + 2, r + 6):
            put(k)
        total = bias[...]
        for a in range(3):
            piece = taps[r + a : r + a + 4].reshape(4 * columns, 1536)
            total = total + dot(piece, weight[a * 1536 : (a + 1) * 1536])
        for k in range(4):
            limit = row_limit(place, sample, start + r + k)
            part = total[k * columns : (k + 1) * columns]
            out[0, r + k] = jnp.where(column < limit, part, 0.0).astype(BF)


def conv_forward(place, sums, sums_below, hidden, weight, bias, height):
    samples, rows, columns, width = sums.shape
    fields = (*near(sums), *far(sums_below, *hidden))
    return pl.pallas_call(
        functools.partial(conv_forward_body, height),
        grid=(samples,),
        in_specs=[SMEM_SPEC]
        + [field_spec(a) for a in fields]
        + [const_spec(weight.shape), const_spec(bias.shape)],
        out_specs=field_spec(sums),
        out_shape=jax.ShapeDtypeStruct(sums.shape, BF),
        scratch_shapes=[pltpu.VMEM((rows + 2, columns, 6 * width), BF)],
        compiler_params=params(32),
        cost_estimate=SMALL_COST,
        name="conv_forward",
    )(place, *fields, *far(weight, bias))


def shards(
    layer_input,
    hidden_state,
    crop_rows,
    crop_cols,
    first_gain,
    first_shift,
    qkv_weight,
    bias_table,
    output_weight,
    output_bias,
    second_gain,
    second_shift,
    up_weight,
    up_bias,
    down_weight,
    down_bias,
    conv_weight_in,
    conv_bias,
    cotangent,
):
    samples, grid_rows, columns, width = layer_input.shape
    shape = layer_input.shape
    heads = bias_table.shape[1]
    scale = float((width // heads) ** (-0.5))
    half = WIN // 2
    devices = device_count()
    row_devices = lax.axis_size("rows")
    height = grid_rows * row_devices
    row_place = lax.axis_index("rows")
    row_start = row_place * grid_rows
    place = jnp.concatenate(
        [(row_start - half)[None].astype(jnp.int32), crop_rows, crop_cols]
    ).astype(jnp.int32)

    hidden_width = up_weight.shape[1]

    def vec(v):
        return v.reshape(1, -1)

    input_above = ring(layer_input[:, grid_rows - half :], 1)
    rows_out, rows_down = output_weight.shape[0], down_weight.shape[0]
    weights = pack_near(qkv_weight, output_weight, up_weight, down_weight)
    offsets = bias_table.shape[0]

    def beside(held):
        grad, hidden, weight, table = after(
            (cotangent, hidden_state, conv_weight_in, bias_table), held
        )
        halo_above = jnp.concatenate([grad[:, grid_rows - half - 1 :], hidden[:, grid_rows - 1 :]], 1)
        halo_below = jnp.concatenate([grad[:, :1], hidden[:, :1]], 1)
        table = jnp.pad(table.T, ((0, 0), (0, 256 - offsets)))
        return halo_above, halo_below, make_copies(weight, devices), table, input_above, place

    held, order, (halo_above, halo_below, conv_copies, table, *_) = gather_steps(weights, beside)
    halo_above, halo_below, conv_copies = after((halo_above, halo_below, conv_copies), held)
    halo_above, halo_below = ring(halo_above, 1), ring(halo_below, -1)
    grads = (halo_above, cotangent, halo_below)
    conv_full = gather_copies(conv_copies).reshape(-1, width)

    qkv_full, output_full, up_full, down_full = unpack_near(
        order, held, (qkv_weight, output_weight, up_weight, down_weight)
    )
    mask = jnp.asarray(head_mask(), BF)

    x, normed, xhat, rstd, qkv, prob, mix = attn_forward(
        place, input_above, layer_input, vec(first_gain), vec(first_shift), qkv_full, table,
        jnp.asarray(offset_places(False), BF), mask, height, scale,
    )
    normed_2, xhat_2, rstd_2, act, slope, sums, sums_first = ffn_forward(
        place, x, mix, output_full, vec(output_bias), vec(second_gain), vec(second_shift),
        up_full, vec(up_bias), down_full, vec(down_bias), height, shape,
    )
    conv_local, conv_bias_part = conv_weight(place, grads, sums, hidden_state, height)
    conv_local, exchange = scatter_pairs(conv_local.reshape(devices, -1, width))
    conv_all = exchange(conv_local)
    sums_below = ring(after(sums_first, conv_local), -1)
    conv_blocks = after(conv_full.reshape(9, 2, width, width), conv_local)
    first_grad, mixed, down_acc, up_acc, out_acc, vec_ffn = ffn_backward(
        place, halo_above, cotangent, act, slope, normed_2, xhat_2, rstd_2, mix, conv_blocks,
        output_full, vec(second_gain), up_full, down_full, height,
    )
    input_grad, input_up, qkv_acc, vec_attn = attn_backward(
        after(mixed, sums_below), qkv, prob, normed, xhat, rstd, first_grad, qkv_full,
        vec(first_gain), mask, conv_bias_part, jnp.asarray(offset_places(True), BF).T, scale, shape,
    )
    down_acc, up_acc, out_acc, vec_ffn = after((down_acc, up_acc, out_acc, vec_ffn), qkv_acc)
    down_local = down_acc.reshape(devices, -1, rows_out, width).transpose(0, 2, 1, 3)
    parts = [
        down_local.reshape(devices, rows_out, -1),
        *(a.reshape(devices, rows_out, -1) for a in (out_acc, up_acc, qkv_acc)),
    ]
    last_local, exchange = scatter_pairs(
        with_vectors(parts, jnp.concatenate([vec_ffn, vec_attn], 1))
    )
    last_all = exchange(last_local)
    input_from_below = ring(after(input_up, last_local), -1)
    hidden_grad = conv_data(after(place, last_local), grads, conv_blocks, height)
    layer_output = conv_forward(
        after(place, hidden_grad), sums, sums_below, (halo_above, hidden_state, halo_below),
        conv_full, vec(conv_bias), height,
    )

    input_grad = lax.dynamic_update_slice(
        after(input_grad, layer_output), input_from_below.astype(F32), (0, grid_rows - half, 0, 0)
    )

    def total(parts):
        return jnp.sum(parts.astype(F32), 0)

    conv_weight_grad = total(conv_all)
    down_weight_grad, output_weight_grad, up_weight_grad, qkv_weight_grad, vectors = last_sums(
        last_all,
        (rows_down, width),
        [
            (rows_out, width), (rows_out, hidden_width), (rows_out, 3 * width),
            (rows_out, 24 * width // rows_out),
        ],
    )
    vectors = vectors.reshape(8, 3, width)
    ffn_vec, table_grad, attn_vec = (vectors[:, k] for k in range(3))
    down_bias_grad, second_gain_grad, second_shift_grad, output_bias_grad = (
        ffn_vec[k] for k in range(4)
    )
    up_bias_grad = ffn_vec[4:].reshape(-1)
    bias_table_grad = table_grad[:, :offsets][:, ::-1].T
    first_gain_grad, first_shift_grad, conv_bias_grad = (attn_vec[k] for k in range(3))
    return (
        layer_output,
        input_grad,
        hidden_grad,
        first_gain_grad,
        first_shift_grad,
        qkv_weight_grad,
        bias_table_grad,
        output_weight_grad,
        output_bias_grad,
        second_gain_grad,
        second_shift_grad,
        up_weight_grad,
        up_bias_grad,
        down_weight_grad,
        down_bias_grad,
        conv_weight_grad,
        conv_bias_grad,
    )


def solution(mesh):
    field = P("batch", "rows", None, None)
    weight = P(AXES, None)
    in_specs = (
        field, field, P("batch"), P("batch"), P(), P(), weight, P(), weight, P(), P(), P(),
        weight, P(), weight, P(), weight, P(), field,
    )
    out_specs = (
        field, field, field, P(), P(), weight, P(), weight, P(), P(), P(), weight, P(), weight,
        P(), weight, P(),
    )
    return jax.shard_map(shards, mesh=mesh, in_specs=in_specs, out_specs=out_specs, check_vma=False)
```

```python
import functools

import jax
import jax.numpy as jnp
import numpy as np
from jax import lax
from jax.experimental import pallas as pl
from jax.experimental.pallas import tpu as pltpu
from jax.sharding import PartitionSpec as P

WIN = 8
EPSILON = 1e-05
MASKED = -100.0
HIGHEST = lax.Precision.HIGHEST
AXES = ("rows", "batch")
BF = jnp.bfloat16
F32 = jnp.float32
MIB = 1024 * 1024
BACK_MIB = 56
LOG2E = 1.4426950408889634


def dot(left, right):
    return jnp.dot(left, right, preferred_element_type=F32)


def dot_nt(left, right):
    return lax.dot_general(left, right, (((1,), (1,)), ((), ())), preferred_element_type=F32)


def dot_tn(left, right):
    return lax.dot_general(left, right, (((0,), (0,)), ((), ())), preferred_element_type=F32)


def iota(shape, dim):
    return lax.broadcasted_iota(jnp.int32, shape, dim)


def device_index():
    return lax.axis_index("rows") * lax.axis_size("batch") + lax.axis_index("batch")


def device_count():
    return lax.axis_size("rows") * lax.axis_size("batch")


def after(x, *others):
    return lax.optimization_barrier((x, *others))[0]


def bit_groups():
    batch, rows = lax.axis_size("batch"), lax.axis_size("rows")
    batch_bits = [1 << k for k in range(batch.bit_length() - 1)]
    row_bits = [batch << k for k in range(rows.bit_length() - 1)]
    chips = row_bits[1:]
    groups = [batch_bits[k : k + 2] for k in range(0, len(batch_bits), 2)]
    groups += [chips[k : k + 2] for k in range(0, len(chips), 2)]
    return groups + [row_bits[:1]]


def gather_steps(x, beside):
    devices = device_count()
    held = x[None]
    places = [0]
    groups = bit_groups()
    for k, group in enumerate(groups):
        masks = [0]
        for bit in group:
            masks = masks + [m | bit for m in masks]
        if k == 1:
            other = beside(held)
        if k == len(groups) - 1:
            held = after(held, *other)
        pieces = [held]
        for mask in masks[1:]:
            pieces.append(lax.ppermute(held, AXES, [(i, i ^ mask) for i in range(devices)]))
        held = jnp.concatenate(pieces, 0)
        places = [p ^ m for m in masks for p in places]
    order = np.zeros(devices, np.int32)
    for place, mask in enumerate(places):
        order[mask] = place
    return held, jnp.asarray(order)[jnp.arange(devices) ^ device_index()], other


def scatter_pairs(x):
    rows, batch = lax.axis_size("rows"), lax.axis_size("batch")
    core = lax.axis_index("rows") % 2
    by_core = x.reshape((rows // 2, 2, batch) + x.shape[1:])
    mine = lax.dynamic_index_in_dim(by_core, core, 1, False)
    other = lax.dynamic_index_in_dim(by_core, 1 - core, 1, False)
    return add_pairs(*(a.reshape((-1,) + x.shape[1:]) for a in (mine, other)))


def add_pairs(mine, other):
    rows, batch = lax.axis_size("rows"), lax.axis_size("batch")
    other = lax.ppermute(other, "rows", [(i, i ^ 1) for i in range(rows)])
    pairs = (mine.astype(F32) + other.astype(F32)).astype(BF)
    groups = [
        [(2 * chip + k) * batch + b for chip in range(rows // 2) for b in range(batch)]
        for k in range(2)
    ]
    return pairs, lambda a: lax.all_to_all(a, AXES, 0, 0, axis_index_groups=groups, tiled=True)


def gather_copies(copies):
    return lax.all_to_all(copies, AXES, 0, 0, tiled=True)


def with_vectors(parts, vectors):
    rows = parts[0].shape[1]
    flat = vectors.reshape(1, rows, -1)
    flat = jnp.broadcast_to(flat, (parts[0].shape[0],) + flat.shape[1:])
    return jnp.concatenate(list(parts) + [flat], 2)


def ring(x, by):
    devices = lax.axis_size("rows")
    return lax.ppermute(x, "rows", [(i, (i + by) % devices) for i in range(devices)])


def norm_parts(x):
    centred = x - jnp.mean(x, -1, keepdims=True)
    rstd = lax.rsqrt(jnp.mean(centred * centred, -1, keepdims=True) + EPSILON)
    return centred * rstd, rstd


def norm_back(dy, xhat, rstd, gain):
    scaled = dy * gain
    first = jnp.mean(scaled, -1, keepdims=True)
    second = jnp.mean(scaled * xhat, -1, keepdims=True)
    return (scaled - first - xhat * second) * rstd


def head_mask():
    rows, lanes = np.arange(256)[:, None], np.arange(256)[None, :]
    return (rows // 64 == (lanes % 128) // 32).astype(np.float32)


def pair_of(ref, pair, column):
    first = ref[pl.ds(pair * 128, 64), column : column + 128]
    second = ref[pl.ds(pair * 128 + 64, 64), column : column + 128]
    return jnp.concatenate([first, second], 1)


def blocks_of(ref, pair, column):
    first = ref[pl.ds(pair * 128, 64), column : column + 128]
    second = ref[pl.ds(pair * 128 + 64, 64), column : column + 128]
    nothing = jnp.zeros_like(first)
    return jnp.concatenate(
        [jnp.concatenate([first, nothing], 1), jnp.concatenate([nothing, second], 1)], 0
    )


def spread_heads(pair, mask):
    return jnp.concatenate([pair] * 4, 0) * mask


def offset_places(turned):
    rows, lanes = np.arange(256)[:, None], np.arange(128)[None, :] % 64
    row, col = lanes // WIN, lanes % WIN
    if turned:
        row, col = WIN - 1 - row, WIN - 1 - col
    return (rows == row * (2 * WIN - 1) + col).astype(np.float32)


def three_parts(x):
    high = x.astype(BF)
    rest = x - high.astype(F32)
    middle = rest.astype(BF)
    return high, middle, (rest - middle.astype(F32)).astype(BF)


def spread_bias(table, places, bias, factor):
    line = 2 * WIN - 1
    for head in range(8):
        row = jnp.broadcast_to(table[head : head + 1], (WIN, 256))
        turns = []
        for r in range(WIN):
            by = 256 - (WIN - 1 - r) * line - (WIN - 1)
            turns.append(pltpu.roll(row, by, 1, stride=1, stride_axis=0))
        wide = jnp.concatenate(turns, 0)
        total = 0.0
        for part in three_parts(wide):
            total = total + dot(part, places[...])
        bias[head * 64 : head * 64 + 64] = total * factor


def collect_bias(grad, places):
    line = 2 * WIN - 1
    wide = 0.0
    for part in three_parts(grad):
        wide = wide + dot(part, places)
    out = []
    for head in range(8):
        total = jnp.zeros((WIN, 256), F32)
        for r in range(WIN):
            at = head * 64 + r * WIN
            total = total + pltpu.roll(wide[at : at + WIN], r * line, 1, stride=1, stride_axis=0)
        out.append(jnp.sum(total, 0, keepdims=True))
    return jnp.concatenate(out, 0)


def attn_forward_body(
    height, scale, step_of, place, above, upper, lower, gain, shift, weight, table, places, mask,
    x_out, norm_out, xhat_out, rstd_out, qkv_out, prob_out, mix_out, xs, bias,
):
    sample, band = step_of(pl.program_id(0))
    columns = lower.shape[2]

    @pl.when(pl.program_id(0) == 0)
    def _():
        spread_bias(table, places, bias, 1.0 / scale)

    def rows_from(ref, first):
        def rows_in(r, _):
            x = pltpu.roll(ref[0, r].astype(F32), WIN // 2, 0)
            xs[:, first + r] = x.reshape(columns // WIN, WIN, 256)
            return 0

        lax.fori_loop(0, WIN // 2, rows_in, 0, unroll=True)

    @pl.when(band == 0)
    def _():
        rows_from(above, 0)

    @pl.when(band > 0)
    def _():
        rows_from(upper, 0)

    rows_from(lower, WIN // 2)

    def norm_in(k, _):
        tokens = pl.ds(k * 128, 128)
        x = xs[pl.ds(k * 2, 2)].reshape(128, 256)
        xhat, rstd = norm_parts(x)
        x_out[tokens] = x.astype(BF)
        xhat_out[tokens] = xhat.astype(BF)
        rstd_out[tokens] = jnp.broadcast_to(rstd, (128, 128))
        norm_out[tokens] = (xhat * gain[...] + shift[...]).astype(BF)
        return 0

    lax.fori_loop(0, columns // 16, norm_in, 0, unroll=8)
    for k in range(0, columns * WIN, 256):
        qkv_out[k : k + 256] = dot(norm_out[k : k + 256], weight[...]).astype(BF)

    key_at, query_at = iota((64, 128), 0), iota((64, 128), 1)
    window_at = query_at // 64
    query_at = query_at % 64
    row_base = place[0] + band * WIN
    key_row, query_row = key_at // WIN + row_base, query_at // WIN + row_base
    key_row = jnp.where(key_row < 0, key_row + height, key_row)
    query_row = jnp.where(query_row < 0, query_row + height, query_row)
    rows_differ = (key_row >= height - WIN // 2) != (query_row >= height - WIN // 2)
    row_bad = key_row >= place[1 + sample]

    def attend(pair, _):
        key_col = (pair * 2 + window_at) * WIN + key_at % WIN - WIN // 2
        query_col = (pair * 2 + window_at) * WIN + query_at % WIN - WIN // 2
        key_col = jnp.where(key_col < 0, key_col + columns, key_col)
        query_col = jnp.where(query_col < 0, query_col + columns, query_col)
        cols_differ = (key_col >= columns - WIN // 2) != (query_col >= columns - WIN // 2)
        bad = row_bad | (key_col >= place[3 + sample])
        minus = jnp.where(rows_differ | cols_differ, MASKED / scale, 0.0) + jnp.where(
            bad, MASKED / scale, 0.0
        )
        for half in range(2):
            keys = spread_heads(pair_of(qkv_out, pair, 256 + 128 * half), mask[...])
            queries = blocks_of(qkv_out, pair, 128 * half)
            scores = dot_nt(keys, queries).reshape(4, 64, 128)
            scores = scores + (bias[256 * half : 256 * half + 256].reshape(4, 64, 128) + minus[None])
            top = jnp.max(scores, 1, keepdims=True)
            raised = jnp.exp2((scores - top) * (scale * LOG2E))
            probs = raised * (1.0 / jnp.sum(raised, 1, keepdims=True))
            probs = probs.reshape(256, 128).astype(BF)
            prob_out[pair, 256 * half : 256 * half + 256] = probs
        return 0

    def mix(pair, _):
        for half in range(2):
            probs = prob_out[pair, 256 * half : 256 * half + 256]
            values = spread_heads(pair_of(qkv_out, pair, 512 + 128 * half), mask[...])
            mixed = dot_tn(probs, values).astype(BF)
            mix_out[pl.ds(pair * 128, 64), 128 * half : 128 * half + 128] = mixed[:64, :128]
            mix_out[pl.ds(pair * 128 + 64, 64), 128 * half : 128 * half + 128] = mixed[64:, 128:]
        return 0

    lax.fori_loop(0, columns // 16, attend, 0, unroll=8)
    lax.fori_loop(0, columns // 16, mix, 0, unroll=8)


def near(*arrays):
    return [pltpu.with_memory_space_constraint(a, pltpu.VMEM) for a in arrays]


def const_spec(shape):
    return pl.BlockSpec(shape, lambda *_: (0,) * len(shape))


SMALL_COST = pl.CostEstimate(flops=10**6, bytes_accessed=10**4, transcendentals=0)


def params(mib):
    return pltpu.CompilerParams(vmem_limit_bytes=mib * MIB)


def far(*arrays):
    return [pltpu.with_memory_space_constraint(a, pltpu.HBM) for a in arrays]


SMEM_SPEC = pl.BlockSpec(memory_space=pltpu.SMEM)


def band_steps(samples, bands):
    def step_of(step):
        return step % samples, bands[0] + step // samples

    return step_of, samples * len(bands)


def attn_forward(place, above, own, gain, shift, weight, table, places, mask, height, scale):
    samples, grid_rows, columns, width = own.shape
    half = WIN // 2
    bands = grid_rows // WIN
    tokens = WIN * columns
    steps = samples * bands

    def step_of(step):
        return step // bands, step % bands

    def row_block(step):
        return (step, 0)

    total = steps * tokens
    return pl.pallas_call(
        functools.partial(attn_forward_body, height, scale, step_of),
        grid=(steps,),
        in_specs=[
            SMEM_SPEC,
            pl.BlockSpec((1, half, columns, width), lambda s: (step_of(s)[0], 0, 0, 0)),
            pl.BlockSpec(
                (1, half, columns, width),
                lambda s: (step_of(s)[0], jnp.maximum(2 * step_of(s)[1] - 1, 0), 0, 0),
            ),
            pl.BlockSpec(
                (1, half, columns, width), lambda s: (step_of(s)[0], 2 * step_of(s)[1], 0, 0)
            ),
            const_spec((1, width)),
            const_spec((1, width)),
            const_spec(weight.shape),
            const_spec(table.shape),
            const_spec(places.shape),
            const_spec(mask.shape),
        ],
        out_specs=[
            pl.BlockSpec((tokens, width), row_block),
            pl.BlockSpec((tokens, width), row_block),
            pl.BlockSpec((tokens, width), row_block),
            pl.BlockSpec((tokens, 128), row_block),
            pl.BlockSpec((tokens, 3 * width), row_block),
            pl.BlockSpec((columns // 16, 512, 128), lambda s: (s, 0, 0)),
            pl.BlockSpec((tokens, width), row_block),
        ],
        out_shape=[
            pltpu.VMEM((total, width), BF),
            pltpu.HBM((total, width), BF),
            pltpu.HBM((total, width), BF),
            pltpu.HBM((total, 128), F32),
            pltpu.HBM((total, 3 * width), BF),
            pltpu.HBM((total // 128, 512, 128), BF),
            pltpu.VMEM((total, width), BF),
        ],
        scratch_shapes=[
            pltpu.VMEM((columns // WIN, WIN, WIN, width), F32),
            pltpu.VMEM((512, 128), F32),
        ],
        compiler_params=params(24),
        cost_estimate=SMALL_COST,
        name="attn_forward",
    )(place, *far(above, own, own, gain, shift), *near(weight), *far(table, places, mask))


def gelu_parts(x):
    share = 0.5 + 0.5 * lax.erf(x * 0.7071067811865476)
    bell = jnp.exp2(x * x * (-0.5 * LOG2E))
    return x * share, share + x * (bell * 0.3989422804014327)


def ffn_forward_body(
    height, step_of, place, x_ref, mix, out_w, out_b, gain, shift, up_w, up_b, down_w, down_b,
    norm_out, xhat_out, rstd_out, act_out, slope_out, sum_out, first_rows, sums,
):
    sample, band = step_of(pl.program_id(0))
    columns = sum_out.shape[2]
    chunk = 256
    chunks = columns * WIN // chunk

    def attend_sum(k, _):
        tokens = pl.ds(k * chunk, chunk)
        first = x_ref[tokens].astype(F32) + dot(mix[tokens], out_w[...]) + out_b[...]
        sums[pl.ds(k * (chunk // 64), chunk // 64)] = first.reshape(chunk // 64, WIN, WIN, 256)
        xhat, rstd = norm_parts(first)
        norm_out[tokens] = (xhat * gain[...] + shift[...]).astype(BF)
        xhat_out[tokens] = xhat.astype(BF)
        rstd_out[tokens] = jnp.broadcast_to(rstd, (chunk, 128))
        return 0

    def raise_up(k, _):
        tokens = pl.ds(k * chunk, chunk)
        for f in range(0, 1024, 256):
            raised = dot(norm_out[tokens], up_w[:, f : f + 256]) + up_b[:, f : f + 256]
            act, slope = gelu_parts(raised)
            act_out[tokens, f : f + 256] = act.astype(BF)
            slope_out[tokens, f : f + 256] = slope.astype(BF)
        return 0

    def put_down(k, _):
        tokens = pl.ds(k * chunk, chunk)
        windows = pl.ds(k * (chunk // 64), chunk // 64)
        second = dot(act_out[tokens], down_w[...]) + down_b[...]
        sums[windows] += second.reshape(chunk // 64, WIN, WIN, 256)
        return 0

    lax.fori_loop(0, chunks, attend_sum, 0, unroll=True)
    lax.fori_loop(0, chunks, raise_up, 0, unroll=True)
    lax.fori_loop(0, chunks, put_down, 0, unroll=True)
    column = iota((columns, 1), 0)

    def rows_out(r, _):
        row = place[0] + band * WIN + r
        row = jnp.where(row < 0, row + height, row)
        limit = jnp.where(row < place[1 + sample], place[3 + sample], 0)
        back = pltpu.roll(sums[:, r].reshape(columns, 256), columns - WIN // 2, 0)
        sum_out[0, r] = jnp.where(column < limit, back, 0.0).astype(BF)
        return 0

    lax.fori_loop(0, WIN, rows_out, 0, unroll=True)

    @pl.when(band == 0)
    def _():
        first_rows[0] = sum_out[0, : WIN // 2 + 1]


def ffn_forward(place, x, mix, out_w, out_b, gain, shift, up_w, up_b, down_w, down_b, height, shape):
    samples, grid_rows, columns, width = shape
    bands = grid_rows // WIN
    tokens = WIN * columns
    steps = samples * bands
    hidden = up_w.shape[1]
    total = steps * tokens

    def step_of(step):
        return step // bands, step % bands

    def row_block(step):
        return (step, 0)

    rows = [width, width, 128, hidden, hidden]
    types = [BF, BF, F32, BF, BF]
    return pl.pallas_call(
        functools.partial(ffn_forward_body, height, step_of),
        grid=(steps,),
        in_specs=[SMEM_SPEC]
        + [pl.BlockSpec((tokens, width), row_block)] * 2
        + [const_spec(a.shape) for a in (out_w, out_b, gain, shift, up_w, up_b, down_w, down_b)],
        out_specs=[pl.BlockSpec((tokens, n), row_block) for n in rows]
        + [
            pl.BlockSpec((1, WIN, columns, width), lambda s: (*step_of(s), 0, 0)),
            pl.BlockSpec((1, WIN // 2 + 1, columns, width), lambda s: (step_of(s)[0], 0, 0, 0)),
        ],
        out_shape=[pltpu.HBM((total, n), t) for n, t in zip(rows, types)]
        + [
            pltpu.HBM(shape, BF),
            jax.ShapeDtypeStruct((samples, WIN // 2 + 1, columns, width), BF),
        ],
        scratch_shapes=[pltpu.VMEM((columns // WIN, WIN, WIN, width), F32)],
        compiler_params=params(32),
        cost_estimate=SMALL_COST,
        name="ffn_forward",
    )(
        place, *near(x, mix, out_w), *far(out_b, gain, shift), *near(up_w), *far(up_b), *near(down_w),
        *far(down_b),
    )


def column_sum(x):
    return jnp.sum(x, 0, keepdims=True)


def ffn_backward_step(
    height, step, sample, band, place, above, own, act, slope, normed, xhat_ref, rstd_ref, mix, conv_w,
    out_w, gain, up_w, down_w, first_out, mixed_out,
    taps, turned, branch, low, raised_s, attn, down_acc, up_acc, out_acc, vec,
):
    columns = own.shape[2]
    tokens = columns * WIN
    half = WIN // 2
    column = iota((columns, 1), 0)

    @pl.when(step == 0)
    def _():
        for ref in (down_acc, up_acc, out_acc, vec):
            ref[...] = jnp.zeros_like(ref)
        for k in range(9):
            at = 256 * (k % 3)
            turned[k // 3, :, at : at + 256] = conv_w[k, 0]

    start = place[0] + half
    not_first = start != 0
    lanes = (0, 256, 512)
    top = band == 0
    before = jnp.where(top, jnp.where(not_first, start, height), start + band * WIN) - half - 1

    def put_group(group):
        for k in range(half + 2):
            row = before + k if group == 0 else start + band * WIN + k - 1
            at = band * WIN + (group - 1) * half - 1 + k
            source = own[0, jnp.maximum(at, 0)]
            allowed = True
            if group == 0 and k <= half:
                source = jnp.where(top, above[0, k], source)
            elif group == 0:
                row = start + band * WIN
                allowed = ~top | not_first
            elif k == 0:
                source = jnp.where(top, above[0, ABOVE_LAST], source)
                allowed = ~top | not_first
            limit = row_limit(place, sample, row, allowed)
            put_taps(source, limit, taps, group * (half + 2) + k, lanes)

    put_group(0)
    for group in range(2):
        if group == 0:
            put_group(1)
        total = 0.0
        for a in range(3):
            at = group * (half + 2) + 2 - a
            piece = taps[at : at + half].reshape(half * columns, 768)
            total = total + dot_nt(piece, turned[a])
        for k in range(half):
            row = place[0] + band * WIN + group * half + k
            row = jnp.where(row < 0, row + height, row)
            limit = row_limit(place, sample, row)
            part = jnp.where(column < limit, total[k * columns : (k + 1) * columns], 0.0)
            part = pltpu.roll(part, half, 0)
            branch[:, group * half + k] = part.reshape(columns // WIN, WIN, 256)

    chunk = 256
    windows = chunk // 64
    for k in range(tokens // chunk):
        at = slice(k * chunk, (k + 1) * chunk)
        upper = branch[k * windows : (k + 1) * windows].reshape(chunk, 256)
        low[at] = upper.astype(BF)
        vec[0:1] += column_sum(upper.astype(BF).astype(F32))
    for k in range(tokens // chunk):
        at = slice(k * chunk, (k + 1) * chunk)
        for f in range(0, 1024, 256):
            wide = slice(f, f + 256)
            raised = (dot_nt(low[at], down_w[wide]) * slope[at, wide].astype(F32)).astype(BF)
            raised_s[at, wide] = raised
            row = 4 + f // 256
            vec[row : row + 1] += column_sum(raised.astype(F32))
    for k in range(tokens // chunk):
        at = slice(k * chunk, (k + 1) * chunk)
        dy = dot_nt(raised_s[at], up_w[...])
        xhat = xhat_ref[at].astype(F32)
        rstd = rstd_ref[at]
        rstd = jnp.concatenate([rstd, rstd], 1)
        upper = branch[k * windows : (k + 1) * windows].reshape(chunk, 256)
        first = upper + norm_back(dy, xhat, rstd, gain[...])
        first_out[at] = first
        attn[at] = first.astype(BF)
        vec[1:2] += column_sum(dy * xhat)
        vec[2:3] += column_sum(dy)
        vec[3:4] += column_sum(first.astype(BF).astype(F32))
    for k in range(tokens // chunk):
        at = slice(k * chunk, (k + 1) * chunk)
        mixed_out[at] = dot_nt(attn[at], out_w[...]).astype(BF)
    low_t = low[...].T
    normed_t = normed[...].T
    for f in range(0, 1024, 256):
        wide = slice(f, f + 256)
        down_acc[:, wide] += dot(low_t, act[:, wide])
        up_acc[:, wide] += dot(normed_t, raised_s[:, wide])
    out_acc[...] += dot(mix[...].T, attn[...])


def ffn_backward_end(down_out, up_out, out_out, vec_out, down_acc, up_acc, out_acc, vec):
    for f in range(0, 1024, 256):
        wide = slice(f, f + 256)
        down_out[wide] = down_acc[:, wide].T.astype(BF)
        up_out[:, wide] = up_acc[:, wide].astype(BF)
    out_out[...] = out_acc[...].astype(BF)
    vec_out[...] = vec[...].astype(BF)


def send_rows(core, batch, mine, other, down_rows, down_acc, out_acc, up_acc, qkv_acc, vectors):
    for f in range(0, 1024, 256):
        turned = down_acc[:, f : f + 256].T.reshape(8, 4, 8, 256)
        for k in range(4):
            piece = turned[:, k].reshape(64, 256)
            down_rows[f // 4 : f // 4 + 64, 256 * k : 256 * k + 256] = piece.astype(BF)
    count = 8 * batch
    wide_vectors = jnp.concatenate([vectors] * batch, 0).astype(BF)

    def put(target, k):
        for chip in range(256 // (2 * count)):
            rows = slice((2 * chip + k) * count, (2 * chip + k + 1) * count)
            to = slice(chip * count, (chip + 1) * count)
            at = 0
            for ref in (down_rows, out_acc, up_acc, qkv_acc):
                target[to, at : at + ref.shape[1]] = ref[rows].astype(BF)
                at += ref.shape[1]
            target[to, at:] = wide_vectors

    for k in range(2):

        @pl.when(core == k)
        def _():
            put(mine, k)
            put(other, 1 - k)


def backward_body(height, scale, step_of, batch, *refs):
    place, above, own, *refs = refs
    ffn_rows, refs = refs[:6], refs[6:]
    attn_rows, refs = refs[:5], refs[5:]
    ffn_consts, refs = refs[:5], refs[5:]
    (weight, gain, mask, conv_vec, places), refs = refs[:5], refs[5:]
    input_out, up_out, *refs = refs
    outs, refs = (refs[:2], refs[2:]) if batch else (refs[:6], refs[6:])
    ffn_scratch, (first, mixed, qkv_acc, table_acc, vec_acc, grads, score_grads, sums, down_rows) = (
        refs[:10], refs[10:],
    )
    step = pl.program_id(0)
    sample, band = step_of(step)
    columns = input_out.shape[2]
    half = WIN // 2

    @pl.when(step == 0)
    def _():
        for ref in (qkv_acc, table_acc, vec_acc):
            ref[...] = jnp.zeros_like(ref)

    ffn_backward_step(
        height, step, sample, band, place, above, own, *ffn_rows, *ffn_consts, first, mixed,
        *ffn_scratch,
    )
    qkv, prob, normed, xhat_ref, rstd_ref = attn_rows
    attn_backward_step(
        scale, mixed, qkv, prob, normed, xhat_ref, rstd_ref, first, weight, gain, mask,
        qkv_acc, table_acc, vec_acc, grads, score_grads, sums,
    )

    def row_out(r):
        return pltpu.roll(sums[:, r].reshape(columns, 256), columns - half, 0)

    @pl.when(band == 0)
    def _():
        for r in range(half):
            up_out[0, r] = row_out(r).astype(BF)
            input_out[0, r] = row_out(half + r)

    @pl.when(band > 0)
    def _():
        for r in range(WIN):
            input_out[0, band * WIN - half + r] = row_out(r)

    @pl.when(step == pl.num_programs(0) - 1)
    def _():
        table = collect_bias(table_acc[...], places[...])
        rest = jnp.concatenate([vec_acc[0:2], conv_vec[0:1], jnp.zeros((5, 256), F32)], 0)
        vectors = jnp.concatenate([table, rest], 1)
        down_acc, up_acc, out_acc, vec = ffn_scratch[6:]
        if batch:
            vectors = jnp.concatenate([vec[...], vectors], 1)
            send_rows(
                place[place.shape[0] - 1], batch, *outs, down_rows, down_acc, out_acc, up_acc, qkv_acc,
                vectors,
            )
            return
        *ffn_outs, qkv_out, vec_out = outs
        ffn_backward_end(*ffn_outs, down_acc, up_acc, out_acc, vec)
        for f in range(0, 768, 256):
            qkv_out[:, f : f + 256] = qkv_acc[:, f : f + 256].astype(BF)
        vec_out[...] = vectors.astype(BF)


def attn_backward_step(
    scale, mixed, qkv, prob, normed, xhat_ref, rstd_ref, first, weight, gain, mask,
    qkv_acc, table_acc, vec_acc, grads, score_grads, sums,
):
    tokens = qkv.shape[0]
    columns = tokens // WIN

    def attend(pair, _):
        head_at = mask[...]
        for half in range(2):
            lanes = slice(256 * half, 256 * half + 256)
            low = prob[pair, lanes]
            mixed_blocks = blocks_of(mixed, pair, 128 * half)
            values = spread_heads(pair_of(qkv, pair, 512 + 128 * half), head_at)
            prob_grad = dot_nt(values, mixed_blocks).reshape(4, 64, 128)
            probs = low.astype(F32).reshape(4, 64, 128)
            shared = jnp.sum(prob_grad * probs, 1, keepdims=True)
            score_grad = (probs * (prob_grad - shared)).astype(BF).reshape(256, 128)
            table_acc[lanes] += score_grad.astype(F32)
            score_grads[pair, lanes] = score_grad
        return 0

    def project(pair, _):
        head_at = mask[...]
        for half in range(2):
            lanes = slice(256 * half, 256 * half + 256)
            low = prob[pair, lanes]
            mixed_blocks = blocks_of(mixed, pair, 128 * half)
            score_grad = score_grads[pair, lanes]
            keys = spread_heads(pair_of(qkv, pair, 256 + 128 * half), head_at)
            queries = blocks_of(qkv, pair, 128 * half)
            query_grad = (dot_tn(score_grad, keys) * scale).astype(BF)
            out = slice(128 * half, 128 * half + 128)
            grads[pl.ds(pair * 128, 64), out] = query_grad[:64, :128]
            grads[pl.ds(pair * 128 + 64, 64), out] = query_grad[64:, 128:]
            wide = head_at.astype(F32)
            key_grad = (dot(score_grad, queries) * wide).reshape(4, 64, 256)
            key_grad = (jnp.sum(key_grad, 0) * scale).astype(BF)
            out = slice(256 + 128 * half, 256 + 128 * half + 128)
            grads[pl.ds(pair * 128, 64), out] = key_grad[:, :128]
            grads[pl.ds(pair * 128 + 64, 64), out] = key_grad[:, 128:]
            value_grad = (dot(low, mixed_blocks) * wide).reshape(4, 64, 256)
            value_grad = jnp.sum(value_grad, 0).astype(BF)
            out = slice(512 + 128 * half, 512 + 128 * half + 128)
            grads[pl.ds(pair * 128, 64), out] = value_grad[:, :128]
            grads[pl.ds(pair * 128 + 64, 64), out] = value_grad[:, 128:]
        return 0

    lax.fori_loop(0, columns // 16, attend, 0, unroll=8)
    lax.fori_loop(0, columns // 16, project, 0, unroll=8)
    for f in range(0, 768, 256):
        qkv_acc[:, f : f + 256] += dot_tn(normed[...], grads[:, f : f + 256])

    def part(k, _):
        at = pl.ds(k * 256, 256)
        dy = dot_nt(grads[at], weight[...])
        xhat = xhat_ref[at].astype(F32)
        rstd = rstd_ref[at]
        rstd = jnp.concatenate([rstd, rstd], 1)
        total = first[at] + norm_back(dy, xhat, rstd, gain[...])
        sums[pl.ds(k * 4, 4)] = total.reshape(4, WIN, WIN, 256)
        vec_acc[0:1] += column_sum(dy * xhat)
        vec_acc[1:2] += column_sum(dy)
        return 0

    lax.fori_loop(0, tokens // 256, part, 0, unroll=True)


def backward(place, above, own, ffn_rows, attn_rows, ffn_consts, attn_consts, height, scale, batch):
    samples, grid_rows, columns, width = own.shape
    bands = grid_rows // WIN
    tokens = WIN * columns
    steps = samples * bands
    hidden = ffn_rows[0].shape[1]
    half = WIN // 2

    def step_of(step):
        return step // bands, step % bands

    def row_block(step):
        return (step, 0)

    def sample_block(step):
        return (step_of(step)[0], 0, 0, 0)

    in_specs = [
        SMEM_SPEC,
        pl.BlockSpec((1,) + above.shape[1:], sample_block),
        pl.BlockSpec((1,) + own.shape[1:], sample_block),
    ]
    in_specs += [pl.BlockSpec((tokens, a.shape[1]), row_block) for a in (*ffn_rows, *attn_rows)]
    in_specs[10] = pl.BlockSpec((columns // 16, 512, 128), lambda s: (s, 0, 0))
    in_specs += [pl.BlockSpec((9, 1, width, width), lambda s: (0, 0, 0, 0))]
    in_specs += [const_spec(a.shape) for a in (*ffn_consts[1:], *attn_consts)]
    outs = [(own.shape, F32), ((samples, half, columns, width), BF)]
    if batch:
        outs += [((width // 2, 2 * hidden + 7 * width), BF)] * 2
    else:
        outs += [
            ((hidden, width), BF), ((width, hidden), BF), ((width, width), BF), ((8, width), BF),
            ((width, 3 * width), BF), ((8, 2 * width), BF),
        ]
    out_specs = [const_spec(a) for a, _ in outs]
    out_specs[0] = pl.BlockSpec((1,) + own.shape[1:], sample_block)
    out_specs[1] = pl.BlockSpec((1, half, columns, width), sample_block)
    return pl.pallas_call(
        functools.partial(backward_body, height, scale, step_of, batch),
        grid=(steps,),
        in_specs=in_specs,
        out_specs=out_specs,
        out_shape=[pltpu.HBM(a, t) for a, t in outs],
        scratch_shapes=[
            pltpu.VMEM((WIN + 4, columns, 3 * width), BF),
            pltpu.VMEM((3, width, 3 * width), BF),
            pltpu.VMEM((columns // WIN, WIN, WIN, width), F32),
            pltpu.VMEM((tokens, width), BF),
            pltpu.VMEM((tokens, hidden), BF),
            pltpu.VMEM((tokens, width), BF),
            pltpu.VMEM((width, hidden), F32),
            pltpu.VMEM((width, hidden), F32),
            pltpu.VMEM((width, width), F32),
            pltpu.VMEM((8, width), F32),
            pltpu.VMEM((tokens, width), F32),
            pltpu.VMEM((tokens, width), BF),
            pltpu.VMEM((width, 3 * width), F32),
            pltpu.VMEM((512, 128), F32),
            pltpu.VMEM((8, width), F32),
            pltpu.VMEM((tokens, 3 * width), BF),
            pltpu.VMEM((columns // 16, 512, 128), BF),
            pltpu.VMEM((columns // WIN, WIN, WIN, width), F32),
            pltpu.VMEM((width, hidden), BF),
        ],
        compiler_params=params(BACK_MIB),
        cost_estimate=pl.CostEstimate(
            flops=4 * 10**10, bytes_accessed=10**7, transcendentals=0
        ),
        name="backward",
    )(
        place, *far(above, own, *ffn_rows, *attn_rows, *ffn_consts, *attn_consts),
    )


def shifted(row, by):
    columns = row.shape[0]
    moved = pltpu.roll(row, by % columns, 0)
    place = iota((8, 1), 0)
    if by == 1:
        return jnp.concatenate([jnp.where(place == 0, 0.0, moved[:8]), moved[8:]], 0)
    return jnp.concatenate([moved[:-8], jnp.where(place == 7, 0.0, moved[-8:])], 0)


def pack_near_body(qkv, out_w, up, down, near):
    rows = qkv.shape[0]
    at = 0
    for ref in (qkv, out_w, up):
        near[:, at : at + ref.shape[1]] = ref[...].astype(BF)
        at += ref.shape[1]
    for k in range(down.shape[0] // rows):
        near[:, at : at + down.shape[1]] = down[k * rows : (k + 1) * rows].astype(BF)
        at += down.shape[1]


def pack_near(qkv, out_w, up, down):
    rows = qkv.shape[0]
    lanes = (qkv.size + out_w.size + up.size + down.size) // rows
    return pl.pallas_call(
        pack_near_body,
        out_shape=jax.ShapeDtypeStruct((rows, lanes), BF),
        compiler_params=params(16),
        cost_estimate=SMALL_COST,
        name="pack_near",
    )(*far(qkv, out_w, up, down))


def unpack_near_body(order, held, qkv, out_w, up, down):
    devices, rows, _ = held.shape
    count = max(16 // rows, 1)

    def some(k, _):
        pieces = [held[order[k * count + n]] for n in range(count)]
        at = 0
        place = pl.ds(pl.multiple_of(k * count * rows, count * rows), count * rows)
        for ref in (qkv, out_w, up):
            lanes = slice(at, at + ref.shape[1])
            ref[place] = jnp.concatenate([piece[:, lanes] for piece in pieces], 0)
            at = lanes.stop
        width = down.shape[1]
        parts = down.shape[0] // (devices * rows)
        tall = [
            piece[:, at + n * width : at + (n + 1) * width] for piece in pieces for n in range(parts)
        ]
        size = count * rows * parts
        down[pl.ds(pl.multiple_of(k * size, size), size)] = jnp.concatenate(tall, 0)
        return 0

    lax.fori_loop(0, devices // count, some, 0, unroll=4)


def unpack_near(order, held, weights):
    devices = held.shape[0]
    return pl.pallas_call(
        unpack_near_body,
        in_specs=[SMEM_SPEC, pl.BlockSpec(memory_space=pltpu.VMEM)],
        out_shape=[pltpu.VMEM((devices * w.shape[0], w.shape[1]), BF) for w in weights],
        compiler_params=params(24),
        cost_estimate=SMALL_COST,
        name="unpack_near",
    )(order, held)


def last_sums_body(parts, down, out_w, up, qkv, *vectors):
    count, rows, lanes = parts.shape
    total = parts[0].astype(F32)
    for k in range(1, count):
        total = total + parts[k].astype(F32)
    width = down.shape[1]
    for k in range(down.shape[0] // rows):
        down[k * rows : (k + 1) * rows] = total[:, k * width : (k + 1) * width]
    at = down.size // rows
    for ref in (out_w, up, qkv):
        ref[...] = total[:, at : at + ref.shape[1]]
        at += ref.shape[1]

    def vector(row, group):
        row, lane = divmod((row * 3 + group) * width, lanes - at)
        return total[row : row + 1, at + lane : at + lane + width]

    singles, (up_bias, table), more = vectors[:4], vectors[4:6], vectors[6:]
    for k, ref in enumerate(singles):
        ref[...] = vector(k, 0)
    for k in range(4):
        up_bias[:, k * width : (k + 1) * width] = vector(4 + k, 0)
    for k in range(8):
        table[k : k + 1] = vector(k, 1)
    for k, ref in enumerate(more):
        ref[...] = vector(k, 2)


def last_sums(parts, down, rest):
    width = down[1]
    vectors = [(1, width)] * 4 + [(1, 4 * width), (8, width)] + [(1, width)] * 3
    shapes = (down, *rest, *vectors)
    return pl.pallas_call(
        last_sums_body,
        out_shape=[jax.ShapeDtypeStruct(a, F32) for a in shapes],
        compiler_params=params(24),
        cost_estimate=SMALL_COST,
        name="last_sums",
    )(parts)


def sum_body(parts, out):
    total = parts[0].astype(F32)
    for k in range(1, parts.shape[0]):
        total = total + parts[k].astype(F32)
    out[...] = total


def sum_parts(parts):
    return pl.pallas_call(
        sum_body,
        out_shape=jax.ShapeDtypeStruct(parts.shape[1:], F32),
        compiler_params=params(16),
        cost_estimate=SMALL_COST,
        name="sum_parts",
    )(parts)


def copies_body(x, out):
    low = x[...].astype(BF)
    for k in range(out.shape[0]):
        out[k] = low


def make_copies(x, count):
    return pl.pallas_call(
        copies_body,
        out_shape=jax.ShapeDtypeStruct((count,) + x.shape, BF),
        compiler_params=params(16),
        cost_estimate=SMALL_COST,
        name="make_copies",
    )(*far(x))


def row_limit(place, sample, row, allowed=True):
    return jnp.where((row < place[1 + sample]) & allowed, place[3 + sample], 0)


def put_taps(row, limit, target, at, lanes):
    column = iota((row.shape[0], 1), 0)
    wide = jnp.where(column < limit, row.astype(F32), 0.0)
    target[at, :, lanes[0] : lanes[0] + 256] = shifted(wide, -1).astype(BF)
    target[at, :, lanes[1] : lanes[1] + 256] = wide.astype(BF)
    target[at, :, lanes[2] : lanes[2] + 256] = shifted(wide, 1).astype(BF)


ABOVE_LAST = WIN // 2
ABOVE_HIDDEN = WIN // 2 + 1


def own_taps(height, place, above, own, below, taps, at):
    sample = pl.program_id(0)
    rows = own.shape[1]
    start = place[0] + WIN // 2

    def put(r):
        allowed = True
        if r == 0:
            source, allowed = above[0, ABOVE_LAST], start != 0
        elif r <= rows:
            source = own[0, r - 1]
        else:
            source, allowed = below[0, 0], start + rows != height
        limit = row_limit(place, sample, start + r - 1, allowed)
        put_taps(source, limit, taps, at + r, (0, 256, 512))

    return put


def conv_weight_body(
    height, place, above, own, below, sums, hidden, out, vec, taps, held, acc, acc_hidden
):
    sample = pl.program_id(0)

    @pl.when(sample == 0)
    def _():
        for ref in (acc, acc_hidden, vec):
            ref[...] = jnp.zeros_like(ref)

    rows, columns = own.shape[1:3]
    half = WIN // 2
    column = iota((columns, 1), 0)
    start = place[0] + half
    not_first = start != 0

    before = jnp.where(not_first, start, height) - half - 1
    put = own_taps(height, place, above, own, below, taps, half + 2)
    for r in range(half + 1):
        limit = row_limit(place, sample, before + r)
        put_taps(above[0, r], limit, taps, r, (0, 256, 512))
    limit = row_limit(place, sample, start, not_first)
    put_taps(own[0, 0], limit, taps, half + 1, (0, 256, 512))

    def add(source, first, acc):
        count = source.shape[0]
        turned = source.reshape(count * columns, 256).T
        for a in range(3):
            piece = taps[first + 2 - a : first + 2 - a + count].reshape(count * columns, 768)
            acc[a] += dot(turned, piece)

    put(0)
    put(1)
    add(sums[0, :half], 0, acc)
    step = 8
    for r in range(0, rows, step):
        for k in range(r, r + step):
            put(k + 2)
            limit = row_limit(place, sample, start + k)
            held[k] = jnp.where(column < limit, hidden[0, k].astype(F32), 0.0).astype(BF)
            vec[0:1] += jnp.sum(taps[half + 3 + k, :, 256:512].astype(F32), 0, keepdims=True)
        add(held[r : r + step], half + 2 + r, acc_hidden)
        last = min(r + step, rows - half)
        add(sums[0, half + r : half + last], half + 2 + r, acc)

    @pl.when(sample == pl.num_programs(0) - 1)
    def _():
        for k in range(9):
            at = 256 * (k % 3)
            out[k, 0] = acc[k // 3, :, at : at + 256].astype(BF)
            out[k, 1] = acc_hidden[k // 3, :, at : at + 256].astype(BF)


def field_spec(a):
    return pl.BlockSpec((1,) + a.shape[1:], lambda s: (s, 0, 0, 0))


def conv_call(
    body, name, mib, place, fields, consts, height, out_specs, out_shape, scratch, cost=None
):
    return pl.pallas_call(
        functools.partial(body, height),
        grid=(fields[0][1].shape[0],),
        in_specs=[SMEM_SPEC] + [s for s, _ in fields] + [s for s, _ in consts],
        out_specs=out_specs,
        out_shape=out_shape,
        scratch_shapes=scratch,
        compiler_params=params(mib),
        cost_estimate=cost or SMALL_COST,
        name=name,
    )(place, *[a for _, a in fields], *far(*[a for _, a in consts]))


def whole(a):
    return field_spec(a), far(a)[0]


def conv_weight(place, grads, sums, hidden, height):
    _, rows, columns, width = sums.shape
    shape = (9, 2, width, width)
    acc = pltpu.VMEM((3, width, 3 * width), F32)
    return conv_call(
        conv_weight_body, "conv_weight", 34, place, [*map(whole, grads), whole(sums), whole(hidden)], (),
        height, [const_spec(shape), const_spec((8, width))],
        [jax.ShapeDtypeStruct(shape, BF), jax.ShapeDtypeStruct((8, width), F32)],
        [
            pltpu.VMEM((rows + WIN, columns, 3 * width), BF),
            pltpu.VMEM((rows, columns, width), BF),
            acc,
            acc,
        ],
        pl.CostEstimate(flops=2 * 10**10, bytes_accessed=10**7, transcendentals=0),
    )


def conv_data_body(height, place, above, own, below, weight, out, taps, turned):
    sample = pl.program_id(0)
    columns = own.shape[2]
    column = iota((columns, 1), 0)

    @pl.when(sample == 0)
    def _():
        for k in range(9):
            at = 256 * (k % 3)
            turned[k // 3, :, at : at + 256] = weight[k, 0]

    put = own_taps(height, place, above, own, below, taps, 0)
    for r in range(2):
        put(r)
    for r in range(0, own.shape[1], 4):
        for k in range(r + 2, r + 6):
            put(k)
        total = 0.0
        for a in range(3):
            piece = taps[r + 2 - a : r + 6 - a].reshape(4 * columns, 768)
            total = total + dot_nt(piece, turned[a])
        for k in range(4):
            limit = row_limit(place, sample, place[0] + WIN // 2 + r + k)
            part = total[k * columns : (k + 1) * columns]
            out[0, r + k] = jnp.where(column < limit, part, 0.0)


def conv_data(place, grads, weight, height):
    own = grads[1]
    width = own.shape[-1]
    weight_spec = pl.BlockSpec((9, 1, width, width), lambda s: (0, 1, 0, 0))
    return conv_call(
        conv_data_body, "conv_data", 28, place, [whole(a) for a in grads], ((weight_spec, weight),),
        height, field_spec(own), jax.ShapeDtypeStruct(own.shape, F32),
        [
            pltpu.VMEM((own.shape[1] + 2, own.shape[2], 3 * width), BF),
            pltpu.VMEM((3, width, 3 * width), BF),
        ],
        pl.CostEstimate(flops=10**10, bytes_accessed=10**7, transcendentals=0),
    )


def conv_forward_body(
    height, place, sums, sums_below, above, hidden, below, weight, bias, out, taps
):
    sample = pl.program_id(0)
    rows, columns = out.shape[1:3]
    column = iota((columns, 1), 0)
    half = WIN // 2
    start = place[0] + half
    not_first, not_last = start != 0, start + rows != height

    def put(r):
        allowed = True
        if r == 0:
            first, second, allowed = sums[0, half - 1], above[0, ABOVE_HIDDEN], not_first
        elif r <= rows:
            first, second = None, hidden[0, r - 1]
            if r <= rows - half:
                first = sums[0, half + r - 1]
            else:
                first = sums_below[0, r - 1 - rows + half]
        else:
            first, second, allowed = sums_below[0, half], below[0, 1], not_last
        limit = row_limit(place, sample, start + r - 1, allowed)
        put_taps(first, limit, taps, r, (1024, 512, 0))
        put_taps(second, limit, taps, r, (1280, 768, 256))

    for r in range(2):
        put(r)
    for r in range(0, rows, 4):
        for k in range(r + 2, r + 6):
            put(k)
        total = bias[...]
        for a in range(3):
            piece = taps[r + a : r + a + 4].reshape(4 * columns, 1536)
            total = total + dot(piece, weight[a * 1536 : (a + 1) * 1536])
        for k in range(4):
            limit = row_limit(place, sample, start + r + k)
            part = total[k * columns : (k + 1) * columns]
            out[0, r + k] = jnp.where(column < limit, part, 0.0).astype(BF)


def conv_forward(place, sums, sums_below, hidden, weight, bias, height):
    samples, rows, columns, width = sums.shape
    fields = far(sums, sums_below, *hidden)
    return pl.pallas_call(
        functools.partial(conv_forward_body, height),
        grid=(samples,),
        in_specs=[SMEM_SPEC]
        + [field_spec(a) for a in fields]
        + [const_spec(weight.shape), const_spec(bias.shape)],
        out_specs=field_spec(sums),
        out_shape=jax.ShapeDtypeStruct(sums.shape, BF),
        scratch_shapes=[pltpu.VMEM((rows + 2, columns, 6 * width), BF)],
        compiler_params=params(32),
        cost_estimate=SMALL_COST,
        name="conv_forward",
    )(place, *fields, *far(weight, bias))


def shards(
    layer_input,
    hidden_state,
    crop_rows,
    crop_cols,
    first_gain,
    first_shift,
    qkv_weight,
    bias_table,
    output_weight,
    output_bias,
    second_gain,
    second_shift,
    up_weight,
    up_bias,
    down_weight,
    down_bias,
    conv_weight_in,
    conv_bias,
    cotangent,
):
    samples, grid_rows, columns, width = layer_input.shape
    shape = layer_input.shape
    heads = bias_table.shape[1]
    scale = float((width // heads) ** (-0.5))
    half = WIN // 2
    devices = device_count()
    row_devices = lax.axis_size("rows")
    height = grid_rows * row_devices
    row_place = lax.axis_index("rows")
    row_start = row_place * grid_rows
    place = jnp.concatenate(
        [(row_start - half)[None].astype(jnp.int32), crop_rows, crop_cols, (row_place % 2)[None]]
    ).astype(jnp.int32)

    hidden_width = up_weight.shape[1]

    def vec(v):
        return v.reshape(1, -1)

    input_above = ring(layer_input[:, grid_rows - half :], 1)
    rows_out, rows_down = output_weight.shape[0], down_weight.shape[0]
    weights = pack_near(qkv_weight, output_weight, up_weight, down_weight)
    offsets = bias_table.shape[0]

    def beside(held):
        grad, hidden, weight, table = after(
            (cotangent, hidden_state, conv_weight_in, bias_table), held
        )
        halo_above = jnp.concatenate([grad[:, grid_rows - half - 1 :], hidden[:, grid_rows - 1 :]], 1)
        halo_below = jnp.concatenate([grad[:, :1], hidden[:, :1]], 1)
        table = jnp.pad(table.T, ((0, 0), (0, 256 - offsets)))
        return halo_above, halo_below, make_copies(weight, devices), table, input_above, place

    held, order, (halo_above, halo_below, conv_copies, table, *_) = gather_steps(weights, beside)
    halo_above, halo_below, conv_copies = after((halo_above, halo_below, conv_copies), held)
    halo_above, halo_below = ring(halo_above, 1), ring(halo_below, -1)
    grads = (halo_above, cotangent, halo_below)
    conv_full = gather_copies(conv_copies).reshape(-1, width)

    qkv_full, output_full, up_full, down_full = unpack_near(
        order, held, (qkv_weight, output_weight, up_weight, down_weight)
    )
    mask = jnp.asarray(head_mask(), BF)

    x, normed, xhat, rstd, qkv, prob, mix = attn_forward(
        place, input_above, layer_input, vec(first_gain), vec(first_shift), qkv_full, table,
        jnp.asarray(offset_places(False), BF), mask, height, scale,
    )
    normed_2, xhat_2, rstd_2, act, slope, sums, sums_first = ffn_forward(
        place, x, mix, output_full, vec(output_bias), vec(second_gain), vec(second_shift),
        up_full, vec(up_bias), down_full, vec(down_bias), height, shape,
    )
    conv_local, conv_bias_part = conv_weight(place, grads, sums, hidden_state, height)
    conv_local, exchange = scatter_pairs(conv_local.reshape(devices, -1, width))
    conv_all = exchange(conv_local)
    sums_below = ring(after(sums_first, conv_local), -1)
    conv_blocks = after(conv_full.reshape(9, 2, width, width), conv_local)
    input_grad, input_up, *last_parts = backward(
        place, halo_above, cotangent,
        (act, slope, normed_2, xhat_2, rstd_2, mix),
        (qkv, prob, normed, xhat, rstd),
        (conv_blocks, output_full, vec(second_gain), up_full, down_full),
        (
            qkv_full, vec(first_gain), mask, conv_bias_part,
            jnp.asarray(offset_places(True), BF).T,
        ),
        height, scale, lax.axis_size("batch") if rows_out == 8 else 0,
    )
    last_parts = after(tuple(last_parts), sums_below)
    if rows_out == 8:
        last_local, exchange = add_pairs(*(a.reshape(-1, rows_out, a.shape[1]) for a in last_parts))
    else:
        down_acc, up_acc, out_acc, vec_ffn, qkv_acc, vec_attn = last_parts
        down_local = down_acc.reshape(devices, -1, rows_out, width).transpose(0, 2, 1, 3)
        parts = [
            down_local.reshape(devices, rows_out, -1),
            *(a.reshape(devices, rows_out, -1) for a in (out_acc, up_acc, qkv_acc)),
        ]
        last_local, exchange = scatter_pairs(
            with_vectors(parts, jnp.concatenate([vec_ffn, vec_attn], 1))
        )
    last_all = exchange(last_local)
    input_from_below = ring(after(input_up, last_local), -1)
    hidden_grad = conv_data(after(place, last_local), grads, conv_blocks, height)
    layer_output = conv_forward(
        after(place, hidden_grad), sums, sums_below, (halo_above, hidden_state, halo_below),
        conv_full, vec(conv_bias), height,
    )

    input_grad = lax.dynamic_update_slice(
        after(input_grad, layer_output), input_from_below.astype(F32), (0, grid_rows - half, 0, 0)
    )

    conv_weight_grad = sum_parts(conv_all)
    down_weight_grad, output_weight_grad, up_weight_grad, qkv_weight_grad, *vectors = last_sums(
        last_all,
        (rows_down, width),
        [(rows_out, width), (rows_out, hidden_width), (rows_out, 3 * width)],
    )
    bias_table_grad = vectors.pop(5)[:, :offsets][:, ::-1].T
    (
        down_bias_grad, second_gain_grad, second_shift_grad, output_bias_grad, up_bias_grad,
        first_gain_grad, first_shift_grad, conv_bias_grad,
    ) = (v.reshape(-1) for v in vectors)
    return (
        layer_output,
        input_grad,
        hidden_grad,
        first_gain_grad,
        first_shift_grad,
        qkv_weight_grad,
        bias_table_grad,
        output_weight_grad,
        output_bias_grad,
        second_gain_grad,
        second_shift_grad,
        up_weight_grad,
        up_bias_grad,
        down_weight_grad,
        down_bias_grad,
        conv_weight_grad,
        conv_bias_grad,
    )


def solution(mesh):
    field = P("batch", "rows", None, None)
    weight = P(AXES, None)
    in_specs = (
        field, field, P("batch"), P("batch"), P(), P(), weight, P(), weight, P(), P(), P(),
        weight, P(), weight, P(), weight, P(), field,
    )
    out_specs = (
        field, field, field, P(), P(), weight, P(), weight, P(), P(), P(), weight, P(), weight,
        P(), weight, P(),
    )
    return jax.shard_map(shards, mesh=mesh, in_specs=in_specs, out_specs=out_specs, check_vma=False)
```

```python
import functools

import jax
import jax.numpy as jnp
import numpy as np
from jax import lax
from jax.experimental import pallas as pl
from jax.experimental.pallas import tpu as pltpu
from jax.sharding import PartitionSpec as P

WIN = 8
EPSILON = 1e-05
MASKED = -100.0
HIGHEST = lax.Precision.HIGHEST
AXES = ("rows", "batch")
BF = jnp.bfloat16
F32 = jnp.float32
MIB = 1024 * 1024
BACK_MIB = 54
LOG2E = 1.4426950408889634


def dot(left, right):
    return jnp.dot(left, right, preferred_element_type=F32)


def dot_nt(left, right):
    return lax.dot_general(left, right, (((1,), (1,)), ((), ())), preferred_element_type=F32)


def dot_tn(left, right):
    return lax.dot_general(left, right, (((0,), (0,)), ((), ())), preferred_element_type=F32)


def iota(shape, dim):
    return lax.broadcasted_iota(jnp.int32, shape, dim)


def device_index():
    return lax.axis_index("rows") * lax.axis_size("batch") + lax.axis_index("batch")


def device_count():
    return lax.axis_size("rows") * lax.axis_size("batch")


def after(x, *others):
    return lax.optimization_barrier((x, *others))[0]


def bit_groups():
    batch, rows = lax.axis_size("batch"), lax.axis_size("rows")
    batch_bits = [1 << k for k in range(batch.bit_length() - 1)]
    row_bits = [batch << k for k in range(rows.bit_length() - 1)]
    chips = row_bits[1:]
    groups = [batch_bits[k : k + 2] for k in range(0, len(batch_bits), 2)]
    groups += [chips[k : k + 2] for k in range(0, len(chips), 2)]
    return groups + [row_bits[:1]]


def gather_steps(x, beside):
    devices = device_count()
    held = x[None]
    places = [0]
    groups = bit_groups()
    for k, group in enumerate(groups):
        masks = [0]
        for bit in group:
            masks = masks + [m | bit for m in masks]
        if k == 1:
            other = beside(held)
        if k == len(groups) - 1:
            held = after(held, *other)
        pieces = [held]
        for mask in masks[1:]:
            pieces.append(lax.ppermute(held, AXES, [(i, i ^ mask) for i in range(devices)]))
        held = jnp.concatenate(pieces, 0)
        places = [p ^ m for m in masks for p in places]
    order = np.zeros(devices, np.int32)
    for place, mask in enumerate(places):
        order[mask] = place
    return held, jnp.asarray(order)[jnp.arange(devices) ^ device_index()], other


def scatter_pairs(x):
    rows, batch = lax.axis_size("rows"), lax.axis_size("batch")
    core = lax.axis_index("rows") % 2
    by_core = x.reshape((rows // 2, 2, batch) + x.shape[1:])
    mine = lax.dynamic_index_in_dim(by_core, core, 1, False)
    other = lax.dynamic_index_in_dim(by_core, 1 - core, 1, False)
    return add_pairs(*(a.reshape((-1,) + x.shape[1:]) for a in (mine, other)))


def add_pairs(mine, other):
    rows, batch = lax.axis_size("rows"), lax.axis_size("batch")
    other = lax.ppermute(other, "rows", [(i, i ^ 1) for i in range(rows)])
    pairs = (mine.astype(F32) + other.astype(F32)).astype(BF)
    groups = [
        [(2 * chip + k) * batch + b for chip in range(rows // 2) for b in range(batch)]
        for k in range(2)
    ]
    return pairs, lambda a: lax.all_to_all(a, AXES, 0, 0, axis_index_groups=groups, tiled=True)


def gather_copies(copies):
    return lax.all_to_all(copies, AXES, 0, 0, tiled=True)


def with_vectors(parts, vectors):
    rows = parts[0].shape[1]
    flat = vectors.reshape(1, rows, -1)
    flat = jnp.broadcast_to(flat, (parts[0].shape[0],) + flat.shape[1:])
    return jnp.concatenate(list(parts) + [flat], 2)


def ring(x, by):
    devices = lax.axis_size("rows")
    return lax.ppermute(x, "rows", [(i, (i + by) % devices) for i in range(devices)])


def norm_parts(x):
    centred = x - jnp.mean(x, -1, keepdims=True)
    rstd = lax.rsqrt(jnp.mean(centred * centred, -1, keepdims=True) + EPSILON)
    return centred * rstd, rstd


def norm_back(dy, xhat, rstd, gain):
    scaled = dy * gain
    first = jnp.mean(scaled, -1, keepdims=True)
    second = jnp.mean(scaled * xhat, -1, keepdims=True)
    return (scaled - first - xhat * second) * rstd


def head_mask():
    rows, lanes = np.arange(256)[:, None], np.arange(256)[None, :]
    return (rows // 64 == (lanes % 128) // 32).astype(np.float32)


def pair_of(ref, pair, column):
    first = ref[pl.ds(pair * 128, 64), column : column + 128]
    second = ref[pl.ds(pair * 128 + 64, 64), column : column + 128]
    return jnp.concatenate([first, second], 1)


def blocks_of(ref, pair, column):
    first = ref[pl.ds(pair * 128, 64), column : column + 128]
    second = ref[pl.ds(pair * 128 + 64, 64), column : column + 128]
    nothing = jnp.zeros_like(first)
    return jnp.concatenate(
        [jnp.concatenate([first, nothing], 1), jnp.concatenate([nothing, second], 1)], 0
    )


def spread_heads(pair, mask):
    return jnp.concatenate([pair] * 4, 0) * mask


def offset_places(turned):
    rows, lanes = np.arange(256)[:, None], np.arange(128)[None, :] % 64
    row, col = lanes // WIN, lanes % WIN
    if turned:
        row, col = WIN - 1 - row, WIN - 1 - col
    return (rows == row * (2 * WIN - 1) + col).astype(np.float32)


def three_parts(x):
    high = x.astype(BF)
    rest = x - high.astype(F32)
    middle = rest.astype(BF)
    return high, middle, (rest - middle.astype(F32)).astype(BF)


def spread_bias(table, places, bias, factor):
    line = 2 * WIN - 1
    for head in range(8):
        row = jnp.broadcast_to(table[head : head + 1], (WIN, 256))
        turns = []
        for r in range(WIN):
            by = 256 - (WIN - 1 - r) * line - (WIN - 1)
            turns.append(pltpu.roll(row, by, 1, stride=1, stride_axis=0))
        wide = jnp.concatenate(turns, 0)
        total = 0.0
        for part in three_parts(wide):
            total = total + dot(part, places[...])
        bias[head * 64 : head * 64 + 64] = total * factor


def collect_bias(grad, places):
    line = 2 * WIN - 1
    wide = 0.0
    for part in three_parts(grad):
        wide = wide + dot(part, places)
    out = []
    for head in range(8):
        total = jnp.zeros((WIN, 256), F32)
        for r in range(WIN):
            at = head * 64 + r * WIN
            total = total + pltpu.roll(wide[at : at + WIN], r * line, 1, stride=1, stride_axis=0)
        out.append(jnp.sum(total, 0, keepdims=True))
    return jnp.concatenate(out, 0)


def attn_forward_body(
    height, scale, step_of, place, above, upper, lower, gain, shift, weight, table, places, mask,
    x_out, norm_out, xhat_out, rstd_out, qkv_out, prob_out, mix_out, xs, bias,
):
    sample, band = step_of(pl.program_id(0))
    columns = lower.shape[2]

    @pl.when(pl.program_id(0) == 0)
    def _():
        spread_bias(table, places, bias, 1.0 / scale)

    def rows_from(ref, first):
        def rows_in(r, _):
            x = pltpu.roll(ref[0, r].astype(F32), WIN // 2, 0)
            xs[:, first + r] = x.reshape(columns // WIN, WIN, 256)
            return 0

        lax.fori_loop(0, WIN // 2, rows_in, 0, unroll=True)

    @pl.when(band == 0)
    def _():
        rows_from(above, 0)

    @pl.when(band > 0)
    def _():
        rows_from(upper, 0)

    rows_from(lower, WIN // 2)

    def norm_in(k, _):
        tokens = pl.ds(k * 128, 128)
        x = xs[pl.ds(k * 2, 2)].reshape(128, 256)
        xhat, rstd = norm_parts(x)
        x_out[tokens] = x.astype(BF)
        xhat_out[tokens] = xhat.astype(BF)
        rstd_out[tokens] = jnp.broadcast_to(rstd, (128, 128))
        norm_out[tokens] = (xhat * gain[...] + shift[...]).astype(BF)
        return 0

    lax.fori_loop(0, columns // 16, norm_in, 0, unroll=8)
    for k in range(0, columns * WIN, 256):
        qkv_out[k : k + 256] = dot(norm_out[k : k + 256], weight[...]).astype(BF)

    key_at, query_at = iota((64, 128), 0), iota((64, 128), 1)
    window_at = query_at // 64
    query_at = query_at % 64
    row_base = place[0] + band * WIN
    key_row, query_row = key_at // WIN + row_base, query_at // WIN + row_base
    key_row = jnp.where(key_row < 0, key_row + height, key_row)
    query_row = jnp.where(query_row < 0, query_row + height, query_row)
    rows_differ = (key_row >= height - WIN // 2) != (query_row >= height - WIN // 2)
    row_bad = key_row >= place[1 + sample]

    def attend(pair, _):
        key_col = (pair * 2 + window_at) * WIN + key_at % WIN - WIN // 2
        query_col = (pair * 2 + window_at) * WIN + query_at % WIN - WIN // 2
        key_col = jnp.where(key_col < 0, key_col + columns, key_col)
        query_col = jnp.where(query_col < 0, query_col + columns, query_col)
        cols_differ = (key_col >= columns - WIN // 2) != (query_col >= columns - WIN // 2)
        bad = row_bad | (key_col >= place[3 + sample])
        minus = jnp.where(rows_differ | cols_differ, MASKED / scale, 0.0) + jnp.where(
            bad, MASKED / scale, 0.0
        )
        for half in range(2):
            keys = spread_heads(pair_of(qkv_out, pair, 256 + 128 * half), mask[...])
            queries = blocks_of(qkv_out, pair, 128 * half)
            scores = dot_nt(keys, queries).reshape(4, 64, 128)
            scores = scores + (bias[256 * half : 256 * half + 256].reshape(4, 64, 128) + minus[None])
            top = jnp.max(scores, 1, keepdims=True)
            raised = jnp.exp2((scores - top) * (scale * LOG2E))
            probs = raised * (1.0 / jnp.sum(raised, 1, keepdims=True))
            probs = probs.reshape(256, 128).astype(BF)
            prob_out[pair, 256 * half : 256 * half + 256] = probs
        return 0

    def mix(pair, _):
        for half in range(2):
            probs = prob_out[pair, 256 * half : 256 * half + 256]
            values = spread_heads(pair_of(qkv_out, pair, 512 + 128 * half), mask[...])
            mixed = dot_tn(probs, values).astype(BF)
            mix_out[pl.ds(pair * 128, 64), 128 * half : 128 * half + 128] = mixed[:64, :128]
            mix_out[pl.ds(pair * 128 + 64, 64), 128 * half : 128 * half + 128] = mixed[64:, 128:]
        return 0

    lax.fori_loop(0, columns // 16, attend, 0, unroll=8)
    lax.fori_loop(0, columns // 16, mix, 0, unroll=8)


def near(*arrays):
    return [pltpu.with_memory_space_constraint(a, pltpu.VMEM) for a in arrays]


def const_spec(shape):
    return pl.BlockSpec(shape, lambda *_: (0,) * len(shape))


SMALL_COST = pl.CostEstimate(flops=10**6, bytes_accessed=10**4, transcendentals=0)


def params(mib):
    return pltpu.CompilerParams(vmem_limit_bytes=mib * MIB)


def far(*arrays):
    return [pltpu.with_memory_space_constraint(a, pltpu.HBM) for a in arrays]


SMEM_SPEC = pl.BlockSpec(memory_space=pltpu.SMEM)


def band_steps(samples, bands):
    def step_of(step):
        return step % samples, bands[0] + step // samples

    return step_of, samples * len(bands)


def attn_forward(place, above, own, gain, shift, weight, table, places, mask, height, scale):
    samples, grid_rows, columns, width = own.shape
    half = WIN // 2
    bands = grid_rows // WIN
    tokens = WIN * columns
    steps = samples * bands

    def step_of(step):
        return step // bands, step % bands

    def row_block(step):
        return (step, 0)

    total = steps * tokens
    return pl.pallas_call(
        functools.partial(attn_forward_body, height, scale, step_of),
        grid=(steps,),
        in_specs=[
            SMEM_SPEC,
            pl.BlockSpec((1, half, columns, width), lambda s: (step_of(s)[0], 0, 0, 0)),
            pl.BlockSpec(
                (1, half, columns, width),
                lambda s: (step_of(s)[0], jnp.maximum(2 * step_of(s)[1] - 1, 0), 0, 0),
            ),
            pl.BlockSpec(
                (1, half, columns, width), lambda s: (step_of(s)[0], 2 * step_of(s)[1], 0, 0)
            ),
            const_spec((1, width)),
            const_spec((1, width)),
            const_spec(weight.shape),
            const_spec(table.shape),
            const_spec(places.shape),
            const_spec(mask.shape),
        ],
        out_specs=[
            pl.BlockSpec((tokens, width), row_block),
            pl.BlockSpec((tokens, width), row_block),
            pl.BlockSpec((tokens, width), row_block),
            pl.BlockSpec((tokens, 128), row_block),
            pl.BlockSpec((tokens, 3 * width), row_block),
            pl.BlockSpec((columns // 16, 512, 128), lambda s: (s, 0, 0)),
            pl.BlockSpec((tokens, width), row_block),
        ],
        out_shape=[
            pltpu.VMEM((total, width), BF),
            pltpu.HBM((total, width), BF),
            pltpu.HBM((total, width), BF),
            pltpu.HBM((total, 128), F32),
            pltpu.HBM((total, 3 * width), BF),
            pltpu.HBM((total // 128, 512, 128), BF),
            pltpu.VMEM((total, width), BF),
        ],
        scratch_shapes=[
            pltpu.VMEM((columns // WIN, WIN, WIN, width), F32),
            pltpu.VMEM((512, 128), F32),
        ],
        compiler_params=params(24),
        cost_estimate=SMALL_COST,
        name="attn_forward",
    )(place, *far(above, own, own, gain, shift), *near(weight), *far(table, places, mask))


def gelu_parts(x):
    share = 0.5 + 0.5 * lax.erf(x * 0.7071067811865476)
    bell = jnp.exp2(x * x * (-0.5 * LOG2E))
    return x * share, share + x * (bell * 0.3989422804014327)


def ffn_forward_body(
    height, step_of, place, x_ref, mix, out_w, out_b, gain, shift, up_w, up_b, down_w, down_b,
    norm_out, xhat_out, rstd_out, act_out, slope_out, sum_out, first_rows, sums,
):
    sample, band = step_of(pl.program_id(0))
    columns = sum_out.shape[2]
    chunk = 256
    chunks = columns * WIN // chunk

    def attend_sum(k, _):
        tokens = pl.ds(k * chunk, chunk)
        first = x_ref[tokens].astype(F32) + dot(mix[tokens], out_w[...]) + out_b[...]
        sums[pl.ds(k * (chunk // 64), chunk // 64)] = first.reshape(chunk // 64, WIN, WIN, 256)
        xhat, rstd = norm_parts(first)
        norm_out[tokens] = (xhat * gain[...] + shift[...]).astype(BF)
        xhat_out[tokens] = xhat.astype(BF)
        rstd_out[tokens] = jnp.broadcast_to(rstd, (chunk, 128))
        return 0

    def raise_up(k, _):
        tokens = pl.ds(k * chunk, chunk)
        for f in range(0, 1024, 256):
            raised = dot(norm_out[tokens], up_w[:, f : f + 256]) + up_b[:, f : f + 256]
            act, slope = gelu_parts(raised)
            act_out[tokens, f : f + 256] = act.astype(BF)
            slope_out[tokens, f : f + 256] = slope.astype(BF)
        return 0

    def put_down(k, _):
        tokens = pl.ds(k * chunk, chunk)
        windows = pl.ds(k * (chunk // 64), chunk // 64)
        second = dot(act_out[tokens], down_w[...]) + down_b[...]
        sums[windows] += second.reshape(chunk // 64, WIN, WIN, 256)
        return 0

    lax.fori_loop(0, chunks, attend_sum, 0, unroll=True)
    lax.fori_loop(0, chunks, raise_up, 0, unroll=True)
    lax.fori_loop(0, chunks, put_down, 0, unroll=True)
    column = iota((columns, 1), 0)

    def rows_out(r, _):
        row = place[0] + band * WIN + r
        row = jnp.where(row < 0, row + height, row)
        limit = jnp.where(row < place[1 + sample], place[3 + sample], 0)
        back = pltpu.roll(sums[:, r].reshape(columns, 256), columns - WIN // 2, 0)
        sum_out[0, r] = jnp.where(column < limit, back, 0.0).astype(BF)
        return 0

    lax.fori_loop(0, WIN, rows_out, 0, unroll=True)

    @pl.when(band == 0)
    def _():
        first_rows[0] = sum_out[0, : WIN // 2 + 1]


def ffn_forward(place, x, mix, out_w, out_b, gain, shift, up_w, up_b, down_w, down_b, height, shape):
    samples, grid_rows, columns, width = shape
    bands = grid_rows // WIN
    tokens = WIN * columns
    steps = samples * bands
    hidden = up_w.shape[1]
    total = steps * tokens

    def step_of(step):
        return step // bands, step % bands

    def row_block(step):
        return (step, 0)

    rows = [width, width, 128, hidden, hidden]
    types = [BF, BF, F32, BF, BF]
    return pl.pallas_call(
        functools.partial(ffn_forward_body, height, step_of),
        grid=(steps,),
        in_specs=[SMEM_SPEC]
        + [pl.BlockSpec((tokens, width), row_block)] * 2
        + [const_spec(a.shape) for a in (out_w, out_b, gain, shift, up_w, up_b, down_w, down_b)],
        out_specs=[pl.BlockSpec((tokens, n), row_block) for n in rows]
        + [
            pl.BlockSpec((1, WIN, columns, width), lambda s: (*step_of(s), 0, 0)),
            pl.BlockSpec((1, WIN // 2 + 1, columns, width), lambda s: (step_of(s)[0], 0, 0, 0)),
        ],
        out_shape=[pltpu.HBM((total, n), t) for n, t in zip(rows, types)]
        + [
            pltpu.HBM(shape, BF),
            jax.ShapeDtypeStruct((samples, WIN // 2 + 1, columns, width), BF),
        ],
        scratch_shapes=[pltpu.VMEM((columns // WIN, WIN, WIN, width), F32)],
        compiler_params=params(32),
        cost_estimate=SMALL_COST,
        name="ffn_forward",
    )(
        place, *near(x, mix, out_w), *far(out_b, gain, shift), *near(up_w), *far(up_b), *near(down_w),
        *far(down_b),
    )


def column_sum(x):
    return jnp.sum(x, 0, keepdims=True)


def ffn_backward_step(
    height, step, sample, band, place, above, own, act, slope, normed, xhat_ref, rstd_ref, mix, conv_w,
    out_w, gain, up_w, down_w, first_out, mixed_out,
    taps, turned, branch, low, raised_s, attn, down_acc, up_acc, out_acc, vec,
):
    columns = own.shape[2]
    tokens = columns * WIN
    half = WIN // 2
    column = iota((columns, 1), 0)

    @pl.when(step == 0)
    def _():
        for ref in (down_acc, up_acc, out_acc, vec):
            ref[...] = jnp.zeros_like(ref)
        for k in range(9):
            at = 256 * (k % 3)
            turned[k // 3, :, at : at + 256] = conv_w[k, 0]

    start = place[0] + half
    not_first = start != 0
    lanes = (0, 256, 512)
    top = band == 0
    before = jnp.where(top, jnp.where(not_first, start, height), start + band * WIN) - half - 1

    def put_group(group):
        for k in range(half + 2):
            row = before + k if group == 0 else start + band * WIN + k - 1
            at = band * WIN + (group - 1) * half - 1 + k
            source = own[0, jnp.maximum(at, 0)]
            allowed = True
            if group == 0 and k <= half:
                source = jnp.where(top, above[0, k], source)
            elif group == 0:
                row = start + band * WIN
                allowed = ~top | not_first
            elif k == 0:
                source = jnp.where(top, above[0, ABOVE_LAST], source)
                allowed = ~top | not_first
            limit = row_limit(place, sample, row, allowed)
            put_taps(source, limit, taps, group * (half + 2) + k, lanes)

    put_group(0)
    for group in range(2):
        if group == 0:
            put_group(1)
        total = 0.0
        for a in range(3):
            at = group * (half + 2) + 2 - a
            piece = taps[at : at + half].reshape(half * columns, 768)
            total = total + dot_nt(piece, turned[a])
        for k in range(half):
            row = place[0] + band * WIN + group * half + k
            row = jnp.where(row < 0, row + height, row)
            limit = row_limit(place, sample, row)
            part = jnp.where(column < limit, total[k * columns : (k + 1) * columns], 0.0)
            part = pltpu.roll(part, half, 0)
            branch[:, group * half + k] = part.reshape(columns // WIN, WIN, 256)

    chunk = 256
    windows = chunk // 64
    for k in range(tokens // chunk):
        at = slice(k * chunk, (k + 1) * chunk)
        upper = branch[k * windows : (k + 1) * windows].reshape(chunk, 256)
        low[at] = upper.astype(BF)
        vec[0:1] += column_sum(upper.astype(BF).astype(F32))
    for k in range(tokens // chunk):
        at = slice(k * chunk, (k + 1) * chunk)
        for f in range(0, 1024, 256):
            wide = slice(f, f + 256)
            raised = (dot_nt(low[at], down_w[wide]) * slope[at, wide].astype(F32)).astype(BF)
            raised_s[at, wide] = raised
            row = 4 + f // 256
            vec[row : row + 1] += column_sum(raised.astype(F32))
    for k in range(tokens // chunk):
        at = slice(k * chunk, (k + 1) * chunk)
        dy = dot_nt(raised_s[at], up_w[...])
        xhat = xhat_ref[at].astype(F32)
        rstd = rstd_ref[at]
        rstd = jnp.concatenate([rstd, rstd], 1)
        upper = branch[k * windows : (k + 1) * windows].reshape(chunk, 256)
        first = upper + norm_back(dy, xhat, rstd, gain[...])
        first_out[at] = first
        attn[at] = first.astype(BF)
        vec[1:2] += column_sum(dy * xhat)
        vec[2:3] += column_sum(dy)
        vec[3:4] += column_sum(first.astype(BF).astype(F32))
    for k in range(tokens // chunk):
        at = slice(k * chunk, (k + 1) * chunk)
        mixed_out[at] = dot_nt(attn[at], out_w[...]).astype(BF)
    low_t = low[...].T
    normed_t = normed[...].T
    for f in range(0, 1024, 256):
        wide = slice(f, f + 256)
        down_acc[:, wide] += dot(low_t, act[:, wide])
        up_acc[:, wide] += dot(normed_t, raised_s[:, wide])
    out_acc[...] += dot(mix[...].T, attn[...])


def ffn_backward_end(down_out, up_out, out_out, vec_out, down_acc, up_acc, out_acc, vec):
    for f in range(0, 1024, 256):
        wide = slice(f, f + 256)
        down_out[wide] = down_acc[:, wide].T.astype(BF)
        up_out[:, wide] = up_acc[:, wide].astype(BF)
    out_out[...] = out_acc[...].astype(BF)
    vec_out[...] = vec[...].astype(BF)


def send_rows(core, batch, mine, other, down_rows, down_acc, out_acc, up_acc, qkv_acc, vectors):
    for f in range(0, 1024, 256):
        turned = down_acc[:, f : f + 256].T.reshape(8, 4, 8, 256)
        for k in range(4):
            piece = turned[:, k].reshape(64, 256)
            down_rows[f // 4 : f // 4 + 64, 256 * k : 256 * k + 256] = piece.astype(BF)
    count = 8 * batch
    wide_vectors = jnp.concatenate([vectors] * batch, 0).astype(BF)

    def put(target, k):
        for chip in range(256 // (2 * count)):
            rows = slice((2 * chip + k) * count, (2 * chip + k + 1) * count)
            to = slice(chip * count, (chip + 1) * count)
            at = 0
            for ref in (down_rows, out_acc, up_acc, qkv_acc):
                target[to, at : at + ref.shape[1]] = ref[rows].astype(BF)
                at += ref.shape[1]
            target[to, at:] = wide_vectors

    for k in range(2):

        @pl.when(core == k)
        def _():
            put(mine, k)
            put(other, 1 - k)


def backward_body(height, scale, step_of, batch, *refs):
    place, above, own, *refs = refs
    ffn_rows, refs = refs[:6], refs[6:]
    attn_rows, refs = refs[:5], refs[5:]
    ffn_consts, refs = refs[:5], refs[5:]
    (weight, gain, mask, conv_vec, places), refs = refs[:5], refs[5:]
    input_out, up_out, *refs = refs
    outs, refs = (refs[:2], refs[2:]) if batch else (refs[:6], refs[6:])
    ffn_scratch, (first, mixed, qkv_acc, table_acc, vec_acc, grads, score_grads, sums, down_rows) = (
        refs[:10], refs[10:],
    )
    step = pl.program_id(0)
    sample, band = step_of(step)
    columns = input_out.shape[2]
    half = WIN // 2

    @pl.when(step == 0)
    def _():
        for ref in (qkv_acc, table_acc, vec_acc):
            ref[...] = jnp.zeros_like(ref)

    ffn_backward_step(
        height, step, sample, band, place, above, own, *ffn_rows, *ffn_consts, first, mixed,
        *ffn_scratch,
    )
    qkv, prob, normed, xhat_ref, rstd_ref = attn_rows
    attn_backward_step(
        scale, mixed, qkv, prob, normed, xhat_ref, rstd_ref, first, weight, gain, mask,
        qkv_acc, table_acc, vec_acc, grads, score_grads, sums,
    )

    def row_out(r):
        return pltpu.roll(sums[:, r].reshape(columns, 256), columns - half, 0)

    @pl.when(band == 0)
    def _():
        for r in range(half):
            up_out[0, r] = row_out(r).astype(BF)
            input_out[0, r] = row_out(half + r)

    @pl.when(band > 0)
    def _():
        for r in range(WIN):
            input_out[0, band * WIN - half + r] = row_out(r)

    @pl.when(step == pl.num_programs(0) - 1)
    def _():
        table = collect_bias(table_acc[...], places[...])
        rest = jnp.concatenate([vec_acc[0:2], conv_vec[0:1], jnp.zeros((5, 256), F32)], 0)
        vectors = jnp.concatenate([table, rest], 1)
        down_acc, up_acc, out_acc, vec = ffn_scratch[6:]
        if batch:
            vectors = jnp.concatenate([vec[...], vectors], 1)
            send_rows(
                place[place.shape[0] - 1], batch, *outs, down_rows, down_acc, out_acc, up_acc, qkv_acc,
                vectors,
            )
            return
        *ffn_outs, qkv_out, vec_out = outs
        ffn_backward_end(*ffn_outs, down_acc, up_acc, out_acc, vec)
        for f in range(0, 768, 256):
            qkv_out[:, f : f + 256] = qkv_acc[:, f : f + 256].astype(BF)
        vec_out[...] = vectors.astype(BF)


def attn_backward_step(
    scale, mixed, qkv, prob, normed, xhat_ref, rstd_ref, first, weight, gain, mask,
    qkv_acc, table_acc, vec_acc, grads, score_grads, sums,
):
    tokens = qkv.shape[0]
    columns = tokens // WIN

    def attend(pair, _):
        head_at = mask[...]
        for half in range(2):
            lanes = slice(256 * half, 256 * half + 256)
            low = prob[pair, lanes]
            mixed_blocks = blocks_of(mixed, pair, 128 * half)
            values = spread_heads(pair_of(qkv, pair, 512 + 128 * half), head_at)
            prob_grad = dot_nt(values, mixed_blocks).reshape(4, 64, 128)
            probs = low.astype(F32).reshape(4, 64, 128)
            shared = jnp.sum(prob_grad * probs, 1, keepdims=True)
            score_grad = (probs * (prob_grad - shared)).astype(BF).reshape(256, 128)
            table_acc[lanes] += score_grad.astype(F32)
            score_grads[pair, lanes] = score_grad
        return 0

    def project(pair, _):
        head_at = mask[...]
        for half in range(2):
            lanes = slice(256 * half, 256 * half + 256)
            low = prob[pair, lanes]
            mixed_blocks = blocks_of(mixed, pair, 128 * half)
            score_grad = score_grads[pair, lanes]
            keys = spread_heads(pair_of(qkv, pair, 256 + 128 * half), head_at)
            queries = blocks_of(qkv, pair, 128 * half)
            query_grad = (dot_tn(score_grad, keys) * scale).astype(BF)
            out = slice(128 * half, 128 * half + 128)
            grads[pl.ds(pair * 128, 64), out] = query_grad[:64, :128]
            grads[pl.ds(pair * 128 + 64, 64), out] = query_grad[64:, 128:]
            wide = head_at.astype(F32)
            key_grad = (dot(score_grad, queries) * wide).reshape(4, 64, 256)
            key_grad = (jnp.sum(key_grad, 0) * scale).astype(BF)
            out = slice(256 + 128 * half, 256 + 128 * half + 128)
            grads[pl.ds(pair * 128, 64), out] = key_grad[:, :128]
            grads[pl.ds(pair * 128 + 64, 64), out] = key_grad[:, 128:]
            value_grad = (dot(low, mixed_blocks) * wide).reshape(4, 64, 256)
            value_grad = jnp.sum(value_grad, 0).astype(BF)
            out = slice(512 + 128 * half, 512 + 128 * half + 128)
            grads[pl.ds(pair * 128, 64), out] = value_grad[:, :128]
            grads[pl.ds(pair * 128 + 64, 64), out] = value_grad[:, 128:]
        return 0

    lax.fori_loop(0, columns // 16, attend, 0, unroll=8)
    lax.fori_loop(0, columns // 16, project, 0, unroll=8)
    for f in range(0, 768, 256):
        qkv_acc[:, f : f + 256] += dot_tn(normed[...], grads[:, f : f + 256])

    def part(k, _):
        at = pl.ds(k * 256, 256)
        dy = dot_nt(grads[at], weight[...])
        xhat = xhat_ref[at].astype(F32)
        rstd = rstd_ref[at]
        rstd = jnp.concatenate([rstd, rstd], 1)
        total = first[at] + norm_back(dy, xhat, rstd, gain[...])
        sums[pl.ds(k * 4, 4)] = total.reshape(4, WIN, WIN, 256)
        vec_acc[0:1] += column_sum(dy * xhat)
        vec_acc[1:2] += column_sum(dy)
        return 0

    lax.fori_loop(0, tokens // 256, part, 0, unroll=True)


def backward(place, above, own, ffn_rows, attn_rows, ffn_consts, attn_consts, height, scale, batch):
    samples, grid_rows, columns, width = own.shape
    bands = grid_rows // WIN
    tokens = WIN * columns
    steps = samples * bands
    hidden = ffn_rows[0].shape[1]
    half = WIN // 2

    def step_of(step):
        return step // bands, step % bands

    def row_block(step):
        return (step, 0)

    def sample_block(step):
        return (step_of(step)[0], 0, 0, 0)

    in_specs = [
        SMEM_SPEC,
        pl.BlockSpec((1,) + above.shape[1:], sample_block),
        pl.BlockSpec((1,) + own.shape[1:], sample_block),
    ]
    in_specs += [pl.BlockSpec((tokens, a.shape[1]), row_block) for a in (*ffn_rows, *attn_rows)]
    in_specs[10] = pl.BlockSpec((columns // 16, 512, 128), lambda s: (s, 0, 0))
    in_specs += [pl.BlockSpec((9, 1, width, width), lambda s: (0, 0, 0, 0))]
    in_specs += [const_spec(a.shape) for a in (*ffn_consts[1:], *attn_consts)]
    outs = [(own.shape, F32), ((samples, half, columns, width), BF)]
    if batch:
        outs += [((width // 2, 2 * hidden + 7 * width), BF)] * 2
    else:
        outs += [
            ((hidden, width), BF), ((width, hidden), BF), ((width, width), BF), ((8, width), BF),
            ((width, 3 * width), BF), ((8, 2 * width), BF),
        ]
    out_specs = [const_spec(a) for a, _ in outs]
    out_specs[0] = pl.BlockSpec((1,) + own.shape[1:], sample_block)
    out_specs[1] = pl.BlockSpec((1, half, columns, width), sample_block)
    return pl.pallas_call(
        functools.partial(backward_body, height, scale, step_of, batch),
        grid=(steps,),
        in_specs=in_specs,
        out_specs=out_specs,
        out_shape=[pltpu.HBM(a, t) for a, t in outs[:2]]
        + [jax.ShapeDtypeStruct(a, t) for a, t in outs[2:]],
        scratch_shapes=[
            pltpu.VMEM((WIN + 4, columns, 3 * width), BF),
            pltpu.VMEM((3, width, 3 * width), BF),
            pltpu.VMEM((columns // WIN, WIN, WIN, width), F32),
            pltpu.VMEM((tokens, width), BF),
            pltpu.VMEM((tokens, hidden), BF),
            pltpu.VMEM((tokens, width), BF),
            pltpu.VMEM((width, hidden), F32),
            pltpu.VMEM((width, hidden), F32),
            pltpu.VMEM((width, width), F32),
            pltpu.VMEM((8, width), F32),
            pltpu.VMEM((tokens, width), F32),
            pltpu.VMEM((tokens, width), BF),
            pltpu.VMEM((width, 3 * width), F32),
            pltpu.VMEM((512, 128), F32),
            pltpu.VMEM((8, width), F32),
            pltpu.VMEM((tokens, 3 * width), BF),
            pltpu.VMEM((columns // 16, 512, 128), BF),
            pltpu.VMEM((columns // WIN, WIN, WIN, width), F32),
            pltpu.VMEM((width, hidden), BF),
        ],
        compiler_params=params(BACK_MIB),
        cost_estimate=pl.CostEstimate(
            flops=4 * 10**10, bytes_accessed=10**7, transcendentals=0
        ),
        name="backward",
    )(
        place, *far(above, own, *ffn_rows, *attn_rows, *ffn_consts, *attn_consts),
    )


def shifted(row, by):
    columns = row.shape[0]
    moved = pltpu.roll(row, by % columns, 0)
    place = iota((8, 1), 0)
    if by == 1:
        return jnp.concatenate([jnp.where(place == 0, 0.0, moved[:8]), moved[8:]], 0)
    return jnp.concatenate([moved[:-8], jnp.where(place == 7, 0.0, moved[-8:])], 0)


def pack_near_body(qkv, out_w, up, down, near):
    rows = qkv.shape[0]
    at = 0
    for ref in (qkv, out_w, up):
        near[:, at : at + ref.shape[1]] = ref[...].astype(BF)
        at += ref.shape[1]
    for k in range(down.shape[0] // rows):
        near[:, at : at + down.shape[1]] = down[k * rows : (k + 1) * rows].astype(BF)
        at += down.shape[1]


def pack_near(qkv, out_w, up, down):
    rows = qkv.shape[0]
    lanes = (qkv.size + out_w.size + up.size + down.size) // rows
    return pl.pallas_call(
        pack_near_body,
        out_shape=jax.ShapeDtypeStruct((rows, lanes), BF),
        compiler_params=params(16),
        cost_estimate=SMALL_COST,
        name="pack_near",
    )(*far(qkv, out_w, up, down))


def unpack_near_body(order, held, qkv, out_w, up, down):
    devices, rows, _ = held.shape
    count = max(16 // rows, 1)

    def some(k, _):
        pieces = [held[order[k * count + n]] for n in range(count)]
        at = 0
        place = pl.ds(pl.multiple_of(k * count * rows, count * rows), count * rows)
        for ref in (qkv, out_w, up):
            lanes = slice(at, at + ref.shape[1])
            ref[place] = jnp.concatenate([piece[:, lanes] for piece in pieces], 0)
            at = lanes.stop
        width = down.shape[1]
        parts = down.shape[0] // (devices * rows)
        tall = [
            piece[:, at + n * width : at + (n + 1) * width] for piece in pieces for n in range(parts)
        ]
        size = count * rows * parts
        down[pl.ds(pl.multiple_of(k * size, size), size)] = jnp.concatenate(tall, 0)
        return 0

    lax.fori_loop(0, devices // count, some, 0, unroll=4)


def unpack_near(order, held, weights):
    devices = held.shape[0]
    return pl.pallas_call(
        unpack_near_body,
        in_specs=[SMEM_SPEC, pl.BlockSpec(memory_space=pltpu.VMEM)],
        out_shape=[pltpu.VMEM((devices * w.shape[0], w.shape[1]), BF) for w in weights],
        compiler_params=params(24),
        cost_estimate=SMALL_COST,
        name="unpack_near",
    )(order, held)


def last_sums_body(parts, down, out_w, up, qkv, *vectors):
    count, rows, lanes = parts.shape
    total = parts[0].astype(F32)
    for k in range(1, count):
        total = total + parts[k].astype(F32)
    width = down.shape[1]
    for k in range(down.shape[0] // rows):
        down[k * rows : (k + 1) * rows] = total[:, k * width : (k + 1) * width]
    at = down.size // rows
    for ref in (out_w, up, qkv):
        ref[...] = total[:, at : at + ref.shape[1]]
        at += ref.shape[1]

    def vector(row, group):
        row, lane = divmod((row * 3 + group) * width, lanes - at)
        return total[row : row + 1, at + lane : at + lane + width]

    singles, (up_bias, table), more = vectors[:4], vectors[4:6], vectors[6:]
    for k, ref in enumerate(singles):
        ref[...] = vector(k, 0)
    for k in range(4):
        up_bias[:, k * width : (k + 1) * width] = vector(4 + k, 0)
    for k in range(8):
        table[k : k + 1] = vector(k, 1)
    for k, ref in enumerate(more):
        ref[...] = vector(k, 2)


def last_sums(parts, down, rest):
    width = down[1]
    vectors = [(1, width)] * 4 + [(1, 4 * width), (8, width)] + [(1, width)] * 3
    shapes = (down, *rest, *vectors)
    return pl.pallas_call(
        last_sums_body,
        out_shape=[jax.ShapeDtypeStruct(a, F32) for a in shapes],
        compiler_params=params(24),
        cost_estimate=SMALL_COST,
        name="last_sums",
    )(parts)


def sum_body(parts, out):
    total = parts[0].astype(F32)
    for k in range(1, parts.shape[0]):
        total = total + parts[k].astype(F32)
    out[...] = total


def sum_parts(parts):
    return pl.pallas_call(
        sum_body,
        out_shape=jax.ShapeDtypeStruct(parts.shape[1:], F32),
        compiler_params=params(16),
        cost_estimate=SMALL_COST,
        name="sum_parts",
    )(parts)


def copies_body(x, out):
    low = x[...].astype(BF)
    for k in range(out.shape[0]):
        out[k] = low


def make_copies(x, count):
    return pl.pallas_call(
        copies_body,
        out_shape=jax.ShapeDtypeStruct((count,) + x.shape, BF),
        compiler_params=params(16),
        cost_estimate=SMALL_COST,
        name="make_copies",
    )(*far(x))


def row_limit(place, sample, row, allowed=True):
    return jnp.where((row < place[1 + sample]) & allowed, place[3 + sample], 0)


def put_taps(row, limit, target, at, lanes):
    column = iota((row.shape[0], 1), 0)
    wide = jnp.where(column < limit, row.astype(F32), 0.0)
    target[at, :, lanes[0] : lanes[0] + 256] = shifted(wide, -1).astype(BF)
    target[at, :, lanes[1] : lanes[1] + 256] = wide.astype(BF)
    target[at, :, lanes[2] : lanes[2] + 256] = shifted(wide, 1).astype(BF)


ABOVE_LAST = WIN // 2
ABOVE_HIDDEN = WIN // 2 + 1


def own_taps(height, place, above, own, below, taps, at):
    sample = pl.program_id(0)
    rows = own.shape[1]
    start = place[0] + WIN // 2

    def put(r):
        allowed = True
        if r == 0:
            source, allowed = above[0, ABOVE_LAST], start != 0
        elif r <= rows:
            source = own[0, r - 1]
        else:
            source, allowed = below[0, 0], start + rows != height
        limit = row_limit(place, sample, start + r - 1, allowed)
        put_taps(source, limit, taps, at + r, (0, 256, 512))

    return put


def conv_weight_body(
    height, place, above, own, below, sums, hidden, out, vec, taps, held, acc, acc_hidden
):
    sample = pl.program_id(0)

    @pl.when(sample == 0)
    def _():
        for ref in (acc, acc_hidden, vec):
            ref[...] = jnp.zeros_like(ref)

    rows, columns = own.shape[1:3]
    half = WIN // 2
    column = iota((columns, 1), 0)
    start = place[0] + half
    not_first = start != 0

    before = jnp.where(not_first, start, height) - half - 1
    put = own_taps(height, place, above, own, below, taps, half + 2)
    for r in range(half + 1):
        limit = row_limit(place, sample, before + r)
        put_taps(above[0, r], limit, taps, r, (0, 256, 512))
    limit = row_limit(place, sample, start, not_first)
    put_taps(own[0, 0], limit, taps, half + 1, (0, 256, 512))

    def add(source, first, acc):
        count = source.shape[0]
        turned = source.reshape(count * columns, 256).T
        for a in range(3):
            piece = taps[first + 2 - a : first + 2 - a + count].reshape(count * columns, 768)
            acc[a] += dot(turned, piece)

    put(0)
    put(1)
    add(sums[0, :half], 0, acc)
    step = 8
    for r in range(0, rows, step):
        for k in range(r, r + step):
            put(k + 2)
            limit = row_limit(place, sample, start + k)
            held[k] = jnp.where(column < limit, hidden[0, k].astype(F32), 0.0).astype(BF)
            vec[0:1] += jnp.sum(taps[half + 3 + k, :, 256:512].astype(F32), 0, keepdims=True)
        add(held[r : r + step], half + 2 + r, acc_hidden)
        last = min(r + step, rows - half)
        add(sums[0, half + r : half + last], half + 2 + r, acc)

    @pl.when(sample == pl.num_programs(0) - 1)
    def _():
        for k in range(9):
            at = 256 * (k % 3)
            out[k, 0] = acc[k // 3, :, at : at + 256].astype(BF)
            out[k, 1] = acc_hidden[k // 3, :, at : at + 256].astype(BF)


def field_spec(a):
    return pl.BlockSpec((1,) + a.shape[1:], lambda s: (s, 0, 0, 0))


def conv_call(
    body, name, mib, place, fields, consts, height, out_specs, out_shape, scratch, cost=None
):
    return pl.pallas_call(
        functools.partial(body, height),
        grid=(fields[0][1].shape[0],),
        in_specs=[SMEM_SPEC] + [s for s, _ in fields] + [s for s, _ in consts],
        out_specs=out_specs,
        out_shape=out_shape,
        scratch_shapes=scratch,
        compiler_params=params(mib),
        cost_estimate=cost or SMALL_COST,
        name=name,
    )(place, *[a for _, a in fields], *far(*[a for _, a in consts]))


def whole(a):
    return field_spec(a), far(a)[0]


def conv_weight(place, grads, sums, hidden, height):
    _, rows, columns, width = sums.shape
    shape = (9, 2, width, width)
    acc = pltpu.VMEM((3, width, 3 * width), F32)
    return conv_call(
        conv_weight_body, "conv_weight", 34, place, [*map(whole, grads), whole(sums), whole(hidden)], (),
        height, [const_spec(shape), const_spec((8, width))],
        [jax.ShapeDtypeStruct(shape, BF), jax.ShapeDtypeStruct((8, width), F32)],
        [
            pltpu.VMEM((rows + WIN, columns, 3 * width), BF),
            pltpu.VMEM((rows, columns, width), BF),
            acc,
            acc,
        ],
        pl.CostEstimate(flops=2 * 10**10, bytes_accessed=10**7, transcendentals=0),
    )


def conv_data_body(height, place, above, own, below, weight, out, taps, turned):
    sample = pl.program_id(0)
    columns = own.shape[2]
    column = iota((columns, 1), 0)

    @pl.when(sample == 0)
    def _():
        for k in range(9):
            at = 256 * (k % 3)
            turned[k // 3, :, at : at + 256] = weight[k, 0]

    put = own_taps(height, place, above, own, below, taps, 0)
    for r in range(2):
        put(r)
    for r in range(0, own.shape[1], 4):
        for k in range(r + 2, r + 6):
            put(k)
        total = 0.0
        for a in range(3):
            piece = taps[r + 2 - a : r + 6 - a].reshape(4 * columns, 768)
            total = total + dot_nt(piece, turned[a])
        for k in range(4):
            limit = row_limit(place, sample, place[0] + WIN // 2 + r + k)
            part = total[k * columns : (k + 1) * columns]
            out[0, r + k] = jnp.where(column < limit, part, 0.0)


def conv_data(place, grads, weight, height):
    own = grads[1]
    width = own.shape[-1]
    weight_spec = pl.BlockSpec((9, 1, width, width), lambda s: (0, 1, 0, 0))
    return conv_call(
        conv_data_body, "conv_data", 28, place, [whole(a) for a in grads], ((weight_spec, weight),),
        height, field_spec(own), jax.ShapeDtypeStruct(own.shape, F32),
        [
            pltpu.VMEM((own.shape[1] + 2, own.shape[2], 3 * width), BF),
            pltpu.VMEM((3, width, 3 * width), BF),
        ],
        pl.CostEstimate(flops=10**10, bytes_accessed=10**7, transcendentals=0),
    )


def conv_forward_body(
    height, place, sums, sums_below, above, hidden, below, weight, bias, out, taps
):
    sample = pl.program_id(0)
    rows, columns = out.shape[1:3]
    column = iota((columns, 1), 0)
    half = WIN // 2
    start = place[0] + half
    not_first, not_last = start != 0, start + rows != height

    def put(r):
        allowed = True
        if r == 0:
            first, second, allowed = sums[0, half - 1], above[0, ABOVE_HIDDEN], not_first
        elif r <= rows:
            first, second = None, hidden[0, r - 1]
            if r <= rows - half:
                first = sums[0, half + r - 1]
            else:
                first = sums_below[0, r - 1 - rows + half]
        else:
            first, second, allowed = sums_below[0, half], below[0, 1], not_last
        limit = row_limit(place, sample, start + r - 1, allowed)
        put_taps(first, limit, taps, r, (1024, 512, 0))
        put_taps(second, limit, taps, r, (1280, 768, 256))

    for r in range(2):
        put(r)
    for r in range(0, rows, 4):
        for k in range(r + 2, r + 6):
            put(k)
        total = bias[...]
        for a in range(3):
            piece = taps[r + a : r + a + 4].reshape(4 * columns, 1536)
            total = total + dot(piece, weight[a * 1536 : (a + 1) * 1536])
        for k in range(4):
            limit = row_limit(place, sample, start + r + k)
            part = total[k * columns : (k + 1) * columns]
            out[0, r + k] = jnp.where(column < limit, part, 0.0).astype(BF)


def conv_forward(place, sums, sums_below, hidden, weight, bias, height):
    samples, rows, columns, width = sums.shape
    fields = (*near(sums), *far(sums_below, *hidden))
    return pl.pallas_call(
        functools.partial(conv_forward_body, height),
        grid=(samples,),
        in_specs=[SMEM_SPEC]
        + [field_spec(a) for a in fields]
        + [const_spec(weight.shape), const_spec(bias.shape)],
        out_specs=field_spec(sums),
        out_shape=jax.ShapeDtypeStruct(sums.shape, BF),
        scratch_shapes=[pltpu.VMEM((rows + 2, columns, 6 * width), BF)],
        compiler_params=params(32),
        cost_estimate=SMALL_COST,
        name="conv_forward",
    )(place, *fields, *far(weight, bias))


def shards(
    layer_input,
    hidden_state,
    crop_rows,
    crop_cols,
    first_gain,
    first_shift,
    qkv_weight,
    bias_table,
    output_weight,
    output_bias,
    second_gain,
    second_shift,
    up_weight,
    up_bias,
    down_weight,
    down_bias,
    conv_weight_in,
    conv_bias,
    cotangent,
):
    samples, grid_rows, columns, width = layer_input.shape
    shape = layer_input.shape
    heads = bias_table.shape[1]
    scale = float((width // heads) ** (-0.5))
    half = WIN // 2
    devices = device_count()
    row_devices = lax.axis_size("rows")
    height = grid_rows * row_devices
    row_place = lax.axis_index("rows")
    row_start = row_place * grid_rows
    place = jnp.concatenate(
        [(row_start - half)[None].astype(jnp.int32), crop_rows, crop_cols, (row_place % 2)[None]]
    ).astype(jnp.int32)

    hidden_width = up_weight.shape[1]

    def vec(v):
        return v.reshape(1, -1)

    input_above = ring(layer_input[:, grid_rows - half :], 1)
    rows_out, rows_down = output_weight.shape[0], down_weight.shape[0]
    weights = pack_near(qkv_weight, output_weight, up_weight, down_weight)
    offsets = bias_table.shape[0]

    def beside(held):
        grad, hidden, weight, table = after(
            (cotangent, hidden_state, conv_weight_in, bias_table), held
        )
        halo_above = jnp.concatenate([grad[:, grid_rows - half - 1 :], hidden[:, grid_rows - 1 :]], 1)
        halo_below = jnp.concatenate([grad[:, :1], hidden[:, :1]], 1)
        table = jnp.pad(table.T, ((0, 0), (0, 256 - offsets)))
        return halo_above, halo_below, make_copies(weight, devices), table, input_above, place

    held, order, (halo_above, halo_below, conv_copies, table, *_) = gather_steps(weights, beside)
    halo_above, halo_below, conv_copies = after((halo_above, halo_below, conv_copies), held)
    halo_above, halo_below = ring(halo_above, 1), ring(halo_below, -1)
    grads = (halo_above, cotangent, halo_below)
    conv_full = gather_copies(conv_copies).reshape(-1, width)

    qkv_full, output_full, up_full, down_full = unpack_near(
        order, held, (qkv_weight, output_weight, up_weight, down_weight)
    )
    mask = jnp.asarray(head_mask(), BF)

    x, normed, xhat, rstd, qkv, prob, mix = attn_forward(
        place, input_above, layer_input, vec(first_gain), vec(first_shift), qkv_full, table,
        jnp.asarray(offset_places(False), BF), mask, height, scale,
    )
    normed_2, xhat_2, rstd_2, act, slope, sums, sums_first = ffn_forward(
        place, x, mix, output_full, vec(output_bias), vec(second_gain), vec(second_shift),
        up_full, vec(up_bias), down_full, vec(down_bias), height, shape,
    )
    conv_local, conv_bias_part = conv_weight(place, grads, sums, hidden_state, height)
    conv_local, exchange = scatter_pairs(conv_local.reshape(devices, -1, width))
    conv_all = exchange(conv_local)
    sums_below = ring(after(sums_first, conv_local), -1)
    conv_blocks = after(conv_full.reshape(9, 2, width, width), conv_local)
    input_grad, input_up, *last_parts = backward(
        place, halo_above, cotangent,
        (act, slope, normed_2, xhat_2, rstd_2, mix),
        (qkv, prob, normed, xhat, rstd),
        (conv_blocks, output_full, vec(second_gain), up_full, down_full),
        (
            qkv_full, vec(first_gain), mask, conv_bias_part,
            jnp.asarray(offset_places(True), BF).T,
        ),
        height, scale, lax.axis_size("batch") if rows_out == 8 else 0,
    )
    last_parts = after(tuple(last_parts), sums_below)
    if rows_out == 8:
        last_local, exchange = add_pairs(*(a.reshape(-1, rows_out, a.shape[1]) for a in last_parts))
    else:
        down_acc, up_acc, out_acc, vec_ffn, qkv_acc, vec_attn = last_parts
        down_local = down_acc.reshape(devices, -1, rows_out, width).transpose(0, 2, 1, 3)
        parts = [
            down_local.reshape(devices, rows_out, -1),
            *(a.reshape(devices, rows_out, -1) for a in (out_acc, up_acc, qkv_acc)),
        ]
        last_local, exchange = scatter_pairs(
            with_vectors(parts, jnp.concatenate([vec_ffn, vec_attn], 1))
        )
    last_all = exchange(last_local)
    input_from_below = ring(after(input_up, last_local), -1)
    hidden_grad = conv_data(after(place, last_local), grads, conv_blocks, height)
    layer_output = conv_forward(
        after(place, hidden_grad), sums, sums_below, (halo_above, hidden_state, halo_below),
        conv_full, vec(conv_bias), height,
    )

    input_grad = lax.dynamic_update_slice(
        after(input_grad, layer_output), input_from_below.astype(F32), (0, grid_rows - half, 0, 0)
    )

    conv_weight_grad = sum_parts(conv_all)
    down_weight_grad, output_weight_grad, up_weight_grad, qkv_weight_grad, *vectors = last_sums(
        last_all,
        (rows_down, width),
        [(rows_out, width), (rows_out, hidden_width), (rows_out, 3 * width)],
    )
    bias_table_grad = vectors.pop(5)[:, :offsets][:, ::-1].T
    (
        down_bias_grad, second_gain_grad, second_shift_grad, output_bias_grad, up_bias_grad,
        first_gain_grad, first_shift_grad, conv_bias_grad,
    ) = (v.reshape(-1) for v in vectors)
    return (
        layer_output,
        input_grad,
        hidden_grad,
        first_gain_grad,
        first_shift_grad,
        qkv_weight_grad,
        bias_table_grad,
        output_weight_grad,
        output_bias_grad,
        second_gain_grad,
        second_shift_grad,
        up_weight_grad,
        up_bias_grad,
        down_weight_grad,
        down_bias_grad,
        conv_weight_grad,
        conv_bias_grad,
    )


def solution(mesh):
    field = P("batch", "rows", None, None)
    weight = P(AXES, None)
    in_specs = (
        field, field, P("batch"), P("batch"), P(), P(), weight, P(), weight, P(), P(), P(),
        weight, P(), weight, P(), weight, P(), field,
    )
    out_specs = (
        field, field, field, P(), P(), weight, P(), weight, P(), P(), P(), weight, P(), weight,
        P(), weight, P(),
    )
    return jax.shard_map(shards, mesh=mesh, in_specs=in_specs, out_specs=out_specs, check_vma=False)
```

```python
import functools

import jax
import jax.numpy as jnp
import numpy as np
from jax import lax
from jax.experimental import pallas as pl
from jax.experimental.pallas import tpu as pltpu
from jax.sharding import PartitionSpec as P

WIN = 8
EPSILON = 1e-05
MASKED = -100.0
HIGHEST = lax.Precision.HIGHEST
AXES = ("rows", "batch")
BF = jnp.bfloat16
F32 = jnp.float32
MIB = 1024 * 1024
BACK_MIB = 54
LOG2E = 1.4426950408889634


def dot(left, right):
    return jnp.dot(left, right, preferred_element_type=F32)


def dot_nt(left, right):
    return lax.dot_general(left, right, (((1,), (1,)), ((), ())), preferred_element_type=F32)


def dot_tn(left, right):
    return lax.dot_general(left, right, (((0,), (0,)), ((), ())), preferred_element_type=F32)


def iota(shape, dim):
    return lax.broadcasted_iota(jnp.int32, shape, dim)


def device_index():
    return lax.axis_index("rows") * lax.axis_size("batch") + lax.axis_index("batch")


def device_count():
    return lax.axis_size("rows") * lax.axis_size("batch")


def after(x, *others):
    return lax.optimization_barrier((x, *others))[0]


def bit_groups():
    batch, rows = lax.axis_size("batch"), lax.axis_size("rows")
    batch_bits = [1 << k for k in range(batch.bit_length() - 1)]
    row_bits = [batch << k for k in range(rows.bit_length() - 1)]
    chips = row_bits[1:]
    groups = [batch_bits[k : k + 2] for k in range(0, len(batch_bits), 2)]
    groups += [chips[k : k + 2] for k in range(0, len(chips), 2)]
    return groups + [row_bits[:1]]


def gather_steps(x, beside):
    devices = device_count()
    held = x[None]
    places = [0]
    groups = bit_groups()
    for k, group in enumerate(groups):
        masks = [0]
        for bit in group:
            masks = masks + [m | bit for m in masks]
        if k == 1:
            other = beside(held)
        if k == len(groups) - 1:
            held = after(held, *other)
        pieces = [held]
        for mask in masks[1:]:
            pieces.append(lax.ppermute(held, AXES, [(i, i ^ mask) for i in range(devices)]))
        held = jnp.concatenate(pieces, 0)
        places = [p ^ m for m in masks for p in places]
    order = np.zeros(devices, np.int32)
    for place, mask in enumerate(places):
        order[mask] = place
    return held, jnp.asarray(order), other


def scatter_pairs(x):
    rows, batch = lax.axis_size("rows"), lax.axis_size("batch")
    core = lax.axis_index("rows") % 2
    by_core = x.reshape((rows // 2, 2, batch) + x.shape[1:])
    mine = lax.dynamic_index_in_dim(by_core, core, 1, False)
    other = lax.dynamic_index_in_dim(by_core, 1 - core, 1, False)
    return add_pairs(*(a.reshape((-1,) + x.shape[1:]) for a in (mine, other)))


def add_pairs(mine, other):
    rows, batch = lax.axis_size("rows"), lax.axis_size("batch")
    other = lax.ppermute(other, "rows", [(i, i ^ 1) for i in range(rows)])
    pairs = (mine.astype(F32) + other.astype(F32)).astype(BF)
    groups = [
        [(2 * chip + k) * batch + b for chip in range(rows // 2) for b in range(batch)]
        for k in range(2)
    ]
    return pairs, lambda a: lax.all_to_all(a, AXES, 0, 0, axis_index_groups=groups, tiled=True)


def gather_copies(copies):
    return lax.all_to_all(copies, AXES, 0, 0, tiled=True)


def with_vectors(parts, vectors):
    rows = parts[0].shape[1]
    flat = vectors.reshape(1, rows, -1)
    flat = jnp.broadcast_to(flat, (parts[0].shape[0],) + flat.shape[1:])
    return jnp.concatenate(list(parts) + [flat], 2)


def ring(x, by):
    devices = lax.axis_size("rows")
    return lax.ppermute(x, "rows", [(i, (i + by) % devices) for i in range(devices)])


def norm_parts(x):
    centred = x - jnp.mean(x, -1, keepdims=True)
    rstd = lax.rsqrt(jnp.mean(centred * centred, -1, keepdims=True) + EPSILON)
    return centred * rstd, rstd


def norm_back(dy, xhat, rstd, gain):
    scaled = dy * gain
    first = jnp.mean(scaled, -1, keepdims=True)
    second = jnp.mean(scaled * xhat, -1, keepdims=True)
    return (scaled - first - xhat * second) * rstd


def head_mask():
    rows, lanes = np.arange(256)[:, None], np.arange(256)[None, :]
    return (rows // 64 == (lanes % 128) // 32).astype(np.float32)


def pair_of(ref, pair, column):
    first = ref[pl.ds(pair * 128, 64), column : column + 128]
    second = ref[pl.ds(pair * 128 + 64, 64), column : column + 128]
    return jnp.concatenate([first, second], 1)


def blocks_of(ref, pair, column):
    first = ref[pl.ds(pair * 128, 64), column : column + 128]
    second = ref[pl.ds(pair * 128 + 64, 64), column : column + 128]
    nothing = jnp.zeros_like(first)
    return jnp.concatenate(
        [jnp.concatenate([first, nothing], 1), jnp.concatenate([nothing, second], 1)], 0
    )


def spread_heads(pair, mask):
    return jnp.concatenate([pair] * 4, 0) * mask


def offset_places(turned):
    rows, lanes = np.arange(256)[:, None], np.arange(128)[None, :] % 64
    row, col = lanes // WIN, lanes % WIN
    if turned:
        row, col = WIN - 1 - row, WIN - 1 - col
    return (rows == row * (2 * WIN - 1) + col).astype(np.float32)


def three_parts(x):
    high = x.astype(BF)
    rest = x - high.astype(F32)
    middle = rest.astype(BF)
    return high, middle, (rest - middle.astype(F32)).astype(BF)


def spread_bias(table, places, bias, factor):
    line = 2 * WIN - 1
    for head in range(8):
        row = jnp.broadcast_to(table[head : head + 1], (WIN, 256))
        turns = []
        for r in range(WIN):
            by = 256 - (WIN - 1 - r) * line - (WIN - 1)
            turns.append(pltpu.roll(row, by, 1, stride=1, stride_axis=0))
        wide = jnp.concatenate(turns, 0)
        total = 0.0
        for part in three_parts(wide):
            total = total + dot(part, places[...])
        bias[head * 64 : head * 64 + 64] = total * factor


def collect_bias(grad, places):
    line = 2 * WIN - 1
    wide = 0.0
    for part in three_parts(grad):
        wide = wide + dot(part, places)
    out = []
    for head in range(8):
        total = jnp.zeros((WIN, 256), F32)
        for r in range(WIN):
            at = head * 64 + r * WIN
            total = total + pltpu.roll(wide[at : at + WIN], r * line, 1, stride=1, stride_axis=0)
        out.append(jnp.sum(total, 0, keepdims=True))
    return jnp.concatenate(out, 0)


def attn_forward_body(
    height, scale, step_of, place, above, upper, lower, gain, shift, weight, table, places, mask,
    x_out, norm_out, xhat_out, rstd_out, qkv_out, prob_out, mix_out, xs, bias,
):
    sample, band = step_of(pl.program_id(0))
    columns = lower.shape[2]

    @pl.when(pl.program_id(0) == 0)
    def _():
        spread_bias(table, places, bias, 1.0 / scale)

    def rows_from(ref, first):
        def rows_in(r, _):
            x = pltpu.roll(ref[0, r].astype(F32), WIN // 2, 0)
            xs[:, first + r] = x.reshape(columns // WIN, WIN, 256)
            return 0

        lax.fori_loop(0, WIN // 2, rows_in, 0, unroll=True)

    @pl.when(band == 0)
    def _():
        rows_from(above, 0)

    @pl.when(band > 0)
    def _():
        rows_from(upper, 0)

    rows_from(lower, WIN // 2)

    def norm_in(k, _):
        tokens = pl.ds(k * 128, 128)
        x = xs[pl.ds(k * 2, 2)].reshape(128, 256)
        xhat, rstd = norm_parts(x)
        x_out[tokens] = x.astype(BF)
        xhat_out[tokens] = xhat.astype(BF)
        rstd_out[tokens] = jnp.broadcast_to(rstd, (128, 128))
        norm_out[tokens] = (xhat * gain[...] + shift[...]).astype(BF)
        return 0

    lax.fori_loop(0, columns // 16, norm_in, 0, unroll=8)
    for k in range(0, columns * WIN, 256):
        qkv_out[k : k + 256] = dot(norm_out[k : k + 256], weight[...]).astype(BF)

    key_at, query_at = iota((64, 128), 0), iota((64, 128), 1)
    window_at = query_at // 64
    query_at = query_at % 64
    row_base = place[0] + band * WIN
    key_row, query_row = key_at // WIN + row_base, query_at // WIN + row_base
    key_row = jnp.where(key_row < 0, key_row + height, key_row)
    query_row = jnp.where(query_row < 0, query_row + height, query_row)
    rows_differ = (key_row >= height - WIN // 2) != (query_row >= height - WIN // 2)
    row_bad = key_row >= place[1 + sample]

    def attend(pair, _):
        key_col = (pair * 2 + window_at) * WIN + key_at % WIN - WIN // 2
        query_col = (pair * 2 + window_at) * WIN + query_at % WIN - WIN // 2
        key_col = jnp.where(key_col < 0, key_col + columns, key_col)
        query_col = jnp.where(query_col < 0, query_col + columns, query_col)
        cols_differ = (key_col >= columns - WIN // 2) != (query_col >= columns - WIN // 2)
        bad = row_bad | (key_col >= place[3 + sample])
        minus = jnp.where(rows_differ | cols_differ, MASKED / scale, 0.0) + jnp.where(
            bad, MASKED / scale, 0.0
        )
        for half in range(2):
            keys = spread_heads(pair_of(qkv_out, pair, 256 + 128 * half), mask[...])
            queries = blocks_of(qkv_out, pair, 128 * half)
            scores = dot_nt(keys, queries).reshape(4, 64, 128)
            scores = scores + (bias[256 * half : 256 * half + 256].reshape(4, 64, 128) + minus[None])
            top = jnp.max(scores, 1, keepdims=True)
            raised = jnp.exp2((scores - top) * (scale * LOG2E))
            probs = raised * (1.0 / jnp.sum(raised, 1, keepdims=True))
            probs = probs.reshape(256, 128).astype(BF)
            prob_out[pair, 256 * half : 256 * half + 256] = probs
        return 0

    def mix(pair, _):
        for half in range(2):
            probs = prob_out[pair, 256 * half : 256 * half + 256]
            values = spread_heads(pair_of(qkv_out, pair, 512 + 128 * half), mask[...])
            mixed = dot_tn(probs, values).astype(BF)
            mix_out[pl.ds(pair * 128, 64), 128 * half : 128 * half + 128] = mixed[:64, :128]
            mix_out[pl.ds(pair * 128 + 64, 64), 128 * half : 128 * half + 128] = mixed[64:, 128:]
        return 0

    lax.fori_loop(0, columns // 16, attend, 0, unroll=8)
    lax.fori_loop(0, columns // 16, mix, 0, unroll=8)


def near(*arrays):
    return [pltpu.with_memory_space_constraint(a, pltpu.VMEM) for a in arrays]


def const_spec(shape):
    return pl.BlockSpec(shape, lambda *_: (0,) * len(shape))


SMALL_COST = pl.CostEstimate(flops=10**6, bytes_accessed=10**4, transcendentals=0)


def params(mib):
    return pltpu.CompilerParams(vmem_limit_bytes=mib * MIB)


def far(*arrays):
    return [pltpu.with_memory_space_constraint(a, pltpu.HBM) for a in arrays]


SMEM_SPEC = pl.BlockSpec(memory_space=pltpu.SMEM)


def band_steps(samples, bands):
    def step_of(step):
        return step % samples, bands[0] + step // samples

    return step_of, samples * len(bands)


def attn_forward(place, above, own, gain, shift, weight, table, places, mask, height, scale):
    samples, grid_rows, columns, width = own.shape
    half = WIN // 2
    bands = grid_rows // WIN
    tokens = WIN * columns
    steps = samples * bands

    def step_of(step):
        return step // bands, step % bands

    def row_block(step):
        return (step, 0)

    total = steps * tokens
    return pl.pallas_call(
        functools.partial(attn_forward_body, height, scale, step_of),
        grid=(steps,),
        in_specs=[
            SMEM_SPEC,
            pl.BlockSpec((1, half, columns, width), lambda s: (step_of(s)[0], 0, 0, 0)),
            pl.BlockSpec(
                (1, half, columns, width),
                lambda s: (step_of(s)[0], jnp.maximum(2 * step_of(s)[1] - 1, 0), 0, 0),
            ),
            pl.BlockSpec(
                (1, half, columns, width), lambda s: (step_of(s)[0], 2 * step_of(s)[1], 0, 0)
            ),
            const_spec((1, width)),
            const_spec((1, width)),
            const_spec(weight.shape),
            const_spec(table.shape),
            const_spec(places.shape),
            const_spec(mask.shape),
        ],
        out_specs=[
            pl.BlockSpec((tokens, width), row_block),
            pl.BlockSpec((tokens, width), row_block),
            pl.BlockSpec((tokens, width), row_block),
            pl.BlockSpec((tokens, 128), row_block),
            pl.BlockSpec((tokens, 3 * width), row_block),
            pl.BlockSpec((columns // 16, 512, 128), lambda s: (s, 0, 0)),
            pl.BlockSpec((tokens, width), row_block),
        ],
        out_shape=[
            pltpu.VMEM((total, width), BF),
            pltpu.HBM((total, width), BF),
            pltpu.HBM((total, width), BF),
            pltpu.HBM((total, 128), F32),
            pltpu.HBM((total, 3 * width), BF),
            pltpu.HBM((total // 128, 512, 128), BF),
            pltpu.VMEM((total, width), BF),
        ],
        scratch_shapes=[
            pltpu.VMEM((columns // WIN, WIN, WIN, width), F32),
            pltpu.VMEM((512, 128), F32),
        ],
        compiler_params=params(24),
        cost_estimate=SMALL_COST,
        name="attn_forward",
    )(place, *far(above, own, own, gain, shift), *near(weight), *far(table, places, mask))


def gelu_parts(x):
    share = 0.5 + 0.5 * lax.erf(x * 0.7071067811865476)
    bell = jnp.exp2(x * x * (-0.5 * LOG2E))
    return x * share, share + x * (bell * 0.3989422804014327)


def ffn_forward_body(
    height, step_of, place, x_ref, mix, out_w, out_b, gain, shift, up_w, up_b, down_w, down_b,
    norm_out, xhat_out, rstd_out, act_out, slope_out, sum_out, first_rows, sums,
):
    sample, band = step_of(pl.program_id(0))
    columns = sum_out.shape[2]
    chunk = 256
    chunks = columns * WIN // chunk

    def attend_sum(k, _):
        tokens = pl.ds(k * chunk, chunk)
        first = x_ref[tokens].astype(F32) + dot(mix[tokens], out_w[...]) + out_b[...]
        sums[pl.ds(k * (chunk // 64), chunk // 64)] = first.reshape(chunk // 64, WIN, WIN, 256)
        xhat, rstd = norm_parts(first)
        norm_out[tokens] = (xhat * gain[...] + shift[...]).astype(BF)
        xhat_out[tokens] = xhat.astype(BF)
        rstd_out[tokens] = jnp.broadcast_to(rstd, (chunk, 128))
        return 0

    def raise_up(k, _):
        tokens = pl.ds(k * chunk, chunk)
        for f in range(0, 1024, 256):
            raised = dot(norm_out[tokens], up_w[:, f : f + 256]) + up_b[:, f : f + 256]
            act, slope = gelu_parts(raised)
            act_out[tokens, f : f + 256] = act.astype(BF)
            slope_out[tokens, f : f + 256] = slope.astype(BF)
        return 0

    def put_down(k, _):
        tokens = pl.ds(k * chunk, chunk)
        windows = pl.ds(k * (chunk // 64), chunk // 64)
        second = dot(act_out[tokens], down_w[...]) + down_b[...]
        sums[windows] += second.reshape(chunk // 64, WIN, WIN, 256)
        return 0

    lax.fori_loop(0, chunks, attend_sum, 0, unroll=True)
    lax.fori_loop(0, chunks, raise_up, 0, unroll=True)
    lax.fori_loop(0, chunks, put_down, 0, unroll=True)
    column = iota((columns, 1), 0)

    def rows_out(r, _):
        row = place[0] + band * WIN + r
        row = jnp.where(row < 0, row + height, row)
        limit = jnp.where(row < place[1 + sample], place[3 + sample], 0)
        back = pltpu.roll(sums[:, r].reshape(columns, 256), columns - WIN // 2, 0)
        sum_out[0, r] = jnp.where(column < limit, back, 0.0).astype(BF)
        return 0

    lax.fori_loop(0, WIN, rows_out, 0, unroll=True)

    @pl.when(band == 0)
    def _():
        first_rows[0] = sum_out[0, : WIN // 2 + 1]


def ffn_forward(place, x, mix, out_w, out_b, gain, shift, up_w, up_b, down_w, down_b, height, shape):
    samples, grid_rows, columns, width = shape
    bands = grid_rows // WIN
    tokens = WIN * columns
    steps = samples * bands
    hidden = up_w.shape[1]
    total = steps * tokens

    def step_of(step):
        return step // bands, step % bands

    def row_block(step):
        return (step, 0)

    rows = [width, width, 128, hidden, hidden]
    types = [BF, BF, F32, BF, BF]
    return pl.pallas_call(
        functools.partial(ffn_forward_body, height, step_of),
        grid=(steps,),
        in_specs=[SMEM_SPEC]
        + [pl.BlockSpec((tokens, width), row_block)] * 2
        + [const_spec(a.shape) for a in (out_w, out_b, gain, shift, up_w, up_b, down_w, down_b)],
        out_specs=[pl.BlockSpec((tokens, n), row_block) for n in rows]
        + [
            pl.BlockSpec((1, WIN, columns, width), lambda s: (*step_of(s), 0, 0)),
            pl.BlockSpec((1, WIN // 2 + 1, columns, width), lambda s: (step_of(s)[0], 0, 0, 0)),
        ],
        out_shape=[pltpu.HBM((total, n), t) for n, t in zip(rows, types)]
        + [
            pltpu.HBM(shape, BF),
            jax.ShapeDtypeStruct((samples, WIN // 2 + 1, columns, width), BF),
        ],
        scratch_shapes=[pltpu.VMEM((columns // WIN, WIN, WIN, width), F32)],
        compiler_params=params(32),
        cost_estimate=SMALL_COST,
        name="ffn_forward",
    )(
        place, *near(x, mix, out_w), *far(out_b, gain, shift), *near(up_w), *far(up_b), *near(down_w),
        *far(down_b),
    )


def column_sum(x):
    return jnp.sum(x, 0, keepdims=True)


def ffn_backward_step(
    height, step, sample, band, place, above, own, act, slope, normed, xhat_ref, rstd_ref, mix, conv_w,
    out_w, gain, up_w, down_w, first_out, mixed_out,
    taps, turned, branch, low, raised_s, attn, down_acc, up_acc, out_acc, vec,
):
    columns = own.shape[2]
    tokens = columns * WIN
    half = WIN // 2
    column = iota((columns, 1), 0)

    @pl.when(step == 0)
    def _():
        for ref in (down_acc, up_acc, out_acc, vec):
            ref[...] = jnp.zeros_like(ref)
        for k in range(9):
            at = 256 * (k % 3)
            turned[k // 3, :, at : at + 256] = conv_w[k, 0]

    start = place[0] + half
    not_first = start != 0
    lanes = (0, 256, 512)
    top = band == 0
    before = jnp.where(top, jnp.where(not_first, start, height), start + band * WIN) - half - 1

    def put_group(group):
        for k in range(half + 2):
            row = before + k if group == 0 else start + band * WIN + k - 1
            at = band * WIN + (group - 1) * half - 1 + k
            source = own[0, jnp.maximum(at, 0)]
            allowed = True
            if group == 0 and k <= half:
                source = jnp.where(top, above[0, k], source)
            elif group == 0:
                row = start + band * WIN
                allowed = ~top | not_first
            elif k == 0:
                source = jnp.where(top, above[0, ABOVE_LAST], source)
                allowed = ~top | not_first
            limit = row_limit(place, sample, row, allowed)
            put_taps(source, limit, taps, group * (half + 2) + k, lanes)

    put_group(0)
    for group in range(2):
        if group == 0:
            put_group(1)
        total = 0.0
        for a in range(3):
            at = group * (half + 2) + 2 - a
            piece = taps[at : at + half].reshape(half * columns, 768)
            total = total + dot_nt(piece, turned[a])
        for k in range(half):
            row = place[0] + band * WIN + group * half + k
            row = jnp.where(row < 0, row + height, row)
            limit = row_limit(place, sample, row)
            part = jnp.where(column < limit, total[k * columns : (k + 1) * columns], 0.0)
            part = pltpu.roll(part, half, 0)
            branch[:, group * half + k] = part.reshape(columns // WIN, WIN, 256)

    chunk = 256
    windows = chunk // 64
    for k in range(tokens // chunk):
        at = slice(k * chunk, (k + 1) * chunk)
        upper = branch[k * windows : (k + 1) * windows].reshape(chunk, 256)
        low[at] = upper.astype(BF)
        vec[0:1] += column_sum(upper.astype(BF).astype(F32))
    for k in range(tokens // chunk):
        at = slice(k * chunk, (k + 1) * chunk)
        for f in range(0, 1024, 256):
            wide = slice(f, f + 256)
            raised = (dot_nt(low[at], down_w[wide]) * slope[at, wide].astype(F32)).astype(BF)
            raised_s[at, wide] = raised
            row = 4 + f // 256
            vec[row : row + 1] += column_sum(raised.astype(F32))
    for k in range(tokens // chunk):
        at = slice(k * chunk, (k + 1) * chunk)
        dy = dot_nt(raised_s[at], up_w[...])
        xhat = xhat_ref[at].astype(F32)
        rstd = rstd_ref[at]
        rstd = jnp.concatenate([rstd, rstd], 1)
        upper = branch[k * windows : (k + 1) * windows].reshape(chunk, 256)
        first = upper + norm_back(dy, xhat, rstd, gain[...])
        first_out[at] = first
        attn[at] = first.astype(BF)
        vec[1:2] += column_sum(dy * xhat)
        vec[2:3] += column_sum(dy)
        vec[3:4] += column_sum(first.astype(BF).astype(F32))
    for k in range(tokens // chunk):
        at = slice(k * chunk, (k + 1) * chunk)
        mixed_out[at] = dot_nt(attn[at], out_w[...]).astype(BF)
    low_t = low[...].T
    normed_t = normed[...].T
    for f in range(0, 1024, 256):
        wide = slice(f, f + 256)
        down_acc[:, wide] += dot(low_t, act[:, wide])
        up_acc[:, wide] += dot(normed_t, raised_s[:, wide])
    out_acc[...] += dot(mix[...].T, attn[...])


def ffn_backward_end(down_out, up_out, out_out, vec_out, down_acc, up_acc, out_acc, vec):
    for f in range(0, 1024, 256):
        wide = slice(f, f + 256)
        down_out[wide] = down_acc[:, wide].T.astype(BF)
        up_out[:, wide] = up_acc[:, wide].astype(BF)
    out_out[...] = out_acc[...].astype(BF)
    vec_out[...] = vec[...].astype(BF)


def send_rows(core, batch, mine, other, down_rows, down_acc, out_acc, up_acc, qkv_acc, vectors):
    for f in range(0, 1024, 256):
        turned = down_acc[:, f : f + 256].T.reshape(8, 4, 8, 256)
        for k in range(4):
            piece = turned[:, k].reshape(64, 256)
            down_rows[f // 4 : f // 4 + 64, 256 * k : 256 * k + 256] = piece.astype(BF)
    count = 8 * batch
    wide_vectors = jnp.concatenate([vectors] * batch, 0).astype(BF)

    def put(target, k):
        for chip in range(256 // (2 * count)):
            rows = slice((2 * chip + k) * count, (2 * chip + k + 1) * count)
            to = slice(chip * count, (chip + 1) * count)
            at = 0
            for ref in (down_rows, out_acc, up_acc, qkv_acc):
                target[to, at : at + ref.shape[1]] = ref[rows].astype(BF)
                at += ref.shape[1]
            target[to, at:] = wide_vectors

    for k in range(2):

        @pl.when(core == k)
        def _():
            put(mine, k)
            put(other, 1 - k)


def backward_body(height, scale, step_of, batch, *refs):
    place, above, own, *refs = refs
    ffn_rows, refs = refs[:6], refs[6:]
    attn_rows, refs = refs[:5], refs[5:]
    ffn_consts, refs = refs[:5], refs[5:]
    (weight, gain, mask, conv_vec, places), refs = refs[:5], refs[5:]
    input_out, up_out, *refs = refs
    outs, refs = (refs[:2], refs[2:]) if batch else (refs[:6], refs[6:])
    ffn_scratch, (first, mixed, qkv_acc, table_acc, vec_acc, grads, score_grads, sums, down_rows) = (
        refs[:10], refs[10:],
    )
    step = pl.program_id(0)
    sample, band = step_of(step)
    columns = input_out.shape[2]
    half = WIN // 2

    @pl.when(step == 0)
    def _():
        for ref in (qkv_acc, table_acc, vec_acc):
            ref[...] = jnp.zeros_like(ref)

    ffn_backward_step(
        height, step, sample, band, place, above, own, *ffn_rows, *ffn_consts, first, mixed,
        *ffn_scratch,
    )
    qkv, prob, normed, xhat_ref, rstd_ref = attn_rows
    attn_backward_step(
        scale, mixed, qkv, prob, normed, xhat_ref, rstd_ref, first, weight, gain, mask,
        qkv_acc, table_acc, vec_acc, grads, score_grads, sums,
    )

    def row_out(r):
        return pltpu.roll(sums[:, r].reshape(columns, 256), columns - half, 0)

    @pl.when(band == 0)
    def _():
        for r in range(half):
            up_out[0, r] = row_out(r).astype(BF)
            input_out[0, r] = row_out(half + r)

    @pl.when(band > 0)
    def _():
        for r in range(WIN):
            input_out[0, band * WIN - half + r] = row_out(r)

    @pl.when(step == pl.num_programs(0) - 1)
    def _():
        table = collect_bias(table_acc[...], places[...])
        rest = jnp.concatenate([vec_acc[0:2], conv_vec[0:1], jnp.zeros((5, 256), F32)], 0)
        vectors = jnp.concatenate([table, rest], 1)
        down_acc, up_acc, out_acc, vec = ffn_scratch[6:]
        if batch:
            vectors = jnp.concatenate([vec[...], vectors], 1)
            send_rows(
                place[place.shape[0] - 1], batch, *outs, down_rows, down_acc, out_acc, up_acc, qkv_acc,
                vectors,
            )
            return
        *ffn_outs, qkv_out, vec_out = outs
        ffn_backward_end(*ffn_outs, down_acc, up_acc, out_acc, vec)
        for f in range(0, 768, 256):
            qkv_out[:, f : f + 256] = qkv_acc[:, f : f + 256].astype(BF)
        vec_out[...] = vectors.astype(BF)


def attn_backward_step(
    scale, mixed, qkv, prob, normed, xhat_ref, rstd_ref, first, weight, gain, mask,
    qkv_acc, table_acc, vec_acc, grads, score_grads, sums,
):
    tokens = qkv.shape[0]
    columns = tokens // WIN

    def attend(pair, _):
        head_at = mask[...]
        for half in range(2):
            lanes = slice(256 * half, 256 * half + 256)
            low = prob[pair, lanes]
            mixed_blocks = blocks_of(mixed, pair, 128 * half)
            values = spread_heads(pair_of(qkv, pair, 512 + 128 * half), head_at)
            prob_grad = dot_nt(values, mixed_blocks).reshape(4, 64, 128)
            probs = low.astype(F32).reshape(4, 64, 128)
            shared = jnp.sum(prob_grad * probs, 1, keepdims=True)
            score_grad = (probs * (prob_grad - shared)).astype(BF).reshape(256, 128)
            table_acc[lanes] += score_grad.astype(F32)
            score_grads[pair, lanes] = score_grad
        return 0

    def project(pair, _):
        head_at = mask[...]
        for half in range(2):
            lanes = slice(256 * half, 256 * half + 256)
            low = prob[pair, lanes]
            mixed_blocks = blocks_of(mixed, pair, 128 * half)
            score_grad = score_grads[pair, lanes]
            keys = spread_heads(pair_of(qkv, pair, 256 + 128 * half), head_at)
            queries = blocks_of(qkv, pair, 128 * half)
            query_grad = (dot_tn(score_grad, keys) * scale).astype(BF)
            out = slice(128 * half, 128 * half + 128)
            grads[pl.ds(pair * 128, 64), out] = query_grad[:64, :128]
            grads[pl.ds(pair * 128 + 64, 64), out] = query_grad[64:, 128:]
            wide = head_at.astype(F32)
            key_grad = (dot(score_grad, queries) * wide).reshape(4, 64, 256)
            key_grad = (jnp.sum(key_grad, 0) * scale).astype(BF)
            out = slice(256 + 128 * half, 256 + 128 * half + 128)
            grads[pl.ds(pair * 128, 64), out] = key_grad[:, :128]
            grads[pl.ds(pair * 128 + 64, 64), out] = key_grad[:, 128:]
            value_grad = (dot(low, mixed_blocks) * wide).reshape(4, 64, 256)
            value_grad = jnp.sum(value_grad, 0).astype(BF)
            out = slice(512 + 128 * half, 512 + 128 * half + 128)
            grads[pl.ds(pair * 128, 64), out] = value_grad[:, :128]
            grads[pl.ds(pair * 128 + 64, 64), out] = value_grad[:, 128:]
        return 0

    lax.fori_loop(0, columns // 16, attend, 0, unroll=8)
    lax.fori_loop(0, columns // 16, project, 0, unroll=8)
    for f in range(0, 768, 256):
        qkv_acc[:, f : f + 256] += dot_tn(normed[...], grads[:, f : f + 256])

    def part(k, _):
        at = pl.ds(k * 256, 256)
        dy = dot_nt(grads[at], weight[...])
        xhat = xhat_ref[at].astype(F32)
        rstd = rstd_ref[at]
        rstd = jnp.concatenate([rstd, rstd], 1)
        total = first[at] + norm_back(dy, xhat, rstd, gain[...])
        sums[pl.ds(k * 4, 4)] = total.reshape(4, WIN, WIN, 256)
        vec_acc[0:1] += column_sum(dy * xhat)
        vec_acc[1:2] += column_sum(dy)
        return 0

    lax.fori_loop(0, tokens // 256, part, 0, unroll=True)


def backward(place, above, own, ffn_rows, attn_rows, ffn_consts, attn_consts, height, scale, batch):
    samples, grid_rows, columns, width = own.shape
    bands = grid_rows // WIN
    tokens = WIN * columns
    steps = samples * bands
    hidden = ffn_rows[0].shape[1]
    half = WIN // 2

    def step_of(step):
        return step // bands, step % bands

    def row_block(step):
        return (step, 0)

    def sample_block(step):
        return (step_of(step)[0], 0, 0, 0)

    in_specs = [
        SMEM_SPEC,
        pl.BlockSpec((1,) + above.shape[1:], sample_block),
        pl.BlockSpec((1,) + own.shape[1:], sample_block),
    ]
    in_specs += [pl.BlockSpec((tokens, a.shape[1]), row_block) for a in (*ffn_rows, *attn_rows)]
    in_specs[10] = pl.BlockSpec((columns // 16, 512, 128), lambda s: (s, 0, 0))
    in_specs += [pl.BlockSpec((9, 1, width, width), lambda s: (0, 0, 0, 0))]
    in_specs += [const_spec(a.shape) for a in (*ffn_consts[1:], *attn_consts)]
    outs = [(own.shape, F32), ((samples, half, columns, width), BF)]
    if batch:
        outs += [((width // 2, 2 * hidden + 7 * width), BF)] * 2
    else:
        outs += [
            ((hidden, width), BF), ((width, hidden), BF), ((width, width), BF), ((8, width), BF),
            ((width, 3 * width), BF), ((8, 2 * width), BF),
        ]
    out_specs = [const_spec(a) for a, _ in outs]
    out_specs[0] = pl.BlockSpec((1,) + own.shape[1:], sample_block)
    out_specs[1] = pl.BlockSpec((1, half, columns, width), sample_block)
    return pl.pallas_call(
        functools.partial(backward_body, height, scale, step_of, batch),
        grid=(steps,),
        in_specs=in_specs,
        out_specs=out_specs,
        out_shape=[pltpu.HBM(a, t) for a, t in outs[:2]]
        + [jax.ShapeDtypeStruct(a, t) for a, t in outs[2:]],
        scratch_shapes=[
            pltpu.VMEM((WIN + 4, columns, 3 * width), BF),
            pltpu.VMEM((3, width, 3 * width), BF),
            pltpu.VMEM((columns // WIN, WIN, WIN, width), F32),
            pltpu.VMEM((tokens, width), BF),
            pltpu.VMEM((tokens, hidden), BF),
            pltpu.VMEM((tokens, width), BF),
            pltpu.VMEM((width, hidden), F32),
            pltpu.VMEM((width, hidden), F32),
            pltpu.VMEM((width, width), F32),
            pltpu.VMEM((8, width), F32),
            pltpu.VMEM((tokens, width), F32),
            pltpu.VMEM((tokens, width), BF),
            pltpu.VMEM((width, 3 * width), F32),
            pltpu.VMEM((512, 128), F32),
            pltpu.VMEM((8, width), F32),
            pltpu.VMEM((tokens, 3 * width), BF),
            pltpu.VMEM((columns // 16, 512, 128), BF),
            pltpu.VMEM((columns // WIN, WIN, WIN, width), F32),
            pltpu.VMEM((width, hidden), BF),
        ],
        compiler_params=params(BACK_MIB),
        cost_estimate=pl.CostEstimate(
            flops=4 * 10**10, bytes_accessed=10**7, transcendentals=0
        ),
        name="backward",
    )(
        place, *far(above, own, *ffn_rows, *attn_rows, *ffn_consts, *attn_consts),
    )


def shifted(row, by):
    columns = row.shape[0]
    moved = pltpu.roll(row, by % columns, 0)
    place = iota((8, 1), 0)
    if by == 1:
        return jnp.concatenate([jnp.where(place == 0, 0.0, moved[:8]), moved[8:]], 0)
    return jnp.concatenate([moved[:-8], jnp.where(place == 7, 0.0, moved[-8:])], 0)


def pack_near_body(qkv, out_w, up, down, near):
    rows = qkv.shape[0]
    at = 0
    for ref in (qkv, out_w, up):
        near[:, at : at + ref.shape[1]] = ref[...].astype(BF)
        at += ref.shape[1]
    for k in range(down.shape[0] // rows):
        near[:, at : at + down.shape[1]] = down[k * rows : (k + 1) * rows].astype(BF)
        at += down.shape[1]


def pack_near(qkv, out_w, up, down):
    rows = qkv.shape[0]
    lanes = (qkv.size + out_w.size + up.size + down.size) // rows
    return pl.pallas_call(
        pack_near_body,
        out_shape=jax.ShapeDtypeStruct((rows, lanes), BF),
        compiler_params=params(16),
        cost_estimate=SMALL_COST,
        name="pack_near",
    )(*far(qkv, out_w, up, down))


def unpack_near_body(place_ref, order, held, qkv, out_w, up, down):
    devices, rows, _ = held.shape
    me = place_ref[place_ref.shape[0] - 2]
    count = max(16 // rows, 1)

    def some(k, _):
        pieces = [held[order[(k * count + n) ^ me]] for n in range(count)]
        at = 0
        place = pl.ds(pl.multiple_of(k * count * rows, count * rows), count * rows)
        for ref in (qkv, out_w, up):
            lanes = slice(at, at + ref.shape[1])
            ref[place] = jnp.concatenate([piece[:, lanes] for piece in pieces], 0)
            at = lanes.stop
        width = down.shape[1]
        parts = down.shape[0] // (devices * rows)
        tall = [
            piece[:, at + n * width : at + (n + 1) * width] for piece in pieces for n in range(parts)
        ]
        size = count * rows * parts
        down[pl.ds(pl.multiple_of(k * size, size), size)] = jnp.concatenate(tall, 0)
        return 0

    lax.fori_loop(0, devices // count, some, 0, unroll=4)


def unpack_near(place, order, held, weights):
    devices = held.shape[0]
    return pl.pallas_call(
        unpack_near_body,
        in_specs=[SMEM_SPEC, SMEM_SPEC, pl.BlockSpec(memory_space=pltpu.VMEM)],
        out_shape=[pltpu.VMEM((devices * w.shape[0], w.shape[1]), BF) for w in weights],
        compiler_params=params(24),
        cost_estimate=SMALL_COST,
        name="unpack_near",
    )(place, order, held)


def last_sums_body(parts, down, out_w, up, qkv, *vectors):
    count, rows, lanes = parts.shape
    total = parts[0].astype(F32)
    for k in range(1, count):
        total = total + parts[k].astype(F32)
    width = down.shape[1]
    for k in range(down.shape[0] // rows):
        down[k * rows : (k + 1) * rows] = total[:, k * width : (k + 1) * width]
    at = down.size // rows
    for ref in (out_w, up, qkv):
        ref[...] = total[:, at : at + ref.shape[1]]
        at += ref.shape[1]

    def vector(row, group):
        row, lane = divmod((row * 3 + group) * width, lanes - at)
        return total[row : row + 1, at + lane : at + lane + width]

    singles, (up_bias, table), more = vectors[:4], vectors[4:6], vectors[6:]
    for k, ref in enumerate(singles):
        ref[...] = vector(k, 0)
    for k in range(4):
        up_bias[:, k * width : (k + 1) * width] = vector(4 + k, 0)
    for k in range(8):
        table[k : k + 1] = vector(k, 1)
    for k, ref in enumerate(more):
        ref[...] = vector(k, 2)


def last_sums(parts, down, rest):
    width = down[1]
    vectors = [(1, width)] * 4 + [(1, 4 * width), (8, width)] + [(1, width)] * 3
    shapes = (down, *rest, *vectors)
    return pl.pallas_call(
        last_sums_body,
        out_shape=[jax.ShapeDtypeStruct(a, F32) for a in shapes],
        compiler_params=params(24),
        cost_estimate=SMALL_COST,
        name="last_sums",
    )(parts)


def sum_body(parts, out):
    total = parts[0].astype(F32)
    for k in range(1, parts.shape[0]):
        total = total + parts[k].astype(F32)
    out[...] = total


def sum_parts(parts):
    return pl.pallas_call(
        sum_body,
        out_shape=jax.ShapeDtypeStruct(parts.shape[1:], F32),
        compiler_params=params(16),
        cost_estimate=SMALL_COST,
        name="sum_parts",
    )(parts)


def copies_body(x, out):
    low = x[...].astype(BF)
    for k in range(out.shape[0]):
        out[k] = low


def make_copies(x, count):
    return pl.pallas_call(
        copies_body,
        out_shape=jax.ShapeDtypeStruct((count,) + x.shape, BF),
        compiler_params=params(16),
        cost_estimate=SMALL_COST,
        name="make_copies",
    )(*far(x))


def row_limit(place, sample, row, allowed=True):
    return jnp.where((row < place[1 + sample]) & allowed, place[3 + sample], 0)


def put_taps(row, limit, target, at, lanes):
    column = iota((row.shape[0], 1), 0)
    wide = jnp.where(column < limit, row.astype(F32), 0.0)
    target[at, :, lanes[0] : lanes[0] + 256] = shifted(wide, -1).astype(BF)
    target[at, :, lanes[1] : lanes[1] + 256] = wide.astype(BF)
    target[at, :, lanes[2] : lanes[2] + 256] = shifted(wide, 1).astype(BF)


ABOVE_LAST = WIN // 2
ABOVE_HIDDEN = WIN // 2 + 1


def own_taps(height, place, above, own, below, taps, at):
    sample = pl.program_id(0)
    rows = own.shape[1]
    start = place[0] + WIN // 2

    def put(r):
        allowed = True
        if r == 0:
            source, allowed = above[0, ABOVE_LAST], start != 0
        elif r <= rows:
            source = own[0, r - 1]
        else:
            source, allowed = below[0, 0], start + rows != height
        limit = row_limit(place, sample, start + r - 1, allowed)
        put_taps(source, limit, taps, at + r, (0, 256, 512))

    return put


def conv_weight_body(
    height, place, above, own, below, sums, hidden, out, vec, taps, held, acc, acc_hidden
):
    sample = pl.program_id(0)

    @pl.when(sample == 0)
    def _():
        for ref in (acc, acc_hidden, vec):
            ref[...] = jnp.zeros_like(ref)

    rows, columns = own.shape[1:3]
    half = WIN // 2
    column = iota((columns, 1), 0)
    start = place[0] + half
    not_first = start != 0

    before = jnp.where(not_first, start, height) - half - 1
    put = own_taps(height, place, above, own, below, taps, half + 2)
    for r in range(half + 1):
        limit = row_limit(place, sample, before + r)
        put_taps(above[0, r], limit, taps, r, (0, 256, 512))
    limit = row_limit(place, sample, start, not_first)
    put_taps(own[0, 0], limit, taps, half + 1, (0, 256, 512))

    def add(source, first, acc):
        count = source.shape[0]
        turned = source.reshape(count * columns, 256).T
        for a in range(3):
            piece = taps[first + 2 - a : first + 2 - a + count].reshape(count * columns, 768)
            acc[a] += dot(turned, piece)

    put(0)
    put(1)
    add(sums[0, :half], 0, acc)
    step = 8
    for r in range(0, rows, step):
        for k in range(r, r + step):
            put(k + 2)
            limit = row_limit(place, sample, start + k)
            held[k] = jnp.where(column < limit, hidden[0, k].astype(F32), 0.0).astype(BF)
            vec[0:1] += jnp.sum(taps[half + 3 + k, :, 256:512].astype(F32), 0, keepdims=True)
        add(held[r : r + step], half + 2 + r, acc_hidden)
        last = min(r + step, rows - half)
        add(sums[0, half + r : half + last], half + 2 + r, acc)

    @pl.when(sample == pl.num_programs(0) - 1)
    def _():
        for k in range(9):
            at = 256 * (k % 3)
            out[k, 0] = acc[k // 3, :, at : at + 256].astype(BF)
            out[k, 1] = acc_hidden[k // 3, :, at : at + 256].astype(BF)


def field_spec(a):
    return pl.BlockSpec((1,) + a.shape[1:], lambda s: (s, 0, 0, 0))


def conv_call(
    body, name, mib, place, fields, consts, height, out_specs, out_shape, scratch, cost=None
):
    return pl.pallas_call(
        functools.partial(body, height),
        grid=(fields[0][1].shape[0],),
        in_specs=[SMEM_SPEC] + [s for s, _ in fields] + [s for s, _ in consts],
        out_specs=out_specs,
        out_shape=out_shape,
        scratch_shapes=scratch,
        compiler_params=params(mib),
        cost_estimate=cost or SMALL_COST,
        name=name,
    )(place, *[a for _, a in fields], *far(*[a for _, a in consts]))


def whole(a):
    return field_spec(a), far(a)[0]


def conv_weight(place, grads, sums, hidden, height):
    _, rows, columns, width = sums.shape
    shape = (9, 2, width, width)
    acc = pltpu.VMEM((3, width, 3 * width), F32)
    return conv_call(
        conv_weight_body, "conv_weight", 34, place, [*map(whole, grads), whole(sums), whole(hidden)], (),
        height, [const_spec(shape), const_spec((8, width))],
        [jax.ShapeDtypeStruct(shape, BF), jax.ShapeDtypeStruct((8, width), F32)],
        [
            pltpu.VMEM((rows + WIN, columns, 3 * width), BF),
            pltpu.VMEM((rows, columns, width), BF),
            acc,
            acc,
        ],
        pl.CostEstimate(flops=2 * 10**10, bytes_accessed=10**7, transcendentals=0),
    )


def conv_data_body(height, place, above, own, below, weight, out, taps, turned):
    sample = pl.program_id(0)
    columns = own.shape[2]
    column = iota((columns, 1), 0)

    @pl.when(sample == 0)
    def _():
        for k in range(9):
            at = 256 * (k % 3)
            turned[k // 3, :, at : at + 256] = weight[k, 0]

    put = own_taps(height, place, above, own, below, taps, 0)
    for r in range(2):
        put(r)
    for r in range(0, own.shape[1], 4):
        for k in range(r + 2, r + 6):
            put(k)
        total = 0.0
        for a in range(3):
            piece = taps[r + 2 - a : r + 6 - a].reshape(4 * columns, 768)
            total = total + dot_nt(piece, turned[a])
        for k in range(4):
            limit = row_limit(place, sample, place[0] + WIN // 2 + r + k)
            part = total[k * columns : (k + 1) * columns]
            out[0, r + k] = jnp.where(column < limit, part, 0.0)


def conv_data(place, grads, weight, height):
    own = grads[1]
    width = own.shape[-1]
    weight_spec = pl.BlockSpec((9, 1, width, width), lambda s: (0, 1, 0, 0))
    return conv_call(
        conv_data_body, "conv_data", 28, place, [whole(a) for a in grads], ((weight_spec, weight),),
        height, field_spec(own), jax.ShapeDtypeStruct(own.shape, F32),
        [
            pltpu.VMEM((own.shape[1] + 2, own.shape[2], 3 * width), BF),
            pltpu.VMEM((3, width, 3 * width), BF),
        ],
        pl.CostEstimate(flops=10**10, bytes_accessed=10**7, transcendentals=0),
    )


def conv_forward_body(
    height, place, sums, sums_below, above, hidden, below, weight, bias, out, taps
):
    sample = pl.program_id(0)
    rows, columns = out.shape[1:3]
    column = iota((columns, 1), 0)
    half = WIN // 2
    start = place[0] + half
    not_first, not_last = start != 0, start + rows != height

    def put(r):
        allowed = True
        if r == 0:
            first, second, allowed = sums[0, half - 1], above[0, ABOVE_HIDDEN], not_first
        elif r <= rows:
            first, second = None, hidden[0, r - 1]
            if r <= rows - half:
                first = sums[0, half + r - 1]
            else:
                first = sums_below[0, r - 1 - rows + half]
        else:
            first, second, allowed = sums_below[0, half], below[0, 1], not_last
        limit = row_limit(place, sample, start + r - 1, allowed)
        put_taps(first, limit, taps, r, (1024, 512, 0))
        put_taps(second, limit, taps, r, (1280, 768, 256))

    for r in range(2):
        put(r)
    for r in range(0, rows, 4):
        for k in range(r + 2, r + 6):
            put(k)
        total = bias[...]
        for a in range(3):
            piece = taps[r + a : r + a + 4].reshape(4 * columns, 1536)
            total = total + dot(piece, weight[a * 1536 : (a + 1) * 1536])
        for k in range(4):
            limit = row_limit(place, sample, start + r + k)
            part = total[k * columns : (k + 1) * columns]
            out[0, r + k] = jnp.where(column < limit, part, 0.0).astype(BF)


def conv_forward(place, sums, sums_below, hidden, weight, bias, height):
    samples, rows, columns, width = sums.shape
    fields = (*near(sums), *far(sums_below, *hidden))
    return pl.pallas_call(
        functools.partial(conv_forward_body, height),
        grid=(samples,),
        in_specs=[SMEM_SPEC]
        + [field_spec(a) for a in fields]
        + [const_spec(weight.shape), const_spec(bias.shape)],
        out_specs=field_spec(sums),
        out_shape=jax.ShapeDtypeStruct(sums.shape, BF),
        scratch_shapes=[pltpu.VMEM((rows + 2, columns, 6 * width), BF)],
        compiler_params=params(32),
        cost_estimate=SMALL_COST,
        name="conv_forward",
    )(place, *fields, *far(weight, bias))


def shards(
    layer_input,
    hidden_state,
    crop_rows,
    crop_cols,
    first_gain,
    first_shift,
    qkv_weight,
    bias_table,
    output_weight,
    output_bias,
    second_gain,
    second_shift,
    up_weight,
    up_bias,
    down_weight,
    down_bias,
    conv_weight_in,
    conv_bias,
    cotangent,
):
    samples, grid_rows, columns, width = layer_input.shape
    shape = layer_input.shape
    heads = bias_table.shape[1]
    scale = float((width // heads) ** (-0.5))
    half = WIN // 2
    devices = device_count()
    row_devices = lax.axis_size("rows")
    height = grid_rows * row_devices
    row_place = lax.axis_index("rows")
    row_start = row_place * grid_rows
    place = jnp.concatenate(
        [
            (row_start - half)[None], crop_rows, crop_cols, device_index()[None], (row_place % 2)[None],
        ]
    ).astype(jnp.int32)

    hidden_width = up_weight.shape[1]

    def vec(v):
        return v.reshape(1, -1)

    input_above = ring(layer_input[:, grid_rows - half :], 1)
    rows_out, rows_down = output_weight.shape[0], down_weight.shape[0]
    weights = pack_near(qkv_weight, output_weight, up_weight, down_weight)
    offsets = bias_table.shape[0]

    def beside(held):
        grad, hidden, weight, table = after(
            (cotangent, hidden_state, conv_weight_in, bias_table), held
        )
        halo_above = jnp.concatenate([grad[:, grid_rows - half - 1 :], hidden[:, grid_rows - 1 :]], 1)
        halo_below = jnp.concatenate([grad[:, :1], hidden[:, :1]], 1)
        table = jnp.pad(table.T, ((0, 0), (0, 256 - offsets)))
        return halo_above, halo_below, make_copies(weight, devices), table, input_above, place

    held, order, (halo_above, halo_below, conv_copies, table, *_) = gather_steps(weights, beside)
    halo_above, halo_below, conv_copies = after((halo_above, halo_below, conv_copies), held)
    halo_above, halo_below = ring(halo_above, 1), ring(halo_below, -1)
    grads = (halo_above, cotangent, halo_below)
    conv_full = gather_copies(conv_copies).reshape(-1, width)

    qkv_full, output_full, up_full, down_full = unpack_near(
        place, order, held, (qkv_weight, output_weight, up_weight, down_weight)
    )
    mask = jnp.asarray(head_mask(), BF)

    x, normed, xhat, rstd, qkv, prob, mix = attn_forward(
        place, input_above, layer_input, vec(first_gain), vec(first_shift), qkv_full, table,
        jnp.asarray(offset_places(False), BF), mask, height, scale,
    )
    normed_2, xhat_2, rstd_2, act, slope, sums, sums_first = ffn_forward(
        place, x, mix, output_full, vec(output_bias), vec(second_gain), vec(second_shift),
        up_full, vec(up_bias), down_full, vec(down_bias), height, shape,
    )
    conv_local, conv_bias_part = conv_weight(place, grads, sums, hidden_state, height)
    conv_local, exchange = scatter_pairs(conv_local.reshape(devices, -1, width))
    conv_all = exchange(conv_local)
    sums_below = ring(after(sums_first, conv_local), -1)
    conv_blocks = after(conv_full.reshape(9, 2, width, width), conv_local)
    input_grad, input_up, *last_parts = backward(
        place, halo_above, cotangent,
        (act, slope, normed_2, xhat_2, rstd_2, mix),
        (qkv, prob, normed, xhat, rstd),
        (conv_blocks, output_full, vec(second_gain), up_full, down_full),
        (
            qkv_full, vec(first_gain), mask, conv_bias_part,
            jnp.asarray(offset_places(True), BF).T,
        ),
        height, scale, lax.axis_size("batch") if rows_out == 8 else 0,
    )
    last_parts = after(tuple(last_parts), sums_below)
    if rows_out == 8:
        last_local, exchange = add_pairs(*(a.reshape(-1, rows_out, a.shape[1]) for a in last_parts))
    else:
        down_acc, up_acc, out_acc, vec_ffn, qkv_acc, vec_attn = last_parts
        down_local = down_acc.reshape(devices, -1, rows_out, width).transpose(0, 2, 1, 3)
        parts = [
            down_local.reshape(devices, rows_out, -1),
            *(a.reshape(devices, rows_out, -1) for a in (out_acc, up_acc, qkv_acc)),
        ]
        last_local, exchange = scatter_pairs(
            with_vectors(parts, jnp.concatenate([vec_ffn, vec_attn], 1))
        )
    last_all = exchange(last_local)
    input_from_below = ring(after(input_up, last_local), -1)
    hidden_grad = conv_data(after(place, last_local), grads, conv_blocks, height)
    layer_output = conv_forward(
        after(place, hidden_grad), sums, sums_below, (halo_above, hidden_state, halo_below),
        conv_full, vec(conv_bias), height,
    )

    input_grad = lax.dynamic_update_slice(
        after(input_grad, layer_output), input_from_below.astype(F32), (0, grid_rows - half, 0, 0)
    )

    conv_weight_grad = sum_parts(conv_all)
    down_weight_grad, output_weight_grad, up_weight_grad, qkv_weight_grad, *vectors = last_sums(
        last_all,
        (rows_down, width),
        [(rows_out, width), (rows_out, hidden_width), (rows_out, 3 * width)],
    )
    bias_table_grad = vectors.pop(5)[:, :offsets][:, ::-1].T
    (
        down_bias_grad, second_gain_grad, second_shift_grad, output_bias_grad, up_bias_grad,
        first_gain_grad, first_shift_grad, conv_bias_grad,
    ) = (v.reshape(-1) for v in vectors)
    return (
        layer_output,
        input_grad,
        hidden_grad,
        first_gain_grad,
        first_shift_grad,
        qkv_weight_grad,
        bias_table_grad,
        output_weight_grad,
        output_bias_grad,
        second_gain_grad,
        second_shift_grad,
        up_weight_grad,
        up_bias_grad,
        down_weight_grad,
        down_bias_grad,
        conv_weight_grad,
        conv_bias_grad,
    )


def solution(mesh):
    field = P("batch", "rows", None, None)
    weight = P(AXES, None)
    in_specs = (
        field, field, P("batch"), P("batch"), P(), P(), weight, P(), weight, P(), P(), P(),
        weight, P(), weight, P(), weight, P(), field,
    )
    out_specs = (
        field, field, field, P(), P(), weight, P(), weight, P(), P(), P(), weight, P(), weight,
        P(), weight, P(),
    )
    return jax.shard_map(shards, mesh=mesh, in_specs=in_specs, out_specs=out_specs, check_vma=False)
```
